128 devices in a mesh: blk: 64 (over y_lo, z, x, core), head: 2 (over y_hi).
Axes of the slice: x: 4, y: 4 (y_hi: 2, y_lo: 2; y = y_hi * 2 + y_lo), z: 4, core: 2. Of those that a mesh axis runs over, the one named last changes fastest.
Arguments:
- tokens: bfloat16 [16384, 1536], P(('blk', 'head')), may hold values from -6 to 6
- segments: int32 [16384], replicated, may hold values from 0 to 31, as said below
- attn_gain: bfloat16 [1536], P(('blk', 'head')), may hold values from 0.25 to 1.75
- w_query: bfloat16 [1536, 1536], P(('blk', 'head')), may hold values from -0.15625 to 0.15625
- key_projection_weight: bfloat16 [1536, 512], P(('blk', 'head')), may hold values from -0.15625 to 0.15625
- value_projection_weight: bfloat16 [1536, 512], P(('blk', 'head')), may hold values from -0.15625 to 0.15625
- q_gain: bfloat16 [64], replicated, may hold values from 0.25 to 1.75
- k_gain: bfloat16 [64], replicated, may hold values from 0.25 to 1.75
- w_out: bfloat16 [1536, 1536], P('head', 'blk'), may hold values from -0.4375 to 0.4375
- ffn_gain: bfloat16 [1536], P(('blk', 'head')), may hold values from 0.25 to 1.75
- w_gate: bfloat16 [1536, 6912], P('blk', 'head'), may hold values from -0.15625 to 0.15625
- w_up: bfloat16 [1536, 6912], P('blk', 'head'), may hold values from -0.15625 to 0.15625
- w_down: bfloat16 [6912, 1536], P('head', 'blk'), may hold values from -0.078125 to 0.078125
- cotangent: bfloat16 [16384, 1536], P(('blk', 'head')), may hold values from -6 to 6
Outputs:
- output: bfloat16 [16384, 1536], P(('blk', 'head'))
- input_grad: bfloat16 [16384, 1536], P(('blk', 'head'))
- attn_gain_grad: float32 [1536], P(('blk', 'head'))
- w_query_grad: float32 [1536, 1536], P(('blk', 'head'))
- w_key_grad: float32 [1536, 512], P(('blk', 'head'))
- w_value_grad: float32 [1536, 512], P(('blk', 'head'))
- q_gain_grad: float32 [64], replicated
- k_gain_grad: float32 [64], replicated
- w_out_grad: float32 [1536, 1536], P('head', 'blk')
- ffn_gain_grad: float32 [1536], P(('blk', 'head'))
- w_gate_grad: float32 [1536, 6912], P('blk', 'head')
- w_up_grad: float32 [1536, 6912], P('blk', 'head')
- w_down_grad: float32 [6912, 1536], P('head', 'blk')
The draws below stay inside these ranges and needn't reach their ends.
Inputs may be any that keep to these rules, and one draw needn't show every extreme that they name: `segments`: segment numbers never fall along the tokens and every number from 0 to 31 occurs; each document holds 1 to 4096 tokens; the first document holds exactly 4096.
All inputs are finite; a program needn't handle non-finite values.
Results may differ from the reference program's by a relative error of at most 0.034.
Values may be sent and summed in bfloat16 or wider, within the bound.
No kernel may reach another device: no remote copies, remote signals or barrier semaphores. Data moves between devices by JAX's collectives and lax.ppermute only.
A program may use at most 256 MiB of HBM per device.

```python
from functools import partial
import jax
import jax.numpy as jnp
from jax import lax

MODEL_WIDTH = 1536
QUERY_HEAD_COUNT = 24
KEY_VALUE_HEADS = 8
HEAD_SIZE = 64
FF = 6912
PACKED_TOKENS = 16384
MAXDOC = 4096
DOCS = 32


def gap_starts(key, first, length, count):
    share = length // count
    jitter = jax.random.randint(key, (count,), 0, max(1, share)).astype(jnp.int32)
    jitter = jitter.at[0].set(0)
    return first + jnp.arange(count, dtype=jnp.int32) * share + jitter


def draw_segments(key, part):
    key = jax.random.fold_in(key, 11)
    total = PACKED_TOKENS
    longest = MAXDOC
    count = DOCS
    key_one, key_two = jax.random.split(key)
    if count >= 3 and 3 * longest + count - 3 <= total:
        middle = total // 2 - longest // 2
        first_count = (count - 3) // 2
        second_count = count - 3 - first_count
        pieces = [jnp.array([0, longest], jnp.int32)]
        if first_count > 0:
            pieces.append(gap_starts(key_one, longest, middle - longest, first_count))
        pieces.append(jnp.array([middle, middle + longest], jnp.int32))
        if second_count > 0:
            pieces.append(gap_starts(key_two, middle + longest, total - longest - middle - longest, second_count))
        pieces.append(jnp.array([total - longest], jnp.int32))
        starts = jnp.concatenate(pieces)
    elif count >= 2 and 2 * longest + count - 2 <= total:
        pieces = [jnp.array([0, longest], jnp.int32)]
        if count > 2:
            pieces.append(gap_starts(key_one, longest, total - 2 * longest, count - 2))
        pieces.append(jnp.array([total - longest], jnp.int32))
        starts = jnp.concatenate(pieces)
    else:
        starts = jnp.concatenate([jnp.array([0], jnp.int32), gap_starts(key_one, longest, total - longest, count - 1)])
    marks = jnp.zeros((total,), jnp.int32).at[starts[1:]].set(1)
    return jnp.cumsum(marks).astype(jnp.int32)


def levels(own_key, dims, cuts, low, largest):
    loudness, own = 1.0, jax.random.fold_in(own_key, 6)
    for axis_at, shards_of in cuts:
        heights = jnp.exp(jax.random.uniform(jax.random.fold_in(own, axis_at), (shards_of,), jnp.float32, low / len(cuts), largest / len(cuts)))
        loudness = loudness * jnp.repeat(heights, dims[axis_at] // shards_of).reshape([-1 if axis == axis_at else 1 for axis in range(len(dims))])
    return loudness


def bell_draw(stream_key, shape, width, reach, shards=(), held_as=jnp.bfloat16):
    values = jax.random.normal(stream_key, shape, jnp.float32) * width
    if len(shards) > 0:
        values = levels(stream_key, shape, shards, -0.22, 0.18) * values
    return jnp.clip(values, min=-reach, max=reach).astype(held_as)


def setup_inputs(seed: int = 0) -> dict:
    key_of = jax.random.split(jax.random.key(seed), 15)
    tokens = bell_draw(key_of[0], (PACKED_TOKENS, MODEL_WIDTH), 1.0, 6.0, ((0, 128),))
    segments = draw_segments(jax.random.fold_in(key_of[14], 71), 0)
    attn_gain = jnp.clip(1.0 + 0.15 * jax.random.normal(key_of[2], (MODEL_WIDTH,), jnp.float32), 0.25, 1.75).astype(jnp.bfloat16)
    w_query = bell_draw(key_of[3], (MODEL_WIDTH, QUERY_HEAD_COUNT * HEAD_SIZE), MODEL_WIDTH ** -0.5, 0.15625, ((0, 128),))
    key_projection_weight = bell_draw(key_of[4], (MODEL_WIDTH, KEY_VALUE_HEADS * HEAD_SIZE), MODEL_WIDTH ** -0.5, 0.15625, ((0, 128),))
    value_projection_weight = bell_draw(key_of[5], (MODEL_WIDTH, KEY_VALUE_HEADS * HEAD_SIZE), MODEL_WIDTH ** -0.5, 0.15625, ((0, 128),))
    q_gain = jnp.clip(1.0 + 0.15 * jax.random.normal(key_of[6], (HEAD_SIZE,), jnp.float32), 0.25, 1.75).astype(jnp.bfloat16)
    k_gain = jnp.clip(1.0 + 0.15 * jax.random.normal(key_of[7], (HEAD_SIZE,), jnp.float32), 0.25, 1.75).astype(jnp.bfloat16)
    w_out = bell_draw(key_of[8], (QUERY_HEAD_COUNT * HEAD_SIZE, MODEL_WIDTH), (QUERY_HEAD_COUNT * HEAD_SIZE // 8) ** -0.5, 0.4375, ((0, 2), (1, 64)))
    ffn_gain = jnp.clip(1.0 + 0.15 * jax.random.normal(key_of[9], (MODEL_WIDTH,), jnp.float32), 0.25, 1.75).astype(jnp.bfloat16)
    w_gate = bell_draw(key_of[10], (MODEL_WIDTH, FF), MODEL_WIDTH ** -0.5, 0.15625, ((0, 64), (1, 2)))
    w_up = bell_draw(key_of[11], (MODEL_WIDTH, FF), MODEL_WIDTH ** -0.5, 0.15625, ((0, 64), (1, 2)))
    w_down = bell_draw(key_of[12], (FF, MODEL_WIDTH), FF ** -0.5, 0.078125, ((0, 2), (1, 64)))
    cotangent = bell_draw(key_of[13], (PACKED_TOKENS, MODEL_WIDTH), 1.0, 6.0, ((0, 128),))
    return {"tokens": tokens, "segments": segments, "attn_gain": attn_gain, "w_query": w_query, "key_projection_weight": key_projection_weight, "value_projection_weight": value_projection_weight, "q_gain": q_gain, "k_gain": k_gain, "w_out": w_out, "ffn_gain": ffn_gain, "w_gate": w_gate, "w_up": w_up, "w_down": w_down, "cotangent": cotangent}


EPS = 1e-05
THETA = 1000000.0
NEG_FILL = -1e+30
PRECISE = lax.Precision.HIGHEST

@jax.custom_vjp
def low(v):
    return lax.optimization_barrier(v.astype(jnp.bfloat16)).astype(jnp.float32)

@jax.custom_vjp
def low_back(v):
    return v

def low_keep(v):
    return (low(v), None)

def low_pass(kept, grad):
    return (grad,)

def back_keep(v):
    return (v, None)

def back_low(kept, grad):
    return (low(grad),)
low.defvjp(low_keep, low_pass)
low_back.defvjp(back_keep, back_low)

def matrix_multiply(left_side, right_side):
    return jnp.dot(left_side, right_side, precision=PRECISE)

def norm_rows(array_in, gain_vector):
    return array_in * lax.rsqrt(lax.optimization_barrier(jnp.mean(array_in * array_in, axis=-1, keepdims=True)) + EPS) * gain_vector

def positions_of(segments):
    token_index = jnp.arange(segments.shape[0], dtype=jnp.int32)
    begins = jnp.concatenate([jnp.ones((1,), jnp.bool_), segments[1:] != segments[:-1]])
    return token_index - lax.cummax(jnp.where(begins, token_index, 0), axis=0)

def rotary_tables(positions):
    half_dim = HEAD_SIZE // 2
    frequency = THETA ** (-jnp.arange(half_dim, dtype=jnp.float32) * 2.0 / HEAD_SIZE)
    angles = positions.astype(jnp.float32)[:, None] * frequency[None, :]
    return (jnp.cos(angles)[:, None, :], jnp.sin(angles)[:, None, :])

def rotate(array_in, cosine_table, sine_table):
    half_dim = array_in.shape[-1] // 2
    first_half = array_in[..., :half_dim]
    second_half = array_in[..., half_dim:]
    return jnp.concatenate([first_half * cosine_table - second_half * sine_table, second_half * cosine_table + first_half * sine_table], axis=-1)

def attention(query_matrix, key_matrix_rows, value_matrix, segments):
    heads_per_group = QUERY_HEAD_COUNT // KEY_VALUE_HEADS
    count_of_rows = min(512, PACKED_TOKENS)
    window = min(PACKED_TOKENS, count_of_rows + MAXDOC)

    def attend_block(first_row_index):
        query_tile_block = lax.dynamic_slice_in_dim(query_matrix, first_row_index, count_of_rows, 0).reshape(count_of_rows, KEY_VALUE_HEADS, heads_per_group, HEAD_SIZE)
        key_start = jnp.clip(first_row_index + count_of_rows - window, 0, PACKED_TOKENS - window).astype(jnp.int32)
        key_block = lax.dynamic_slice_in_dim(key_matrix_rows, key_start, window, 0)
        value_block = lax.dynamic_slice_in_dim(value_matrix, key_start, window, 0)
        query_segments = lax.dynamic_slice_in_dim(segments, first_row_index, count_of_rows, 0)
        key_segments = lax.dynamic_slice_in_dim(segments, key_start, window, 0)
        query_index = first_row_index + jnp.arange(count_of_rows, dtype=jnp.int32)
        key_index = key_start + jnp.arange(window, dtype=jnp.int32)
        scores = jnp.einsum('qkgd,tkd->kgqt', query_tile_block, key_block, precision=PRECISE) * HEAD_SIZE ** (-0.5)
        scores = low_back(scores)
        allowed = (query_segments[:, None] == key_segments[None, :]) & (key_index[None, :] <= query_index[:, None])
        scores = jnp.where(allowed, scores, NEG_FILL)
        row_max = lax.optimization_barrier(jnp.max(scores, axis=-1, keepdims=True))
        weights = jnp.exp(scores - row_max)
        weights = weights / lax.optimization_barrier(jnp.sum(weights, axis=-1, keepdims=True))
        mixed_rows = jnp.einsum('kgqt,tkd->qkgd', low(weights), value_block, precision=PRECISE)
        return mixed_rows.reshape(count_of_rows, QUERY_HEAD_COUNT * HEAD_SIZE)
    starts = jnp.arange(PACKED_TOKENS // count_of_rows, dtype=jnp.int32) * count_of_rows
    return lax.map(jax.checkpoint(attend_block), starts).reshape(PACKED_TOKENS, QUERY_HEAD_COUNT * HEAD_SIZE)

def forward(inputs, attn_gain, w_query, key_projection_weight, value_projection_weight, q_gain, k_gain, w_out, ffn_gain, w_gate, w_up, w_down, segments=None, cosine_table=None, sine_table=None):
    normalized_input = low(norm_rows(inputs, attn_gain))
    query_matrix = low_back(matrix_multiply(normalized_input, w_query)).reshape(PACKED_TOKENS, QUERY_HEAD_COUNT, HEAD_SIZE)
    key_matrix_rows = low_back(matrix_multiply(normalized_input, key_projection_weight)).reshape(PACKED_TOKENS, KEY_VALUE_HEADS, HEAD_SIZE)
    value_matrix = low(low_back(matrix_multiply(normalized_input, value_projection_weight))).reshape(PACKED_TOKENS, KEY_VALUE_HEADS, HEAD_SIZE)
    query_matrix = low(low_back(rotate(norm_rows(query_matrix, q_gain), cosine_table, sine_table)))
    key_matrix_rows = low(low_back(rotate(norm_rows(key_matrix_rows, k_gain), cosine_table, sine_table)))
    mixture = low(low_back(attention(query_matrix, key_matrix_rows, value_matrix, segments)))
    hidden = inputs + low_back(matrix_multiply(mixture, w_out))
    normed_ffn = low(norm_rows(hidden, ffn_gain))
    gate_value = low_back(matrix_multiply(normed_ffn, w_gate))
    up_value = low_back(matrix_multiply(normed_ffn, w_up))
    activation = low(jax.nn.silu(gate_value) * up_value)
    return hidden + matrix_multiply(activation, w_down)

def reference(tokens, segments, attn_gain, w_query, key_projection_weight, value_projection_weight, q_gain, k_gain, w_out, ffn_gain, w_gate, w_up, w_down, cotangent):
    positions = positions_of(segments)
    cosine_table, sine_table = rotary_tables(positions)
    forward_fn = partial(forward, segments=segments, cosine_table=cosine_table, sine_table=sine_table)
    floats = [array_in.astype(jnp.float32) for array_in in (tokens, attn_gain, w_query, key_projection_weight, value_projection_weight, q_gain, k_gain, w_out, ffn_gain, w_gate, w_up, w_down)]
    output, pullback = jax.vjp(forward_fn, *floats)
    gradients = pullback(cotangent.astype(jnp.float32))
    return (output.astype(jnp.bfloat16), gradients[0].astype(jnp.bfloat16), gradients[1], gradients[2], gradients[3], gradients[4], gradients[5], gradients[6], gradients[7], gradients[8], gradients[9], gradients[10], gradients[11])
```

```python
import functools

import jax
import jax.numpy as jnp
import numpy as np
from jax import lax
from jax.experimental import pallas as pl
from jax.experimental.pallas import tpu as pltpu
from jax.sharding import Mesh
from jax.sharding import PartitionSpec as P

EPS = 1e-05
THETA = 1000000.0
HEAD = 64
ROWS = 128
PAIR = 2 * ROWS
GROUP = 3
QUERY = GROUP * HEAD
LANES = ROWS * GROUP
KEY_TILE = 512
SUPER = 2048
EARLIER = 2 * SUPER
PART = 432
PADDED = 512
WIDTH = 1536
ALL = ("ylo", "z", "x", "core", "yhi")
BLK = ("ylo", "z", "x", "core")
WIDE = ("yhi", "ylo", "z")
NEAR = ("x", "core")
NN = (((1,), (0,)), ((), ()))
NT = (((1,), (1,)), ((), ()))
TN = (((0,), (0,)), ((), ()))
F32 = jnp.float32
BF16 = jnp.bfloat16
SCORE = HEAD**-0.5 * 1.4426950408889634


def dot(a, b, numbers=NN):
    return lax.dot_general(a, b, numbers, preferred_element_type=F32)


def rms_scale(v):
    return lax.rsqrt(jnp.mean(v * v, axis=-1, keepdims=True) + EPS)


def rms_back(grad, v, scale):
    inner = jnp.mean(grad * v, axis=-1, keepdims=True)
    return scale * (grad - v * scale * scale * inner)


def shift_x(v, distance):
    return lax.ppermute(v, "x", [((i + distance) % 4, i) for i in range(4)])


def swap(v, axis):
    return lax.ppermute(v, axis, [(0, 1), (1, 0)])


def shift_super(v, distance):
    pairs = [(i, i + distance) for i in range(8) if 0 <= i + distance < 8]
    return lax.ppermute(v, ("ylo", "z"), pairs)


def exchange(v, axes):
    return lax.all_to_all(v, axes, split_axis=0, concat_axis=0, tiled=True)


def near_gather(v):
    blocks = [v] + [shift_x(v, d) for d in (1, 2, 3)]
    return [[b, swap(b, "core")] for b in blocks]


def near_keep(parts):
    return [
        (own.astype(F32) + swap(other, "core").astype(F32)).astype(BF16) for own, other in parts
    ]


def near_sum(kept):
    total = kept[0].astype(F32)
    for d in (1, 2, 3):
        total = total + shift_x(kept[d], -d).astype(F32)
    return total


def rel_to_abs(v, x, core):
    v = jnp.where(core == 0, v, v[:, ::-1])
    return lax.dynamic_slice_in_dim(jnp.concatenate([v, v], axis=0), (4 - x) % 4, 4, 0)


def abs_to_rel(v, x, core):
    v = jnp.where(core == 0, v, v[:, ::-1])
    return lax.dynamic_slice_in_dim(jnp.concatenate([v, v], axis=0), x, 4, 0)


def params(steps, mib):
    return pltpu.CompilerParams(
        dimension_semantics=("arbitrary",) * steps, vmem_limit_bytes=mib * 2**20
    )


def cost(flops, moved, exps=0):
    return pl.CostEstimate(flops=int(flops), bytes_accessed=int(moved), transcendentals=int(exps))


def stacked(a_ref, b_ref):
    return jnp.concatenate([a_ref[...], b_ref[...]], axis=0)


def head_sums(v):
    lane = lax.shift_right_logical(lax.broadcasted_iota(jnp.int32, (4 * HEAD, 4 * HEAD), 1), 6)
    row = lax.shift_right_logical(lax.broadcasted_iota(jnp.int32, (4 * HEAD, 4 * HEAD), 0), 6)
    ones = jnp.where(lane == row, 1.0, 0.0).astype(BF16)
    high = v.astype(BF16)
    low = (v - high.astype(F32)).astype(BF16)
    return dot(high, ones) + dot(low, ones)


def half_turn(v):
    lane = lax.broadcasted_iota(jnp.int32, v.shape, 1)
    return jnp.where(
        (lane & (HEAD - 1)) < HEAD // 2,
        pltpu.roll(v, v.shape[1] - HEAD // 2, 1),
        pltpu.roll(v, HEAD // 2, 1),
    )


def twice(v):
    return jnp.concatenate([v, v], axis=1)


def project_kernel(*refs):
    xs, (w_ref, gain_ref, cos_ref, sin_ref, head_gain_ref) = refs[:8], refs[8:13]
    normed_ref, q_ref, kv_ref, raw_ref = refs[13:]
    lane = lax.broadcasted_iota(jnp.int32, (PAIR, 2 * HEAD), 1)
    for d in range(4):
        rows = slice(d * PAIR, (d + 1) * PAIR)
        tiles = slice(2 * d, 2 * d + 2)
        x = stacked(*xs[tiles]).astype(F32)
        normed = (x * rms_scale(x) * gain_ref[...]).astype(BF16)
        normed_ref[rows, :] = normed
        raw = dot(normed, w_ref[...])
        heads = raw[:, : 4 * HEAD]
        raw_ref[d] = heads
        scale = lax.rsqrt(head_sums(heads * heads) * (1.0 / HEAD) + EPS)
        v = heads * scale * head_gain_ref[...]
        turned = v * twice(cos_ref[d]) + half_turn(v) * twice(sin_ref[d])
        q_ref[tiles] = turned[:, :QUERY].astype(BF16).reshape(2, ROWS, QUERY)
        kv = jnp.where(lane < HEAD, raw[:, 4 * HEAD :], turned[:, 2 * HEAD :])
        kv_ref[tiles] = kv.astype(BF16).reshape(2, ROWS, 2 * HEAD)


def project(xs, w, gain, cos, sin, head_gain):
    return pl.pallas_call(
        project_kernel,
        out_shape=(
            jax.ShapeDtypeStruct((4 * PAIR, WIDTH), BF16),
            jax.ShapeDtypeStruct((8, ROWS, QUERY), BF16),
            jax.ShapeDtypeStruct((8, ROWS, 2 * HEAD), BF16),
            jax.ShapeDtypeStruct((4, PAIR, 4 * HEAD), F32),
        ),
        compiler_params=params(0, 32),
        cost_estimate=cost(8 * PAIR * WIDTH * 384, 1e7),
    )(*xs, w, gain, cos, sin, head_gain)


def unproject_kernel(
    gq_ref, g0_ref, g1_ref, g2_ref, g3_ref, raw_ref, x0_ref, x1_ref, w_ref, cos_ref, sin_ref,
    head_gain_ref, part0_ref, part1_ref, graw_ref, attn_ref, heads_ref,
):
    gq = gq_ref[...].reshape(PAIR, 4 * HEAD).astype(F32)
    gkv = g0_ref[...] + g1_ref[...].astype(F32) + g2_ref[...].astype(F32) + g3_ref[...].astype(F32)
    gkv = gkv.reshape(PAIR, 2 * HEAD)
    lane = lax.broadcasted_iota(jnp.int32, (PAIR, 2 * HEAD), 1)
    gk = (gkv * HEAD**-0.5).astype(BF16).astype(F32)
    g = jnp.concatenate([gq[:, : 2 * HEAD], jnp.where(lane < HEAD, gq[:, 2 * HEAD :], gk)], axis=1)
    g = g * twice(cos_ref[0]) - half_turn(g) * twice(sin_ref[0])
    raw = raw_ref[0]
    scale = lax.rsqrt(head_sums(raw * raw) * (1.0 / HEAD) + EPS)
    heads_ref[...] = jnp.sum(g * raw * scale, axis=0, keepdims=True)
    e = g * head_gain_ref[...]
    inner = head_sums(e * raw) * (1.0 / HEAD)
    graw = scale * (e - raw * scale * scale * inner)
    graw = jnp.concatenate([graw, jnp.where(lane < HEAD, gkv, 0.0)], axis=1).astype(BF16)
    graw_ref[...] = graw
    grad = dot(graw, w_ref[...], NT)
    x = stacked(x0_ref, x1_ref).astype(F32)
    attn_ref[...] = jnp.sum(grad * x * rms_scale(x), axis=0, keepdims=True)
    grad = grad.astype(BF16)
    part0_ref[...] = grad[:ROWS]
    part1_ref[...] = grad[ROWS:]


def unproject(d, gq, gkvs, raw, x0, x1, w, cos, sin, head_gain):
    def whole_of(*shape):
        return pl.BlockSpec(shape, lambda i: (0,) * len(shape))

    def at_d(*shape):
        return pl.BlockSpec(shape, lambda i: (d,) + (0,) * (len(shape) - 1))

    rows = whole_of(ROWS, WIDTH)
    kv = at_d(2, ROWS, 2 * HEAD)
    table = at_d(1, PAIR, 2 * HEAD)
    outs = (
        jax.ShapeDtypeStruct((ROWS, WIDTH), BF16),
        jax.ShapeDtypeStruct((ROWS, WIDTH), BF16),
        jax.ShapeDtypeStruct((PAIR, 6 * HEAD), BF16),
        jax.ShapeDtypeStruct((1, WIDTH), F32),
        jax.ShapeDtypeStruct((1, 4 * HEAD), F32),
    )
    return pl.pallas_call(
        unproject_kernel,
        out_shape=outs,
        grid=(1,),
        in_specs=[at_d(2, ROWS, 4 * HEAD), kv, kv, kv, kv, at_d(1, PAIR, 4 * HEAD), rows, rows]
        + [whole_of(WIDTH, 6 * HEAD), table, table, whole_of(1, 4 * HEAD)],
        out_specs=tuple(whole_of(*o.shape) for o in outs),
        compiler_params=params(1, 24),
        cost_estimate=cost(2 * PAIR * WIDTH * 384, 4e6),
    )(gq, *gkvs, raw, x0, x1, w, cos, sin, head_gain)


def ffn_kernel(x0_ref, x1_ref, c0_ref, c1_ref, w_ref, part0_ref, part1_ref, act_ref, gu_ref, total):
    y = pl.program_id(0)
    x = stacked(x0_ref, x1_ref)
    gate_up = dot(x, w_ref[0, :, : 2 * PADDED])
    gate, up = gate_up[:, :PADDED], gate_up[:, PADDED:]
    grad_act = dot(stacked(c0_ref, c1_ref), w_ref[0, :, 2 * PADDED :])
    sig = 1.0 / (1.0 + jnp.exp(-gate))
    silu = gate * sig
    act_ref[0] = (silu * up).astype(BF16)
    grad_gate = grad_act * up * sig * (1.0 + gate * (1.0 - sig))
    grads = jnp.concatenate([grad_gate, grad_act * silu], axis=1).astype(BF16)
    gu_ref[0] = grads
    part = dot(grads, w_ref[0, :, : 2 * PADDED], NT)

    @pl.when(y == 0)
    def _():
        total[...] = part

    @pl.when(y == 1)
    def _():
        whole_part = (total[...] + part).astype(BF16)
        part0_ref[...] = whole_part[:ROWS]
        part1_ref[...] = whole_part[ROWS:]


def ffn(x0, x1, c0, c1, w):
    rows = pl.BlockSpec((ROWS, WIDTH), lambda y: (0, 0))
    return pl.pallas_call(
        ffn_kernel,
        out_shape=(
            jax.ShapeDtypeStruct((ROWS, WIDTH), BF16),
            jax.ShapeDtypeStruct((ROWS, WIDTH), BF16),
            jax.ShapeDtypeStruct((2, PAIR, PADDED), BF16),
            jax.ShapeDtypeStruct((2, PAIR, 2 * PADDED), BF16),
        ),
        grid=(2,),
        in_specs=[rows] * 4 + [pl.BlockSpec((1, WIDTH, 3 * PADDED), lambda y: (y, 0, 0))],
        out_specs=(
            rows,
            rows,
            pl.BlockSpec((1, PAIR, PADDED), lambda y: (y, 0, 0)),
            pl.BlockSpec((1, PAIR, 2 * PADDED), lambda y: (y, 0, 0)),
        ),
        scratch_shapes=[pltpu.VMEM((PAIR, WIDTH), F32)],
        compiler_params=params(1, 40),
        cost_estimate=cost(2 * 2 * PAIR * WIDTH * 5 * PADDED, 14e6),
    )(x0, x1, c0, c1, w)


def down_kernel(act_ref, w_ref, part0_ref, part1_ref, total):
    y = pl.program_id(0)
    part = dot(act_ref[0], w_ref[0], NT)

    @pl.when(y == 0)
    def _():
        total[...] = part

    @pl.when(y == 1)
    def _():
        whole_part = (total[...] + part).astype(BF16)
        part0_ref[...] = whole_part[:ROWS]
        part1_ref[...] = whole_part[ROWS:]


def down(act, w):
    rows = pl.BlockSpec((ROWS, WIDTH), lambda y: (0, 0))
    return pl.pallas_call(
        down_kernel,
        out_shape=(jax.ShapeDtypeStruct((ROWS, WIDTH), BF16),) * 2,
        grid=(2,),
        in_specs=[
            pl.BlockSpec((1, PAIR, PADDED), lambda y: (y, 0, 0)),
            pl.BlockSpec((1, WIDTH, PADDED), lambda y: (y, 0, 2)),
        ],
        out_specs=(rows, rows),
        scratch_shapes=[pltpu.VMEM((PAIR, WIDTH), F32)],
        compiler_params=params(1, 24),
        cost_estimate=cost(2 * 2 * PAIR * WIDTH * PADDED, 5e6),
    )(act, w)


def ffn_weights_kernel(*refs):
    xs, cs, gus, acts, out_ref = refs[:8], refs[8:16], refs[16:20], refs[20:24], refs[24]
    grad_gu, grad_d = 0.0, 0.0
    for d in range(4):
        grad_gu = grad_gu + dot(stacked(*xs[2 * d : 2 * d + 2]), gus[d][0], TN)
        grad_d = grad_d + dot(stacked(*cs[2 * d : 2 * d + 2]), acts[d][0], TN)
    out_ref[0, :, : 2 * PADDED] = grad_gu.astype(BF16)
    out_ref[0, :, 2 * PADDED :] = grad_d.astype(BF16)


def ffn_weights(xs, cs, gus, acts):
    tall = 256
    rows = pl.BlockSpec((ROWS, tall), lambda y, m: (0, m))
    return pl.pallas_call(
        ffn_weights_kernel,
        out_shape=jax.ShapeDtypeStruct((2, WIDTH, 3 * PADDED), BF16),
        grid=(2, WIDTH // tall),
        in_specs=[rows] * 16
        + [pl.BlockSpec((1, PAIR, 2 * PADDED), lambda y, m: (y, 0, 0))] * 4
        + [pl.BlockSpec((1, PAIR, PADDED), lambda y, m: (y, 0, 0))] * 4,
        out_specs=pl.BlockSpec((1, tall, 3 * PADDED), lambda y, m: (y, m, 0)),
        compiler_params=params(2, 40),
        cost_estimate=cost(2 * 2 * 1024 * WIDTH * 3 * PADDED, 24e6),
    )(*xs, *cs, *gus, *acts)


def side_by_side(t):
    return jnp.concatenate([t[g * HEAD : (g + 1) * HEAD] for g in range(GROUP)], axis=1)


def on_top(t):
    return jnp.concatenate([t[:, g * ROWS : (g + 1) * ROWS] for g in range(GROUP)], axis=0)


def key_loops(plan, at, base, start, visit, state):
    f = pl.program_id(0)
    lo, m1, m2, hi = (plan[f, at + i] for i in range(4))
    place = lax.rem(lax.broadcasted_iota(jnp.int32, (1, LANES), 1), ROWS) + plan[f, 0]

    def masked(j, state):
        key = lax.broadcasted_iota(jnp.int32, (KEY_TILE, LANES), 0) + (j * KEY_TILE + base)
        return visit(j, state, (key >= start) & (key <= place))

    state = lax.fori_loop(lo, m1, masked, state)
    state = lax.fori_loop(m1, m2, lambda j, s: visit(j, s, None), state)
    return lax.fori_loop(m2, hi, masked, state)


def rows_of(j):
    return pl.ds(pl.multiple_of(j * KEY_TILE, KEY_TILE), KEY_TILE)


def chunks(plan, supers):
    for b in range(supers):
        for half in (0, 1):
            for f in range(8):
                side = plan[0, 10] if half == 0 else 1 - plan[0, 10]
                yield b, half, pl.multiple_of(b * SUPER + f * PAIR + side * ROWS, ROWS), plan[f, 1]


def line_up(plan, kv_refs, kv, kvt):
    @pl.when(pl.program_id(0) == 0)
    def _():
        for b, half, place, sent in chunks(plan, len(kv_refs) // 2):
            block = kv_refs[2 * b + half][sent]
            kv[pl.ds(place, ROWS), :] = block
            kvt[:, pl.ds(place, ROWS)] = block.astype(F32).T.astype(BF16)


def attend_body(at, base, plan, q_ref, start_ref, kv, kvt, state):
    qt = side_by_side(q_ref[0].astype(F32).T)
    qt = jnp.concatenate([jnp.zeros_like(qt), qt], axis=0).astype(BF16)

    def visit(j, state, mask):
        total, accum = state
        weights = jnp.exp2(dot(kv[rows_of(j), :], qt) * SCORE)
        if mask is not None:
            weights = jnp.where(mask, weights, 0.0)
        total = total + jnp.sum(weights, axis=0, keepdims=True)
        return total, accum + dot(kvt[:HEAD, rows_of(j)], weights.astype(BF16))

    return key_loops(plan, at, base, start_ref[0], visit, state)


def attend_own_kernel(plan, q_ref, start_ref, *refs):
    kv_refs, (accum_ref, total_ref, kv, kvt) = refs[:2], refs[2:]
    line_up(plan, kv_refs, kv, kvt)
    state = (jnp.zeros((1, LANES), F32), jnp.zeros((HEAD, LANES), F32))
    total, accum = attend_body(6, EARLIER, plan, q_ref, start_ref, kv, kvt, state)
    accum_ref[0] = accum
    total_ref[0] = total


def attend_earlier_kernel(plan, q_ref, start_ref, *refs):
    kv_refs, (accum_ref, total_ref, mix_ref, out_ref, lse_ref, kv, kvt) = refs[:4], refs[4:]
    line_up(plan, kv_refs, kv, kvt)
    state = (total_ref[0], accum_ref[0])
    total, accum = attend_body(2, 0, plan, q_ref, start_ref, kv, kvt, state)
    out = accum / total
    out_ref[0] = out
    mix_ref[0] = on_top(out).astype(BF16)
    lse_ref[0] = jnp.log2(total)


def back_body(at, base, plan, q_ref, start_ref, g_ref, out_ref, lse_ref, kv, kvt, dkv, dqt):
    @pl.when(pl.program_id(0) == 0)
    def _():
        dkv[...] = jnp.zeros_like(dkv)

    qt = side_by_side(q_ref[0].astype(F32).T)
    gt = side_by_side(g_ref[0].astype(F32))
    delta = jnp.sum(gt * out_ref[0], axis=0, keepdims=True)
    zero = jnp.zeros_like(qt)
    gt = jnp.concatenate([gt, zero], axis=0)
    qt = jnp.concatenate([zero, qt], axis=0)
    both_t = jnp.concatenate([gt, qt], axis=1).astype(BF16)
    both = jnp.concatenate([gt.T, qt.T], axis=0).astype(BF16)
    lse = lse_ref[0]

    def visit(j, dqt, mask):
        pair = dot(kv[rows_of(j), :], both_t)
        weights = jnp.exp2(pair[:, LANES:] * SCORE - lse)
        if mask is not None:
            weights = jnp.where(mask, weights, 0.0)
        grads = (weights * (pair[:, :LANES] - delta)).astype(BF16)
        sides = jnp.concatenate([weights.astype(BF16), grads], axis=1)
        dkv[rows_of(j), :] += dot(sides, both)
        return dqt + dot(kvt[HEAD:, rows_of(j)], grads)

    return key_loops(plan, at, base, start_ref[0], visit, dqt)


def hand_out(plan, supers, dkv, mine_ref, theirs_ref):
    @pl.when(pl.program_id(0) == 7)
    def _():
        for b, half, place, sent in chunks(plan, supers):
            ref = (mine_ref, theirs_ref)[half]
            ref[b, sent] = dkv[pl.ds(place, ROWS), :].astype(ref.dtype)


def back_earlier_kernel(plan, q_ref, start_ref, *refs):
    kv_refs, (g_ref, out_ref, lse_ref, dqt_ref, mine_ref, theirs_ref, kv, kvt, dkv) = refs[:4], refs[4:]
    line_up(plan, kv_refs, kv, kvt)
    dqt = jnp.zeros((HEAD, LANES), F32)
    dqt_ref[0] = back_body(
        2, 0, plan, q_ref, start_ref, g_ref, out_ref, lse_ref, kv, kvt, dkv, dqt
    )
    hand_out(plan, 2, dkv, mine_ref, theirs_ref)


def back_own_kernel(plan, q_ref, start_ref, *refs):
    kv_refs, (g_ref, out_ref, lse_ref, dqt_ref) = refs[:2], refs[2:6]
    dq_ref, mine_ref, theirs_ref, kv, kvt, dkv = refs[6:]
    line_up(plan, kv_refs, kv, kvt)
    dqt = back_body(
        6, EARLIER, plan, q_ref, start_ref, g_ref, out_ref, lse_ref, kv, kvt, dkv, dqt_ref[0]
    )
    dq = on_top(dqt * HEAD**-0.5).T
    dq_ref[0] = jnp.concatenate([dq, jnp.zeros((ROWS, HEAD), F32)], axis=1).astype(BF16)
    hand_out(plan, 1, dkv, mine_ref, theirs_ref)


def whole(*shape):
    return pl.BlockSpec(shape, lambda f, plan: (0,) * len(shape))


def tile(*shape):
    return pl.BlockSpec((1,) + shape, lambda f, plan: (f,) + (0,) * len(shape))


def placed(*shape):
    return pl.BlockSpec((1,) + shape, lambda f, plan: (plan[f, 1],) + (0,) * len(shape))


def tiles_call(kernel, supers, outs, more_ins, out_specs, flops, back):
    keys = supers * SUPER
    scratch = [pltpu.VMEM((keys, 2 * HEAD), BF16), pltpu.VMEM((2 * HEAD, keys), BF16)]
    if back:
        scratch.append(pltpu.VMEM((keys, 2 * HEAD), F32))
    ins = [placed(ROWS, QUERY), tile(1, LANES)] + [whole(8, ROWS, 2 * HEAD)] * (2 * supers)
    return pl.pallas_call(
        kernel,
        out_shape=outs,
        grid_spec=pltpu.PrefetchScalarGridSpec(
            num_scalar_prefetch=1,
            grid=(8,),
            in_specs=ins + more_ins,
            out_specs=out_specs,
            scratch_shapes=scratch,
        ),
        compiler_params=params(1, 32),
        cost_estimate=cost(flops, 8e6, 1e7),
    )


TILE_T = jax.ShapeDtypeStruct((8, HEAD, LANES), F32)
TILE_ROW = jax.ShapeDtypeStruct((8, 1, LANES), F32)
STATE = [tile(HEAD, LANES), tile(1, LANES)]


def attend_own(plan, q, start, kvs):
    call = tiles_call(attend_own_kernel, 1, (TILE_T, TILE_ROW), [], tuple(STATE), 4e9, False)
    return call(plan, q, start, *kvs)


def attend_earlier(plan, q, start, kvs, state):
    outs = (jax.ShapeDtypeStruct((8, QUERY, ROWS), BF16), TILE_T, TILE_ROW)
    specs = (tile(QUERY, ROWS),) + tuple(STATE)
    call = tiles_call(attend_earlier_kernel, 2, outs, STATE, specs, 8e9, False)
    return call(plan, q, start, *kvs, *state)


def sent_back(supers):
    shape = (supers, 8, ROWS, 2 * HEAD)
    return [jax.ShapeDtypeStruct(shape, F32), jax.ShapeDtypeStruct(shape, BF16)], [whole(*shape)] * 2


def back_earlier(plan, q, start, kvs, grad, out, lse):
    shapes, specs = sent_back(2)
    call = tiles_call(
        back_earlier_kernel, 2, [TILE_T] + shapes, [tile(QUERY, ROWS)] + STATE,
        [tile(HEAD, LANES)] + specs, 20e9, True,
    )
    return call(plan, q, start, *kvs, grad, out, lse)


def back_own(plan, q, start, kvs, grad, out, lse, dqt):
    shapes, specs = sent_back(1)
    dq = jax.ShapeDtypeStruct((8, ROWS, 4 * HEAD), BF16)
    call = tiles_call(
        back_own_kernel, 1, [dq] + shapes, [tile(QUERY, ROWS)] + STATE + [tile(HEAD, LANES)],
        [placed(ROWS, 4 * HEAD)] + specs, 10e9, True,
    )
    return call(plan, q, start, *kvs, grad, out, lse, dqt)


def out_weights_kernel(plan, mix_ref, *refs):
    branches, (out_ref, total) = refs[:8], refs[8:]
    grad = 0.0
    for t in range(8):
        grad = grad + dot(mix_ref[plan[t, 11]], branches[t][...])
    total[...] = grad
    for half in (0, 1):
        for s in range(8):
            out_ref[half * 8 + s] = total[half * 96 : half * 96 + 96, s * 192 : s * 192 + 192].astype(BF16)


def out_weights(plan, mix, branches):
    return pl.pallas_call(
        out_weights_kernel,
        out_shape=jax.ShapeDtypeStruct((16, 96, 192), BF16),
        grid_spec=pltpu.PrefetchScalarGridSpec(
            num_scalar_prefetch=1,
            grid=(1,),
            in_specs=[whole(8, QUERY, ROWS)] + [whole(ROWS, WIDTH)] * 8,
            out_specs=whole(16, 96, 192),
            scratch_shapes=[pltpu.VMEM((QUERY, WIDTH), F32)],
        ),
        compiler_params=params(1, 24),
        cost_estimate=cost(2 * 1024 * WIDTH * QUERY, 4e6),
    )(plan, mix, *branches)


def after(v, *others):
    return lax.optimization_barrier((v,) + others)[0]


def per_device(
    tokens,
    segments,
    attn_gain,
    w_query,
    w_key,
    w_value,
    q_gain,
    k_gain,
    w_out,
    ffn_gain,
    w_gate,
    w_up,
    w_down,
    cotangent,
):
    ylo, z, x, core, yhi = (lax.axis_index(a) for a in ALL)
    sup = ylo * 4 + z

    qkv_own = jnp.concatenate(
        [
            w_query.reshape(12, 8, QUERY),
            w_key.reshape(12, 8, HEAD),
            w_value.reshape(12, 8, HEAD),
            jnp.broadcast_to(attn_gain[:, None, None], (12, 8, 1)),
            jnp.broadcast_to(ffn_gain[:, None, None], (12, 8, 1)),
            jnp.zeros((12, 8, HEAD - 2), BF16),
        ],
        axis=-1,
    )
    qkv_own = jnp.transpose(qkv_own, (1, 0, 2))
    qkv_sent = jnp.broadcast_to(qkv_own[None, :, None], (8, 8, 2, 12, 6 * HEAD))
    qkv = exchange(qkv_sent.reshape(128, 12, 6 * HEAD), ALL).reshape(WIDTH, 6 * HEAD)
    gain_attn = qkv[:, 5 * HEAD].astype(F32)
    gain_ffn = qkv[:, 5 * HEAD + 1].astype(F32)
    token_blocks = near_gather(tokens)

    out_own = near_gather(w_out.T)
    out_own = rel_to_abs(jnp.stack([jnp.stack(p) for p in out_own]), x, core).reshape(192, 768)
    out_full = lax.all_gather(out_own, WIDE, axis=0, tiled=True).reshape(2, WIDTH, 768)

    token_index = jnp.arange(segments.shape[0], dtype=jnp.int32)
    begins = jnp.concatenate([jnp.ones((1,), jnp.bool_), segments[1:] != segments[:-1]])
    starts = lax.cummax(jnp.where(begins, token_index, 0), axis=0)
    own_starts = lax.dynamic_slice(
        starts.reshape(8, 8, 2, ROWS), (sup, 0, yhi, 0), (1, 8, 1, ROWS)
    ).reshape(8, ROWS)
    first = sup * SUPER + jnp.arange(8, dtype=jnp.int32) * PAIR + yhi * ROWS
    own_places = first[:, None] + jnp.arange(ROWS, dtype=jnp.int32)[None]
    positions = abs_to_rel((own_places - own_starts).reshape(4, 2, ROWS), x, core)
    frequency = THETA ** (-jnp.arange(HEAD // 2, dtype=F32) * 2.0 / HEAD)
    angles = positions.reshape(4, PAIR, 1).astype(F32) * frequency
    cosine, sine = jnp.cos(angles), jnp.sin(angles)
    cos = jnp.concatenate([cosine] * 4, axis=-1)
    sin = jnp.concatenate([-sine, sine] * 2, axis=-1)
    head_gain = jnp.concatenate([q_gain, q_gain, q_gain, k_gain]).astype(F32)[None]

    window = (sup - 2) * SUPER
    lo = (own_starts[:, 0] - window) // KEY_TILE
    hi = (first + ROWS - 1 - window) // KEY_TILE + 1
    m1 = jnp.clip((own_starts[:, -1] - window + KEY_TILE - 1) // KEY_TILE, lo, hi)
    m2 = jnp.clip((first + 1 - window) // KEY_TILE, m1, hi)
    order = jnp.arange(8, dtype=jnp.int32)
    relative = ((order // 2 - x) % 4) * 2 + (order % 2 + core) % 2
    edge = EARLIER // KEY_TILE
    plan = jnp.stack(
        [first - window, relative]
        + [jnp.minimum(v, edge) for v in (lo, m1, m2, hi)]
        + [jnp.maximum(v - edge, 0) for v in (lo, m1, m2, hi)]
        + [jnp.broadcast_to(yhi, (8,)), ((order // 2 + x) % 4) * 2 + (order % 2 + core) % 2],
        axis=1,
    ).astype(jnp.int32)
    start_lanes = jnp.tile(own_starts - window, (1, GROUP)).reshape(8, 1, LANES)

    normed, rot_q, kv, raw = project(
        [b for p in token_blocks for b in p], qkv, gain_attn[None], cos, sin, head_gain
    )

    ffn_own = jnp.concatenate(
        [
            jnp.pad(w.reshape(24, 8, PART), ((0, 0), (0, 0), (0, PADDED - PART)))
            for w in after((w_gate, w_up, w_down.T), qkv)
        ],
        axis=-1,
    )
    ffn_rows = exchange(jnp.transpose(ffn_own, (1, 0, 2)), NEAR).reshape(192, 3 * PADDED)
    ffn_full = lax.all_gather(ffn_rows, WIDE, axis=0, tiled=True).reshape(2, WIDTH, 3 * PADDED)

    kv_one, kv_two = shift_super(kv, 1), shift_super(kv, 2)
    kv_own = [kv, swap(kv, "yhi")]
    kv_earlier = [kv_two, swap(kv_two, "yhi"), kv_one, swap(kv_one, "yhi")]
    state = attend_own(plan, rot_q, start_lanes, kv_own)
    cot_blocks = near_gather(after(cotangent, kv))
    state, cot_blocks = lax.optimization_barrier((state, cot_blocks))
    mix_tiles, out_tiles, lse = attend_earlier(plan, rot_q, start_lanes, kv_earlier, state)

    mixture_t = exchange(mix_tiles, NEAR).reshape(2, 768, ROWS)
    inputs = tokens.astype(F32)
    hidden = inputs
    for y in range(2):
        hidden = hidden + lax.dot_general(
            mixture_t[y], out_full[y], (((0,), (1,)), ((), ())), preferred_element_type=F32
        )
    scale_ffn = rms_scale(hidden)
    scaled_ffn = hidden * scale_ffn
    normed_ffn = (scaled_ffn * gain_ffn).astype(BF16)

    ffn_blocks = near_gather(normed_ffn)
    ffn_outs = [None] * 4
    for d in (0, 1, 3, 2):
        ffn_outs[d] = ffn(*ffn_blocks[d], *cot_blocks[d], ffn_full)
    acts, gus = [o[2] for o in ffn_outs], [o[3] for o in ffn_outs]
    kept, gus = lax.optimization_barrier((near_keep([o[:2] for o in ffn_outs]), gus))
    pair_total = near_sum(kept)
    weight_grads = ffn_weights(
        [b for p in ffn_blocks for b in p], [b for p in cot_blocks for b in p], gus, acts
    )
    pair_total, weight_grads = lax.optimization_barrier((pair_total, weight_grads))
    ffn_got = exchange(weight_grads.reshape(16, 192, 3 * PADDED), WIDE)

    ffn_gain_part = jnp.sum(pair_total * scaled_ffn, axis=0)
    grad_hidden = cotangent.astype(F32) + rms_back(pair_total * gain_ffn, hidden, scale_ffn)
    grad_branch = grad_hidden.astype(BF16)
    grad_mixture = jnp.concatenate(
        [
            lax.dot_general(
                out_full[y], grad_branch, (((0,), (1,)), ((), ())), preferred_element_type=F32
            )
            for y in range(2)
        ],
        axis=0,
    ).astype(BF16)
    grad_tiles = exchange(grad_mixture.reshape(8, QUERY, ROWS), NEAR)

    dqt, mine, theirs = back_earlier(
        plan, rot_q, start_lanes, kv_earlier, grad_tiles, out_tiles, lse
    )
    earlier = (mine + swap(theirs, "yhi").astype(F32)).astype(BF16)
    back_one, back_two = shift_super(earlier[1], -1), shift_super(earlier[0], -2)
    grad_q, mine, theirs = back_own(
        plan, rot_q, start_lanes, kv_own, grad_tiles, out_tiles, lse, dqt
    )
    grad_kvs = (mine[0], swap(theirs[0], "yhi"), back_one, back_two)

    acts, grad_tiles = lax.optimization_barrier((acts, grad_tiles))
    output = (hidden + near_sum(near_keep([down(a, ffn_full) for a in acts]))).astype(BF16)
    branches = near_gather(after(grad_branch, grad_tiles))
    grad_out = exchange(out_weights(plan, mix_tiles, [b for p in branches for b in p]), WIDE)
    grad_out = jnp.sum(grad_out.astype(F32), axis=0).astype(BF16)
    grad_out = jnp.transpose(grad_out.reshape(96, 8, 24), (1, 2, 0))
    grad_out = exchange(grad_out, NEAR).reshape(2, 4, 24, 96)
    kept = jnp.where(yhi == 0, grad_out[0], grad_out[1])
    got = swap(jnp.where(yhi == 0, grad_out[1], grad_out[0]), "yhi")
    w_out_grad = jnp.stack(
        [jnp.where(yhi == 0, kept, got), jnp.where(yhi == 0, got, kept)], axis=1
    )
    w_out_grad = jnp.transpose(w_out_grad, (0, 1, 3, 2)).reshape(768, 24).astype(F32)

    unprojected = [None] * 4
    for d in (2, 1, 3, 0):
        unprojected[d] = unproject(
            d, grad_q, grad_kvs, raw, *token_blocks[d], qkv, cos, sin, head_gain
        )
    grad_normed = near_sum(near_keep([u[:2] for u in unprojected]))
    qkv_grad = dot(normed, jnp.concatenate([u[2] for u in unprojected], axis=0), TN)

    attn_gain_part = sum(u[3] for u in unprojected).reshape(128, 12, 1)
    head_part = sum(u[4] for u in unprojected)[0]
    q_gain_part = head_part[:HEAD] + head_part[HEAD : 2 * HEAD] + head_part[2 * HEAD : QUERY]
    head_part = jnp.concatenate([q_gain_part, head_part[QUERY:], jnp.zeros((4,), F32)])
    gain_parts = jnp.concatenate(
        [
            attn_gain_part,
            ffn_gain_part.reshape(128, 12, 1),
            jnp.broadcast_to(head_part.reshape(1, 12, 11), (128, 12, 11)),
        ],
        axis=2,
    )
    gain_high = gain_parts.astype(BF16)
    gain_low = (gain_parts - gain_high.astype(F32)).astype(BF16)
    qkv_grad = jnp.concatenate(
        [
            qkv_grad[:, : 5 * HEAD].astype(BF16).reshape(128, 12, 5 * HEAD),
            gain_high,
            gain_low,
            jnp.zeros((128, 12, HEAD - 26), BF16),
        ],
        axis=2,
    )
    qkv_grad = exchange(qkv_grad, ALL).reshape(8, 8, 2, 12, 6 * HEAD).astype(F32)
    qkv_grad = jnp.sum(qkv_grad, axis=(0, 2))
    gains = jnp.sum(qkv_grad[:, :, 5 * HEAD :], axis=0)
    gains = gains[:, :13] + gains[:, 13:26]
    head_gains = gains[:, 2:].reshape(-1)
    qkv_grad = jnp.transpose(qkv_grad, (1, 0, 2))
    w_query_grad = qkv_grad[:, :, :QUERY].reshape(12, -1)
    w_key_grad = qkv_grad[:, :, QUERY : QUERY + HEAD].reshape(12, -1)
    w_value_grad = qkv_grad[:, :, QUERY + HEAD : QUERY + 2 * HEAD].reshape(12, -1)

    scale_attn = rms_scale(inputs)
    input_grad = (grad_hidden + rms_back(grad_normed * gain_attn, inputs, scale_attn)).astype(BF16)

    ffn_sum = jnp.sum(ffn_got.astype(F32), axis=0).astype(BF16)
    ffn_grad = exchange(ffn_sum.reshape(8, 24, 3 * PADDED), NEAR)
    ffn_grad = jnp.transpose(ffn_grad, (1, 0, 2)).astype(F32)
    w_gate_grad, w_up_grad, w_down_grad = (
        ffn_grad[:, :, i * PADDED : i * PADDED + PART].reshape(24, -1) for i in range(3)
    )
    return (
        output,
        input_grad,
        gains[:, 0],
        w_query_grad,
        w_key_grad,
        w_value_grad,
        head_gains[:HEAD],
        head_gains[HEAD : 2 * HEAD],
        w_out_grad,
        gains[:, 1],
        w_gate_grad,
        w_up_grad,
        w_down_grad.T,
    )


def solution(mesh):
    mesh = Mesh(np.asarray(mesh.devices).reshape(2, 4, 4, 2, 2), ALL)
    rows = P(ALL, None)
    weights = (P("yhi", BLK), P(ALL), P(BLK, "yhi"), P(BLK, "yhi"), P("yhi", BLK))
    placed_in = (rows, P(), P(ALL), rows, rows, rows, P(), P()) + weights + (rows,)
    placed_out = (rows, rows, P(ALL), rows, rows, rows, P(), P()) + weights
    return jax.shard_map(
        per_device, mesh=mesh, in_specs=placed_in, out_specs=placed_out, check_vma=False
    )
```

```python
import functools

import jax
import jax.numpy as jnp
import numpy as np
from jax import lax
from jax.experimental import pallas as pl
from jax.experimental.pallas import tpu as pltpu
from jax.sharding import Mesh
from jax.sharding import PartitionSpec as P

EPS = 1e-05
THETA = 1000000.0
HEAD = 64
ROWS = 128
PAIR = 2 * ROWS
GROUP = 3
QUERY = GROUP * HEAD
LANES = ROWS * GROUP
KEY_TILE = 512
SUPER = 2048
EARLIER = 2 * SUPER
PART = 432
PADDED = 512
WIDTH = 1536
ALL = ("ylo", "z", "x", "core", "yhi")
BLK = ("ylo", "z", "x", "core")
WIDE = ("yhi", "ylo", "z")
NEAR = ("x", "core")
NN = (((1,), (0,)), ((), ()))
NT = (((1,), (1,)), ((), ()))
TN = (((0,), (0,)), ((), ()))
F32 = jnp.float32
BF16 = jnp.bfloat16
SCORE = HEAD**-0.5 * 1.4426950408889634


def dot(a, b, numbers=NN):
    return lax.dot_general(a, b, numbers, preferred_element_type=F32)


def rms_scale(v):
    return lax.rsqrt(jnp.mean(v * v, axis=-1, keepdims=True) + EPS)


def rms_back(grad, v, scale):
    inner = jnp.mean(grad * v, axis=-1, keepdims=True)
    return scale * (grad - v * scale * scale * inner)


def shift_x(v, distance):
    return lax.ppermute(v, "x", [((i + distance) % 4, i) for i in range(4)])


def swap(v, axis):
    return lax.ppermute(v, axis, [(0, 1), (1, 0)])


def shift_super(v, distance, other):
    pairs = [
        (2 * i + h, 2 * (i + distance) + (h + other) % 2)
        for i in range(8)
        for h in (0, 1)
        if 0 <= i + distance < 8
    ]
    return lax.ppermute(v, ("ylo", "z", "yhi"), pairs)


def exchange(v, axes):
    return lax.all_to_all(v, axes, split_axis=0, concat_axis=0, tiled=True)


def near_gather(v):
    blocks = [v] + [shift_x(v, d) for d in (1, 2, 3)]
    return [[b, swap(b, "core")] for b in blocks]


def near_keep(parts):
    return [
        (own.astype(F32) + swap(other, "core").astype(F32)).astype(BF16) for own, other in parts
    ]


def near_sum(kept):
    total = kept[0].astype(F32)
    for d in (1, 2, 3):
        total = total + shift_x(kept[d], -d).astype(F32)
    return total


def rel_to_abs(v, x, core):
    v = jnp.where(core == 0, v, v[:, ::-1])
    return lax.dynamic_slice_in_dim(jnp.concatenate([v, v], axis=0), (4 - x) % 4, 4, 0)


def abs_to_rel(v, x, core):
    v = jnp.where(core == 0, v, v[:, ::-1])
    return lax.dynamic_slice_in_dim(jnp.concatenate([v, v], axis=0), x, 4, 0)


def params(steps, mib):
    return pltpu.CompilerParams(
        dimension_semantics=("arbitrary",) * steps, vmem_limit_bytes=mib * 2**20
    )


def cost(flops, moved, exps=0):
    return pl.CostEstimate(flops=int(flops), bytes_accessed=int(moved), transcendentals=int(exps))


def stacked(a_ref, b_ref):
    return jnp.concatenate([a_ref[...], b_ref[...]], axis=0)


def head_sums(v):
    lane = lax.shift_right_logical(lax.broadcasted_iota(jnp.int32, (4 * HEAD, 4 * HEAD), 1), 6)
    row = lax.shift_right_logical(lax.broadcasted_iota(jnp.int32, (4 * HEAD, 4 * HEAD), 0), 6)
    ones = jnp.where(lane == row, 1.0, 0.0).astype(BF16)
    high = v.astype(BF16)
    low = (v - high.astype(F32)).astype(BF16)
    return dot(high, ones) + dot(low, ones)


def half_turn(v):
    lane = lax.broadcasted_iota(jnp.int32, v.shape, 1)
    return jnp.where(
        (lane & (HEAD - 1)) < HEAD // 2,
        pltpu.roll(v, v.shape[1] - HEAD // 2, 1),
        pltpu.roll(v, HEAD // 2, 1),
    )


def twice(v):
    return jnp.concatenate([v, v], axis=1)


def project_kernel(*refs):
    xs, (w_ref, gain_ref, cos_ref, sin_ref, head_gain_ref) = refs[:8], refs[8:13]
    normed_ref, q_ref, kv_ref, raw_ref = refs[13:]
    lane = lax.broadcasted_iota(jnp.int32, (PAIR, 2 * HEAD), 1)
    for d in range(4):
        rows = slice(d * PAIR, (d + 1) * PAIR)
        tiles = slice(2 * d, 2 * d + 2)
        x = stacked(*xs[tiles]).astype(F32)
        normed = (x * rms_scale(x) * gain_ref[...]).astype(BF16)
        normed_ref[rows, :] = normed
        raw = dot(normed, w_ref[...])
        heads = raw[:, : 4 * HEAD]
        raw_ref[d] = heads
        scale = lax.rsqrt(head_sums(heads * heads) * (1.0 / HEAD) + EPS)
        v = heads * scale * head_gain_ref[...]
        turned = v * twice(cos_ref[d]) + half_turn(v) * twice(sin_ref[d])
        q_ref[tiles] = turned[:, :QUERY].astype(BF16).reshape(2, ROWS, QUERY)
        kv = jnp.where(lane < HEAD, raw[:, 4 * HEAD :], turned[:, 2 * HEAD :])
        kv_ref[tiles] = kv.astype(BF16).reshape(2, ROWS, 2 * HEAD)


def project(xs, w, gain, cos, sin, head_gain):
    return pl.pallas_call(
        project_kernel,
        out_shape=(
            jax.ShapeDtypeStruct((4 * PAIR, WIDTH), BF16),
            jax.ShapeDtypeStruct((8, ROWS, QUERY), BF16),
            jax.ShapeDtypeStruct((8, ROWS, 2 * HEAD), BF16),
            jax.ShapeDtypeStruct((4, PAIR, 4 * HEAD), F32),
        ),
        compiler_params=params(0, 32),
        cost_estimate=cost(8 * PAIR * WIDTH * 384, 1e7),
    )(*xs, w, gain, cos, sin, head_gain)


def unproject_kernel(
    gq_ref, g0_ref, g1_ref, g2_ref, g3_ref, g4_ref, g5_ref, raw_ref, x0_ref, x1_ref, w_ref, cos_ref,
    sin_ref, head_gain_ref, part0_ref, part1_ref, graw_ref, attn_ref, heads_ref,
):
    gq = gq_ref[...].reshape(PAIR, 4 * HEAD).astype(F32)
    gkv = g0_ref[...]
    for ref in (g1_ref, g2_ref, g3_ref, g4_ref, g5_ref):
        gkv = gkv + ref[...].astype(F32)
    gkv = gkv.reshape(PAIR, 2 * HEAD)
    lane = lax.broadcasted_iota(jnp.int32, (PAIR, 2 * HEAD), 1)
    gk = (gkv * HEAD**-0.5).astype(BF16).astype(F32)
    g = jnp.concatenate([gq[:, : 2 * HEAD], jnp.where(lane < HEAD, gq[:, 2 * HEAD :], gk)], axis=1)
    g = g * twice(cos_ref[0]) - half_turn(g) * twice(sin_ref[0])
    raw = raw_ref[0]
    scale = lax.rsqrt(head_sums(raw * raw) * (1.0 / HEAD) + EPS)
    heads_ref[...] = jnp.sum(g * raw * scale, axis=0, keepdims=True)
    e = g * head_gain_ref[...]
    inner = head_sums(e * raw) * (1.0 / HEAD)
    graw = scale * (e - raw * scale * scale * inner)
    graw = jnp.concatenate([graw, jnp.where(lane < HEAD, gkv, 0.0)], axis=1).astype(BF16)
    graw_ref[...] = graw
    grad = dot(graw, w_ref[...], NT)
    x = stacked(x0_ref, x1_ref).astype(F32)
    attn_ref[...] = jnp.sum(grad * x * rms_scale(x), axis=0, keepdims=True)
    grad = grad.astype(BF16)
    part0_ref[...] = grad[:ROWS]
    part1_ref[...] = grad[ROWS:]


def unproject(d, gq, gkvs, raw, x0, x1, w, cos, sin, head_gain):
    def whole_of(*shape):
        return pl.BlockSpec(shape, lambda i: (0,) * len(shape))

    def at_d(*shape):
        return pl.BlockSpec(shape, lambda i: (d,) + (0,) * (len(shape) - 1))

    rows = whole_of(ROWS, WIDTH)
    kv = at_d(2, ROWS, 2 * HEAD)
    table = at_d(1, PAIR, 2 * HEAD)
    outs = (
        jax.ShapeDtypeStruct((ROWS, WIDTH), BF16),
        jax.ShapeDtypeStruct((ROWS, WIDTH), BF16),
        jax.ShapeDtypeStruct((PAIR, 6 * HEAD), BF16),
        jax.ShapeDtypeStruct((1, WIDTH), F32),
        jax.ShapeDtypeStruct((1, 4 * HEAD), F32),
    )
    return pl.pallas_call(
        unproject_kernel,
        out_shape=outs,
        grid=(1,),
        in_specs=[at_d(2, ROWS, 4 * HEAD)] + [kv] * 6 + [at_d(1, PAIR, 4 * HEAD), rows, rows]
        + [whole_of(WIDTH, 6 * HEAD), table, table, whole_of(1, 4 * HEAD)],
        out_specs=tuple(whole_of(*o.shape) for o in outs),
        compiler_params=params(1, 24),
        cost_estimate=cost(2 * PAIR * WIDTH * 384, 4e6),
    )(gq, *gkvs, raw, x0, x1, w, cos, sin, head_gain)


def ffn_kernel(x0_ref, x1_ref, c0_ref, c1_ref, w_ref, part0_ref, part1_ref, act_ref, gu_ref, total):
    y = pl.program_id(0)
    x = stacked(x0_ref, x1_ref)
    gate_up = dot(x, w_ref[0, :, : 2 * PADDED])
    gate, up = gate_up[:, :PADDED], gate_up[:, PADDED:]
    grad_act = dot(stacked(c0_ref, c1_ref), w_ref[0, :, 2 * PADDED :])
    sig = 1.0 / (1.0 + jnp.exp(-gate))
    silu = gate * sig
    act_ref[0] = (silu * up).astype(BF16)
    grad_gate = grad_act * up * sig * (1.0 + gate * (1.0 - sig))
    grads = jnp.concatenate([grad_gate, grad_act * silu], axis=1).astype(BF16)
    gu_ref[0] = grads
    part = dot(grads, w_ref[0, :, : 2 * PADDED], NT)

    @pl.when(y == 0)
    def _():
        total[...] = part

    @pl.when(y == 1)
    def _():
        whole_part = (total[...] + part).astype(BF16)
        part0_ref[...] = whole_part[:ROWS]
        part1_ref[...] = whole_part[ROWS:]


def ffn(x0, x1, c0, c1, w):
    rows = pl.BlockSpec((ROWS, WIDTH), lambda y: (0, 0))
    return pl.pallas_call(
        ffn_kernel,
        out_shape=(
            jax.ShapeDtypeStruct((ROWS, WIDTH), BF16),
            jax.ShapeDtypeStruct((ROWS, WIDTH), BF16),
            jax.ShapeDtypeStruct((2, PAIR, PADDED), BF16),
            jax.ShapeDtypeStruct((2, PAIR, 2 * PADDED), BF16),
        ),
        grid=(2,),
        in_specs=[rows] * 4 + [pl.BlockSpec((1, WIDTH, 3 * PADDED), lambda y: (y, 0, 0))],
        out_specs=(
            rows,
            rows,
            pl.BlockSpec((1, PAIR, PADDED), lambda y: (y, 0, 0)),
            pl.BlockSpec((1, PAIR, 2 * PADDED), lambda y: (y, 0, 0)),
        ),
        scratch_shapes=[pltpu.VMEM((PAIR, WIDTH), F32)],
        compiler_params=params(1, 40),
        cost_estimate=cost(2 * 2 * PAIR * WIDTH * 5 * PADDED, 14e6),
    )(x0, x1, c0, c1, w)


def down_kernel(act_ref, w_ref, part0_ref, part1_ref, total):
    y = pl.program_id(0)
    part = dot(act_ref[0], w_ref[0], NT)

    @pl.when(y == 0)
    def _():
        total[...] = part

    @pl.when(y == 1)
    def _():
        whole_part = (total[...] + part).astype(BF16)
        part0_ref[...] = whole_part[:ROWS]
        part1_ref[...] = whole_part[ROWS:]


def down(act, w):
    rows = pl.BlockSpec((ROWS, WIDTH), lambda y: (0, 0))
    return pl.pallas_call(
        down_kernel,
        out_shape=(jax.ShapeDtypeStruct((ROWS, WIDTH), BF16),) * 2,
        grid=(2,),
        in_specs=[
            pl.BlockSpec((1, PAIR, PADDED), lambda y: (y, 0, 0)),
            pl.BlockSpec((1, WIDTH, PADDED), lambda y: (y, 0, 2)),
        ],
        out_specs=(rows, rows),
        scratch_shapes=[pltpu.VMEM((PAIR, WIDTH), F32)],
        compiler_params=params(1, 24),
        cost_estimate=cost(2 * 2 * PAIR * WIDTH * PADDED, 5e6),
    )(act, w)


def ffn_weights_kernel(*refs):
    xs, cs, gus, acts, out_ref = refs[:8], refs[8:16], refs[16:20], refs[20:24], refs[24]
    grad_gu, grad_d = 0.0, 0.0
    for d in range(4):
        grad_gu = grad_gu + dot(stacked(*xs[2 * d : 2 * d + 2]), gus[d][0], TN)
        grad_d = grad_d + dot(stacked(*cs[2 * d : 2 * d + 2]), acts[d][0], TN)
    out_ref[0, :, :PART] = grad_gu[:, :PART]
    out_ref[0, :, PART : 2 * PART] = grad_gu[:, PADDED : PADDED + PART]
    out_ref[0, :, 2 * PART :] = grad_d[:, :PART]


def ffn_weights(xs, cs, gus, acts):
    tall = 256
    rows = pl.BlockSpec((ROWS, tall), lambda y, m: (0, m))
    return pl.pallas_call(
        ffn_weights_kernel,
        out_shape=jax.ShapeDtypeStruct((2, WIDTH, 3 * PART), F32),
        grid=(2, WIDTH // tall),
        in_specs=[rows] * 16
        + [pl.BlockSpec((1, PAIR, 2 * PADDED), lambda y, m: (y, 0, 0))] * 4
        + [pl.BlockSpec((1, PAIR, PADDED), lambda y, m: (y, 0, 0))] * 4,
        out_specs=pl.BlockSpec((1, tall, 3 * PART), lambda y, m: (y, m, 0)),
        compiler_params=params(2, 40),
        cost_estimate=cost(2 * 2 * 1024 * WIDTH * 3 * PADDED, 24e6),
    )(*xs, *cs, *gus, *acts)


def out_project_kernel(mix_ref, w_ref, part0_ref, part1_ref):
    part = dot(mix_ref[...].reshape(PAIR, QUERY), w_ref[...], NT).astype(BF16)
    part0_ref[...] = part[:ROWS]
    part1_ref[...] = part[ROWS:]


def out_project(d, mix, w):
    rows = pl.BlockSpec((ROWS, WIDTH), lambda i: (0, 0))
    return pl.pallas_call(
        out_project_kernel,
        out_shape=(jax.ShapeDtypeStruct((ROWS, WIDTH), BF16),) * 2,
        grid=(1,),
        in_specs=[
            pl.BlockSpec((2, ROWS, QUERY), lambda i: (d, 0, 0)),
            pl.BlockSpec((WIDTH, QUERY), lambda i: (0, 0)),
        ],
        out_specs=(rows, rows),
        compiler_params=params(1, 16),
        cost_estimate=cost(2 * PAIR * WIDTH * QUERY, 2e6),
    )(mix, w)


def out_back_kernel(w_ref, *refs):
    for t in range(8):
        refs[8][t] = dot(refs[t][...], w_ref[...]).astype(BF16)


def out_back(branches, w):
    return pl.pallas_call(
        out_back_kernel,
        out_shape=jax.ShapeDtypeStruct((8, ROWS, QUERY), BF16),
        compiler_params=params(0, 16),
        cost_estimate=cost(8 * PAIR * WIDTH * QUERY, 4e6),
    )(w, *branches)


def out_weights_kernel(mix_ref, *refs):
    branches, (out_ref, total) = refs[:8], refs[8:]
    grad = 0.0
    for d in range(4):
        mix = mix_ref[2 * d : 2 * d + 2].reshape(PAIR, QUERY)
        grad = grad + dot(mix, stacked(*branches[2 * d : 2 * d + 2]), TN)
    total[...] = grad
    for half in (0, 1):
        for s in range(8):
            piece = total[half * 96 : half * 96 + 96, s * 192 : s * 192 + 192]
            out_ref[half * 8 + s] = piece.astype(BF16)


def out_weights(mix, branches):
    return pl.pallas_call(
        out_weights_kernel,
        out_shape=jax.ShapeDtypeStruct((16, 96, 192), BF16),
        scratch_shapes=[pltpu.VMEM((QUERY, WIDTH), F32)],
        compiler_params=params(0, 24),
        cost_estimate=cost(2 * 1024 * WIDTH * QUERY, 4e6),
    )(mix, *branches)


def side_by_side(t):
    return jnp.concatenate([t[g * HEAD : (g + 1) * HEAD] for g in range(GROUP)], axis=1)


def on_top(t):
    return jnp.concatenate([t[:, g * ROWS : (g + 1) * ROWS] for g in range(GROUP)], axis=0)


def key_loops(plan, at, base, start, visit, state):
    f = pl.program_id(0)
    lo, m1, m2, hi = (plan[f, at + i] for i in range(4))
    place = lax.rem(lax.broadcasted_iota(jnp.int32, (1, LANES), 1), ROWS) + plan[f, 0]

    def masked(j, state):
        key = lax.broadcasted_iota(jnp.int32, (KEY_TILE, LANES), 0) + (j * KEY_TILE + base)
        return visit(j, state, (key >= start) & (key <= place))

    state = lax.fori_loop(lo, m1, masked, state)
    state = lax.fori_loop(m1, m2, lambda j, s: visit(j, s, None), state)
    return lax.fori_loop(m2, hi, masked, state)


def rows_of(j):
    return pl.ds(pl.multiple_of(j * KEY_TILE, KEY_TILE), KEY_TILE)


def chunks(plan, supers):
    for b in range(supers):
        for half in (0, 1):
            for f in range(8):
                side = plan[0, 10] if half == 0 else 1 - plan[0, 10]
                yield b, half, pl.multiple_of(b * SUPER + f * PAIR + side * ROWS, ROWS), plan[f, 1]


def line_up(plan, kv_refs, kv, kvt):
    @pl.when(pl.program_id(0) == 0)
    def _():
        for b, half, place, sent in chunks(plan, len(kv_refs) // 2):
            block = kv_refs[2 * b + half][sent]
            kv[pl.ds(place, ROWS), :] = block
            kvt[:, pl.ds(place, ROWS)] = block.astype(F32).T.astype(BF16)


def attend_body(at, base, plan, q_ref, start_ref, kv, kvt, state):
    qt = side_by_side(q_ref[0].astype(F32).T)
    qt = jnp.concatenate([jnp.zeros_like(qt), qt], axis=0).astype(BF16)

    def visit(j, state, mask):
        total, accum = state
        weights = jnp.exp2(dot(kv[rows_of(j), :], qt) * SCORE)
        if mask is not None:
            weights = jnp.where(mask, weights, 0.0)
        total = total + jnp.sum(weights, axis=0, keepdims=True)
        return total, accum + dot(kvt[:HEAD, rows_of(j)], weights.astype(BF16))

    return key_loops(plan, at, base, start_ref[0], visit, state)


def attend_own_kernel(plan, q_ref, start_ref, *refs):
    kv_refs, (accum_ref, total_ref, kv, kvt) = refs[:2], refs[2:]
    line_up(plan, kv_refs, kv, kvt)
    state = (jnp.zeros((1, LANES), F32), jnp.zeros((HEAD, LANES), F32))
    total, accum = attend_body(6, EARLIER, plan, q_ref, start_ref, kv, kvt, state)
    accum_ref[0] = accum
    total_ref[0] = total


def attend_earlier_kernel(plan, q_ref, start_ref, *refs):
    kv_refs, (accum_ref, total_ref, mix_ref, out_ref, lse_ref, kv, kvt) = refs[:4], refs[4:]
    line_up(plan, kv_refs, kv, kvt)
    state = (total_ref[0], accum_ref[0])
    total, accum = attend_body(2, 0, plan, q_ref, start_ref, kv, kvt, state)
    out = accum / total
    out_ref[0] = out
    mix_ref[0] = on_top(out).T.astype(BF16)
    lse_ref[0] = jnp.log2(total)


def back_body(at, base, plan, q_ref, start_ref, g_ref, out_ref, lse_ref, kv, kvt, dkv, dqt):
    @pl.when(pl.program_id(0) == 0)
    def _():
        dkv[...] = jnp.zeros_like(dkv)

    qt = side_by_side(q_ref[0].astype(F32).T)
    gt = side_by_side(g_ref[0].astype(F32).T)
    delta = jnp.sum(gt * out_ref[0], axis=0, keepdims=True)
    zero = jnp.zeros_like(qt)
    gt = jnp.concatenate([gt, zero], axis=0)
    qt = jnp.concatenate([zero, qt], axis=0)
    both_t = jnp.concatenate([gt, qt], axis=1).astype(BF16)
    both = jnp.concatenate([gt.T, qt.T], axis=0).astype(BF16)
    lse = lse_ref[0]

    def visit(j, dqt, mask):
        pair = dot(kv[rows_of(j), :], both_t)
        weights = jnp.exp2(pair[:, LANES:] * SCORE - lse)
        if mask is not None:
            weights = jnp.where(mask, weights, 0.0)
        grads = (weights * (pair[:, :LANES] - delta)).astype(BF16)
        sides = jnp.concatenate([weights.astype(BF16), grads], axis=1)
        dkv[rows_of(j), :] += dot(sides, both)
        return dqt + dot(kvt[HEAD:, rows_of(j)], grads)

    return key_loops(plan, at, base, start_ref[0], visit, dqt)


def hand_out(plan, supers, dkv, mine_ref, theirs_ref):
    @pl.when(pl.program_id(0) == 7)
    def _():
        for b, half, place, sent in chunks(plan, supers):
            ref = (mine_ref, theirs_ref)[half]
            ref[b, sent] = dkv[pl.ds(place, ROWS), :].astype(ref.dtype)


def back_earlier_kernel(plan, q_ref, start_ref, *refs):
    kv_refs, (g_ref, out_ref, lse_ref, dqt_ref, mine_ref, theirs_ref, kv, kvt, dkv) = refs[:4], refs[4:]
    line_up(plan, kv_refs, kv, kvt)
    dqt = jnp.zeros((HEAD, LANES), F32)
    dqt_ref[0] = back_body(
        2, 0, plan, q_ref, start_ref, g_ref, out_ref, lse_ref, kv, kvt, dkv, dqt
    )
    hand_out(plan, 2, dkv, mine_ref, theirs_ref)


def back_own_kernel(plan, q_ref, start_ref, *refs):
    kv_refs, (g_ref, out_ref, lse_ref, dqt_ref) = refs[:2], refs[2:6]
    dq_ref, mine_ref, theirs_ref, kv, kvt, dkv = refs[6:]
    line_up(plan, kv_refs, kv, kvt)
    dqt = back_body(
        6, EARLIER, plan, q_ref, start_ref, g_ref, out_ref, lse_ref, kv, kvt, dkv, dqt_ref[0]
    )
    dq = on_top(dqt * HEAD**-0.5).T
    dq_ref[0] = jnp.concatenate([dq, jnp.zeros((ROWS, HEAD), F32)], axis=1).astype(BF16)
    hand_out(plan, 1, dkv, mine_ref, theirs_ref)


def whole(*shape):
    return pl.BlockSpec(shape, lambda f, plan: (0,) * len(shape))


def tile(*shape):
    return pl.BlockSpec((1,) + shape, lambda f, plan: (f,) + (0,) * len(shape))


def placed(*shape):
    return pl.BlockSpec((1,) + shape, lambda f, plan: (plan[f, 1],) + (0,) * len(shape))


def tiles_call(kernel, supers, outs, more_ins, out_specs, flops, back):
    keys = supers * SUPER
    scratch = [pltpu.VMEM((keys, 2 * HEAD), BF16), pltpu.VMEM((2 * HEAD, keys), BF16)]
    if back:
        scratch.append(pltpu.VMEM((keys, 2 * HEAD), F32))
    ins = [placed(ROWS, QUERY), tile(1, LANES)] + [whole(8, ROWS, 2 * HEAD)] * (2 * supers)
    return pl.pallas_call(
        kernel,
        out_shape=outs,
        grid_spec=pltpu.PrefetchScalarGridSpec(
            num_scalar_prefetch=1,
            grid=(8,),
            in_specs=ins + more_ins,
            out_specs=out_specs,
            scratch_shapes=scratch,
        ),
        compiler_params=params(1, 32),
        cost_estimate=cost(flops, 8e6, 1e7),
    )


TILE_T = jax.ShapeDtypeStruct((8, HEAD, LANES), F32)
TILE_ROW = jax.ShapeDtypeStruct((8, 1, LANES), F32)
STATE = [tile(HEAD, LANES), tile(1, LANES)]


def attend_own(plan, q, start, kvs):
    call = tiles_call(attend_own_kernel, 1, (TILE_T, TILE_ROW), [], tuple(STATE), 4e9, False)
    return call(plan, q, start, *kvs)


def attend_earlier(plan, q, start, kvs, state):
    outs = (jax.ShapeDtypeStruct((8, ROWS, QUERY), BF16), TILE_T, TILE_ROW)
    specs = (placed(ROWS, QUERY),) + tuple(STATE)
    call = tiles_call(attend_earlier_kernel, 2, outs, STATE, specs, 8e9, False)
    return call(plan, q, start, *kvs, *state)


def sent_back(supers):
    shape = (supers, 8, ROWS, 2 * HEAD)
    return [jax.ShapeDtypeStruct(shape, F32), jax.ShapeDtypeStruct(shape, BF16)], [whole(*shape)] * 2


def back_earlier(plan, q, start, kvs, grad, out, lse):
    shapes, specs = sent_back(2)
    call = tiles_call(
        back_earlier_kernel, 2, [TILE_T] + shapes, [placed(ROWS, QUERY)] + STATE,
        [tile(HEAD, LANES)] + specs, 20e9, True,
    )
    return call(plan, q, start, *kvs, grad, out, lse)


def back_own(plan, q, start, kvs, grad, out, lse, dqt):
    shapes, specs = sent_back(1)
    dq = jax.ShapeDtypeStruct((8, ROWS, 4 * HEAD), BF16)
    call = tiles_call(
        back_own_kernel, 1, [dq] + shapes, [placed(ROWS, QUERY)] + STATE + [tile(HEAD, LANES)],
        [placed(ROWS, 4 * HEAD)] + specs, 10e9, True,
    )
    return call(plan, q, start, *kvs, grad, out, lse, dqt)


def after(v, *others):
    return lax.optimization_barrier((v,) + others)[0]


def per_device(
    tokens,
    segments,
    attn_gain,
    w_query,
    w_key,
    w_value,
    q_gain,
    k_gain,
    w_out,
    ffn_gain,
    w_gate,
    w_up,
    w_down,
    cotangent,
):
    ylo, z, x, core, yhi = (lax.axis_index(a) for a in ALL)
    sup = ylo * 4 + z

    qkv_own = jnp.concatenate(
        [
            w_query.reshape(12, 8, QUERY),
            w_key.reshape(12, 8, HEAD),
            w_value.reshape(12, 8, HEAD),
            jnp.broadcast_to(attn_gain[:, None, None], (12, 8, 1)),
            jnp.broadcast_to(ffn_gain[:, None, None], (12, 8, 1)),
            jnp.zeros((12, 8, HEAD - 2), BF16),
        ],
        axis=-1,
    )
    token_blocks = near_gather(tokens)
    qkv_rows = exchange(jnp.transpose(qkv_own, (1, 0, 2)), NEAR).reshape(1, 96, 6 * HEAD)
    qkv = exchange(jnp.broadcast_to(qkv_rows, (16, 96, 6 * HEAD)), WIDE)
    qkv = jnp.transpose(qkv.reshape(2, 8, 8, 12, 6 * HEAD), (1, 2, 0, 3, 4)).reshape(WIDTH, 6 * HEAD)
    gain_attn = qkv[:, 5 * HEAD].astype(F32)
    gain_ffn = qkv[:, 5 * HEAD + 1].astype(F32)

    token_index = jnp.arange(segments.shape[0], dtype=jnp.int32)
    begins = jnp.concatenate([jnp.ones((1,), jnp.bool_), segments[1:] != segments[:-1]])
    starts = lax.cummax(jnp.where(begins, token_index, 0), axis=0)
    own_starts = lax.dynamic_slice(
        starts.reshape(8, 8, 2, ROWS), (sup, 0, yhi, 0), (1, 8, 1, ROWS)
    ).reshape(8, ROWS)
    first = sup * SUPER + jnp.arange(8, dtype=jnp.int32) * PAIR + yhi * ROWS
    own_places = first[:, None] + jnp.arange(ROWS, dtype=jnp.int32)[None]
    positions = abs_to_rel((own_places - own_starts).reshape(4, 2, ROWS), x, core)
    frequency = THETA ** (-jnp.arange(HEAD // 2, dtype=F32) * 2.0 / HEAD)
    angles = positions.reshape(4, PAIR, 1).astype(F32) * frequency
    cosine, sine = jnp.cos(angles), jnp.sin(angles)
    cos = jnp.concatenate([cosine] * 4, axis=-1)
    sin = jnp.concatenate([-sine, sine] * 2, axis=-1)
    head_gain = jnp.concatenate([q_gain, q_gain, q_gain, k_gain]).astype(F32)[None]

    window = (sup - 2) * SUPER
    lo = (own_starts[:, 0] - window) // KEY_TILE
    hi = (first + ROWS - 1 - window) // KEY_TILE + 1
    m1 = jnp.clip((own_starts[:, -1] - window + KEY_TILE - 1) // KEY_TILE, lo, hi)
    m2 = jnp.clip((first + 1 - window) // KEY_TILE, m1, hi)
    order = jnp.arange(8, dtype=jnp.int32)
    relative = ((order // 2 - x) % 4) * 2 + (order % 2 + core) % 2
    edge = EARLIER // KEY_TILE
    plan = jnp.stack(
        [first - window, relative]
        + [jnp.minimum(v, edge) for v in (lo, m1, m2, hi)]
        + [jnp.maximum(v - edge, 0) for v in (lo, m1, m2, hi)]
        + [jnp.broadcast_to(yhi, (8,))],
        axis=1,
    ).astype(jnp.int32)
    start_lanes = jnp.tile(own_starts - window, (1, GROUP)).reshape(8, 1, LANES)

    normed, rot_q, kv, raw = project(
        [b for p in token_blocks for b in p], qkv, gain_attn[None], cos, sin, head_gain
    )

    out_own = jnp.transpose(w_out.reshape(4, QUERY, 24), (0, 2, 1))
    rows_own = jnp.concatenate(
        [
            jnp.pad(w.reshape(24, 8, PART), ((0, 0), (0, 0), (0, PADDED - PART))).transpose(1, 0, 2)
            for w in (w_gate, w_up, w_down.T)
        ]
        + [jnp.concatenate([out_own, out_own], axis=0)],
        axis=-1,
    )
    rows_own = exchange(after(rows_own, kv), NEAR).reshape(192, 3 * PADDED + QUERY)
    ffn_full = lax.all_gather(rows_own[:, : 3 * PADDED], WIDE, axis=0, tiled=True)
    ffn_full = ffn_full.reshape(2, WIDTH, 3 * PADDED)

    kv_own = [kv, swap(kv, "yhi")]
    kv_earlier = [shift_super(kv, 2, 0), shift_super(kv, 2, 1), shift_super(kv, 1, 0), shift_super(kv, 1, 1)]
    state = attend_own(plan, rot_q, start_lanes, kv_own)
    out_rows = jnp.broadcast_to(rows_own[None, :, 3 * PADDED :], (16, 192, QUERY))
    out_both = exchange(out_rows, WIDE).reshape(2, WIDTH, QUERY)
    w_out_t = jnp.where(x < 2, out_both[0], out_both[1])
    cot_blocks = near_gather(after(cotangent, kv))
    mix, out_tiles, lse = attend_earlier(plan, rot_q, start_lanes, kv_earlier, state)
    mix, cot_blocks, w_out_t = lax.optimization_barrier((mix, cot_blocks, w_out_t))

    inputs = tokens.astype(F32)
    parts = [None] * 4
    for d in (2, 1, 3, 0):
        parts[d] = out_project(d, mix, w_out_t)
    hidden = inputs + near_sum(near_keep(parts))
    scale_ffn = rms_scale(hidden)
    scaled_ffn = hidden * scale_ffn
    normed_ffn = (scaled_ffn * gain_ffn).astype(BF16)

    ffn_blocks = [[b] for b in [normed_ffn] + [shift_x(normed_ffn, d) for d in (1, 2, 3)]]
    ffn_blocks[0].append(swap(normed_ffn, "core"))
    ffn_outs = [None] * 4
    before = {1: 0, 3: 0, 2: 1}
    for d in (0, 1, 3, 2):
        if d > 0:
            block = after(ffn_blocks[d][0], ffn_outs[before[d]][0])
            ffn_blocks[d] = [block, swap(block, "core")]
        blocks = ffn_blocks[d]
        if d == 3:
            blocks = after(blocks, ffn_outs[1][0])
        if d == 2:
            blocks = after(blocks, ffn_outs[3][0])
        ffn_outs[d] = ffn(*blocks, *cot_blocks[d], ffn_full)
    acts, gus = [o[2] for o in ffn_outs], [o[3] for o in ffn_outs]
    kept, gus = lax.optimization_barrier((near_keep([o[:2] for o in ffn_outs]), gus))
    pair_total = near_sum(kept)
    weight_grads = ffn_weights(
        [b for p in ffn_blocks for b in p], [b for p in cot_blocks for b in p], gus, acts
    )
    pair_total, weight_grads = lax.optimization_barrier((pair_total, weight_grads))
    ffn_sum = lax.psum_scatter(
        weight_grads.reshape(2 * WIDTH, 3 * PART), WIDE, scatter_dimension=0, tiled=True
    )

    ffn_gain_part = jnp.sum(pair_total * scaled_ffn, axis=0)
    grad_hidden = cotangent.astype(F32) + rms_back(pair_total * gain_ffn, hidden, scale_ffn)
    grad_branch = grad_hidden.astype(BF16)
    branches = [b for p in near_gather(grad_branch) for b in p]
    grad_mix = out_back(branches, w_out_t)

    dqt, mine, theirs = back_earlier(plan, rot_q, start_lanes, kv_earlier, grad_mix, out_tiles, lse)
    mine = mine.astype(BF16)
    sent = [
        shift_super(mine[1], -1, 0),
        shift_super(theirs[1], -1, 1),
        shift_super(mine[0], -2, 0),
        shift_super(theirs[0], -2, 1),
    ]
    grad_q, mine, theirs = back_own(
        plan, rot_q, start_lanes, kv_own, grad_mix, out_tiles, lse, dqt
    )
    grad_kvs = [mine[0], swap(theirs[0], "yhi")] + sent

    acts, branches, dqt = lax.optimization_barrier((acts, branches, dqt))
    output = (hidden + near_sum(near_keep([down(a, ffn_full) for a in acts]))).astype(BF16)
    grad_out = exchange(out_weights(mix, branches), WIDE)
    grad_out = jnp.sum(grad_out.astype(F32), axis=0).astype(BF16)
    grad_out = jnp.transpose(grad_out.reshape(96, 8, 24), (1, 2, 0))
    grad_out = exchange(grad_out, NEAR).reshape(2, 4, 24, 96)
    kept = jnp.where(yhi == 0, grad_out[0], grad_out[1])
    got = swap(jnp.where(yhi == 0, grad_out[1], grad_out[0]), "yhi")
    w_out_grad = jnp.stack(
        [jnp.where(yhi == 0, kept, got), jnp.where(yhi == 0, got, kept)], axis=1
    )
    w_out_grad = jnp.transpose(w_out_grad, (0, 1, 3, 2)).reshape(768, 24).astype(F32)

    unprojected = [None] * 4
    for d in (2, 1, 3, 0):
        unprojected[d] = unproject(
            d, grad_q, grad_kvs, raw, *token_blocks[d], qkv, cos, sin, head_gain
        )
    kept = near_keep([u[:2] for u in unprojected])
    kept, normed = lax.optimization_barrier((kept, normed))
    grad_normed = near_sum(kept)
    qkv_grad = dot(normed, jnp.concatenate([u[2] for u in unprojected], axis=0), TN)

    attn_gain_part = sum(u[3] for u in unprojected).reshape(128, 12, 1)
    head_part = sum(u[4] for u in unprojected)[0]
    q_gain_part = head_part[:HEAD] + head_part[HEAD : 2 * HEAD] + head_part[2 * HEAD : QUERY]
    head_part = jnp.concatenate([q_gain_part, head_part[QUERY:], jnp.zeros((4,), F32)])
    gain_parts = jnp.concatenate(
        [
            attn_gain_part,
            ffn_gain_part.reshape(128, 12, 1),
            jnp.broadcast_to(head_part.reshape(1, 12, 11), (128, 12, 11)),
        ],
        axis=2,
    )
    gain_high = gain_parts.astype(BF16)
    gain_low = (gain_parts - gain_high.astype(F32)).astype(BF16)
    qkv_grad = jnp.concatenate(
        [
            qkv_grad[:, : 5 * HEAD].astype(BF16).reshape(128, 12, 5 * HEAD),
            gain_high,
            gain_low,
            jnp.zeros((128, 12, HEAD - 26), BF16),
        ],
        axis=2,
    )
    qkv_grad = exchange(qkv_grad, ALL).reshape(8, 8, 2, 12, 6 * HEAD).astype(F32)
    qkv_grad = jnp.sum(qkv_grad, axis=(0, 2))
    gains = jnp.sum(qkv_grad[:, :, 5 * HEAD :], axis=0)
    gains = gains[:, :13] + gains[:, 13:26]
    head_gains = gains[:, 2:].reshape(-1)
    qkv_grad = jnp.transpose(qkv_grad, (1, 0, 2))
    w_query_grad = qkv_grad[:, :, :QUERY].reshape(12, -1)
    w_key_grad = qkv_grad[:, :, QUERY : QUERY + HEAD].reshape(12, -1)
    w_value_grad = qkv_grad[:, :, QUERY + HEAD : QUERY + 2 * HEAD].reshape(12, -1)

    scale_attn = rms_scale(inputs)
    input_grad = (grad_hidden + rms_back(grad_normed * gain_attn, inputs, scale_attn)).astype(BF16)

    ffn_grad = exchange(ffn_sum.astype(BF16).reshape(8, 24, 3 * PART), NEAR)
    ffn_grad = jnp.transpose(ffn_grad, (1, 0, 2)).astype(F32)
    w_gate_grad, w_up_grad, w_down_grad = (
        ffn_grad[:, :, i * PART : (i + 1) * PART].reshape(24, -1) for i in range(3)
    )
    return (
        output,
        input_grad,
        gains[:, 0],
        w_query_grad,
        w_key_grad,
        w_value_grad,
        head_gains[:HEAD],
        head_gains[HEAD : 2 * HEAD],
        w_out_grad,
        gains[:, 1],
        w_gate_grad,
        w_up_grad,
        w_down_grad.T,
    )


def solution(mesh):
    mesh = Mesh(np.asarray(mesh.devices).reshape(2, 4, 4, 2, 2), ALL)
    rows = P(ALL, None)
    weights = (P("yhi", BLK), P(ALL), P(BLK, "yhi"), P(BLK, "yhi"), P("yhi", BLK))
    placed_in = (rows, P(), P(ALL), rows, rows, rows, P(), P()) + weights + (rows,)
    placed_out = (rows, rows, P(ALL), rows, rows, rows, P(), P()) + weights
    return jax.shard_map(
        per_device, mesh=mesh, in_specs=placed_in, out_specs=placed_out, check_vma=False
    )
```

```python
import functools

import jax
import jax.numpy as jnp
import numpy as np
from jax import lax
from jax.experimental import pallas as pl
from jax.experimental.pallas import tpu as pltpu
from jax.sharding import Mesh
from jax.sharding import PartitionSpec as P

EPS = 1e-05
THETA = 1000000.0
HEAD = 64
ROWS = 128
PAIR = 2 * ROWS
GROUP = 3
QUERY = GROUP * HEAD
LANES = ROWS * GROUP
KEY_TILE = 512
SUPER = 2048
EARLIER = 2 * SUPER
PART = 432
PADDED = 512
WIDTH = 1536
ALL = ("ylo", "z", "x", "core", "yhi")
BLK = ("ylo", "z", "x", "core")
WIDE = ("yhi", "ylo", "z")
NEAR = ("x", "core")
NN = (((1,), (0,)), ((), ()))
NT = (((1,), (1,)), ((), ()))
TN = (((0,), (0,)), ((), ()))
F32 = jnp.float32
BF16 = jnp.bfloat16
SCORE = HEAD**-0.5 * 1.4426950408889634


def dot(a, b, numbers=NN):
    return lax.dot_general(a, b, numbers, preferred_element_type=F32)


def rms_scale(v):
    return lax.rsqrt(jnp.mean(v * v, axis=-1, keepdims=True) + EPS)


def rms_back(grad, v, scale):
    inner = jnp.mean(grad * v, axis=-1, keepdims=True)
    return scale * (grad - v * scale * scale * inner)


def shift_x(v, distance):
    return lax.ppermute(v, "x", [((i + distance) % 4, i) for i in range(4)])


def swap(v, axis):
    return lax.ppermute(v, axis, [(0, 1), (1, 0)])


def shift_super(v, distance, other):
    pairs = [
        (2 * i + h, 2 * (i + distance) + (h + other) % 2)
        for i in range(8)
        for h in (0, 1)
        if 0 <= i + distance < 8
    ]
    return lax.ppermute(v, ("ylo", "z", "yhi"), pairs)


def exchange(v, axes):
    return lax.all_to_all(v, axes, split_axis=0, concat_axis=0, tiled=True)


def near_gather(v):
    blocks = [v] + [shift_x(v, d) for d in (1, 2, 3)]
    return [[b, swap(b, "core")] for b in blocks]


def near_keep(parts):
    return [
        (own.astype(F32) + swap(other, "core").astype(F32)).astype(BF16) for own, other in parts
    ]


def near_sum(kept):
    total = kept[0].astype(F32)
    for d in (1, 2, 3):
        total = total + shift_x(kept[d], -d).astype(F32)
    return total


def rel_to_abs(v, x, core):
    v = jnp.where(core == 0, v, v[:, ::-1])
    return lax.dynamic_slice_in_dim(jnp.concatenate([v, v], axis=0), (4 - x) % 4, 4, 0)


def abs_to_rel(v, x, core):
    v = jnp.where(core == 0, v, v[:, ::-1])
    return lax.dynamic_slice_in_dim(jnp.concatenate([v, v], axis=0), x, 4, 0)


def params(steps, mib):
    return pltpu.CompilerParams(
        dimension_semantics=("arbitrary",) * steps, vmem_limit_bytes=mib * 2**20
    )


def cost(flops, moved, exps=0):
    return pl.CostEstimate(flops=int(flops), bytes_accessed=int(moved), transcendentals=int(exps))


def stacked(a_ref, b_ref):
    return jnp.concatenate([a_ref[...], b_ref[...]], axis=0)


def head_sums(v):
    lane = lax.shift_right_logical(lax.broadcasted_iota(jnp.int32, (4 * HEAD, 4 * HEAD), 1), 6)
    row = lax.shift_right_logical(lax.broadcasted_iota(jnp.int32, (4 * HEAD, 4 * HEAD), 0), 6)
    ones = jnp.where(lane == row, 1.0, 0.0).astype(BF16)
    high = v.astype(BF16)
    low = (v - high.astype(F32)).astype(BF16)
    return dot(high, ones) + dot(low, ones)


def half_turn(v):
    lane = lax.broadcasted_iota(jnp.int32, v.shape, 1)
    return jnp.where(
        (lane & (HEAD - 1)) < HEAD // 2,
        pltpu.roll(v, v.shape[1] - HEAD // 2, 1),
        pltpu.roll(v, HEAD // 2, 1),
    )


def twice(v):
    return jnp.concatenate([v, v], axis=1)


def project_kernel(*refs):
    xs, (w_ref, gain_ref, cos_ref, sin_ref, head_gain_ref) = refs[:8], refs[8:13]
    normed_ref, q_ref, kv_ref, raw_ref = refs[13:]
    lane = lax.broadcasted_iota(jnp.int32, (PAIR, 2 * HEAD), 1)
    for d in range(4):
        rows = slice(d * PAIR, (d + 1) * PAIR)
        tiles = slice(2 * d, 2 * d + 2)
        x = stacked(*xs[tiles]).astype(F32)
        normed = (x * rms_scale(x) * gain_ref[...]).astype(BF16)
        normed_ref[rows, :] = normed
        raw = dot(normed, w_ref[...])
        heads = raw[:, : 4 * HEAD]
        raw_ref[d] = heads
        scale = lax.rsqrt(head_sums(heads * heads) * (1.0 / HEAD) + EPS)
        v = heads * scale * head_gain_ref[...]
        turned = v * twice(cos_ref[d]) + half_turn(v) * twice(sin_ref[d])
        q_ref[tiles] = turned[:, :QUERY].astype(BF16).reshape(2, ROWS, QUERY)
        kv = jnp.where(lane < HEAD, raw[:, 4 * HEAD :], turned[:, 2 * HEAD :])
        kv_ref[tiles] = kv.astype(BF16).reshape(2, ROWS, 2 * HEAD)


def project(xs, w, gain, cos, sin, head_gain):
    return pl.pallas_call(
        project_kernel,
        out_shape=(
            jax.ShapeDtypeStruct((4 * PAIR, WIDTH), BF16),
            jax.ShapeDtypeStruct((8, ROWS, QUERY), BF16),
            jax.ShapeDtypeStruct((8, ROWS, 2 * HEAD), BF16),
            jax.ShapeDtypeStruct((4, PAIR, 4 * HEAD), F32),
        ),
        compiler_params=params(0, 24),
        cost_estimate=cost(8 * PAIR * WIDTH * 384, 1e7),
    )(*xs, w, gain, cos, sin, head_gain)


def unproject_kernel(*refs):
    gq_ref, g_refs, raw_ref, xs, (w_ref, cos_ref, sin_ref, head_gain_ref) = (
        refs[0], refs[1:7], refs[7], refs[8:12], refs[12:16],
    )
    parts, (graw_ref, attn_ref, heads_ref) = refs[16:20], refs[20:]
    attn, sums = 0.0, 0.0
    for i in range(2):
        tiles = slice(2 * i, 2 * i + 2)
        gq = gq_ref[tiles].reshape(PAIR, 4 * HEAD).astype(F32)
        gkv = g_refs[0][tiles]
        for ref in g_refs[1:]:
            gkv = gkv + ref[tiles].astype(F32)
        gkv = gkv.reshape(PAIR, 2 * HEAD)
        lane = lax.broadcasted_iota(jnp.int32, (PAIR, 2 * HEAD), 1)
        gk = (gkv * HEAD**-0.5).astype(BF16).astype(F32)
        gk = jnp.where(lane < HEAD, gq[:, 2 * HEAD :], gk)
        g = jnp.concatenate([gq[:, : 2 * HEAD], gk], axis=1)
        g = g * twice(cos_ref[i]) - half_turn(g) * twice(sin_ref[i])
        raw = raw_ref[i]
        scale = lax.rsqrt(head_sums(raw * raw) * (1.0 / HEAD) + EPS)
        sums = sums + jnp.sum(g * raw * scale, axis=0, keepdims=True)
        e = g * head_gain_ref[...]
        inner = head_sums(e * raw) * (1.0 / HEAD)
        graw = scale * (e - raw * scale * scale * inner)
        graw = jnp.concatenate([graw, jnp.where(lane < HEAD, gkv, 0.0)], axis=1).astype(BF16)
        graw_ref[i * PAIR : (i + 1) * PAIR, :] = graw
        grad = dot(graw, w_ref[...], NT)
        x = stacked(*xs[tiles]).astype(F32)
        attn = attn + jnp.sum(grad * x * rms_scale(x), axis=0, keepdims=True)
        grad = grad.astype(BF16)
        parts[2 * i][...] = grad[:ROWS]
        parts[2 * i + 1][...] = grad[ROWS:]
    attn_ref[...] = attn
    heads_ref[...] = sums


def unproject(half, gq, gkvs, raw, xs, w, cos, sin, head_gain):
    def whole_of(*shape):
        return pl.BlockSpec(shape, lambda i: (0,) * len(shape))

    def at_half(*shape):
        return pl.BlockSpec(shape, lambda i: (half,) + (0,) * (len(shape) - 1))

    rows = whole_of(ROWS, WIDTH)
    table = at_half(2, PAIR, 2 * HEAD)
    outs = (jax.ShapeDtypeStruct((ROWS, WIDTH), BF16),) * 4 + (
        jax.ShapeDtypeStruct((2 * PAIR, 6 * HEAD), BF16),
        jax.ShapeDtypeStruct((1, WIDTH), F32),
        jax.ShapeDtypeStruct((1, 4 * HEAD), F32),
    )
    return pl.pallas_call(
        unproject_kernel,
        out_shape=outs,
        grid=(1,),
        in_specs=[at_half(4, ROWS, 4 * HEAD)]
        + [at_half(4, ROWS, 2 * HEAD)] * 6
        + [at_half(2, PAIR, 4 * HEAD)]
        + [rows] * 4
        + [whole_of(WIDTH, 6 * HEAD), table, table, whole_of(1, 4 * HEAD)],
        out_specs=tuple(whole_of(*o.shape) for o in outs),
        compiler_params=params(1, 24),
        cost_estimate=cost(4 * PAIR * WIDTH * 384, 8e6),
    )(gq, *gkvs, raw, *xs, w, cos, sin, head_gain)


def ffn_kernel(
    x0_ref, x1_ref, c0_ref, c1_ref, gu_w_ref, d_w_ref, part0_ref, part1_ref, act_ref, gu_ref, total
):
    y = pl.program_id(0)
    x = stacked(x0_ref, x1_ref)
    gate_up = dot(x, gu_w_ref[0])
    gate, up = gate_up[:, :PADDED], gate_up[:, PADDED:]
    grad_act = dot(stacked(c0_ref, c1_ref), d_w_ref[0])
    sig = 1.0 / (1.0 + jnp.exp(-gate))
    silu = gate * sig
    act_ref[0] = (silu * up).astype(BF16)
    grad_gate = grad_act * up * sig * (1.0 + gate * (1.0 - sig))
    grads = jnp.concatenate([grad_gate, grad_act * silu], axis=1).astype(BF16)
    gu_ref[0] = grads
    part = dot(grads, gu_w_ref[0], NT)

    @pl.when(y == 0)
    def _():
        total[...] = part

    @pl.when(y == 1)
    def _():
        whole_part = (total[...] + part).astype(BF16)
        part0_ref[...] = whole_part[:ROWS]
        part1_ref[...] = whole_part[ROWS:]


def ffn(x0, x1, c0, c1, gu_w, d_w):
    rows = pl.BlockSpec((ROWS, WIDTH), lambda y: (0, 0))
    return pl.pallas_call(
        ffn_kernel,
        out_shape=(
            jax.ShapeDtypeStruct((ROWS, WIDTH), BF16),
            jax.ShapeDtypeStruct((ROWS, WIDTH), BF16),
            jax.ShapeDtypeStruct((2, PAIR, PADDED), BF16),
            jax.ShapeDtypeStruct((2, PAIR, 2 * PADDED), BF16),
        ),
        grid=(2,),
        in_specs=[rows] * 4
        + [pl.BlockSpec((1, WIDTH, n * PADDED), lambda y: (y, 0, 0)) for n in (2, 1)],
        out_specs=(
            rows,
            rows,
            pl.BlockSpec((1, PAIR, PADDED), lambda y: (y, 0, 0)),
            pl.BlockSpec((1, PAIR, 2 * PADDED), lambda y: (y, 0, 0)),
        ),
        scratch_shapes=[pltpu.VMEM((PAIR, WIDTH), F32)],
        compiler_params=params(1, 32),
        cost_estimate=cost(2 * 2 * PAIR * WIDTH * 5 * PADDED, 14e6),
    )(x0, x1, c0, c1, gu_w, d_w)


def down_kernel(act_ref, w_ref, part0_ref, part1_ref, total):
    y = pl.program_id(0)
    part = dot(act_ref[0], w_ref[0], NT)

    @pl.when(y == 0)
    def _():
        total[...] = part

    @pl.when(y == 1)
    def _():
        whole_part = (total[...] + part).astype(BF16)
        part0_ref[...] = whole_part[:ROWS]
        part1_ref[...] = whole_part[ROWS:]


def down(act, w):
    rows = pl.BlockSpec((ROWS, WIDTH), lambda y: (0, 0))
    return pl.pallas_call(
        down_kernel,
        out_shape=(jax.ShapeDtypeStruct((ROWS, WIDTH), BF16),) * 2,
        grid=(2,),
        in_specs=[
            pl.BlockSpec((1, PAIR, PADDED), lambda y: (y, 0, 0)),
            pl.BlockSpec((1, WIDTH, PADDED), lambda y: (y, 0, 0)),
        ],
        out_specs=(rows, rows),
        scratch_shapes=[pltpu.VMEM((PAIR, WIDTH), F32)],
        compiler_params=params(1, 24),
        cost_estimate=cost(2 * 2 * PAIR * WIDTH * PADDED, 5e6),
    )(act, w)


def ffn_weights_kernel(*refs):
    xs, cs, gus, acts, out_ref = refs[:8], refs[8:16], refs[16:20], refs[20:24], refs[24]
    def all_tokens(refs):
        return jnp.concatenate([ref[...] for ref in refs], axis=0)

    grad_gu = dot(all_tokens(xs), all_tokens([g.at[0] for g in gus]), TN)
    grad_d = dot(all_tokens(cs), all_tokens([a.at[0] for a in acts]), TN)
    out_ref[0, :, :PART] = grad_gu[:, :PART].astype(BF16)
    out_ref[0, :, PART : 2 * PART] = grad_gu[:, PADDED : PADDED + PART].astype(BF16)
    out_ref[0, :, 2 * PART :] = grad_d[:, :PART].astype(BF16)


def ffn_weights(xs, cs, gus, acts):
    tall = 256
    rows = pl.BlockSpec((ROWS, tall), lambda y, m: (0, m))
    return pl.pallas_call(
        ffn_weights_kernel,
        out_shape=jax.ShapeDtypeStruct((2, WIDTH, 3 * PART), BF16),
        grid=(2, WIDTH // tall),
        in_specs=[rows] * 16
        + [pl.BlockSpec((1, PAIR, 2 * PADDED), lambda y, m: (y, 0, 0))] * 4
        + [pl.BlockSpec((1, PAIR, PADDED), lambda y, m: (y, 0, 0))] * 4,
        out_specs=pl.BlockSpec((1, tall, 3 * PART), lambda y, m: (y, m, 0)),
        compiler_params=params(2, 28),
        cost_estimate=cost(2 * 2 * 1024 * WIDTH * 3 * PADDED, 24e6),
    )(*xs, *cs, *gus, *acts)


def out_project_kernel(mix_ref, w_ref, part0_ref, part1_ref):
    part = dot(mix_ref[...].reshape(PAIR, QUERY), w_ref[...], NT).astype(BF16)
    part0_ref[...] = part[:ROWS]
    part1_ref[...] = part[ROWS:]


def out_project(d, mix, w):
    rows = pl.BlockSpec((ROWS, WIDTH), lambda i: (0, 0))
    return pl.pallas_call(
        out_project_kernel,
        out_shape=(jax.ShapeDtypeStruct((ROWS, WIDTH), BF16),) * 2,
        grid=(1,),
        in_specs=[
            pl.BlockSpec((2, ROWS, QUERY), lambda i: (d, 0, 0)),
            pl.BlockSpec((WIDTH, QUERY), lambda i: (0, 0)),
        ],
        out_specs=(rows, rows),
        compiler_params=params(1, 16),
        cost_estimate=cost(2 * PAIR * WIDTH * QUERY, 2e6),
    )(mix, w)


def out_back_kernel(w_ref, *refs):
    for t in range(8):
        refs[8][t] = dot(refs[t][...], w_ref[...]).astype(BF16)


def out_back(branches, w):
    return pl.pallas_call(
        out_back_kernel,
        out_shape=jax.ShapeDtypeStruct((8, ROWS, QUERY), BF16),
        compiler_params=params(0, 16),
        cost_estimate=cost(8 * PAIR * WIDTH * QUERY, 4e6),
    )(w, *branches)


def out_weights_kernel(mix_ref, *refs):
    branches, (out_ref, total) = refs[:8], refs[8:]
    grad = 0.0
    for d in range(4):
        mix = mix_ref[2 * d : 2 * d + 2].reshape(PAIR, QUERY)
        grad = grad + dot(mix, stacked(*branches[2 * d : 2 * d + 2]), TN)
    total[...] = grad
    for half in (0, 1):
        for s in range(8):
            piece = total[half * 96 : half * 96 + 96, s * 192 : s * 192 + 192]
            out_ref[half * 8 + s] = piece.astype(BF16)


def out_weights(mix, branches):
    return pl.pallas_call(
        out_weights_kernel,
        out_shape=jax.ShapeDtypeStruct((16, 96, 192), BF16),
        scratch_shapes=[pltpu.VMEM((QUERY, WIDTH), F32)],
        compiler_params=params(0, 24),
        cost_estimate=cost(2 * 1024 * WIDTH * QUERY, 4e6),
    )(mix, *branches)


def side_by_side(t):
    return jnp.concatenate([t[g * HEAD : (g + 1) * HEAD] for g in range(GROUP)], axis=1)


def on_top(t):
    return jnp.concatenate([t[:, g * ROWS : (g + 1) * ROWS] for g in range(GROUP)], axis=0)


def key_loops(plan, at, base, start, visit, state):
    f = pl.program_id(0)
    lo, m1, m2, hi = (plan[f, at + i] for i in range(4))
    place = lax.rem(lax.broadcasted_iota(jnp.int32, (1, LANES), 1), ROWS) + plan[f, 0]

    def masked(j, state):
        key = lax.broadcasted_iota(jnp.int32, (KEY_TILE, LANES), 0) + (j * KEY_TILE + base)
        return visit(j, state, (key >= start) & (key <= place))

    def two(i, state):
        return visit(m1 + 2 * i + 1, visit(m1 + 2 * i, state, None), None)

    pairs = lax.shift_right_logical(m2 - m1, 1)
    state = lax.fori_loop(lo, m1, masked, state)
    state = lax.fori_loop(0, pairs, two, state)
    state = lax.fori_loop(m1 + 2 * pairs, m2, lambda j, s: visit(j, s, None), state)
    return lax.fori_loop(m2, hi, masked, state)


def rows_of(j):
    return pl.ds(pl.multiple_of(j * KEY_TILE, KEY_TILE), KEY_TILE)


def chunks(plan, supers):
    for b in range(supers):
        for half in (0, 1):
            for f in range(8):
                side = plan[0, 10] if half == 0 else 1 - plan[0, 10]
                yield b, half, pl.multiple_of(b * SUPER + f * PAIR + side * ROWS, ROWS), plan[f, 1]


def line_up(plan, kv_refs, kv, kvt):
    @pl.when(pl.program_id(0) == 0)
    def _():
        for b, half, place, sent in chunks(plan, len(kv_refs) // 2):
            block = kv_refs[2 * b + half][sent]
            kv[pl.ds(place, ROWS), :] = block
            kvt[:, pl.ds(place, ROWS)] = block.astype(F32).T.astype(BF16)


def attend_body(at, base, plan, q_ref, start_ref, kv, kvt, state):
    qt = side_by_side(q_ref[0].astype(F32).T)
    qt = jnp.concatenate([jnp.zeros_like(qt), qt], axis=0).astype(BF16)

    def visit(j, state, mask):
        total, accum = state
        weights = jnp.exp2(dot(kv[rows_of(j), :], qt) * SCORE)
        if mask is not None:
            weights = jnp.where(mask, weights, 0.0)
        total = total + jnp.sum(weights, axis=0, keepdims=True)
        return total, accum + dot(kvt[:HEAD, rows_of(j)], weights.astype(BF16))

    return key_loops(plan, at, base, start_ref[0], visit, state)


def attend_own_kernel(plan, q_ref, start_ref, *refs):
    kv_refs, (accum_ref, total_ref, kv, kvt) = refs[:2], refs[2:]
    line_up(plan, kv_refs, kv, kvt)
    state = (jnp.zeros((1, LANES), F32), jnp.zeros((HEAD, LANES), F32))
    total, accum = attend_body(6, EARLIER, plan, q_ref, start_ref, kv, kvt, state)
    accum_ref[0] = accum
    total_ref[0] = total


def attend_earlier_kernel(plan, q_ref, start_ref, *refs):
    kv_refs, (accum_ref, total_ref, mix_ref, out_ref, lse_ref, kv, kvt) = refs[:4], refs[4:]
    line_up(plan, kv_refs, kv, kvt)
    state = (total_ref[0], accum_ref[0])
    total, accum = attend_body(2, 0, plan, q_ref, start_ref, kv, kvt, state)
    out = accum / total
    out_ref[0] = out
    mix_ref[0] = on_top(out).T.astype(BF16)
    lse_ref[0] = jnp.log2(total)


def back_body(at, base, plan, q_ref, start_ref, g_ref, out_ref, lse_ref, kv, kvt, dkv, dqt):
    @pl.when(pl.program_id(0) == 0)
    def _():
        dkv[...] = jnp.zeros_like(dkv)

    qt = side_by_side(q_ref[0].astype(F32).T)
    gt = side_by_side(g_ref[0].astype(F32).T)
    delta = jnp.sum(gt * out_ref[0], axis=0, keepdims=True)
    zero = jnp.zeros_like(qt)
    gt = jnp.concatenate([gt, zero], axis=0)
    qt = jnp.concatenate([zero, qt], axis=0)
    both_t = jnp.concatenate([gt, qt], axis=1).astype(BF16)
    both = jnp.concatenate([gt.T, qt.T], axis=0).astype(BF16)
    lse = lse_ref[0]

    def visit(j, dqt, mask):
        pair = dot(kv[rows_of(j), :], both_t)
        weights = jnp.exp2(pair[:, LANES:] * SCORE - lse)
        if mask is not None:
            weights = jnp.where(mask, weights, 0.0)
        grads = (weights * (pair[:, :LANES] - delta)).astype(BF16)
        sides = jnp.concatenate([weights.astype(BF16), grads], axis=1)
        dkv[rows_of(j), :] += dot(sides, both)
        return dqt + dot(kvt[HEAD:, rows_of(j)], grads)

    return key_loops(plan, at, base, start_ref[0], visit, dqt)


def hand_out(plan, supers, dkv, mine_ref, theirs_ref):
    @pl.when(pl.program_id(0) == 7)
    def _():
        for b, half, place, sent in chunks(plan, supers):
            ref = (mine_ref, theirs_ref)[half]
            ref[b, sent] = dkv[pl.ds(place, ROWS), :].astype(ref.dtype)


def back_earlier_kernel(plan, q_ref, start_ref, *refs):
    kv_refs, (g_ref, out_ref, lse_ref, dqt_ref, mine_ref, theirs_ref, kv, kvt, dkv) = refs[:4], refs[4:]
    line_up(plan, kv_refs, kv, kvt)
    dqt = jnp.zeros((HEAD, LANES), F32)
    dqt_ref[0] = back_body(
        2, 0, plan, q_ref, start_ref, g_ref, out_ref, lse_ref, kv, kvt, dkv, dqt
    )
    hand_out(plan, 2, dkv, mine_ref, theirs_ref)


def back_own_kernel(plan, q_ref, start_ref, *refs):
    kv_refs, (g_ref, out_ref, lse_ref, dqt_ref) = refs[:2], refs[2:6]
    dq_ref, mine_ref, theirs_ref, kv, kvt, dkv = refs[6:]
    line_up(plan, kv_refs, kv, kvt)
    dqt = back_body(
        6, EARLIER, plan, q_ref, start_ref, g_ref, out_ref, lse_ref, kv, kvt, dkv, dqt_ref[0]
    )
    dq = on_top(dqt * HEAD**-0.5).T
    dq_ref[0] = jnp.concatenate([dq, jnp.zeros((ROWS, HEAD), F32)], axis=1).astype(BF16)
    hand_out(plan, 1, dkv, mine_ref, theirs_ref)


def whole(*shape):
    return pl.BlockSpec(shape, lambda f, plan: (0,) * len(shape))


def tile(*shape):
    return pl.BlockSpec((1,) + shape, lambda f, plan: (f,) + (0,) * len(shape))


def placed(*shape):
    return pl.BlockSpec((1,) + shape, lambda f, plan: (plan[f, 1],) + (0,) * len(shape))


def tiles_call(kernel, supers, outs, more_ins, out_specs, flops, back):
    keys = supers * SUPER
    scratch = [pltpu.VMEM((keys, 2 * HEAD), BF16), pltpu.VMEM((2 * HEAD, keys), BF16)]
    if back:
        scratch.append(pltpu.VMEM((keys, 2 * HEAD), F32))
    ins = [placed(ROWS, QUERY), tile(1, LANES)] + [whole(8, ROWS, 2 * HEAD)] * (2 * supers)
    return pl.pallas_call(
        kernel,
        out_shape=outs,
        grid_spec=pltpu.PrefetchScalarGridSpec(
            num_scalar_prefetch=1,
            grid=(8,),
            in_specs=ins + more_ins,
            out_specs=out_specs,
            scratch_shapes=scratch,
        ),
        compiler_params=params(1, 20),
        cost_estimate=cost(flops, 8e6, 1e7),
    )


TILE_T = jax.ShapeDtypeStruct((8, HEAD, LANES), F32)
TILE_ROW = jax.ShapeDtypeStruct((8, 1, LANES), F32)
STATE = [tile(HEAD, LANES), tile(1, LANES)]


def attend_own(plan, q, start, kvs):
    call = tiles_call(attend_own_kernel, 1, (TILE_T, TILE_ROW), [], tuple(STATE), 4e9, False)
    return call(plan, q, start, *kvs)


def attend_earlier(plan, q, start, kvs, state):
    outs = (jax.ShapeDtypeStruct((8, ROWS, QUERY), BF16), TILE_T, TILE_ROW)
    specs = (placed(ROWS, QUERY),) + tuple(STATE)
    call = tiles_call(attend_earlier_kernel, 2, outs, STATE, specs, 8e9, False)
    return call(plan, q, start, *kvs, *state)


def sent_back(supers):
    shape = (supers, 8, ROWS, 2 * HEAD)
    return [jax.ShapeDtypeStruct(shape, F32), jax.ShapeDtypeStruct(shape, BF16)], [whole(*shape)] * 2


def back_earlier(plan, q, start, kvs, grad, out, lse):
    shapes, specs = sent_back(2)
    call = tiles_call(
        back_earlier_kernel, 2, [TILE_T] + shapes, [placed(ROWS, QUERY)] + STATE,
        [tile(HEAD, LANES)] + specs, 20e9, True,
    )
    return call(plan, q, start, *kvs, grad, out, lse)


def back_own(plan, q, start, kvs, grad, out, lse, dqt):
    shapes, specs = sent_back(1)
    dq = jax.ShapeDtypeStruct((8, ROWS, 4 * HEAD), BF16)
    call = tiles_call(
        back_own_kernel, 1, [dq] + shapes, [placed(ROWS, QUERY)] + STATE + [tile(HEAD, LANES)],
        [placed(ROWS, 4 * HEAD)] + specs, 10e9, True,
    )
    return call(plan, q, start, *kvs, grad, out, lse, dqt)


def after(v, *others):
    return lax.optimization_barrier((v,) + others)[0]


def per_device(
    tokens,
    segments,
    attn_gain,
    w_query,
    w_key,
    w_value,
    q_gain,
    k_gain,
    w_out,
    ffn_gain,
    w_gate,
    w_up,
    w_down,
    cotangent,
):
    ylo, z, x, core, yhi = (lax.axis_index(a) for a in ALL)
    sup = ylo * 4 + z

    token_blocks = near_gather(tokens)
    qkv_own = jnp.concatenate(
        [
            w_query.reshape(12, 8, QUERY),
            w_key.reshape(12, 8, HEAD),
            w_value.reshape(12, 8, HEAD),
            jnp.broadcast_to(attn_gain[:, None, None], (12, 8, 1)),
            jnp.broadcast_to(ffn_gain[:, None, None], (12, 8, 1)),
            jnp.zeros((12, 8, HEAD - 2), BF16),
        ],
        axis=-1,
    )
    qkv_own = jnp.pad(jnp.transpose(qkv_own, (1, 0, 2)), ((0, 0), (0, 12), (0, 0)))
    out_own = jnp.transpose(w_out.reshape(4, QUERY, 24), (0, 2, 1))
    rows_own = jnp.concatenate(
        [
            jnp.pad(w.reshape(24, 8, PART), ((0, 0), (0, 0), (0, PADDED - PART))).transpose(1, 0, 2)
            for w in (w_gate, w_up, w_down.T)
        ]
        + [jnp.concatenate([out_own, out_own], axis=0), qkv_own],
        axis=-1,
    )
    rows = exchange(rows_own, NEAR)
    gu_rows = rows[:, :, : 2 * PADDED].reshape(192, 2 * PADDED)
    d_rows = rows[:, :, 2 * PADDED : 3 * PADDED].reshape(192, PADDED)
    d_full = lax.all_gather(d_rows, WIDE, axis=0, tiled=True).reshape(2, WIDTH, PADDED)
    out_rows = rows[:, :, 3 * PADDED : 3 * PADDED + QUERY].reshape(1, 192, QUERY)
    qkv_rows = rows[:, :12, 3 * PADDED + QUERY :].reshape(1, 96, 6 * HEAD)
    qkv = exchange(jnp.broadcast_to(qkv_rows, (16, 96, 6 * HEAD)), WIDE)
    qkv = jnp.transpose(qkv.reshape(2, 8, 8, 12, 6 * HEAD), (1, 2, 0, 3, 4)).reshape(WIDTH, 6 * HEAD)
    gain_attn = qkv[:, 5 * HEAD].astype(F32)
    gain_ffn = qkv[:, 5 * HEAD + 1].astype(F32)

    token_index = jnp.arange(segments.shape[0], dtype=jnp.int32)
    begins = jnp.concatenate([jnp.ones((1,), jnp.bool_), segments[1:] != segments[:-1]])
    starts = lax.cummax(jnp.where(begins, token_index, 0), axis=0)
    own_starts = lax.dynamic_slice(
        starts.reshape(8, 8, 2, ROWS), (sup, 0, yhi, 0), (1, 8, 1, ROWS)
    ).reshape(8, ROWS)
    first = sup * SUPER + jnp.arange(8, dtype=jnp.int32) * PAIR + yhi * ROWS
    own_places = first[:, None] + jnp.arange(ROWS, dtype=jnp.int32)[None]
    positions = abs_to_rel((own_places - own_starts).reshape(4, 2, ROWS), x, core)
    frequency = THETA ** (-jnp.arange(HEAD // 2, dtype=F32) * 2.0 / HEAD)
    angles = positions.reshape(4, PAIR, 1).astype(F32) * frequency
    cosine, sine = jnp.cos(angles), jnp.sin(angles)
    cos = jnp.concatenate([cosine] * 4, axis=-1)
    sin = jnp.concatenate([-sine, sine] * 2, axis=-1)
    head_gain = jnp.concatenate([q_gain, q_gain, q_gain, k_gain]).astype(F32)[None]

    window = (sup - 2) * SUPER
    lo = (own_starts[:, 0] - window) // KEY_TILE
    hi = (first + ROWS - 1 - window) // KEY_TILE + 1
    m1 = jnp.clip((own_starts[:, -1] - window + KEY_TILE - 1) // KEY_TILE, lo, hi)
    m2 = jnp.clip((first + 1 - window) // KEY_TILE, m1, hi)
    order = jnp.arange(8, dtype=jnp.int32)
    relative = ((order // 2 - x) % 4) * 2 + (order % 2 + core) % 2
    edge = EARLIER // KEY_TILE
    plan = jnp.stack(
        [first - window, relative]
        + [jnp.minimum(v, edge) for v in (lo, m1, m2, hi)]
        + [jnp.maximum(v - edge, 0) for v in (lo, m1, m2, hi)]
        + [jnp.broadcast_to(yhi, (8,))],
        axis=1,
    ).astype(jnp.int32)
    start_lanes = jnp.tile(own_starts - window, (1, GROUP)).reshape(8, 1, LANES)

    normed, rot_q, kv, raw = project(
        [b for p in token_blocks for b in p], qkv, gain_attn[None], cos, sin, head_gain
    )

    kv_own = [kv, swap(kv, "yhi")]
    kv_earlier = [shift_super(kv, 2, 0), shift_super(kv, 2, 1), shift_super(kv, 1, 0), shift_super(kv, 1, 1)]
    kv_earlier, gu_rows = lax.optimization_barrier((kv_earlier, gu_rows))
    gu_full = lax.all_gather(gu_rows, WIDE, axis=0, tiled=True).reshape(2, WIDTH, 2 * PADDED)
    state = attend_own(plan, rot_q, start_lanes, kv_own)
    out_both = exchange(jnp.broadcast_to(after(out_rows, kv_own[1]), (16, 192, QUERY)), WIDE)
    out_both = out_both.reshape(2, WIDTH, QUERY)
    state, w_out_t = lax.optimization_barrier((state, jnp.where(x < 2, out_both[0], out_both[1])))
    cot_blocks = near_gather(after(cotangent, kv))
    mix, out_tiles, lse = attend_earlier(plan, rot_q, start_lanes, kv_earlier, state)
    mix, cot_blocks = lax.optimization_barrier((mix, cot_blocks))

    inputs = tokens.astype(F32)
    parts = [None] * 4
    for d in (2, 1, 3, 0):
        parts[d] = out_project(d, mix, w_out_t)
    hidden = inputs + near_sum(near_keep(parts))
    scale_ffn = rms_scale(hidden)
    scaled_ffn = hidden * scale_ffn
    normed_ffn = (scaled_ffn * gain_ffn).astype(BF16)

    ffn_blocks = [[b] for b in [normed_ffn] + [shift_x(normed_ffn, d) for d in (1, 2, 3)]]
    ffn_blocks[0].append(swap(normed_ffn, "core"))
    ffn_outs = [None] * 4
    before = {1: 0, 3: 0, 2: 1}
    for d in (0, 1, 3, 2):
        if d > 0:
            block = after(ffn_blocks[d][0], ffn_outs[before[d]][0])
            ffn_blocks[d] = [block, swap(block, "core")]
        blocks = ffn_blocks[d]
        if d == 3:
            blocks = after(blocks, ffn_outs[1][0])
        if d == 2:
            blocks = after(blocks, ffn_outs[3][0])
        ffn_outs[d] = ffn(*blocks, *cot_blocks[d], gu_full, d_full)
    acts, gus = [o[2] for o in ffn_outs], [o[3] for o in ffn_outs]
    kept, gus = lax.optimization_barrier((near_keep([o[:2] for o in ffn_outs]), gus))
    pair_total = near_sum(kept)
    weight_grads = ffn_weights(
        [b for p in ffn_blocks for b in p], [b for p in cot_blocks for b in p], gus, acts
    )
    pair_total, weight_grads = lax.optimization_barrier((pair_total, weight_grads))
    ffn_sum = lax.psum_scatter(
        weight_grads.reshape(2 * WIDTH, 3 * PART), WIDE, scatter_dimension=0, tiled=True
    )

    ffn_gain_part = jnp.sum(pair_total * scaled_ffn, axis=0)
    grad_hidden = cotangent.astype(F32) + rms_back(pair_total * gain_ffn, hidden, scale_ffn)
    grad_branch = grad_hidden.astype(BF16)
    branches = [b for p in near_gather(grad_branch) for b in p]
    grad_mix = out_back(branches, w_out_t)

    acts, grad_branch = lax.optimization_barrier((acts, grad_branch))
    out_kept = near_keep([down(a, d_full) for a in acts])
    grad_mix, out_kept = lax.optimization_barrier((grad_mix, out_kept))
    grad_out = exchange(out_weights(mix, branches), WIDE)

    dqt, mine, theirs = back_earlier(plan, rot_q, start_lanes, kv_earlier, grad_mix, out_tiles, lse)
    mine = mine.astype(BF16)
    sent = [
        shift_super(mine[1], -1, 0),
        shift_super(theirs[1], -1, 1),
        shift_super(mine[0], -2, 0),
        shift_super(theirs[0], -2, 1),
    ]
    out_total = near_sum(out_kept)
    dqt, out_total = lax.optimization_barrier((dqt, out_total))
    output = (hidden + out_total).astype(BF16)
    grad_q, mine, theirs = back_own(
        plan, rot_q, start_lanes, kv_own, grad_mix, out_tiles, lse, dqt
    )
    grad_q, mine, theirs, sent, grad_out = lax.optimization_barrier(
        (grad_q, mine, theirs, sent, grad_out)
    )
    grad_kvs = [mine[0], swap(theirs[0], "yhi")] + sent
    grad_out = jnp.sum(grad_out.astype(F32), axis=0).astype(BF16)
    grad_out = jnp.transpose(grad_out.reshape(96, 8, 24), (1, 2, 0))

    unprojected = [None] * 2
    for half in (1, 0):
        xs = [b for p in token_blocks[2 * half : 2 * half + 2] for b in p]
        unprojected[half] = unproject(half, grad_q, grad_kvs, raw, xs, qkv, cos, sin, head_gain)
    kept = near_keep([u[2 * i : 2 * i + 2] for u in unprojected for i in (0, 1)])
    kept, normed = lax.optimization_barrier((kept, normed))
    grad_normed = near_sum(kept)
    qkv_grad = dot(normed, jnp.concatenate([u[4] for u in unprojected], axis=0), TN)

    last = jnp.concatenate([ffn_sum.reshape(8, 24, 3 * PART), grad_out], axis=-1)
    last, qkv_grad = lax.optimization_barrier((exchange(last, NEAR), qkv_grad))

    attn_gain_part = sum(u[5] for u in unprojected).reshape(128, 12, 1)
    head_part = sum(u[6] for u in unprojected)[0]
    q_gain_part = head_part[:HEAD] + head_part[HEAD : 2 * HEAD] + head_part[2 * HEAD : QUERY]
    head_part = jnp.concatenate([q_gain_part, head_part[QUERY:], jnp.zeros((4,), F32)])
    gain_parts = jnp.concatenate(
        [
            attn_gain_part,
            ffn_gain_part.reshape(128, 12, 1),
            jnp.broadcast_to(head_part.reshape(1, 12, 11), (128, 12, 11)),
        ],
        axis=2,
    )
    gain_high = gain_parts.astype(BF16)
    gain_low = (gain_parts - gain_high.astype(F32)).astype(BF16)
    qkv_grad = jnp.concatenate(
        [
            qkv_grad[:, : 5 * HEAD].astype(BF16).reshape(128, 12, 5 * HEAD),
            gain_high,
            gain_low,
            jnp.zeros((128, 12, HEAD - 26), BF16),
        ],
        axis=2,
    )
    qkv_grad = exchange(qkv_grad, ALL).reshape(8, 8, 2, 12, 6 * HEAD).astype(F32)
    qkv_grad = jnp.sum(qkv_grad, axis=(0, 2))
    gains = jnp.sum(qkv_grad[:, :, 5 * HEAD :], axis=0)
    gains = gains[:, :13] + gains[:, 13:26]
    head_gains = gains[:, 2:].reshape(-1)
    qkv_grad = jnp.transpose(qkv_grad, (1, 0, 2))
    w_query_grad = qkv_grad[:, :, :QUERY].reshape(12, -1)
    w_key_grad = qkv_grad[:, :, QUERY : QUERY + HEAD].reshape(12, -1)
    w_value_grad = qkv_grad[:, :, QUERY + HEAD : QUERY + 2 * HEAD].reshape(12, -1)

    scale_attn = rms_scale(inputs)
    input_grad = (grad_hidden + rms_back(grad_normed * gain_attn, inputs, scale_attn)).astype(BF16)

    ffn_grad, grad_out = last[:, :, : 3 * PART], last[:, :, 3 * PART :].reshape(2, 4, 24, 96)
    kept = jnp.where(yhi == 0, grad_out[0], grad_out[1])
    got = swap(jnp.where(yhi == 0, grad_out[1], grad_out[0]), "yhi")
    w_out_grad = jnp.stack(
        [jnp.where(yhi == 0, kept, got), jnp.where(yhi == 0, got, kept)], axis=1
    )
    w_out_grad = jnp.transpose(w_out_grad, (0, 1, 3, 2)).reshape(768, 24).astype(F32)
    ffn_grad = jnp.transpose(ffn_grad, (1, 0, 2)).astype(F32)
    w_gate_grad, w_up_grad, w_down_grad = (
        ffn_grad[:, :, i * PART : (i + 1) * PART].reshape(24, -1) for i in range(3)
    )
    return (
        output,
        input_grad,
        gains[:, 0],
        w_query_grad,
        w_key_grad,
        w_value_grad,
        head_gains[:HEAD],
        head_gains[HEAD : 2 * HEAD],
        w_out_grad,
        gains[:, 1],
        w_gate_grad,
        w_up_grad,
        w_down_grad.T,
    )


def solution(mesh):
    mesh = Mesh(np.asarray(mesh.devices).reshape(2, 4, 4, 2, 2), ALL)
    rows = P(ALL, None)
    weights = (P("yhi", BLK), P(ALL), P(BLK, "yhi"), P(BLK, "yhi"), P("yhi", BLK))
    placed_in = (rows, P(), P(ALL), rows, rows, rows, P(), P()) + weights + (rows,)
    placed_out = (rows, rows, P(ALL), rows, rows, rows, P(), P()) + weights
    return jax.shard_map(
        per_device, mesh=mesh, in_specs=placed_in, out_specs=placed_out, check_vma=False
    )
```

```python
import functools

import jax
import jax.numpy as jnp
import numpy as np
from jax import lax
from jax.experimental import pallas as pl
from jax.experimental.pallas import tpu as pltpu
from jax.sharding import Mesh
from jax.sharding import PartitionSpec as P

EPS = 1e-05
THETA = 1000000.0
HEAD = 64
ROWS = 128
PAIR = 2 * ROWS
GROUP = 3
QUERY = GROUP * HEAD
LANES = ROWS * GROUP
KEY_TILE = 512
SUPER = 2048
EARLIER = 2 * SUPER
PART = 432
PADDED = 512
WIDTH = 1536
ALL = ("ylo", "z", "x", "core", "yhi")
BLK = ("ylo", "z", "x", "core")
WIDE = ("yhi", "ylo", "z")
NEAR = ("x", "core")
NN = (((1,), (0,)), ((), ()))
NT = (((1,), (1,)), ((), ()))
TN = (((0,), (0,)), ((), ()))
F32 = jnp.float32
BF16 = jnp.bfloat16
SCORE = HEAD**-0.5 * 1.4426950408889634


def dot(a, b, numbers=NN):
    return lax.dot_general(a, b, numbers, preferred_element_type=F32)


def rms_scale(v):
    return lax.rsqrt(jnp.mean(v * v, axis=-1, keepdims=True) + EPS)


def rms_back(grad, v, scale):
    inner = jnp.mean(grad * v, axis=-1, keepdims=True)
    return scale * (grad - v * scale * scale * inner)


def shift_x(v, distance):
    return lax.ppermute(v, "x", [((i + distance) % 4, i) for i in range(4)])


def swap(v, axis):
    return lax.ppermute(v, axis, [(0, 1), (1, 0)])


def shift_super(v, distance, other):
    pairs = [
        (2 * i + h, 2 * (i + distance) + (h + other) % 2)
        for i in range(8)
        for h in (0, 1)
        if 0 <= i + distance < 8
    ]
    return lax.ppermute(v, ("ylo", "z", "yhi"), pairs)


def exchange(v, axes):
    return lax.all_to_all(v, axes, split_axis=0, concat_axis=0, tiled=True)


def near_gather(v):
    blocks = [v] + [shift_x(v, d) for d in (1, 2, 3)]
    return [[b, swap(b, "core")] for b in blocks]


def near_keep(parts):
    return [
        (own.astype(F32) + swap(other, "core").astype(F32)).astype(BF16) for own, other in parts
    ]


def near_sum(kept):
    total = kept[0].astype(F32)
    for d in (1, 2, 3):
        total = total + shift_x(kept[d], -d).astype(F32)
    return total


def rel_to_abs(v, x, core):
    v = jnp.where(core == 0, v, v[:, ::-1])
    return lax.dynamic_slice_in_dim(jnp.concatenate([v, v], axis=0), (4 - x) % 4, 4, 0)


def abs_to_rel(v, x, core):
    v = jnp.where(core == 0, v, v[:, ::-1])
    return lax.dynamic_slice_in_dim(jnp.concatenate([v, v], axis=0), x, 4, 0)


def params(steps, mib):
    return pltpu.CompilerParams(
        dimension_semantics=("arbitrary",) * steps, vmem_limit_bytes=mib * 2**20
    )


def cost(flops, moved, exps=0):
    return pl.CostEstimate(flops=int(flops), bytes_accessed=int(moved), transcendentals=int(exps))


def all_of(*shape):
    return pl.BlockSpec(shape, lambda *i: (0,) * len(shape))


ROWS_OF = pl.BlockSpec((ROWS, WIDTH), lambda *i: (0, 0))


def stacked(a_ref, b_ref):
    return jnp.concatenate([a_ref[...], b_ref[...]], axis=0)


def head_sums(v):
    lane = lax.shift_right_logical(lax.broadcasted_iota(jnp.int32, (4 * HEAD, 4 * HEAD), 1), 6)
    row = lax.shift_right_logical(lax.broadcasted_iota(jnp.int32, (4 * HEAD, 4 * HEAD), 0), 6)
    ones = jnp.where(lane == row, 1.0, 0.0).astype(BF16)
    high = v.astype(BF16)
    low = (v - high.astype(F32)).astype(BF16)
    return dot(high, ones) + dot(low, ones)


def half_turn(v):
    lane = lax.broadcasted_iota(jnp.int32, v.shape, 1)
    return jnp.where(
        (lane & (HEAD - 1)) < HEAD // 2,
        pltpu.roll(v, v.shape[1] - HEAD // 2, 1),
        pltpu.roll(v, HEAD // 2, 1),
    )


def twice(v):
    return jnp.concatenate([v, v], axis=1)


def project_kernel(*refs):
    xs, (w_ref, gain_ref, cos_ref, sin_ref, head_gain_ref) = refs[:8], refs[8:13]
    normed_ref, q_ref, kv_ref, raw_ref = refs[13:]
    lane = lax.broadcasted_iota(jnp.int32, (PAIR, 2 * HEAD), 1)
    for d in range(4):
        rows = slice(d * PAIR, (d + 1) * PAIR)
        tiles = slice(2 * d, 2 * d + 2)
        x = stacked(*xs[tiles]).astype(F32)
        normed = (x * rms_scale(x) * gain_ref[...]).astype(BF16)
        normed_ref[rows, :] = normed
        raw = dot(normed, w_ref[...])
        heads = raw[:, : 4 * HEAD]
        raw_ref[d] = heads
        scale = lax.rsqrt(head_sums(heads * heads) * (1.0 / HEAD) + EPS)
        v = heads * scale * head_gain_ref[...]
        turned = v * twice(cos_ref[d]) + half_turn(v) * twice(sin_ref[d])
        q_ref[tiles] = turned[:, :QUERY].astype(BF16).reshape(2, ROWS, QUERY)
        kv = jnp.where(lane < HEAD, raw[:, 4 * HEAD :], turned[:, 2 * HEAD :])
        kv_ref[tiles] = kv.astype(BF16).reshape(2, ROWS, 2 * HEAD)


def project(xs, w, gain, cos, sin, head_gain):
    return pl.pallas_call(
        project_kernel,
        out_shape=(
            jax.ShapeDtypeStruct((4 * PAIR, WIDTH), BF16),
            jax.ShapeDtypeStruct((8, ROWS, QUERY), BF16),
            jax.ShapeDtypeStruct((8, ROWS, 2 * HEAD), BF16),
            jax.ShapeDtypeStruct((4, PAIR, 4 * HEAD), F32),
        ),
        grid=(1,),
        in_specs=[ROWS_OF] * 8
        + [all_of(WIDTH, 384), all_of(1, WIDTH)]
        + [all_of(4, PAIR, 2 * HEAD)] * 2
        + [all_of(1, 4 * HEAD)],
        out_specs=(
            all_of(4 * PAIR, WIDTH),
            all_of(8, ROWS, QUERY),
            all_of(8, ROWS, 2 * HEAD),
            all_of(4, PAIR, 4 * HEAD),
        ),
        compiler_params=params(1, 40),
        cost_estimate=cost(8 * PAIR * WIDTH * 384, 1e7),
    )(*xs, w, gain, cos, sin, head_gain)


def unproject_kernel(*refs):
    gq_ref, g_refs, raw_ref, xs, (w_ref, cos_ref, sin_ref, head_gain_ref) = (
        refs[0], refs[1:7], refs[7], refs[8:12], refs[12:16],
    )
    parts, (graw_ref, attn_ref, heads_ref) = refs[16:20], refs[20:]
    attn, sums = 0.0, 0.0
    for i in range(2):
        tiles = slice(2 * i, 2 * i + 2)
        gq = gq_ref[tiles].reshape(PAIR, 4 * HEAD).astype(F32)
        gkv = g_refs[0][tiles].astype(F32)
        for ref in g_refs[1:]:
            gkv = gkv + ref[tiles].astype(F32)
        gkv = gkv.reshape(PAIR, 2 * HEAD)
        lane = lax.broadcasted_iota(jnp.int32, (PAIR, 2 * HEAD), 1)
        gk = (gkv * HEAD**-0.5).astype(BF16).astype(F32)
        gk = jnp.where(lane < HEAD, gq[:, 2 * HEAD :], gk)
        g = jnp.concatenate([gq[:, : 2 * HEAD], gk], axis=1)
        g = g * twice(cos_ref[i]) - half_turn(g) * twice(sin_ref[i])
        raw = raw_ref[i]
        scale = lax.rsqrt(head_sums(raw * raw) * (1.0 / HEAD) + EPS)
        sums = sums + jnp.sum(g * raw * scale, axis=0, keepdims=True)
        e = g * head_gain_ref[...]
        inner = head_sums(e * raw) * (1.0 / HEAD)
        graw = scale * (e - raw * scale * scale * inner)
        graw = jnp.concatenate([graw, jnp.where(lane < HEAD, gkv, 0.0)], axis=1).astype(BF16)
        graw_ref[i * PAIR : (i + 1) * PAIR, :] = graw
        grad = dot(graw, w_ref[...], NT)
        x = stacked(*xs[tiles]).astype(F32)
        attn = attn + jnp.sum(grad * x * rms_scale(x), axis=0, keepdims=True)
        grad = grad.astype(BF16)
        parts[2 * i][...] = grad[:ROWS]
        parts[2 * i + 1][...] = grad[ROWS:]
    attn_ref[...] = attn
    heads_ref[...] = sums


def unproject(half, gq, gkvs, raw, xs, w, cos, sin, head_gain):
    def at_half(*shape):
        return pl.BlockSpec(shape, lambda i: (half,) + (0,) * (len(shape) - 1))

    table = at_half(2, PAIR, 2 * HEAD)
    outs = (jax.ShapeDtypeStruct((ROWS, WIDTH), BF16),) * 4 + (
        jax.ShapeDtypeStruct((2 * PAIR, 6 * HEAD), BF16),
        jax.ShapeDtypeStruct((1, WIDTH), F32),
        jax.ShapeDtypeStruct((1, 4 * HEAD), F32),
    )
    return pl.pallas_call(
        unproject_kernel,
        out_shape=outs,
        grid=(1,),
        in_specs=[at_half(4, ROWS, 4 * HEAD)]
        + [at_half(4, ROWS, 2 * HEAD)] * 6
        + [at_half(2, PAIR, 4 * HEAD)]
        + [ROWS_OF] * 4
        + [all_of(WIDTH, 6 * HEAD), table, table, all_of(1, 4 * HEAD)],
        out_specs=tuple(all_of(*o.shape) for o in outs),
        compiler_params=params(1, 28),
        cost_estimate=cost(4 * PAIR * WIDTH * 384, 8e6),
    )(gq, *gkvs, raw, *xs, w, cos, sin, head_gain)


def ffn_kernel(
    x0_ref, x1_ref, c0_ref, c1_ref, gu_w_ref, d_w_ref,
    part0_ref, part1_ref, out0_ref, out1_ref, act_ref, gu_ref, total, out_total,
):
    y = pl.program_id(0)
    x = stacked(x0_ref, x1_ref)
    gate_up = dot(x, gu_w_ref[0])
    gate, up = gate_up[:, :PADDED], gate_up[:, PADDED:]
    grad_act = dot(stacked(c0_ref, c1_ref), d_w_ref[0])
    sig = 1.0 / (1.0 + jnp.exp(-gate))
    silu = gate * sig
    act = (silu * up).astype(BF16)
    act_ref[0] = act
    out_part = dot(act, d_w_ref[0], NT)
    grad_gate = grad_act * up * sig * (1.0 + gate * (1.0 - sig))
    grads = jnp.concatenate([grad_gate, grad_act * silu], axis=1).astype(BF16)
    gu_ref[0] = grads
    part = dot(grads, gu_w_ref[0], NT)

    @pl.when(y == 0)
    def _():
        total[...] = part
        out_total[...] = out_part

    @pl.when(y == 1)
    def _():
        whole_part = (total[...] + part).astype(BF16)
        part0_ref[...] = whole_part[:ROWS]
        part1_ref[...] = whole_part[ROWS:]
        whole_part = (out_total[...] + out_part).astype(BF16)
        out0_ref[...] = whole_part[:ROWS]
        out1_ref[...] = whole_part[ROWS:]


def ffn(x0, x1, c0, c1, w):
    rows = ROWS_OF
    return pl.pallas_call(
        ffn_kernel,
        out_shape=(jax.ShapeDtypeStruct((ROWS, WIDTH), BF16),) * 4
        + (
            jax.ShapeDtypeStruct((2, PAIR, PADDED), BF16),
            jax.ShapeDtypeStruct((2, PAIR, 2 * PADDED), BF16),
        ),
        grid=(2,),
        in_specs=[rows] * 4
        + [pl.BlockSpec((1, WIDTH, n * PADDED), lambda y, c=c: (y, 0, c)) for n, c in ((2, 0), (1, 2))],
        out_specs=(rows,) * 4
        + (
            pl.BlockSpec((1, PAIR, PADDED), lambda y: (y, 0, 0)),
            pl.BlockSpec((1, PAIR, 2 * PADDED), lambda y: (y, 0, 0)),
        ),
        scratch_shapes=[pltpu.VMEM((PAIR, WIDTH), F32)] * 2,
        compiler_params=params(1, 32),
        cost_estimate=cost(2 * 2 * PAIR * WIDTH * 6 * PADDED, 14e6),
    )(x0, x1, c0, c1, w, w)


def ffn_weights_kernel(*refs):
    xs, cs, gus, acts, out_ref = refs[:8], refs[8:16], refs[16:20], refs[20:24], refs[24]
    def all_tokens(refs):
        return jnp.concatenate([ref[...] for ref in refs], axis=0)

    grad_gu = dot(all_tokens(xs), all_tokens([g.at[0] for g in gus]), TN)
    grad_d = dot(all_tokens(cs), all_tokens([a.at[0] for a in acts]), TN)
    out_ref[0, :, :PART] = grad_gu[:, :PART].astype(BF16)
    out_ref[0, :, PART : 2 * PART] = grad_gu[:, PADDED : PADDED + PART].astype(BF16)
    out_ref[0, :, 2 * PART :] = grad_d[:, :PART].astype(BF16)


def ffn_weights(xs, cs, gus, acts):
    tall = 256
    rows = pl.BlockSpec((ROWS, tall), lambda y, m: (0, m))
    return pl.pallas_call(
        ffn_weights_kernel,
        out_shape=jax.ShapeDtypeStruct((2, WIDTH, 3 * PART), BF16),
        grid=(2, WIDTH // tall),
        in_specs=[rows] * 16
        + [pl.BlockSpec((1, PAIR, 2 * PADDED), lambda y, m: (y, 0, 0))] * 4
        + [pl.BlockSpec((1, PAIR, PADDED), lambda y, m: (y, 0, 0))] * 4,
        out_specs=pl.BlockSpec((1, tall, 3 * PART), lambda y, m: (y, m, 0)),
        compiler_params=params(2, 28),
        cost_estimate=cost(2 * 2 * 1024 * WIDTH * 3 * PADDED, 24e6),
    )(*xs, *cs, *gus, *acts)


def out_project_kernel(mix_ref, w_ref, part0_ref, part1_ref):
    part = dot(mix_ref[...].reshape(PAIR, QUERY), w_ref[...], NT).astype(BF16)
    part0_ref[...] = part[:ROWS]
    part1_ref[...] = part[ROWS:]


def out_project(d, mix, w):
    rows = pl.BlockSpec((ROWS, WIDTH), lambda i: (0, 0))
    return pl.pallas_call(
        out_project_kernel,
        out_shape=(jax.ShapeDtypeStruct((ROWS, WIDTH), BF16),) * 2,
        grid=(1,),
        in_specs=[
            pl.BlockSpec((2, ROWS, QUERY), lambda i: (d, 0, 0)),
            pl.BlockSpec((WIDTH, QUERY), lambda i: (0, 0)),
        ],
        out_specs=(rows, rows),
        compiler_params=params(1, 16),
        cost_estimate=cost(2 * PAIR * WIDTH * QUERY, 2e6),
    )(mix, w)


def out_back_kernel(w_ref, *refs):
    for t in range(8):
        refs[8][t] = dot(refs[t][...], w_ref[...]).astype(BF16)


def out_back(branches, w):
    return pl.pallas_call(
        out_back_kernel,
        out_shape=jax.ShapeDtypeStruct((8, ROWS, QUERY), BF16),
        compiler_params=params(0, 16),
        cost_estimate=cost(8 * PAIR * WIDTH * QUERY, 4e6),
    )(w, *branches)


def out_weights_kernel(mix_ref, *refs):
    branch = jnp.concatenate([b[...] for b in refs[:8]], axis=0)
    refs[8][...] = dot(branch, mix_ref[...].reshape(8 * ROWS, QUERY), TN)


def out_weights(mix, branches):
    return pl.pallas_call(
        out_weights_kernel,
        out_shape=jax.ShapeDtypeStruct((WIDTH, QUERY), F32),
        compiler_params=params(0, 24),
        cost_estimate=cost(2 * 1024 * WIDTH * QUERY, 4e6),
    )(mix, *branches)


def pack_kernel(normed_ref, graw0_ref, graw1_ref, gains_ref, out_grad_ref, sent_ref):
    graw = jnp.concatenate([graw0_ref[...], graw1_ref[...]], axis=0)
    grad = dot(normed_ref[...], graw, TN)
    gains = gains_ref[...]
    high = gains.astype(BF16).astype(F32)
    gains = jnp.concatenate([high, gains - high, jnp.zeros((HEAD - 32, gains.shape[1]), F32)], axis=0)
    sent_ref[:, : 5 * HEAD] = grad[:, : 5 * HEAD].astype(BF16)
    sent_ref[:, 5 * HEAD : 6 * HEAD] = gains.T.astype(BF16)
    sent_ref[:, 6 * HEAD :] = out_grad_ref[...].astype(BF16)


def pack(normed, graws, gains, out_grad):
    tall = 256
    return pl.pallas_call(
        pack_kernel,
        out_shape=jax.ShapeDtypeStruct((WIDTH, 9 * HEAD), BF16),
        grid=(WIDTH // tall,),
        in_specs=[
            pl.BlockSpec((8 * ROWS, tall), lambda m: (0, m)),
            all_of(4 * ROWS, 6 * HEAD),
            all_of(4 * ROWS, 6 * HEAD),
            pl.BlockSpec((16, tall), lambda m: (0, m)),
            pl.BlockSpec((tall, QUERY), lambda m: (m, 0)),
        ],
        out_specs=pl.BlockSpec((tall, 9 * HEAD), lambda m: (m, 0)),
        compiler_params=params(1, 24),
        cost_estimate=cost(2 * 1024 * WIDTH * 384, 8e6),
    )(normed, *graws, gains, out_grad)


def side_by_side(t):
    return jnp.concatenate([t[g * HEAD : (g + 1) * HEAD] for g in range(GROUP)], axis=1)


def on_top(t):
    return jnp.concatenate([t[:, g * ROWS : (g + 1) * ROWS] for g in range(GROUP)], axis=0)


def key_loops(plan, at, base, start, visit, state):
    f = pl.program_id(0)
    lo, m1, m2, hi = (plan[f, at + i] for i in range(4))
    place = lax.rem(lax.broadcasted_iota(jnp.int32, (1, LANES), 1), ROWS) + plan[f, 0]

    def masked(j, state):
        key = lax.broadcasted_iota(jnp.int32, (KEY_TILE, LANES), 0) + (j * KEY_TILE + base)
        return visit(j, state, (key >= start) & (key <= place))

    def two(i, state):
        return visit(m1 + 2 * i + 1, visit(m1 + 2 * i, state, None), None)

    pairs = lax.shift_right_logical(m2 - m1, 1)
    state = lax.fori_loop(lo, m1, masked, state)
    state = lax.fori_loop(0, pairs, two, state)
    state = lax.fori_loop(m1 + 2 * pairs, m2, lambda j, s: visit(j, s, None), state)
    return lax.fori_loop(m2, hi, masked, state)


def rows_of(j):
    return pl.ds(pl.multiple_of(j * KEY_TILE, KEY_TILE), KEY_TILE)


def chunks(plan, supers):
    for b in range(supers):
        for half in (0, 1):
            for f in range(8):
                side = plan[0, 10] if half == 0 else 1 - plan[0, 10]
                yield b, half, pl.multiple_of(b * SUPER + f * PAIR + side * ROWS, ROWS), plan[f, 1]


def line_up(plan, kv_refs, kv, kvt):
    @pl.when(pl.program_id(0) == 0)
    def _():
        for b, half, place, sent in chunks(plan, len(kv_refs) // 2):
            block = kv_refs[2 * b + half][sent]
            kv[pl.ds(place, ROWS), :] = block
            kvt[:, pl.ds(place, ROWS)] = block.astype(F32).T.astype(BF16)


def attend_body(at, base, plan, q_ref, start_ref, kv, kvt, state):
    qt = side_by_side(q_ref[0].astype(F32).T)
    qt = jnp.concatenate([jnp.zeros_like(qt), qt], axis=0).astype(BF16)

    def visit(j, state, mask):
        total, accum = state
        weights = jnp.exp2(dot(kv[rows_of(j), :], qt) * SCORE)
        if mask is not None:
            weights = jnp.where(mask, weights, 0.0)
        total = total + jnp.sum(weights, axis=0, keepdims=True)
        return total, accum + dot(kvt[:HEAD, rows_of(j)], weights.astype(BF16))

    return key_loops(plan, at, base, start_ref[0], visit, state)


def attend_own_kernel(plan, q_ref, start_ref, *refs):
    kv_refs, (accum_ref, total_ref, kv, kvt) = refs[:2], refs[2:]
    line_up(plan, kv_refs, kv, kvt)
    state = (jnp.zeros((1, LANES), F32), jnp.zeros((HEAD, LANES), F32))
    total, accum = attend_body(6, EARLIER, plan, q_ref, start_ref, kv, kvt, state)
    accum_ref[0] = accum
    total_ref[0] = total


def attend_earlier_kernel(plan, q_ref, start_ref, *refs):
    kv_refs, (accum_ref, total_ref, mix_ref, out_ref, lse_ref, kv, kvt) = refs[:4], refs[4:]
    line_up(plan, kv_refs, kv, kvt)
    state = (total_ref[0], accum_ref[0])
    total, accum = attend_body(2, 0, plan, q_ref, start_ref, kv, kvt, state)
    out = accum / total
    out_ref[0] = out
    mix_ref[0] = on_top(out).T.astype(BF16)
    lse_ref[0] = jnp.log2(total)


def back_kernel(plan, q_ref, start_ref, *refs):
    kv_refs, (g_ref, out_ref, lse_ref, dq_ref), sent_refs, (kv, kvt, dkv) = (
        refs[:6], refs[6:10], refs[10:16], refs[16:],
    )
    line_up(plan, kv_refs, kv, kvt)

    @pl.when(pl.program_id(0) == 0)
    def _():
        dkv[...] = jnp.zeros_like(dkv)

    qt = side_by_side(q_ref[0].astype(F32).T)
    gt = side_by_side(g_ref[0].astype(F32).T)
    delta = jnp.sum(gt * out_ref[0], axis=0, keepdims=True)
    zero = jnp.zeros_like(qt)
    gt = jnp.concatenate([gt, zero], axis=0)
    qt = jnp.concatenate([zero, qt], axis=0)
    both_t = jnp.concatenate([gt, qt], axis=1).astype(BF16)
    both = jnp.concatenate([gt.T, qt.T], axis=0).astype(BF16)
    lse = lse_ref[0]

    def visit(j, dqt, mask):
        pair = dot(kv[rows_of(j), :], both_t)
        weights = jnp.exp2(pair[:, LANES:] * SCORE - lse)
        if mask is not None:
            weights = jnp.where(mask, weights, 0.0)
        grads = (weights * (pair[:, :LANES] - delta)).astype(BF16)
        sides = jnp.concatenate([weights.astype(BF16), grads], axis=1)
        dkv[rows_of(j), :] += dot(sides, both)
        return dqt + dot(kvt[HEAD:, rows_of(j)], grads)

    dqt = key_loops(plan, 11, 0, start_ref[0], visit, jnp.zeros((HEAD, LANES), F32))
    dq = on_top(dqt * HEAD**-0.5).T
    dq_ref[0] = jnp.concatenate([dq, jnp.zeros((ROWS, HEAD), F32)], axis=1).astype(BF16)

    @pl.when(pl.program_id(0) == 7)
    def _():
        for b, half, place, sent in chunks(plan, 3):
            sent_refs[2 * b + half][sent] = dkv[pl.ds(place, ROWS), :].astype(BF16)


def whole(*shape):
    return pl.BlockSpec(shape, lambda f, plan: (0,) * len(shape))


def tile(*shape):
    return pl.BlockSpec((1,) + shape, lambda f, plan: (f,) + (0,) * len(shape))


def placed(*shape):
    return pl.BlockSpec((1,) + shape, lambda f, plan: (plan[f, 1],) + (0,) * len(shape))


def tiles_call(kernel, supers, outs, more_ins, out_specs, flops, back):
    keys = supers * SUPER
    scratch = [pltpu.VMEM((keys, 2 * HEAD), BF16), pltpu.VMEM((2 * HEAD, keys), BF16)]
    if back:
        scratch.append(pltpu.VMEM((keys, 2 * HEAD), F32))
    ins = [placed(ROWS, QUERY), tile(1, LANES)] + [whole(8, ROWS, 2 * HEAD)] * (2 * supers)
    return pl.pallas_call(
        kernel,
        out_shape=outs,
        grid_spec=pltpu.PrefetchScalarGridSpec(
            num_scalar_prefetch=1,
            grid=(8,),
            in_specs=ins + more_ins,
            out_specs=out_specs,
            scratch_shapes=scratch,
        ),
        compiler_params=params(1, 20),
        cost_estimate=cost(flops, 8e6, 1e7),
    )


TILE_T = jax.ShapeDtypeStruct((8, HEAD, LANES), F32)
TILE_ROW = jax.ShapeDtypeStruct((8, 1, LANES), F32)
STATE = [tile(HEAD, LANES), tile(1, LANES)]


def attend_own(plan, q, start, kvs):
    call = tiles_call(attend_own_kernel, 1, (TILE_T, TILE_ROW), [], tuple(STATE), 4e9, False)
    return call(plan, q, start, *kvs)


def attend_earlier(plan, q, start, kvs, state):
    outs = (jax.ShapeDtypeStruct((8, ROWS, QUERY), BF16), TILE_T, TILE_ROW)
    specs = (placed(ROWS, QUERY),) + tuple(STATE)
    call = tiles_call(attend_earlier_kernel, 2, outs, STATE, specs, 8e9, False)
    return call(plan, q, start, *kvs, *state)


def back(plan, q, start, kvs, grad, out, lse):
    sent = jax.ShapeDtypeStruct((8, ROWS, 2 * HEAD), BF16)
    call = tiles_call(
        back_kernel,
        3,
        [jax.ShapeDtypeStruct((8, ROWS, 4 * HEAD), BF16)] + [sent] * 6,
        [placed(ROWS, QUERY)] + STATE,
        [placed(ROWS, 4 * HEAD)] + [whole(*sent.shape)] * 6,
        30e9,
        True,
    )
    return call(plan, q, start, *kvs, grad, out, lse)


def after(v, *others):
    return lax.optimization_barrier((v,) + others)[0]


def per_device(
    tokens,
    segments,
    attn_gain,
    w_query,
    w_key,
    w_value,
    q_gain,
    k_gain,
    w_out,
    ffn_gain,
    w_gate,
    w_up,
    w_down,
    cotangent,
):
    ylo, z, x, core, yhi = (lax.axis_index(a) for a in ALL)
    sup = ylo * 4 + z

    token_shifts = [shift_x(tokens, d) for d in (1, 2, 3)]
    token_blocks = [[b, swap(b, "core")] for b in [tokens] + token_shifts]
    all_tokens = [b for p in token_blocks for b in p]
    qkv_own = jnp.concatenate(
        [
            w_query.reshape(12, 8, QUERY),
            w_key.reshape(12, 8, HEAD),
            w_value.reshape(12, 8, HEAD),
            jnp.broadcast_to(attn_gain[:, None, None], (12, 8, 1)),
            jnp.broadcast_to(ffn_gain[:, None, None], (12, 8, 1)),
            jnp.zeros((12, 8, HEAD - 2), BF16),
        ],
        axis=-1,
    )
    qkv_own = jnp.pad(jnp.transpose(qkv_own, (1, 0, 2)), ((0, 0), (0, 12), (0, 0)))
    out_own = jnp.transpose(w_out.reshape(4, QUERY, 24), (0, 2, 1))
    rows_own = jnp.concatenate(
        [
            jnp.pad(w.reshape(24, 8, PART), ((0, 0), (0, 0), (0, PADDED - PART))).transpose(1, 0, 2)
            for w in (w_gate, w_up, w_down.T)
        ]
        + [jnp.concatenate([out_own, out_own], axis=0), qkv_own],
        axis=-1,
    )
    rows = exchange(rows_own, NEAR)
    ffn_rows = rows[:, :, : 3 * PADDED].reshape(192, 3 * PADDED)
    out_rows = rows[:, :, 3 * PADDED : 3 * PADDED + QUERY].reshape(1, 192, QUERY)
    qkv_rows = rows[:, :12, 3 * PADDED + QUERY :].reshape(1, 96, 6 * HEAD)
    qkv = exchange(jnp.broadcast_to(qkv_rows, (16, 96, 6 * HEAD)), WIDE)
    qkv = jnp.transpose(qkv.reshape(2, 8, 8, 12, 6 * HEAD), (1, 2, 0, 3, 4)).reshape(WIDTH, 6 * HEAD)
    qkv, ffn_rows = lax.optimization_barrier((qkv, ffn_rows))
    ffn_full = lax.all_gather(ffn_rows, WIDE, axis=0, tiled=True).reshape(2, WIDTH, 3 * PADDED)
    gain_attn = qkv[:, 5 * HEAD].astype(F32)
    gain_ffn = qkv[:, 5 * HEAD + 1].astype(F32)

    token_index = jnp.arange(segments.shape[0], dtype=jnp.int32)
    begins = jnp.concatenate([jnp.ones((1,), jnp.bool_), segments[1:] != segments[:-1]])
    starts = lax.cummax(jnp.where(begins, token_index, 0), axis=0)
    own_starts = lax.dynamic_slice(
        starts.reshape(8, 8, 2, ROWS), (sup, 0, yhi, 0), (1, 8, 1, ROWS)
    ).reshape(8, ROWS)
    first = sup * SUPER + jnp.arange(8, dtype=jnp.int32) * PAIR + yhi * ROWS
    own_places = first[:, None] + jnp.arange(ROWS, dtype=jnp.int32)[None]
    positions = abs_to_rel((own_places - own_starts).reshape(4, 2, ROWS), x, core)
    frequency = THETA ** (-jnp.arange(HEAD // 2, dtype=F32) * 2.0 / HEAD)
    angles = positions.reshape(4, PAIR, 1).astype(F32) * frequency
    cosine, sine = jnp.cos(angles), jnp.sin(angles)
    cos = jnp.concatenate([cosine] * 4, axis=-1)
    sin = jnp.concatenate([-sine, sine] * 2, axis=-1)
    head_gain = jnp.concatenate([q_gain, q_gain, q_gain, k_gain]).astype(F32)[None]

    window = (sup - 2) * SUPER
    lo = (own_starts[:, 0] - window) // KEY_TILE
    hi = (first + ROWS - 1 - window) // KEY_TILE + 1
    m1 = jnp.clip((own_starts[:, -1] - window + KEY_TILE - 1) // KEY_TILE, lo, hi)
    m2 = jnp.clip((first + 1 - window) // KEY_TILE, m1, hi)
    order = jnp.arange(8, dtype=jnp.int32)
    relative = ((order // 2 - x) % 4) * 2 + (order % 2 + core) % 2
    edge = EARLIER // KEY_TILE
    plan = jnp.stack(
        [first - window, relative]
        + [jnp.minimum(v, edge) for v in (lo, m1, m2, hi)]
        + [jnp.maximum(v - edge, 0) for v in (lo, m1, m2, hi)]
        + [jnp.broadcast_to(yhi, (8,)), lo, m1, m2, hi],
        axis=1,
    ).astype(jnp.int32)
    start_lanes = jnp.tile(own_starts - window, (1, GROUP)).reshape(8, 1, LANES)

    normed, rot_q, kv, raw = project(
        all_tokens, qkv, gain_attn[None], cos, sin, head_gain
    )

    kv_own = [kv, swap(kv, "yhi")]
    kv_sent = after(kv, kv_own[1])
    kv_earlier = [shift_super(kv_sent, a, b) for a, b in ((2, 0), (2, 1), (1, 0), (1, 1))]
    state = attend_own(plan, rot_q, start_lanes, kv_own)
    state, kv_earlier, out_rows, cot_sent = lax.optimization_barrier(
        (state, kv_earlier, out_rows, cotangent)
    )
    cot_shifts = [shift_x(cot_sent, d) for d in (1, 2, 3)]
    out_both = exchange(jnp.broadcast_to(out_rows, (16, 192, QUERY)), WIDE)
    out_both = out_both.reshape(2, WIDTH, QUERY)
    mix, out_tiles, lse = attend_earlier(plan, rot_q, start_lanes, kv_earlier, state)
    w_out_t = jnp.where(x < 2, out_both[0], out_both[1])
    mix, w_out_t, cot_shifts = lax.optimization_barrier((mix, w_out_t, cot_shifts))
    cot_blocks = [[b, swap(b, "core")] for b in [cotangent] + cot_shifts]
    all_cot = [b for p in cot_blocks for b in p]

    inputs = tokens.astype(F32)
    parts = [None] * 4
    for d in (2, 1, 3, 0):
        parts[d] = out_project(d, mix, w_out_t)
    hidden = inputs + near_sum(near_keep(parts))
    scale_ffn = rms_scale(hidden)
    scaled_ffn = hidden * scale_ffn
    normed_ffn = (scaled_ffn * gain_ffn).astype(BF16)

    ffn_blocks = [[b] for b in [normed_ffn] + [shift_x(normed_ffn, d) for d in (1, 2, 3)]]
    ffn_blocks[0].append(swap(normed_ffn, "core"))
    ffn_outs = [None] * 4
    before = {1: 0, 3: 0, 2: 1}
    for d in (0, 1, 3, 2):
        if d > 0:
            block = after(ffn_blocks[d][0], ffn_outs[before[d]][0])
            ffn_blocks[d] = [block, swap(block, "core")]
        blocks = ffn_blocks[d]
        if d == 3:
            blocks = after(blocks, ffn_outs[1][0])
        if d == 2:
            blocks = after(blocks, ffn_outs[3][0])
        ffn_outs[d] = ffn(*blocks, *cot_blocks[d], ffn_full)
    acts, gus = [o[4] for o in ffn_outs], [o[5] for o in ffn_outs]
    kept, gus, out_own, out_other = lax.optimization_barrier(
        (near_keep([o[:2] for o in ffn_outs]), gus, [o[2] for o in ffn_outs], [o[3] for o in ffn_outs])
    )
    out_kept = jnp.stack(out_own).astype(F32) + swap(jnp.stack(out_other), "core").astype(F32)
    out_kept = out_kept.astype(BF16)
    pair_total = near_sum(kept)
    weight_grads = ffn_weights(
        [b for p in ffn_blocks for b in p], all_cot, gus, acts
    )
    pair_total, weight_grads, out_kept = lax.optimization_barrier((pair_total, weight_grads, out_kept))
    ffn_sum = lax.psum_scatter(
        weight_grads.reshape(2 * WIDTH, 3 * PART), WIDE, scatter_dimension=0, tiled=True
    )

    ffn_gain_part = jnp.sum(pair_total * scaled_ffn, axis=0)
    grad_hidden = cotangent.astype(F32) + rms_back(pair_total * gain_ffn, hidden, scale_ffn)
    grad_branch = grad_hidden.astype(BF16)
    branches = [b for p in near_gather(grad_branch) for b in p]
    grad_mix = out_back(branches, w_out_t)
    out_total = near_sum(after([out_kept[d] for d in range(4)], branches))

    back_outs = back(plan, rot_q, start_lanes, kv_earlier + kv_own, grad_mix, out_tiles, lse)
    back_outs, out_total = lax.optimization_barrier((back_outs, out_total))
    grad_q, two_mine, two_theirs, one_mine, one_theirs, mine, theirs = back_outs
    grad_kvs = [
        mine,
        swap(theirs, "yhi"),
        shift_super(one_mine, -1, 0),
        shift_super(one_theirs, -1, 1),
        shift_super(two_mine, -2, 0),
        shift_super(two_theirs, -2, 1),
    ]

    grad_out = out_weights(after(mix, grad_q), branches)
    grad_kvs, grad_out = lax.optimization_barrier((grad_kvs, grad_out))

    unprojected = [None] * 2
    for half in (1, 0):
        xs = all_tokens[4 * half : 4 * half + 4]
        unprojected[half] = unproject(half, grad_q, grad_kvs, raw, xs, qkv, cos, sin, head_gain)
    head_part = sum(u[6] for u in unprojected)[0]
    q_gain_part = head_part[:HEAD] + head_part[HEAD : 2 * HEAD] + head_part[2 * HEAD : QUERY]
    head_part = jnp.concatenate([q_gain_part, head_part[QUERY:], jnp.zeros((4,), F32)])
    gain_parts = jnp.concatenate(
        [
            sum(u[5] for u in unprojected),
            ffn_gain_part[None],
            jnp.tile(head_part.reshape(12, 11).T, (1, 128)),
            jnp.zeros((3, WIDTH), F32),
        ],
        axis=0,
    )
    sent = pack(normed, [u[4] for u in unprojected], gain_parts, grad_out)
    parts = [u[2 * i : 2 * i + 2] for u in unprojected for i in (0, 1)]
    parts, sent = lax.optimization_barrier((parts, sent))
    grad_normed = near_sum(near_keep(parts))
    got = exchange(sent.reshape(8, 192, 9 * HEAD), ("ylo", "z"))
    got = jnp.sum(got.astype(F32), axis=0).astype(BF16)
    last = jnp.concatenate(
        [ffn_sum.reshape(8, 24, 3 * PART), got.reshape(8, 24, 9 * HEAD)], axis=-1
    )
    last = exchange(last, NEAR)
    ffn_grad, got = last[:, :, : 3 * PART], last[:, :, 3 * PART :].astype(F32)

    qkv_grad, grad_out = got[:, :, : 6 * HEAD], got[:, :, 6 * HEAD :]
    here, there = jnp.where(yhi == 0, 0, 1), jnp.where(yhi == 0, 1, 0)

    def half_of(v, axis, which):
        size = v.shape[axis] // 2
        return lax.dynamic_slice_in_dim(v, which * size, size, axis)

    qkv_other = swap(half_of(qkv_grad, 1, there).astype(BF16), "yhi").astype(F32)
    out_other = swap(half_of(grad_out, 0, there).astype(BF16), "yhi").astype(F32)
    qkv_grad = half_of(qkv_grad, 1, here) + qkv_other
    grad_out = half_of(grad_out, 0, here) + out_other
    gains = jnp.sum(qkv_grad[:, :, 5 * HEAD :], axis=0)
    gains = gains[:, :16] + gains[:, 16:32]
    head_gains = gains[:, 2:13].reshape(-1)
    qkv_grad = jnp.transpose(qkv_grad, (1, 0, 2))
    w_out_grad = jnp.transpose(grad_out, (0, 2, 1)).reshape(768, 24)
    w_query_grad = qkv_grad[:, :, :QUERY].reshape(12, -1)
    w_key_grad = qkv_grad[:, :, QUERY : QUERY + HEAD].reshape(12, -1)
    w_value_grad = qkv_grad[:, :, QUERY + HEAD : QUERY + 2 * HEAD].reshape(12, -1)

    output = (hidden + out_total).astype(BF16)
    scale_attn = rms_scale(inputs)
    input_grad = (grad_hidden + rms_back(grad_normed * gain_attn, inputs, scale_attn)).astype(BF16)

    ffn_grad = jnp.transpose(ffn_grad, (1, 0, 2)).astype(F32)
    w_gate_grad, w_up_grad, w_down_grad = (
        ffn_grad[:, :, i * PART : (i + 1) * PART].reshape(24, -1) for i in range(3)
    )
    return (
        output,
        input_grad,
        gains[:, 0],
        w_query_grad,
        w_key_grad,
        w_value_grad,
        head_gains[:HEAD],
        head_gains[HEAD : 2 * HEAD],
        w_out_grad,
        gains[:, 1],
        w_gate_grad,
        w_up_grad,
        w_down_grad.T,
    )


def solution(mesh):
    mesh = Mesh(np.asarray(mesh.devices).reshape(2, 4, 4, 2, 2), ALL)
    rows = P(ALL, None)
    weights = (P("yhi", BLK), P(ALL), P(BLK, "yhi"), P(BLK, "yhi"), P("yhi", BLK))
    placed_in = (rows, P(), P(ALL), rows, rows, rows, P(), P()) + weights + (rows,)
    placed_out = (rows, rows, P(ALL), rows, rows, rows, P(), P()) + weights
    return jax.shard_map(
        per_device, mesh=mesh, in_specs=placed_in, out_specs=placed_out, check_vma=False
    )
```

```python
import functools

import jax
import jax.numpy as jnp
import numpy as np
from jax import lax
from jax.experimental import pallas as pl
from jax.experimental.pallas import tpu as pltpu
from jax.sharding import Mesh
from jax.sharding import PartitionSpec as P

EPS = 1e-05
THETA = 1000000.0
HEAD = 64
ROWS = 128
PAIR = 2 * ROWS
GROUP = 3
QUERY = GROUP * HEAD
LANES = ROWS * GROUP
KEY_TILE = 512
UNROLL = 4
SUPER = 2048
EARLIER = 2 * SUPER
PART = 432
PADDED = 512
FREE = PADDED - PART
WIDTH = 1536
ALL = ("ylo", "z", "x", "core", "yhi")
BLK = ("ylo", "z", "x", "core")
WIDE = ("yhi", "ylo", "z")
NEAR = ("x", "core")
NN = (((1,), (0,)), ((), ()))
NT = (((1,), (1,)), ((), ()))
TN = (((0,), (0,)), ((), ()))
F32 = jnp.float32
BF16 = jnp.bfloat16
SCORE = HEAD**-0.5 * 1.4426950408889634


def dot(a, b, numbers=NN):
    return lax.dot_general(a, b, numbers, preferred_element_type=F32)


def rms_scale(v):
    return lax.rsqrt(jnp.mean(v * v, axis=-1, keepdims=True) + EPS)


def rms_back(grad, v, scale):
    inner = jnp.mean(grad * v, axis=-1, keepdims=True)
    return scale * (grad - v * scale * scale * inner)


def shift_x(v, distance):
    return lax.ppermute(v, "x", [((i + distance) % 4, i) for i in range(4)])


def swap(v, axis):
    return lax.ppermute(v, axis, [(0, 1), (1, 0)])


def shift_super(v, distance, other):
    pairs = [
        (2 * i + h, 2 * (i + distance) + (h + other) % 2)
        for i in range(8)
        for h in (0, 1)
        if 0 <= i + distance < 8
    ]
    return lax.ppermute(v, ("ylo", "z", "yhi"), pairs)


def exchange(v, axes):
    return lax.all_to_all(v, axes, split_axis=0, concat_axis=0, tiled=True)


def near_gather(v):
    blocks = [v] + [shift_x(v, d) for d in (1, 2, 3)]
    return [[b, swap(b, "core")] for b in blocks]


def near_keep(parts):
    return [
        (own.astype(F32) + swap(other, "core").astype(F32)).astype(BF16) for own, other in parts
    ]


def near_sum(kept):
    total = kept[0].astype(F32)
    for d in (1, 2, 3):
        total = total + shift_x(kept[d], -d).astype(F32)
    return total


def rel_to_abs(v, x, core):
    v = jnp.where(core == 0, v, v[:, ::-1])
    return lax.dynamic_slice_in_dim(jnp.concatenate([v, v], axis=0), (4 - x) % 4, 4, 0)


def abs_to_rel(v, x, core):
    v = jnp.where(core == 0, v, v[:, ::-1])
    return lax.dynamic_slice_in_dim(jnp.concatenate([v, v], axis=0), x, 4, 0)


def params(steps, mib):
    return pltpu.CompilerParams(
        dimension_semantics=("arbitrary",) * steps, vmem_limit_bytes=mib * 2**20
    )


def cost(flops, moved, exps=0):
    return pl.CostEstimate(flops=int(flops), bytes_accessed=int(moved), transcendentals=int(exps))


def all_of(*shape):
    return pl.BlockSpec(shape, lambda *i: (0,) * len(shape))


ROWS_OF = pl.BlockSpec((ROWS, WIDTH), lambda *i: (0, 0))


def stacked(a_ref, b_ref):
    return jnp.concatenate([a_ref[...], b_ref[...]], axis=0)


def head_sums(v):
    lane = lax.shift_right_logical(lax.broadcasted_iota(jnp.int32, (4 * HEAD, 4 * HEAD), 1), 6)
    row = lax.shift_right_logical(lax.broadcasted_iota(jnp.int32, (4 * HEAD, 4 * HEAD), 0), 6)
    ones = jnp.where(lane == row, 1.0, 0.0).astype(BF16)
    high = v.astype(BF16)
    low = (v - high.astype(F32)).astype(BF16)
    return dot(high, ones) + dot(low, ones)


def half_turn(v):
    lane = lax.broadcasted_iota(jnp.int32, v.shape, 1)
    return jnp.where(
        (lane & (HEAD - 1)) < HEAD // 2,
        pltpu.roll(v, v.shape[1] - HEAD // 2, 1),
        pltpu.roll(v, HEAD // 2, 1),
    )


def twice(v):
    return jnp.concatenate([v, v], axis=1)


def project_kernel(*refs):
    xs, (w_ref, gain_ref, cos_ref, sin_ref, head_gain_ref) = refs[:8], refs[8:13]
    normed_ref, q_ref, kv_ref, raw_ref = refs[13:]
    lane = lax.broadcasted_iota(jnp.int32, (PAIR, 2 * HEAD), 1)
    for d in range(4):
        rows = slice(d * PAIR, (d + 1) * PAIR)
        tiles = slice(2 * d, 2 * d + 2)
        x = stacked(*xs[tiles]).astype(F32)
        normed = (x * rms_scale(x) * gain_ref[...]).astype(BF16)
        normed_ref[rows, :] = normed
        raw = dot(normed, w_ref[...])
        heads = raw[:, : 4 * HEAD]
        raw_ref[d] = heads
        scale = lax.rsqrt(head_sums(heads * heads) * (1.0 / HEAD) + EPS)
        v = heads * scale * head_gain_ref[...]
        turned = v * twice(cos_ref[d]) + half_turn(v) * twice(sin_ref[d])
        q_ref[tiles] = turned[:, :QUERY].astype(BF16).reshape(2, ROWS, QUERY)
        kv = jnp.where(lane < HEAD, raw[:, 4 * HEAD :], turned[:, 2 * HEAD :])
        kv_ref[tiles] = kv.astype(BF16).reshape(2, ROWS, 2 * HEAD)


def project(xs, w, gain, cos, sin, head_gain):
    return pl.pallas_call(
        project_kernel,
        out_shape=(
            jax.ShapeDtypeStruct((4 * PAIR, WIDTH), BF16),
            jax.ShapeDtypeStruct((8, ROWS, QUERY), BF16),
            jax.ShapeDtypeStruct((8, ROWS, 2 * HEAD), BF16),
            jax.ShapeDtypeStruct((4, PAIR, 4 * HEAD), F32),
        ),
        grid=(1,),
        in_specs=[ROWS_OF] * 8
        + [all_of(WIDTH, 384), all_of(1, WIDTH)]
        + [all_of(4, PAIR, 2 * HEAD)] * 2
        + [all_of(1, 4 * HEAD)],
        out_specs=(
            all_of(4 * PAIR, WIDTH),
            all_of(8, ROWS, QUERY),
            all_of(8, ROWS, 2 * HEAD),
            all_of(4, PAIR, 4 * HEAD),
        ),
        compiler_params=params(1, 40),
        cost_estimate=cost(8 * PAIR * WIDTH * 384, 1e7),
    )(*xs, w, gain, cos, sin, head_gain)


def unproject_kernel(*refs):
    gq_ref, g_refs, raw_ref, xs, (w_ref, cos_ref, sin_ref, head_gain_ref) = (
        refs[0], refs[1:7], refs[7], refs[8:12], refs[12:16],
    )
    parts, (graw_ref, attn_ref, heads_ref) = refs[16:20], refs[20:]
    attn, sums = 0.0, 0.0
    for i in range(2):
        tiles = slice(2 * i, 2 * i + 2)
        gq = gq_ref[tiles].reshape(PAIR, 4 * HEAD).astype(F32)
        gkv = g_refs[0][tiles].astype(F32)
        for ref in g_refs[1:]:
            gkv = gkv + ref[tiles].astype(F32)
        gkv = gkv.reshape(PAIR, 2 * HEAD)
        lane = lax.broadcasted_iota(jnp.int32, (PAIR, 2 * HEAD), 1)
        gk = (gkv * HEAD**-0.5).astype(BF16).astype(F32)
        gk = jnp.where(lane < HEAD, gq[:, 2 * HEAD :], gk)
        g = jnp.concatenate([gq[:, : 2 * HEAD], gk], axis=1)
        g = g * twice(cos_ref[i]) - half_turn(g) * twice(sin_ref[i])
        raw = raw_ref[i]
        scale = lax.rsqrt(head_sums(raw * raw) * (1.0 / HEAD) + EPS)
        sums = sums + jnp.sum(g * raw * scale, axis=0, keepdims=True)
        e = g * head_gain_ref[...]
        inner = head_sums(e * raw) * (1.0 / HEAD)
        graw = scale * (e - raw * scale * scale * inner)
        graw = jnp.concatenate([graw, jnp.where(lane < HEAD, gkv, 0.0)], axis=1).astype(BF16)
        graw_ref[i * PAIR : (i + 1) * PAIR, :] = graw
        grad = dot(graw, w_ref[...], NT)
        x = stacked(*xs[tiles]).astype(F32)
        attn = attn + jnp.sum(grad * x * rms_scale(x), axis=0, keepdims=True)
        grad = grad.astype(BF16)
        parts[2 * i][...] = grad[:ROWS]
        parts[2 * i + 1][...] = grad[ROWS:]
    attn_ref[...] = attn
    heads_ref[...] = sums


def unproject(half, gq, gkvs, raw, xs, w, cos, sin, head_gain):
    def at_half(*shape):
        return pl.BlockSpec(shape, lambda i: (half,) + (0,) * (len(shape) - 1))

    table = at_half(2, PAIR, 2 * HEAD)
    outs = (jax.ShapeDtypeStruct((ROWS, WIDTH), BF16),) * 4 + (
        jax.ShapeDtypeStruct((2 * PAIR, 6 * HEAD), BF16),
        jax.ShapeDtypeStruct((1, WIDTH), F32),
        jax.ShapeDtypeStruct((1, 4 * HEAD), F32),
    )
    return pl.pallas_call(
        unproject_kernel,
        out_shape=outs,
        grid=(1,),
        in_specs=[at_half(4, ROWS, 4 * HEAD)]
        + [at_half(4, ROWS, 2 * HEAD)] * 6
        + [at_half(2, PAIR, 4 * HEAD)]
        + [ROWS_OF] * 4
        + [all_of(WIDTH, 6 * HEAD), table, table, all_of(1, 4 * HEAD)],
        out_specs=tuple(all_of(*o.shape) for o in outs),
        compiler_params=params(1, 20),
        cost_estimate=cost(4 * PAIR * WIDTH * 384, 8e6),
    )(gq, *gkvs, raw, *xs, w, cos, sin, head_gain)


def ffn_kernel(
    x0_ref, x1_ref, c0_ref, c1_ref, gu_w_ref, d_w_ref,
    part0_ref, part1_ref, out0_ref, out1_ref, act_ref, gu_ref, total, out_total,
):
    y = pl.program_id(0)
    x = stacked(x0_ref, x1_ref)
    gate_up = dot(x, gu_w_ref[0])
    gate, up = gate_up[:, :PADDED], gate_up[:, PADDED:]
    grad_act = dot(stacked(c0_ref, c1_ref), d_w_ref[0])
    own = lax.broadcasted_iota(jnp.int32, (PAIR, PADDED), 1) < PART
    sig = 1.0 / (1.0 + jnp.exp(-gate))
    silu = gate * sig
    act = jnp.where(own, silu * up, 0.0).astype(BF16)
    act_ref[0] = act
    out_part = dot(act, d_w_ref[0], NT)
    grad_act = jnp.where(own, grad_act, 0.0)
    grad_gate = jnp.where(own, grad_act * up * sig * (1.0 + gate * (1.0 - sig)), 0.0)
    grads = jnp.concatenate([grad_gate, jnp.where(own, grad_act * silu, 0.0)], axis=1).astype(BF16)
    gu_ref[0] = grads
    part = dot(grads, gu_w_ref[0], NT)

    @pl.when(y == 0)
    def _():
        total[...] = part
        out_total[...] = out_part

    @pl.when(y == 1)
    def _():
        whole_part = (total[...] + part).astype(BF16)
        part0_ref[...] = whole_part[:ROWS]
        part1_ref[...] = whole_part[ROWS:]
        whole_part = (out_total[...] + out_part).astype(BF16)
        out0_ref[...] = whole_part[:ROWS]
        out1_ref[...] = whole_part[ROWS:]


def ffn(x0, x1, c0, c1, w):
    rows = ROWS_OF
    return pl.pallas_call(
        ffn_kernel,
        out_shape=(jax.ShapeDtypeStruct((ROWS, WIDTH), BF16),) * 4
        + (
            jax.ShapeDtypeStruct((2, PAIR, PADDED), BF16),
            jax.ShapeDtypeStruct((2, PAIR, 2 * PADDED), BF16),
        ),
        grid=(2,),
        in_specs=[rows] * 4
        + [pl.BlockSpec((1, WIDTH, n * PADDED), lambda y, c=c: (y, 0, c)) for n, c in ((2, 0), (1, 2))],
        out_specs=(rows,) * 4
        + (
            pl.BlockSpec((1, PAIR, PADDED), lambda y: (y, 0, 0)),
            pl.BlockSpec((1, PAIR, 2 * PADDED), lambda y: (y, 0, 0)),
        ),
        scratch_shapes=[pltpu.VMEM((PAIR, WIDTH), F32)] * 2,
        compiler_params=params(1, 32),
        cost_estimate=cost(2 * 2 * PAIR * WIDTH * 6 * PADDED, 14e6),
    )(x0, x1, c0, c1, w, w)


def ffn_weights_kernel(*refs):
    xs, cs, gus, acts, out_ref = refs[:8], refs[8:16], refs[16:20], refs[20:24], refs[24]
    def all_tokens(refs):
        return jnp.concatenate([ref[...] for ref in refs], axis=0)

    grad_gu = dot(all_tokens(xs), all_tokens([g.at[0] for g in gus]), TN)
    grad_d = dot(all_tokens(cs), all_tokens([a.at[0] for a in acts]), TN)
    out_ref[0, :, :PART] = grad_gu[:, :PART].astype(BF16)
    out_ref[0, :, PART : 2 * PART] = grad_gu[:, PADDED : PADDED + PART].astype(BF16)
    out_ref[0, :, 2 * PART :] = grad_d[:, :PART].astype(BF16)


def ffn_weights(xs, cs, gus, acts):
    tall = 256
    rows = pl.BlockSpec((ROWS, tall), lambda y, m: (0, m))
    return pl.pallas_call(
        ffn_weights_kernel,
        out_shape=jax.ShapeDtypeStruct((2, WIDTH, 3 * PART), BF16),
        grid=(2, WIDTH // tall),
        in_specs=[rows] * 16
        + [pl.BlockSpec((1, PAIR, 2 * PADDED), lambda y, m: (y, 0, 0))] * 4
        + [pl.BlockSpec((1, PAIR, PADDED), lambda y, m: (y, 0, 0))] * 4,
        out_specs=pl.BlockSpec((1, tall, 3 * PART), lambda y, m: (y, m, 0)),
        compiler_params=params(2, 28),
        cost_estimate=cost(2 * 2 * 1024 * WIDTH * 3 * PADDED, 24e6),
    )(*xs, *cs, *gus, *acts)


def out_project_kernel(mix_ref, w_ref, part0_ref, part1_ref):
    part = dot(mix_ref[...].reshape(PAIR, QUERY), w_ref[...], NT).astype(BF16)
    part0_ref[...] = part[:ROWS]
    part1_ref[...] = part[ROWS:]


def out_project(d, mix, w):
    rows = pl.BlockSpec((ROWS, WIDTH), lambda i: (0, 0))
    return pl.pallas_call(
        out_project_kernel,
        out_shape=(jax.ShapeDtypeStruct((ROWS, WIDTH), BF16),) * 2,
        grid=(1,),
        in_specs=[
            pl.BlockSpec((2, ROWS, QUERY), lambda i: (d, 0, 0)),
            pl.BlockSpec((WIDTH, QUERY), lambda i: (0, 0)),
        ],
        out_specs=(rows, rows),
        compiler_params=params(1, 16),
        cost_estimate=cost(2 * PAIR * WIDTH * QUERY, 2e6),
    )(mix, w)


def out_back_kernel(w_ref, *refs):
    for t in range(8):
        refs[8][t] = dot(refs[t][...], w_ref[...]).astype(BF16)


def out_back(branches, w):
    return pl.pallas_call(
        out_back_kernel,
        out_shape=jax.ShapeDtypeStruct((8, ROWS, QUERY), BF16),
        compiler_params=params(0, 16),
        cost_estimate=cost(8 * PAIR * WIDTH * QUERY, 4e6),
    )(w, *branches)


def out_weights_kernel(mix_ref, *refs):
    branch = jnp.concatenate([b[...] for b in refs[:8]], axis=0)
    refs[8][...] = dot(branch, mix_ref[...].reshape(8 * ROWS, QUERY), TN)


def out_weights(mix, branches):
    return pl.pallas_call(
        out_weights_kernel,
        out_shape=jax.ShapeDtypeStruct((WIDTH, QUERY), F32),
        compiler_params=params(0, 24),
        cost_estimate=cost(2 * 1024 * WIDTH * QUERY, 4e6),
    )(mix, *branches)


def pack_kernel(normed_ref, graw0_ref, graw1_ref, gains_ref, out_grad_ref, sent_ref):
    graw = jnp.concatenate([graw0_ref[...], graw1_ref[...]], axis=0)
    grad = dot(normed_ref[...], graw, TN)
    gains = gains_ref[...]
    high = gains.astype(BF16).astype(F32)
    gains = jnp.concatenate([high, gains - high, jnp.zeros((HEAD - 32, gains.shape[1]), F32)], axis=0)
    sent_ref[:, : 5 * HEAD] = grad[:, : 5 * HEAD].astype(BF16)
    sent_ref[:, 5 * HEAD : 6 * HEAD] = gains.T.astype(BF16)
    sent_ref[:, 6 * HEAD :] = out_grad_ref[...].astype(BF16)


def pack(normed, graws, gains, out_grad):
    tall = 256
    return pl.pallas_call(
        pack_kernel,
        out_shape=jax.ShapeDtypeStruct((WIDTH, 9 * HEAD), BF16),
        grid=(WIDTH // tall,),
        in_specs=[
            pl.BlockSpec((8 * ROWS, tall), lambda m: (0, m)),
            all_of(4 * ROWS, 6 * HEAD),
            all_of(4 * ROWS, 6 * HEAD),
            pl.BlockSpec((16, tall), lambda m: (0, m)),
            pl.BlockSpec((tall, QUERY), lambda m: (m, 0)),
        ],
        out_specs=pl.BlockSpec((tall, 9 * HEAD), lambda m: (m, 0)),
        compiler_params=params(1, 24),
        cost_estimate=cost(2 * 1024 * WIDTH * 384, 8e6),
    )(normed, *graws, gains, out_grad)


def side_by_side(t):
    return jnp.concatenate([t[g * HEAD : (g + 1) * HEAD] for g in range(GROUP)], axis=1)


def on_top(t):
    return jnp.concatenate([t[:, g * ROWS : (g + 1) * ROWS] for g in range(GROUP)], axis=0)


def key_loops(plan, at, base, start, visit, state):
    f = pl.program_id(0)
    lo, m1, m2, hi = (plan[f, at + i] for i in range(4))
    place = lax.rem(lax.broadcasted_iota(jnp.int32, (1, LANES), 1), ROWS) + plan[f, 0]

    def masked(j, state):
        key = lax.broadcasted_iota(jnp.int32, (KEY_TILE, LANES), 0) + (j * KEY_TILE + base)
        return visit(j, state, (key >= start) & (key <= place))

    def several(i, state):
        for k in range(UNROLL):
            state = visit(m1 + UNROLL * i + k, state, None)
        return state

    steps = lax.div(m2 - m1, UNROLL)
    state = lax.fori_loop(lo, m1, masked, state)
    state = lax.fori_loop(0, steps, several, state)
    state = lax.fori_loop(m1 + UNROLL * steps, m2, lambda j, s: visit(j, s, None), state)
    return lax.fori_loop(m2, hi, masked, state)


def rows_of(j):
    return pl.ds(pl.multiple_of(j * KEY_TILE, KEY_TILE), KEY_TILE)


def chunks(plan, supers):
    for b in range(supers):
        for half in (0, 1):
            for f in range(8):
                side = plan[0, 10] if half == 0 else 1 - plan[0, 10]
                yield b, half, pl.multiple_of(b * SUPER + f * PAIR + side * ROWS, ROWS), plan[f, 1]


def line_up(plan, kv_refs, kv, kvt):
    @pl.when(pl.program_id(0) == 0)
    def _():
        for b, half, place, sent in chunks(plan, len(kv_refs) // 2):
            block = kv_refs[2 * b + half][sent]
            kv[pl.ds(place, ROWS), :] = block
            kvt[:, pl.ds(place, ROWS)] = block.astype(F32).T.astype(BF16)


def attend_body(at, base, plan, q_ref, start_ref, kv, kvt, state):
    qt = side_by_side(q_ref[0].astype(F32).T)
    qt = jnp.concatenate([jnp.zeros_like(qt), qt], axis=0).astype(BF16)

    def visit(j, state, mask):
        total, accum = state
        weights = jnp.exp2(dot(kv[rows_of(j), :], qt) * SCORE)
        if mask is not None:
            weights = jnp.where(mask, weights, 0.0)
        total = total + jnp.sum(weights, axis=0, keepdims=True)
        return total, accum + dot(kvt[:HEAD, rows_of(j)], weights.astype(BF16))

    return key_loops(plan, at, base, start_ref[0], visit, state)


def attend_own_kernel(plan, q_ref, start_ref, *refs):
    kv_refs, (accum_ref, total_ref, kv, kvt) = refs[:2], refs[2:]
    line_up(plan, kv_refs, kv, kvt)
    state = (jnp.zeros((1, LANES), F32), jnp.zeros((HEAD, LANES), F32))
    total, accum = attend_body(6, EARLIER, plan, q_ref, start_ref, kv, kvt, state)
    accum_ref[0] = accum
    total_ref[0] = total


def attend_earlier_kernel(plan, q_ref, start_ref, *refs):
    kv_refs, (accum_ref, total_ref, mix_ref, out_ref, lse_ref, kv, kvt) = refs[:4], refs[4:]
    line_up(plan, kv_refs, kv, kvt)
    state = (total_ref[0], accum_ref[0])
    total, accum = attend_body(2, 0, plan, q_ref, start_ref, kv, kvt, state)
    out = accum / total
    out_ref[0] = out
    mix_ref[0] = on_top(out).T.astype(BF16)
    lse_ref[0] = jnp.log2(total)


def back_kernel(plan, q_ref, start_ref, *refs):
    kv_refs, (g_ref, out_ref, lse_ref, dq_ref), sent_refs, (kv, kvt, dkv) = (
        refs[:6], refs[6:10], refs[10:16], refs[16:],
    )
    line_up(plan, kv_refs, kv, kvt)

    @pl.when(pl.program_id(0) == 0)
    def _():
        dkv[...] = jnp.zeros_like(dkv)

    qt = side_by_side(q_ref[0].astype(F32).T)
    gt = side_by_side(g_ref[0].astype(F32).T)
    delta = jnp.sum(gt * out_ref[0], axis=0, keepdims=True)
    zero = jnp.zeros_like(qt)
    gt = jnp.concatenate([gt, zero], axis=0)
    qt = jnp.concatenate([zero, qt], axis=0)
    both_t = jnp.concatenate([gt, qt], axis=1).astype(BF16)
    both = jnp.concatenate([gt.T, qt.T], axis=0).astype(BF16)
    lse = lse_ref[0]

    def visit(j, dqt, mask):
        pair = dot(kv[rows_of(j), :], both_t)
        weights = jnp.exp2(pair[:, LANES:] * SCORE - lse)
        if mask is not None:
            weights = jnp.where(mask, weights, 0.0)
        grads = (weights * (pair[:, :LANES] - delta)).astype(BF16)
        sides = jnp.concatenate([weights.astype(BF16), grads], axis=1)
        dkv[rows_of(j), :] += dot(sides, both)
        return dqt + dot(kvt[HEAD:, rows_of(j)], grads)

    dqt = key_loops(plan, 11, 0, start_ref[0], visit, jnp.zeros((HEAD, LANES), F32))
    dq = on_top(dqt * HEAD**-0.5).T
    dq_ref[0] = jnp.concatenate([dq, jnp.zeros((ROWS, HEAD), F32)], axis=1).astype(BF16)

    @pl.when(pl.program_id(0) == 7)
    def _():
        for b, half, place, sent in chunks(plan, 3):
            sent_refs[2 * b + half][sent] = dkv[pl.ds(place, ROWS), :].astype(BF16)


def whole(*shape):
    return pl.BlockSpec(shape, lambda f, plan: (0,) * len(shape))


def tile(*shape):
    return pl.BlockSpec((1,) + shape, lambda f, plan: (f,) + (0,) * len(shape))


def placed(*shape):
    return pl.BlockSpec((1,) + shape, lambda f, plan: (plan[f, 1],) + (0,) * len(shape))


def tiles_call(kernel, supers, outs, more_ins, out_specs, flops, back):
    keys = supers * SUPER
    scratch = [pltpu.VMEM((keys, 2 * HEAD), BF16), pltpu.VMEM((2 * HEAD, keys), BF16)]
    if back:
        scratch.append(pltpu.VMEM((keys, 2 * HEAD), F32))
    ins = [placed(ROWS, QUERY), tile(1, LANES)] + [whole(8, ROWS, 2 * HEAD)] * (2 * supers)
    return pl.pallas_call(
        kernel,
        out_shape=outs,
        grid_spec=pltpu.PrefetchScalarGridSpec(
            num_scalar_prefetch=1,
            grid=(8,),
            in_specs=ins + more_ins,
            out_specs=out_specs,
            scratch_shapes=scratch,
        ),
        compiler_params=params(1, 20),
        cost_estimate=cost(flops, 8e6, 1e7),
    )


TILE_T = jax.ShapeDtypeStruct((8, HEAD, LANES), F32)
TILE_ROW = jax.ShapeDtypeStruct((8, 1, LANES), F32)
STATE = [tile(HEAD, LANES), tile(1, LANES)]


def attend_own(plan, q, start, kvs):
    call = tiles_call(attend_own_kernel, 1, (TILE_T, TILE_ROW), [], tuple(STATE), 4e9, False)
    return call(plan, q, start, *kvs)


def attend_earlier(plan, q, start, kvs, state):
    outs = (jax.ShapeDtypeStruct((8, ROWS, QUERY), BF16), TILE_T, TILE_ROW)
    specs = (placed(ROWS, QUERY),) + tuple(STATE)
    call = tiles_call(attend_earlier_kernel, 2, outs, STATE, specs, 8e9, False)
    return call(plan, q, start, *kvs, *state)


def back(plan, q, start, kvs, grad, out, lse):
    sent = jax.ShapeDtypeStruct((8, ROWS, 2 * HEAD), BF16)
    call = tiles_call(
        back_kernel,
        3,
        [jax.ShapeDtypeStruct((8, ROWS, 4 * HEAD), BF16)] + [sent] * 6,
        [placed(ROWS, QUERY)] + STATE,
        [placed(ROWS, 4 * HEAD)] + [whole(*sent.shape)] * 6,
        30e9,
        True,
    )
    return call(plan, q, start, *kvs, grad, out, lse)


def after(v, *others):
    return lax.optimization_barrier((v,) + others)[0]


def per_device(
    tokens,
    segments,
    attn_gain,
    w_query,
    w_key,
    w_value,
    q_gain,
    k_gain,
    w_out,
    ffn_gain,
    w_gate,
    w_up,
    w_down,
    cotangent,
):
    ylo, z, x, core, yhi = (lax.axis_index(a) for a in ALL)
    sup = ylo * 4 + z

    token_shifts = [shift_x(tokens, d) for d in (1, 2, 3)]
    token_blocks = [[b, swap(b, "core")] for b in [tokens] + token_shifts]
    all_tokens = [b for p in token_blocks for b in p]
    qkv_own = jnp.concatenate(
        [
            w_query.reshape(12, 8, QUERY),
            w_key.reshape(12, 8, HEAD),
            w_value.reshape(12, 8, HEAD),
            jnp.broadcast_to(attn_gain[:, None, None], (12, 8, 1)),
            jnp.broadcast_to(ffn_gain[:, None, None], (12, 8, 1)),
            jnp.zeros((12, 8, HEAD - 2), BF16),
        ],
        axis=-1,
    )
    qkv_own = jnp.pad(jnp.transpose(qkv_own, (1, 0, 2)), ((0, 0), (0, 12), (0, 0)))
    out_own = jnp.transpose(w_out.reshape(4, QUERY, 24), (0, 2, 1))
    out_own = jnp.pad(jnp.concatenate([out_own, out_own], axis=0), ((0, 0), (0, 0), (0, 3 * FREE - QUERY)))
    rows_own = jnp.concatenate(
        [
            part
            for i, w in enumerate((w_gate, w_up, w_down.T))
            for part in (
                w.reshape(24, 8, PART).transpose(1, 0, 2),
                out_own[:, :, i * FREE : (i + 1) * FREE],
            )
        ]
        + [qkv_own],
        axis=-1,
    )
    rows = exchange(rows_own, NEAR)
    ffn_rows = rows[:, :, : 3 * PADDED].reshape(192, 3 * PADDED)
    qkv_rows = rows[:, :12, 3 * PADDED :].reshape(1, 96, 6 * HEAD)
    qkv = exchange(jnp.broadcast_to(qkv_rows, (16, 96, 6 * HEAD)), WIDE)
    qkv = jnp.transpose(qkv.reshape(2, 8, 8, 12, 6 * HEAD), (1, 2, 0, 3, 4)).reshape(WIDTH, 6 * HEAD)
    ffn_full = lax.all_gather(ffn_rows, WIDE, axis=0, tiled=True).reshape(2, WIDTH, 3 * PADDED)
    gain_attn = qkv[:, 5 * HEAD].astype(F32)
    gain_ffn = qkv[:, 5 * HEAD + 1].astype(F32)

    token_index = jnp.arange(segments.shape[0], dtype=jnp.int32)
    begins = jnp.concatenate([jnp.ones((1,), jnp.bool_), segments[1:] != segments[:-1]])
    starts = lax.cummax(jnp.where(begins, token_index, 0), axis=0)
    own_starts = lax.dynamic_slice(
        starts.reshape(8, 8, 2, ROWS), (sup, 0, yhi, 0), (1, 8, 1, ROWS)
    ).reshape(8, ROWS)
    first = sup * SUPER + jnp.arange(8, dtype=jnp.int32) * PAIR + yhi * ROWS
    own_places = first[:, None] + jnp.arange(ROWS, dtype=jnp.int32)[None]
    positions = abs_to_rel((own_places - own_starts).reshape(4, 2, ROWS), x, core)
    frequency = THETA ** (-jnp.arange(HEAD // 2, dtype=F32) * 2.0 / HEAD)
    angles = positions.reshape(4, PAIR, 1).astype(F32) * frequency
    cosine, sine = jnp.cos(angles), jnp.sin(angles)
    cos = jnp.concatenate([cosine] * 4, axis=-1)
    sin = jnp.concatenate([-sine, sine] * 2, axis=-1)
    head_gain = jnp.concatenate([q_gain, q_gain, q_gain, k_gain]).astype(F32)[None]

    window = (sup - 2) * SUPER
    lo = (own_starts[:, 0] - window) // KEY_TILE
    hi = (first + ROWS - 1 - window) // KEY_TILE + 1
    m1 = jnp.clip((own_starts[:, -1] - window + KEY_TILE - 1) // KEY_TILE, lo, hi)
    m2 = jnp.clip((first + 1 - window) // KEY_TILE, m1, hi)
    order = jnp.arange(8, dtype=jnp.int32)
    relative = ((order // 2 - x) % 4) * 2 + (order % 2 + core) % 2
    edge = EARLIER // KEY_TILE
    plan = jnp.stack(
        [first - window, relative]
        + [jnp.minimum(v, edge) for v in (lo, m1, m2, hi)]
        + [jnp.maximum(v - edge, 0) for v in (lo, m1, m2, hi)]
        + [jnp.broadcast_to(yhi, (8,)), lo, m1, m2, hi],
        axis=1,
    ).astype(jnp.int32)
    start_lanes = jnp.tile(own_starts - window, (1, GROUP)).reshape(8, 1, LANES)

    normed, rot_q, kv, raw = project(
        all_tokens, qkv, gain_attn[None], cos, sin, head_gain
    )

    kv_own = [kv, swap(kv, "yhi")]
    kv_sent = after(kv, kv_own[1])
    kv_earlier = [shift_super(kv_sent, a, b) for a, b in ((2, 0), (2, 1), (1, 0), (1, 1))]
    state = attend_own(plan, rot_q, start_lanes, kv_own)
    state, kv_earlier, cot_sent = lax.optimization_barrier((state, kv_earlier, cotangent))
    cot_shifts = [shift_x(cot_sent, d) for d in (1, 2, 3)]
    mix, out_tiles, lse = attend_earlier(plan, rot_q, start_lanes, kv_earlier, state)
    mix, cot_shifts = lax.optimization_barrier((mix, cot_shifts))
    out_half = lax.dynamic_index_in_dim(ffn_full, x // 2, 0, keepdims=False)
    w_out_t = jnp.concatenate(
        [out_half[:, i * PADDED + PART : (i + 1) * PADDED] for i in range(3)], axis=1
    )[:, :QUERY]
    w_out_t, mix = lax.optimization_barrier((w_out_t, mix))
    cot_blocks = [[b, swap(b, "core")] for b in [cotangent] + cot_shifts]
    all_cot = [b for p in cot_blocks for b in p]

    inputs = tokens.astype(F32)
    parts = [None] * 4
    for d in (2, 1, 3, 0):
        parts[d] = out_project(d, mix, w_out_t)
    hidden = inputs + near_sum(near_keep(parts))
    scale_ffn = rms_scale(hidden)
    scaled_ffn = hidden * scale_ffn
    normed_ffn = (scaled_ffn * gain_ffn).astype(BF16)

    ffn_blocks = [[b] for b in [normed_ffn] + [shift_x(normed_ffn, d) for d in (1, 2, 3)]]
    ffn_blocks[0].append(swap(normed_ffn, "core"))
    ffn_outs = [None] * 4
    before = {1: 0, 3: 0, 2: 1}
    for d in (0, 1, 3, 2):
        if d > 0:
            block = after(ffn_blocks[d][0], ffn_outs[before[d]][0])
            ffn_blocks[d] = [block, swap(block, "core")]
        blocks = ffn_blocks[d]
        if d == 3:
            blocks = after(blocks, ffn_outs[1][0])
        if d == 2:
            blocks = after(blocks, ffn_outs[3][0])
        ffn_outs[d] = ffn(*blocks, *cot_blocks[d], ffn_full)
    acts, gus = [o[4] for o in ffn_outs], [o[5] for o in ffn_outs]
    kept, gus, out_own, out_other = lax.optimization_barrier(
        (near_keep([o[:2] for o in ffn_outs]), gus, [o[2] for o in ffn_outs], [o[3] for o in ffn_outs])
    )
    out_kept = jnp.stack(out_own).astype(F32) + swap(jnp.stack(out_other), "core").astype(F32)
    out_kept = out_kept.astype(BF16)
    pair_total = near_sum(kept)
    weight_grads = ffn_weights([b for p in ffn_blocks for b in p], all_cot, gus, acts)
    pair_total, weight_grads, out_kept = lax.optimization_barrier((pair_total, weight_grads, out_kept))
    ffn_sum = lax.psum_scatter(
        weight_grads.reshape(2 * WIDTH, 3 * PART), WIDE, scatter_dimension=0, tiled=True
    )
    ffn_gain_part = jnp.sum(pair_total * scaled_ffn, axis=0)
    grad_hidden = cotangent.astype(F32) + rms_back(pair_total * gain_ffn, hidden, scale_ffn)
    grad_branch = grad_hidden.astype(BF16)
    branches = [b for p in near_gather(grad_branch) for b in p]
    grad_mix = out_back(branches, w_out_t)
    out_total = near_sum(after([out_kept[d] for d in range(4)], branches))

    back_outs = back(plan, rot_q, start_lanes, kv_earlier + kv_own, grad_mix, out_tiles, lse)
    back_outs, out_total = lax.optimization_barrier((back_outs, out_total))
    grad_q, two_mine, two_theirs, one_mine, one_theirs, mine, theirs = back_outs
    grad_kvs = [
        mine,
        swap(theirs, "yhi"),
        shift_super(one_mine, -1, 0),
        shift_super(one_theirs, -1, 1),
        shift_super(two_mine, -2, 0),
        shift_super(two_theirs, -2, 1),
    ]

    grad_out = out_weights(after(mix, grad_q), branches)
    grad_kvs, grad_out = lax.optimization_barrier((grad_kvs, grad_out))

    unprojected = [None] * 2
    for half in (1, 0):
        xs = all_tokens[4 * half : 4 * half + 4]
        unprojected[half] = unproject(half, grad_q, grad_kvs, raw, xs, qkv, cos, sin, head_gain)
    head_part = sum(u[6] for u in unprojected)[0]
    q_gain_part = head_part[:HEAD] + head_part[HEAD : 2 * HEAD] + head_part[2 * HEAD : QUERY]
    head_part = jnp.concatenate([q_gain_part, head_part[QUERY:], jnp.zeros((4,), F32)])
    gain_parts = jnp.concatenate(
        [
            sum(u[5] for u in unprojected),
            ffn_gain_part[None],
            jnp.tile(head_part.reshape(12, 11).T, (1, 128)),
            jnp.zeros((3, WIDTH), F32),
        ],
        axis=0,
    )
    sent = pack(normed, [u[4] for u in unprojected], gain_parts, grad_out)
    parts = [u[2 * i : 2 * i + 2] for u in unprojected for i in (0, 1)]
    parts, sent = lax.optimization_barrier((parts, sent))
    grad_normed = near_sum(near_keep(parts))
    got = exchange(sent.reshape(8, 192, 9 * HEAD), ("ylo", "z"))
    got = jnp.sum(got.astype(F32), axis=0).astype(BF16)
    last = jnp.concatenate(
        [ffn_sum.reshape(8, 24, 3 * PART), got.reshape(8, 24, 9 * HEAD)], axis=-1
    )
    last = exchange(last, NEAR)
    ffn_grad, got = last[:, :, : 3 * PART], last[:, :, 3 * PART :].astype(F32)

    qkv_grad, grad_out = got[:, :, : 6 * HEAD], got[:, :, 6 * HEAD :]
    here, there = jnp.where(yhi == 0, 0, 1), jnp.where(yhi == 0, 1, 0)

    def half_of(v, axis, which):
        size = v.shape[axis] // 2
        return lax.dynamic_slice_in_dim(v, which * size, size, axis)

    qkv_other = swap(half_of(qkv_grad, 1, there).astype(BF16), "yhi").astype(F32)
    out_other = swap(half_of(grad_out, 0, there).astype(BF16), "yhi").astype(F32)
    qkv_grad = half_of(qkv_grad, 1, here) + qkv_other
    grad_out = half_of(grad_out, 0, here) + out_other
    gains = jnp.sum(qkv_grad[:, :, 5 * HEAD :], axis=0)
    gains = gains[:, :16] + gains[:, 16:32]
    head_gains = gains[:, 2:13].reshape(-1)
    qkv_grad = jnp.transpose(qkv_grad, (1, 0, 2))
    w_out_grad = jnp.transpose(grad_out, (0, 2, 1)).reshape(768, 24)
    w_query_grad = qkv_grad[:, :, :QUERY].reshape(12, -1)
    w_key_grad = qkv_grad[:, :, QUERY : QUERY + HEAD].reshape(12, -1)
    w_value_grad = qkv_grad[:, :, QUERY + HEAD : QUERY + 2 * HEAD].reshape(12, -1)

    output = (hidden + out_total).astype(BF16)
    scale_attn = rms_scale(inputs)
    input_grad = (grad_hidden + rms_back(grad_normed * gain_attn, inputs, scale_attn)).astype(BF16)

    ffn_grad = jnp.transpose(ffn_grad, (1, 0, 2)).astype(F32)
    w_gate_grad, w_up_grad, w_down_grad = (
        ffn_grad[:, :, i * PART : (i + 1) * PART].reshape(24, -1) for i in range(3)
    )
    return (
        output,
        input_grad,
        gains[:, 0],
        w_query_grad,
        w_key_grad,
        w_value_grad,
        head_gains[:HEAD],
        head_gains[HEAD : 2 * HEAD],
        w_out_grad,
        gains[:, 1],
        w_gate_grad,
        w_up_grad,
        w_down_grad.T,
    )


def solution(mesh):
    mesh = Mesh(np.asarray(mesh.devices).reshape(2, 4, 4, 2, 2), ALL)
    rows = P(ALL, None)
    weights = (P("yhi", BLK), P(ALL), P(BLK, "yhi"), P(BLK, "yhi"), P("yhi", BLK))
    placed_in = (rows, P(), P(ALL), rows, rows, rows, P(), P()) + weights + (rows,)
    placed_out = (rows, rows, P(ALL), rows, rows, rows, P(), P()) + weights
    return jax.shard_map(
        per_device, mesh=mesh, in_specs=placed_in, out_specs=placed_out, check_vma=False
    )
```

```python
import functools

import jax
import jax.numpy as jnp
import numpy as np
from jax import lax
from jax.experimental import pallas as pl
from jax.experimental.pallas import tpu as pltpu
from jax.sharding import Mesh
from jax.sharding import PartitionSpec as P

EPS = 1e-05
THETA = 1000000.0
HEAD = 64
ROWS = 128
PAIR = 2 * ROWS
GROUP = 3
QUERY = GROUP * HEAD
LANES = PAIR * GROUP
KEY_TILE = 512
SUPER = 2048
EARLIER = 2 * SUPER
PART = 432
PADDED = 512
FREE = PADDED - PART
WIDTH = 1536
ALL = ("ylo", "z", "x", "core", "yhi")
BLK = ("ylo", "z", "x", "core")
WIDE = ("yhi", "ylo", "z")
NEAR = ("x", "core")
NN = (((1,), (0,)), ((), ()))
NT = (((1,), (1,)), ((), ()))
TN = (((0,), (0,)), ((), ()))
F32 = jnp.float32
BF16 = jnp.bfloat16
SCORE = HEAD**-0.5 * 1.4426950408889634


def dot(a, b, numbers=NN):
    return lax.dot_general(a, b, numbers, preferred_element_type=F32)


def rms_scale(v):
    return lax.rsqrt(jnp.mean(v * v, axis=-1, keepdims=True) + EPS)


def rms_back(grad, v, scale):
    inner = jnp.mean(grad * v, axis=-1, keepdims=True)
    return scale * (grad - v * scale * scale * inner)


def shift_x(v, distance):
    return lax.ppermute(v, "x", [((i + distance) % 4, i) for i in range(4)])


def swap(v, axis):
    return lax.ppermute(v, axis, [(0, 1), (1, 0)])


def shift_super(v, distance, other):
    pairs = [
        (2 * i + h, 2 * (i + distance) + (h + other) % 2)
        for i in range(8)
        for h in (0, 1)
        if 0 <= i + distance < 8
    ]
    return lax.ppermute(v, ("ylo", "z", "yhi"), pairs)


def exchange(v, axes):
    return lax.all_to_all(v, axes, split_axis=0, concat_axis=0, tiled=True)


def near_gather(v):
    blocks = [v] + [shift_x(v, d) for d in (1, 2, 3)]
    return [[b, swap(b, "core")] for b in blocks]


def near_keep(parts):
    return [
        (own.astype(F32) + swap(other, "core").astype(F32)).astype(BF16) for own, other in parts
    ]


def near_sum(kept):
    total = kept[0].astype(F32)
    for d in (1, 2, 3):
        total = total + shift_x(kept[d], -d).astype(F32)
    return total


def rel_to_abs(v, x, core):
    v = jnp.where(core == 0, v, v[:, ::-1])
    return lax.dynamic_slice_in_dim(jnp.concatenate([v, v], axis=0), (4 - x) % 4, 4, 0)


def abs_to_rel(v, x, core):
    v = jnp.where(core == 0, v, v[:, ::-1])
    return lax.dynamic_slice_in_dim(jnp.concatenate([v, v], axis=0), x, 4, 0)


def params(steps, mib):
    return pltpu.CompilerParams(
        dimension_semantics=("arbitrary",) * steps, vmem_limit_bytes=mib * 2**20
    )


def cost(flops, moved, exps=0):
    return pl.CostEstimate(flops=int(flops), bytes_accessed=int(moved), transcendentals=int(exps))


def all_of(*shape):
    return pl.BlockSpec(shape, lambda *i: (0,) * len(shape))


ROWS_OF = pl.BlockSpec((ROWS, WIDTH), lambda *i: (0, 0))


def stacked(a_ref, b_ref):
    return jnp.concatenate([a_ref[...], b_ref[...]], axis=0)


def head_sums(v):
    shape = (v.shape[1], v.shape[1])
    lane = lax.shift_right_logical(lax.broadcasted_iota(jnp.int32, shape, 1), 6)
    row = lax.shift_right_logical(lax.broadcasted_iota(jnp.int32, shape, 0), 6)
    ones = jnp.where(lane == row, 1.0, 0.0).astype(BF16)
    high = v.astype(BF16)
    low = (v - high.astype(F32)).astype(BF16)
    return dot(high, ones) + dot(low, ones)


def half_turn(v):
    lane = lax.broadcasted_iota(jnp.int32, v.shape, 1)
    return jnp.where(
        (lane & (HEAD - 1)) < HEAD // 2,
        pltpu.roll(v, v.shape[1] - HEAD // 2, 1),
        pltpu.roll(v, HEAD // 2, 1),
    )


def twice(v):
    return jnp.concatenate([v, v], axis=1)


def project_kernel(*refs):
    xs, (w_ref, gain_ref, cos_ref, sin_ref, head_gain_ref) = refs[:8], refs[8:13]
    normed_ref, q_ref, kv_ref, raw_ref = refs[13:]
    lane = lax.broadcasted_iota(jnp.int32, (PAIR, 2 * HEAD), 1)
    for d in range(4):
        rows = slice(d * PAIR, (d + 1) * PAIR)
        tiles = slice(2 * d, 2 * d + 2)
        x = stacked(*xs[tiles]).astype(F32)
        normed = (x * rms_scale(x) * gain_ref[...]).astype(BF16)
        normed_ref[rows, :] = normed
        raw = dot(normed, w_ref[...])
        heads = raw[:, : 4 * HEAD]
        raw_ref[d] = heads
        scale = lax.rsqrt(head_sums(heads * heads) * (1.0 / HEAD) + EPS)
        v = heads * scale * head_gain_ref[...]
        turned = v * twice(cos_ref[d]) + half_turn(v) * twice(sin_ref[d])
        q_ref[tiles] = turned[:, :QUERY].astype(BF16).reshape(2, ROWS, QUERY)
        kv = jnp.where(lane < HEAD, raw[:, 4 * HEAD :], turned[:, 2 * HEAD :])
        kv_ref[tiles] = kv.astype(BF16).reshape(2, ROWS, 2 * HEAD)


def project(xs, w, gain, cos, sin, head_gain):
    return pl.pallas_call(
        project_kernel,
        out_shape=(
            jax.ShapeDtypeStruct((4 * PAIR, WIDTH), BF16),
            jax.ShapeDtypeStruct((8, ROWS, QUERY), BF16),
            jax.ShapeDtypeStruct((8, ROWS, 2 * HEAD), BF16),
            jax.ShapeDtypeStruct((4, PAIR, 4 * HEAD), F32),
        ),
        grid=(1,),
        in_specs=[ROWS_OF] * 8
        + [all_of(WIDTH, 384), all_of(1, WIDTH)]
        + [all_of(4, PAIR, 2 * HEAD)] * 2
        + [all_of(1, 4 * HEAD)],
        out_specs=(
            all_of(4 * PAIR, WIDTH),
            all_of(8, ROWS, QUERY),
            all_of(8, ROWS, 2 * HEAD),
            all_of(4, PAIR, 4 * HEAD),
        ),
        compiler_params=params(1, 40),
        cost_estimate=cost(8 * PAIR * WIDTH * 384, 1e7),
    )(*xs, w, gain, cos, sin, head_gain)


def turned_back(g, raw, cos, sin, head_gain):
    width = g.shape[1]
    g = g * cos - half_turn(g) * sin
    scale = lax.rsqrt(head_sums(raw * raw) * (1.0 / HEAD) + EPS)
    gain = jnp.sum(g * raw * scale, axis=0, keepdims=True)
    e = g * head_gain[:, -width:]
    inner = head_sums(e * raw) * (1.0 / HEAD)
    return scale * (e - raw * scale * scale * inner), gain


def unproject_q_kernel(gq_ref, raw_ref, cos_ref, sin_ref, head_gain_ref, graw_ref, gain_ref):
    gains = 0.0
    for d in range(4):
        g = gq_ref[2 * d : 2 * d + 2].reshape(PAIR, 4 * HEAD).astype(F32)
        graw, gain = turned_back(
            g, raw_ref[d], twice(cos_ref[d]), twice(sin_ref[d]), head_gain_ref[...]
        )
        graw_ref[d] = graw.astype(BF16)
        gains = gains + gain
    gain_ref[...] = gains


def unproject_q(gq, raw, cos, sin, head_gain):
    return pl.pallas_call(
        unproject_q_kernel,
        out_shape=(
            jax.ShapeDtypeStruct((4, PAIR, 4 * HEAD), BF16),
            jax.ShapeDtypeStruct((1, 4 * HEAD), F32),
        ),
        compiler_params=params(0, 20),
        cost_estimate=cost(1e8, 4e6),
    )(gq, raw, cos, sin, head_gain)


def unproject_kernel(*refs):
    graw_q_ref, g_refs, raw_ref, xs, (w_ref, cos_ref, sin_ref, head_gain_ref) = (
        refs[0], refs[1:7], refs[7], refs[8:12], refs[12:16],
    )
    parts, (gkv_ref, attn_ref, gain_ref) = refs[16:20], refs[20:]
    attn, gains = 0.0, 0.0
    lane = lax.broadcasted_iota(jnp.int32, (PAIR, 2 * HEAD), 1)
    for i in range(2):
        tiles = slice(2 * i, 2 * i + 2)
        gkv = g_refs[0][tiles].astype(F32)
        for ref in g_refs[1:]:
            gkv = gkv + ref[tiles].astype(F32)
        gkv = gkv.reshape(PAIR, 2 * HEAD)
        gk = jnp.where(lane < HEAD, 0.0, (gkv * HEAD**-0.5).astype(BF16).astype(F32))
        graw_k, gain = turned_back(
            gk, raw_ref[i][:, 2 * HEAD :], cos_ref[i], sin_ref[i], head_gain_ref[...]
        )
        gains = gains + gain
        graw_q = graw_q_ref[i].astype(F32)
        graw = [
            graw_q[:, : 2 * HEAD],
            jnp.where(lane < HEAD, graw_q[:, 2 * HEAD :], graw_k),
            jnp.where(lane < HEAD, gkv, 0.0),
        ]
        gkv_ref[i * PAIR : (i + 1) * PAIR, :] = jnp.where(lane < HEAD, gkv, graw_k).astype(BF16)
        grad = dot(jnp.concatenate(graw, axis=1).astype(BF16), w_ref[...], NT)
        x = stacked(*xs[tiles]).astype(F32)
        attn = attn + jnp.sum(grad * x * rms_scale(x), axis=0, keepdims=True)
        grad = grad.astype(BF16)
        parts[2 * i][...] = grad[:ROWS]
        parts[2 * i + 1][...] = grad[ROWS:]
    attn_ref[...] = attn
    gain_ref[...] = gains


def unproject(half, graw_q, gkvs, raw, xs, w, cos, sin, head_gain):
    def at_half(*shape):
        return pl.BlockSpec(shape, lambda i: (half,) + (0,) * (len(shape) - 1))

    table = at_half(2, PAIR, 2 * HEAD)
    outs = (jax.ShapeDtypeStruct((ROWS, WIDTH), BF16),) * 4 + (
        jax.ShapeDtypeStruct((2 * PAIR, 2 * HEAD), BF16),
        jax.ShapeDtypeStruct((1, WIDTH), F32),
        jax.ShapeDtypeStruct((1, 2 * HEAD), F32),
    )
    return pl.pallas_call(
        unproject_kernel,
        out_shape=outs,
        grid=(1,),
        in_specs=[at_half(2, PAIR, 4 * HEAD)]
        + [at_half(4, ROWS, 2 * HEAD)] * 6
        + [at_half(2, PAIR, 4 * HEAD)]
        + [ROWS_OF] * 4
        + [all_of(WIDTH, 6 * HEAD), table, table, all_of(1, 4 * HEAD)],
        out_specs=tuple(all_of(*o.shape) for o in outs),
        compiler_params=params(1, 20),
        cost_estimate=cost(4 * PAIR * WIDTH * 384, 8e6),
    )(graw_q, *gkvs, raw, *xs, w, cos, sin, head_gain)


def ffn_kernel(
    x0_ref, x1_ref, c0_ref, c1_ref, gu_w_ref, d_w_ref,
    part0_ref, part1_ref, out0_ref, out1_ref, act_ref, gu_ref, total, out_total,
):
    y = pl.program_id(0)
    x = stacked(x0_ref, x1_ref)
    gate_up = dot(x, gu_w_ref[0])
    gate, up = gate_up[:, :PADDED], gate_up[:, PADDED:]
    grad_act = dot(stacked(c0_ref, c1_ref), d_w_ref[0])
    own = lax.broadcasted_iota(jnp.int32, (PAIR, PADDED), 1) < PART
    sig = 1.0 / (1.0 + jnp.exp(-gate))
    silu = gate * sig
    act = jnp.where(own, silu * up, 0.0).astype(BF16)
    act_ref[0] = act
    out_part = dot(act, d_w_ref[0], NT)
    grad_act = jnp.where(own, grad_act, 0.0)
    grad_gate = jnp.where(own, grad_act * up * sig * (1.0 + gate * (1.0 - sig)), 0.0)
    grads = jnp.concatenate([grad_gate, jnp.where(own, grad_act * silu, 0.0)], axis=1).astype(BF16)
    gu_ref[0] = grads
    part = dot(grads, gu_w_ref[0], NT)

    @pl.when(y == 0)
    def _():
        total[...] = part
        out_total[...] = out_part

    @pl.when(y == 1)
    def _():
        whole_part = (total[...] + part).astype(BF16)
        part0_ref[...] = whole_part[:ROWS]
        part1_ref[...] = whole_part[ROWS:]
        whole_part = (out_total[...] + out_part).astype(BF16)
        out0_ref[...] = whole_part[:ROWS]
        out1_ref[...] = whole_part[ROWS:]


def ffn(x0, x1, c0, c1, w):
    rows = ROWS_OF
    return pl.pallas_call(
        ffn_kernel,
        out_shape=(jax.ShapeDtypeStruct((ROWS, WIDTH), BF16),) * 4
        + (
            jax.ShapeDtypeStruct((2, PAIR, PADDED), BF16),
            jax.ShapeDtypeStruct((2, PAIR, 2 * PADDED), BF16),
        ),
        grid=(2,),
        in_specs=[rows] * 4
        + [pl.BlockSpec((1, WIDTH, n * PADDED), lambda y, c=c: (y, 0, c)) for n, c in ((2, 0), (1, 2))],
        out_specs=(rows,) * 4
        + (
            pl.BlockSpec((1, PAIR, PADDED), lambda y: (y, 0, 0)),
            pl.BlockSpec((1, PAIR, 2 * PADDED), lambda y: (y, 0, 0)),
        ),
        scratch_shapes=[pltpu.VMEM((PAIR, WIDTH), F32)] * 2,
        compiler_params=params(1, 32),
        cost_estimate=cost(2 * 2 * PAIR * WIDTH * 6 * PADDED, 14e6),
    )(x0, x1, c0, c1, w, w)


def ffn_weights_kernel(*refs):
    xs, cs, gus, acts, out_ref = refs[:8], refs[8:16], refs[16:20], refs[20:24], refs[24]
    def all_tokens(refs):
        return jnp.concatenate([ref[...] for ref in refs], axis=0)

    grad_gu = dot(all_tokens(xs), all_tokens([g.at[0] for g in gus]), TN)
    grad_d = dot(all_tokens(cs), all_tokens([a.at[0] for a in acts]), TN)
    out_ref[0, :, :PART] = grad_gu[:, :PART].astype(BF16)
    out_ref[0, :, PART : 2 * PART] = grad_gu[:, PADDED : PADDED + PART].astype(BF16)
    out_ref[0, :, 2 * PART :] = grad_d[:, :PART].astype(BF16)


def ffn_weights(xs, cs, gus, acts):
    tall = 256
    rows = pl.BlockSpec((ROWS, tall), lambda y, m: (0, m))
    return pl.pallas_call(
        ffn_weights_kernel,
        out_shape=jax.ShapeDtypeStruct((2, WIDTH, 3 * PART), BF16),
        grid=(2, WIDTH // tall),
        in_specs=[rows] * 16
        + [pl.BlockSpec((1, PAIR, 2 * PADDED), lambda y, m: (y, 0, 0))] * 4
        + [pl.BlockSpec((1, PAIR, PADDED), lambda y, m: (y, 0, 0))] * 4,
        out_specs=pl.BlockSpec((1, tall, 3 * PART), lambda y, m: (y, m, 0)),
        compiler_params=params(2, 28),
        cost_estimate=cost(2 * 2 * 1024 * WIDTH * 3 * PADDED, 24e6),
    )(*xs, *cs, *gus, *acts)


def out_project_kernel(mix_ref, w_ref, part0_ref, part1_ref):
    part = dot(mix_ref[...].reshape(PAIR, QUERY), w_ref[...], NT).astype(BF16)
    part0_ref[...] = part[:ROWS]
    part1_ref[...] = part[ROWS:]


def out_project(d, mix, w):
    rows = pl.BlockSpec((ROWS, WIDTH), lambda i: (0, 0))
    return pl.pallas_call(
        out_project_kernel,
        out_shape=(jax.ShapeDtypeStruct((ROWS, WIDTH), BF16),) * 2,
        grid=(1,),
        in_specs=[
            pl.BlockSpec((2, ROWS, QUERY), lambda i: (d, 0, 0)),
            pl.BlockSpec((WIDTH, QUERY), lambda i: (0, 0)),
        ],
        out_specs=(rows, rows),
        compiler_params=params(1, 16),
        cost_estimate=cost(2 * PAIR * WIDTH * QUERY, 2e6),
    )(mix, w)


def out_back_kernel(w_ref, *refs):
    for t in range(8):
        refs[8][t] = dot(refs[t][...], w_ref[...]).astype(BF16)


def out_back(branches, w):
    return pl.pallas_call(
        out_back_kernel,
        out_shape=jax.ShapeDtypeStruct((8, ROWS, QUERY), BF16),
        compiler_params=params(0, 16),
        cost_estimate=cost(8 * PAIR * WIDTH * QUERY, 4e6),
    )(w, *branches)


def out_weights_kernel(mix_ref, *refs):
    branch = jnp.concatenate([b[...] for b in refs[:8]], axis=0)
    refs[8][...] = dot(branch, mix_ref[...].reshape(8 * ROWS, QUERY), TN)


def out_weights(mix, branches):
    return pl.pallas_call(
        out_weights_kernel,
        out_shape=jax.ShapeDtypeStruct((WIDTH, QUERY), F32),
        compiler_params=params(0, 24),
        cost_estimate=cost(2 * 1024 * WIDTH * QUERY, 4e6),
    )(mix, *branches)


def pack_q_kernel(normed_ref, graw_ref, out_grad_ref, sent_ref):
    graw = graw_ref[...].reshape(8 * ROWS, 4 * HEAD)
    sent_ref[:, :QUERY] = dot(normed_ref[...], graw, TN)[:, :QUERY].astype(BF16)
    sent_ref[:, QUERY:] = out_grad_ref[...].astype(BF16)


def pack_q(normed, graw, out_grad):
    tall = 256
    return pl.pallas_call(
        pack_q_kernel,
        out_shape=jax.ShapeDtypeStruct((WIDTH, 2 * QUERY), BF16),
        grid=(WIDTH // tall,),
        in_specs=[
            pl.BlockSpec((8 * ROWS, tall), lambda m: (0, m)),
            all_of(4, PAIR, 4 * HEAD),
            pl.BlockSpec((tall, QUERY), lambda m: (m, 0)),
        ],
        out_specs=pl.BlockSpec((tall, 2 * QUERY), lambda m: (m, 0)),
        compiler_params=params(1, 16),
        cost_estimate=cost(2 * 1024 * WIDTH * 256, 8e6),
    )(normed, graw, out_grad)


def pack_kv_kernel(normed_ref, gkv0_ref, gkv1_ref, gains_ref, sent_ref):
    grad = dot(normed_ref[...], stacked(gkv0_ref, gkv1_ref), TN)
    gains = gains_ref[...]
    high = gains.astype(BF16).astype(F32)
    gains = jnp.concatenate([high, gains - high, jnp.zeros((HEAD - 32, gains.shape[1]), F32)], axis=0)
    sent_ref[:, : 2 * HEAD] = grad.astype(BF16)
    sent_ref[:, 2 * HEAD :] = gains.T.astype(BF16)


def pack_kv(normed, gkvs, gains):
    tall = 256
    return pl.pallas_call(
        pack_kv_kernel,
        out_shape=jax.ShapeDtypeStruct((WIDTH, QUERY), BF16),
        grid=(WIDTH // tall,),
        in_specs=[
            pl.BlockSpec((8 * ROWS, tall), lambda m: (0, m)),
            all_of(4 * ROWS, 2 * HEAD),
            all_of(4 * ROWS, 2 * HEAD),
            pl.BlockSpec((16, tall), lambda m: (0, m)),
        ],
        out_specs=pl.BlockSpec((tall, QUERY), lambda m: (m, 0)),
        compiler_params=params(1, 16),
        cost_estimate=cost(2 * 1024 * WIDTH * 128, 6e6),
    )(normed, *gkvs, gains)


def to_lanes(v):
    parts = []
    for c in (0, 1):
        t = v[c].astype(F32).T
        parts += [t[g * HEAD : (g + 1) * HEAD] for g in range(GROUP)]
    return jnp.concatenate(parts, axis=1)


def from_lanes(t, c):
    at = [(c * GROUP + g) * ROWS for g in range(GROUP)]
    return jnp.concatenate([t[:, i : i + ROWS] for i in at], axis=0).T


def key_loops(plan, at, base, unrolls, start, visit, state):
    p = 2 * pl.program_id(0)
    lo, m1, hi = plan[p, at], plan[p + 1, at + 1], plan[p + 1, at + 3]
    m2 = jnp.maximum(plan[p, at + 2], m1)
    core = plan[0, 15]
    lane = lax.broadcasted_iota(jnp.int32, (1, LANES), 1)
    place = lax.rem(lane, ROWS) + jnp.where(lane < LANES // 2, plan[p + core, 0], plan[p + 1 - core, 0])

    def masked(j, state):
        key = lax.broadcasted_iota(jnp.int32, (KEY_TILE, LANES), 0) + (j * KEY_TILE + base)
        return visit(j, state, (key >= start) & (key <= place))

    state = lax.fori_loop(lo, m1, masked, state)
    done = m1
    for unroll in unrolls:
        steps = lax.div(m2 - done, unroll)

        def several(i, state, done=done, unroll=unroll):
            for k in range(unroll):
                state = visit(done + unroll * i + k, state, None)
            return state

        state = lax.fori_loop(0, steps, several, state)
        done = done + unroll * steps
    return lax.fori_loop(m2, hi, masked, state)


def rows_of(j):
    return pl.ds(pl.multiple_of(j * KEY_TILE, KEY_TILE), KEY_TILE)


def chunks(plan, supers):
    for b in range(supers):
        for half in (0, 1):
            for f in range(8):
                side = plan[0, 10] if half == 0 else 1 - plan[0, 10]
                yield b, half, pl.multiple_of(b * SUPER + f * PAIR + side * ROWS, ROWS), plan[f, 1]


def line_up(plan, kv_refs, kv, kvt):
    @pl.when(pl.program_id(0) == 0)
    def _():
        for b, half, place, sent in chunks(plan, len(kv_refs) // 2):
            block = kv_refs[2 * b + half][sent]
            kv[pl.ds(place, ROWS), :] = block
            kvt[:, pl.ds(place, ROWS)] = block.astype(F32).T.astype(BF16)


def attend_body(at, base, plan, q_ref, start_ref, kv, kvt, state):
    qt = to_lanes(q_ref)
    qt = jnp.concatenate([jnp.zeros_like(qt), qt], axis=0).astype(BF16)

    def visit(j, state, mask):
        total, accum = state
        weights = jnp.exp2(dot(kv[rows_of(j), :], qt) * SCORE)
        if mask is not None:
            weights = jnp.where(mask, weights, 0.0)
        total = total + jnp.sum(weights, axis=0, keepdims=True)
        return total, accum + dot(kvt[:HEAD, rows_of(j)], weights.astype(BF16))

    return key_loops(plan, at, base, (4, 2, 1), start_ref[0], visit, state)


def attend_own_kernel(plan, q_ref, start_ref, *refs):
    kv_refs, (accum_ref, total_ref, kv, kvt) = refs[:2], refs[2:]
    line_up(plan, kv_refs, kv, kvt)
    state = (jnp.zeros((1, LANES), F32), jnp.zeros((HEAD, LANES), F32))
    total, accum = attend_body(6, EARLIER, plan, q_ref, start_ref, kv, kvt, state)
    accum_ref[0] = accum
    total_ref[0] = total


def attend_earlier_kernel(plan, q_ref, start_ref, *refs):
    kv_refs, (accum_ref, total_ref, mix_ref, out_ref, lse_ref, kv, kvt) = refs[:4], refs[4:]
    line_up(plan, kv_refs, kv, kvt)
    state = (total_ref[0], accum_ref[0])
    total, accum = attend_body(2, 0, plan, q_ref, start_ref, kv, kvt, state)
    out = accum / total
    out_ref[0] = out
    for c in (0, 1):
        mix_ref[c] = from_lanes(out, c).astype(BF16)
    lse_ref[0] = jnp.log2(total)


def back_kernel(plan, q_ref, start_ref, *refs):
    kv_refs, (g_ref, out_ref, lse_ref, dq_ref), sent_refs, (kv, kvt, dkv) = (
        refs[:6], refs[6:10], refs[10:16], refs[16:],
    )
    line_up(plan, kv_refs, kv, kvt)

    @pl.when(pl.program_id(0) == 0)
    def _():
        dkv[...] = jnp.zeros_like(dkv)

    qt = to_lanes(q_ref)
    gt = to_lanes(g_ref)
    delta = jnp.sum(gt * out_ref[0], axis=0, keepdims=True)
    zero = jnp.zeros_like(qt)
    gt = jnp.concatenate([gt, zero], axis=0)
    qt = jnp.concatenate([zero, qt], axis=0)
    both_t = jnp.concatenate([gt, qt], axis=1).astype(BF16)
    both = jnp.concatenate([gt.T, qt.T], axis=0).astype(BF16)
    lse = lse_ref[0]

    def visit(j, dqt, mask):
        pair = dot(kv[rows_of(j), :], both_t)
        weights = jnp.exp2(pair[:, LANES:] * SCORE - lse)
        if mask is not None:
            weights = jnp.where(mask, weights, 0.0)
        grads = (weights * (pair[:, :LANES] - delta)).astype(BF16)
        sides = jnp.concatenate([weights.astype(BF16), grads], axis=1)
        dkv[rows_of(j), :] += dot(sides, both)
        return dqt + dot(kvt[HEAD:, rows_of(j)], grads)

    dqt = key_loops(plan, 11, 0, (2, 1), start_ref[0], visit, jnp.zeros((HEAD, LANES), F32))
    for c in (0, 1):
        dq = from_lanes(dqt * HEAD**-0.5, c)
        dq_ref[c] = jnp.concatenate([dq, jnp.zeros((ROWS, HEAD), F32)], axis=1).astype(BF16)

    @pl.when(pl.program_id(0) == 3)
    def _():
        for b, half, place, sent in chunks(plan, 3):
            sent_refs[2 * b + half][sent] = dkv[pl.ds(place, ROWS), :].astype(BF16)


def whole(*shape):
    return pl.BlockSpec(shape, lambda f, plan: (0,) * len(shape))


def tile(*shape):
    return pl.BlockSpec((1,) + shape, lambda f, plan: (f,) + (0,) * len(shape))


def placed(*shape):
    return pl.BlockSpec((2,) + shape, lambda f, plan: (plan[2 * f, 16],) + (0,) * len(shape))


def tiles_call(kernel, supers, outs, more_ins, out_specs, flops, back):
    keys = supers * SUPER
    scratch = [pltpu.VMEM((keys, 2 * HEAD), BF16), pltpu.VMEM((2 * HEAD, keys), BF16)]
    if back:
        scratch.append(pltpu.VMEM((keys, 2 * HEAD), F32))
    ins = [placed(ROWS, QUERY), tile(1, LANES)] + [whole(8, ROWS, 2 * HEAD)] * (2 * supers)
    return pl.pallas_call(
        kernel,
        out_shape=outs,
        grid_spec=pltpu.PrefetchScalarGridSpec(
            num_scalar_prefetch=1,
            grid=(4,),
            in_specs=ins + more_ins,
            out_specs=out_specs,
            scratch_shapes=scratch,
        ),
        compiler_params=params(1, 36 if back else 28),
        cost_estimate=cost(flops, 8e6, 1e7),
    )


TILE_T = jax.ShapeDtypeStruct((4, HEAD, LANES), F32)
TILE_ROW = jax.ShapeDtypeStruct((4, 1, LANES), F32)
STATE = [tile(HEAD, LANES), tile(1, LANES)]


def attend_own(plan, q, start, kvs):
    call = tiles_call(attend_own_kernel, 1, (TILE_T, TILE_ROW), [], tuple(STATE), 4e9, False)
    return call(plan, q, start, *kvs)


def attend_earlier(plan, q, start, kvs, state):
    outs = (jax.ShapeDtypeStruct((8, ROWS, QUERY), BF16), TILE_T, TILE_ROW)
    specs = (placed(ROWS, QUERY),) + tuple(STATE)
    call = tiles_call(attend_earlier_kernel, 2, outs, STATE, specs, 8e9, False)
    return call(plan, q, start, *kvs, *state)


def back(plan, q, start, kvs, grad, out, lse):
    sent = jax.ShapeDtypeStruct((8, ROWS, 2 * HEAD), BF16)
    call = tiles_call(
        back_kernel,
        3,
        [jax.ShapeDtypeStruct((8, ROWS, 4 * HEAD), BF16)] + [sent] * 6,
        [placed(ROWS, QUERY)] + STATE,
        [placed(ROWS, 4 * HEAD)] + [whole(*sent.shape)] * 6,
        30e9,
        True,
    )
    return call(plan, q, start, *kvs, grad, out, lse)


def after(v, *others):
    return lax.optimization_barrier((v,) + others)[0]


def per_device(
    tokens,
    segments,
    attn_gain,
    w_query,
    w_key,
    w_value,
    q_gain,
    k_gain,
    w_out,
    ffn_gain,
    w_gate,
    w_up,
    w_down,
    cotangent,
):
    ylo, z, x, core, yhi = (lax.axis_index(a) for a in ALL)
    sup = ylo * 4 + z

    token_shifts = [shift_x(tokens, d) for d in (1, 2, 3)]
    token_blocks = [[b, swap(b, "core")] for b in [tokens] + token_shifts]
    all_tokens = [b for p in token_blocks for b in p]
    qkv_own = jnp.concatenate(
        [
            w_query.reshape(12, 8, QUERY),
            w_key.reshape(12, 8, HEAD),
            w_value.reshape(12, 8, HEAD),
            jnp.broadcast_to(attn_gain[:, None, None], (12, 8, 1)),
            jnp.broadcast_to(ffn_gain[:, None, None], (12, 8, 1)),
            jnp.zeros((12, 8, HEAD - 2), BF16),
        ],
        axis=-1,
    )
    qkv_own = jnp.pad(jnp.transpose(qkv_own, (1, 0, 2)), ((0, 0), (0, 12), (0, 0)))
    out_own = jnp.transpose(w_out.reshape(4, QUERY, 24), (0, 2, 1))
    out_own = jnp.pad(jnp.concatenate([out_own, out_own], axis=0), ((0, 0), (0, 0), (0, 3 * FREE - QUERY)))
    rows_own = jnp.concatenate(
        [
            part
            for i, w in enumerate((w_gate, w_up, w_down.T))
            for part in (
                w.reshape(24, 8, PART).transpose(1, 0, 2),
                out_own[:, :, i * FREE : (i + 1) * FREE],
            )
        ]
        + [qkv_own],
        axis=-1,
    )
    rows = exchange(rows_own, NEAR)
    ffn_rows = rows[:, :, : 3 * PADDED].reshape(192, 3 * PADDED)
    qkv_rows = rows[:, :12, 3 * PADDED :].reshape(1, 96, 6 * HEAD)
    qkv = exchange(jnp.broadcast_to(qkv_rows, (16, 96, 6 * HEAD)), WIDE)
    qkv = jnp.transpose(qkv.reshape(2, 8, 8, 12, 6 * HEAD), (1, 2, 0, 3, 4)).reshape(WIDTH, 6 * HEAD)
    ffn_full = lax.all_gather(ffn_rows, WIDE, axis=0, tiled=True).reshape(2, WIDTH, 3 * PADDED)
    gain_attn = qkv[:, 5 * HEAD].astype(F32)
    gain_ffn = qkv[:, 5 * HEAD + 1].astype(F32)

    token_index = jnp.arange(segments.shape[0], dtype=jnp.int32)
    begins = jnp.concatenate([jnp.ones((1,), jnp.bool_), segments[1:] != segments[:-1]])
    starts = lax.cummax(jnp.where(begins, token_index, 0), axis=0)
    own_starts = lax.dynamic_slice(
        starts.reshape(8, 8, 2, ROWS), (sup, 0, yhi, 0), (1, 8, 1, ROWS)
    ).reshape(8, ROWS)
    first = sup * SUPER + jnp.arange(8, dtype=jnp.int32) * PAIR + yhi * ROWS
    own_places = first[:, None] + jnp.arange(ROWS, dtype=jnp.int32)[None]
    positions = abs_to_rel((own_places - own_starts).reshape(4, 2, ROWS), x, core)
    frequency = THETA ** (-jnp.arange(HEAD // 2, dtype=F32) * 2.0 / HEAD)
    angles = positions.reshape(4, PAIR, 1).astype(F32) * frequency
    cosine, sine = jnp.cos(angles), jnp.sin(angles)
    cos = jnp.concatenate([cosine] * 4, axis=-1)
    sin = jnp.concatenate([-sine, sine] * 2, axis=-1)
    head_gain = jnp.concatenate([q_gain, q_gain, q_gain, k_gain]).astype(F32)[None]

    window = (sup - 2) * SUPER
    lo = (own_starts[:, 0] - window) // KEY_TILE
    hi = (first + ROWS - 1 - window) // KEY_TILE + 1
    m1 = jnp.clip((own_starts[:, -1] - window + KEY_TILE - 1) // KEY_TILE, lo, hi)
    m2 = jnp.clip((first + 1 - window) // KEY_TILE, m1, hi)
    order = jnp.arange(8, dtype=jnp.int32)
    relative = ((order // 2 - x) % 4) * 2 + (order % 2 + core) % 2
    edge = EARLIER // KEY_TILE
    plan = jnp.stack(
        [first - window, relative]
        + [jnp.minimum(v, edge) for v in (lo, m1, m2, hi)]
        + [jnp.maximum(v - edge, 0) for v in (lo, m1, m2, hi)]
        + [jnp.broadcast_to(yhi, (8,)), lo, m1, m2, hi]
        + [jnp.broadcast_to(core, (8,)), (order // 2 - x) % 4],
        axis=1,
    ).astype(jnp.int32)
    pair_starts = (own_starts - window).reshape(4, 2, 1, ROWS)
    pair_starts = jnp.where(core == 0, pair_starts, pair_starts[:, ::-1])
    start_lanes = jnp.broadcast_to(pair_starts, (4, 2, GROUP, ROWS)).reshape(4, 1, LANES)

    normed, rot_q, kv, raw = project(
        all_tokens, qkv, gain_attn[None], cos, sin, head_gain
    )

    kv_own = [kv, swap(kv, "yhi")]
    kv_sent = after(kv, kv_own[1])
    kv_earlier = [shift_super(kv_sent, a, b) for a, b in ((2, 0), (2, 1), (1, 0), (1, 1))]
    state = attend_own(plan, rot_q, start_lanes, kv_own)
    state, kv_earlier, cot_sent = lax.optimization_barrier((state, kv_earlier, cotangent))
    cot_shifts = [shift_x(cot_sent, d) for d in (1, 2, 3)]
    mix, out_tiles, lse = attend_earlier(plan, rot_q, start_lanes, kv_earlier, state)
    mix, cot_shifts = lax.optimization_barrier((mix, cot_shifts))
    out_half = lax.dynamic_index_in_dim(ffn_full, x // 2, 0, keepdims=False)
    w_out_t = jnp.concatenate(
        [out_half[:, i * PADDED + PART : (i + 1) * PADDED] for i in range(3)], axis=1
    )[:, :QUERY]
    w_out_t, mix = lax.optimization_barrier((w_out_t, mix))
    cot_blocks = [[b, swap(b, "core")] for b in [cotangent] + cot_shifts]
    all_cot = [b for p in cot_blocks for b in p]

    inputs = tokens.astype(F32)
    parts = [None] * 4
    for d in (2, 1, 3, 0):
        parts[d] = out_project(d, mix, w_out_t)
    hidden = inputs + near_sum(near_keep(parts))
    scale_ffn = rms_scale(hidden)
    scaled_ffn = hidden * scale_ffn
    normed_ffn = (scaled_ffn * gain_ffn).astype(BF16)

    ffn_blocks = [[b] for b in [normed_ffn] + [shift_x(normed_ffn, d) for d in (1, 2, 3)]]
    ffn_blocks[0].append(swap(normed_ffn, "core"))
    ffn_outs = [None] * 4
    before = {1: 0, 3: 0, 2: 1}
    for d in (0, 1, 3, 2):
        if d > 0:
            block = after(ffn_blocks[d][0], ffn_outs[before[d]][0])
            ffn_blocks[d] = [block, swap(block, "core")]
        blocks = ffn_blocks[d]
        if d == 3:
            blocks = after(blocks, ffn_outs[1][0])
        if d == 2:
            blocks = after(blocks, ffn_outs[3][0])
        ffn_outs[d] = ffn(*blocks, *cot_blocks[d], ffn_full)
    acts, gus = [o[4] for o in ffn_outs], [o[5] for o in ffn_outs]
    kept, gus, out_own, out_other = lax.optimization_barrier(
        (near_keep([o[:2] for o in ffn_outs]), gus, [o[2] for o in ffn_outs], [o[3] for o in ffn_outs])
    )
    out_kept = jnp.stack(out_own).astype(F32) + swap(jnp.stack(out_other), "core").astype(F32)
    out_kept = out_kept.astype(BF16)
    pair_total = near_sum(kept)
    weight_grads = ffn_weights([b for p in ffn_blocks for b in p], all_cot, gus, acts)
    pair_total, weight_grads, out_kept = lax.optimization_barrier((pair_total, weight_grads, out_kept))
    ffn_sum = lax.psum_scatter(
        weight_grads.reshape(2 * WIDTH, 3 * PART), WIDE, scatter_dimension=0, tiled=True
    )
    ffn_gain_part = jnp.sum(pair_total * scaled_ffn, axis=0)
    grad_hidden = cotangent.astype(F32) + rms_back(pair_total * gain_ffn, hidden, scale_ffn)
    grad_branch = grad_hidden.astype(BF16)
    branches = [b for p in near_gather(grad_branch) for b in p]
    grad_mix = out_back(branches, w_out_t)
    out_total = near_sum(after([out_kept[d] for d in range(4)], branches))

    back_outs = back(plan, rot_q, start_lanes, kv_earlier + kv_own, grad_mix, out_tiles, lse)
    back_outs, out_total = lax.optimization_barrier((back_outs, out_total))
    grad_q, two_mine, two_theirs, one_mine, one_theirs, mine, theirs = back_outs
    grad_kvs = [
        mine,
        swap(theirs, "yhi"),
        shift_super(one_mine, -1, 0),
        shift_super(one_theirs, -1, 1),
        shift_super(two_mine, -2, 0),
        shift_super(two_theirs, -2, 1),
    ]

    grad_out = out_weights(after(mix, grad_q), branches)
    graw_q, q_gain_part = unproject_q(grad_q, raw, cos, sin, head_gain)
    sent_q = pack_q(normed, graw_q, grad_out)
    grad_kvs, sent_q = lax.optimization_barrier((grad_kvs, sent_q))
    got_q = exchange(sent_q.reshape(8, 192, 2 * QUERY), ("ylo", "z"))

    unprojected = [None] * 2
    for half in (1, 0):
        xs = all_tokens[4 * half : 4 * half + 4]
        unprojected[half] = unproject(half, graw_q, grad_kvs, raw, xs, qkv, cos, sin, head_gain)
    q_gain_part = q_gain_part[0, :HEAD] + q_gain_part[0, HEAD : 2 * HEAD] + q_gain_part[0, 2 * HEAD : QUERY]
    k_gain_part = (unprojected[0][6] + unprojected[1][6])[0, HEAD:]
    head_part = jnp.concatenate([q_gain_part, k_gain_part, jnp.zeros((4,), F32)])
    gain_parts = jnp.concatenate(
        [
            sum(u[5] for u in unprojected),
            ffn_gain_part[None],
            jnp.tile(head_part.reshape(12, 11).T, (1, 128)),
            jnp.zeros((3, WIDTH), F32),
        ],
        axis=0,
    )
    sent = pack_kv(normed, [u[4] for u in unprojected], gain_parts)
    parts = [u[2 * i : 2 * i + 2] for u in unprojected for i in (0, 1)]
    parts, sent = lax.optimization_barrier((parts, sent))
    grad_normed = near_sum(near_keep(parts))
    got = exchange(sent.reshape(8, 192, QUERY), ("ylo", "z"))

    def added(v):
        return jnp.sum(v.astype(F32), axis=0).astype(BF16).reshape(8, 24, -1)

    last = jnp.concatenate([ffn_sum.reshape(8, 24, 3 * PART), added(got_q), added(got)], axis=-1)
    last = exchange(last, NEAR)
    ffn_grad, got = last[:, :, : 3 * PART], last[:, :, 3 * PART :].astype(F32)

    grad_out = got[:, :, QUERY : 2 * QUERY]
    qkv_grad = jnp.concatenate([got[:, :, :QUERY], got[:, :, 2 * QUERY :]], axis=-1)
    here, there = jnp.where(yhi == 0, 0, 1), jnp.where(yhi == 0, 1, 0)

    def half_of(v, axis, which):
        size = v.shape[axis] // 2
        return lax.dynamic_slice_in_dim(v, which * size, size, axis)

    qkv_other = swap(half_of(qkv_grad, 1, there).astype(BF16), "yhi").astype(F32)
    out_other = swap(half_of(grad_out, 0, there).astype(BF16), "yhi").astype(F32)
    qkv_grad = half_of(qkv_grad, 1, here) + qkv_other
    grad_out = half_of(grad_out, 0, here) + out_other
    gains = jnp.sum(qkv_grad[:, :, 5 * HEAD :], axis=0)
    gains = gains[:, :16] + gains[:, 16:32]
    head_gains = gains[:, 2:13].reshape(-1)
    qkv_grad = jnp.transpose(qkv_grad, (1, 0, 2))
    w_out_grad = jnp.transpose(grad_out, (0, 2, 1)).reshape(768, 24)
    w_query_grad = qkv_grad[:, :, :QUERY].reshape(12, -1)
    w_value_grad = qkv_grad[:, :, QUERY : QUERY + HEAD].reshape(12, -1)
    w_key_grad = qkv_grad[:, :, QUERY + HEAD : QUERY + 2 * HEAD].reshape(12, -1)

    output = (hidden + out_total).astype(BF16)
    scale_attn = rms_scale(inputs)
    input_grad = (grad_hidden + rms_back(grad_normed * gain_attn, inputs, scale_attn)).astype(BF16)

    ffn_grad = jnp.transpose(ffn_grad, (1, 0, 2)).astype(F32)
    w_gate_grad, w_up_grad, w_down_grad = (
        ffn_grad[:, :, i * PART : (i + 1) * PART].reshape(24, -1) for i in range(3)
    )
    return (
        output,
        input_grad,
        gains[:, 0],
        w_query_grad,
        w_key_grad,
        w_value_grad,
        head_gains[:HEAD],
        head_gains[HEAD : 2 * HEAD],
        w_out_grad,
        gains[:, 1],
        w_gate_grad,
        w_up_grad,
        w_down_grad.T,
    )


def solution(mesh):
    mesh = Mesh(np.asarray(mesh.devices).reshape(2, 4, 4, 2, 2), ALL)
    rows = P(ALL, None)
    weights = (P("yhi", BLK), P(ALL), P(BLK, "yhi"), P(BLK, "yhi"), P("yhi", BLK))
    placed_in = (rows, P(), P(ALL), rows, rows, rows, P(), P()) + weights + (rows,)
    placed_out = (rows, rows, P(ALL), rows, rows, rows, P(), P()) + weights
    return jax.shard_map(
        per_device, mesh=mesh, in_specs=placed_in, out_specs=placed_out, check_vma=False
    )
```

```python
import functools

import jax
import jax.numpy as jnp
import numpy as np
from jax import lax
from jax.experimental import pallas as pl
from jax.experimental.pallas import tpu as pltpu
from jax.sharding import Mesh
from jax.sharding import PartitionSpec as P

EPS = 1e-05
THETA = 1000000.0
HEAD = 64
ROWS = 128
PAIR = 2 * ROWS
GROUP = 3
QUERY = GROUP * HEAD
LANES = PAIR * GROUP
KEY_TILE = 512
SUPER = 2048
EARLIER = 2 * SUPER
PART = 432
PADDED = 512
FREE = PADDED - PART
WIDTH = 1536
ALL = ("ylo", "z", "x", "core", "yhi")
BLK = ("ylo", "z", "x", "core")
WIDE = ("yhi", "ylo", "z")
NEAR = ("x", "core")
NN = (((1,), (0,)), ((), ()))
NT = (((1,), (1,)), ((), ()))
TN = (((0,), (0,)), ((), ()))
F32 = jnp.float32
BF16 = jnp.bfloat16
SCORE = HEAD**-0.5 * 1.4426950408889634


def dot(a, b, numbers=NN):
    return lax.dot_general(a, b, numbers, preferred_element_type=F32)


def rms_scale(v):
    return lax.rsqrt(jnp.mean(v * v, axis=-1, keepdims=True) + EPS)


def rms_back(grad, v, scale):
    inner = jnp.mean(grad * v, axis=-1, keepdims=True)
    return scale * (grad - v * scale * scale * inner)


def shift_x(v, distance):
    return lax.ppermute(v, "x", [((i + distance) % 4, i) for i in range(4)])


def swap(v, axis):
    return lax.ppermute(v, axis, [(0, 1), (1, 0)])


def shift_super(v, distance, other):
    pairs = [
        (2 * i + h, 2 * (i + distance) + (h + other) % 2)
        for i in range(8)
        for h in (0, 1)
        if 0 <= i + distance < 8
    ]
    return lax.ppermute(v, ("ylo", "z", "yhi"), pairs)


def exchange(v, axes):
    return lax.all_to_all(v, axes, split_axis=0, concat_axis=0, tiled=True)


def near_gather(v):
    blocks = [v] + [shift_x(v, d) for d in (1, 2, 3)]
    return [[b, swap(b, "core")] for b in blocks]


def near_keep(parts):
    return [
        (own.astype(F32) + swap(other, "core").astype(F32)).astype(BF16) for own, other in parts
    ]


def near_sum(kept):
    total = kept[0].astype(F32)
    for d in (1, 2, 3):
        total = total + shift_x(kept[d], -d).astype(F32)
    return total


def rel_to_abs(v, x, core):
    v = jnp.where(core == 0, v, v[:, ::-1])
    return lax.dynamic_slice_in_dim(jnp.concatenate([v, v], axis=0), (4 - x) % 4, 4, 0)


def abs_to_rel(v, x, core):
    v = jnp.where(core == 0, v, v[:, ::-1])
    return lax.dynamic_slice_in_dim(jnp.concatenate([v, v], axis=0), x, 4, 0)


def params(steps, mib):
    return pltpu.CompilerParams(
        dimension_semantics=("arbitrary",) * steps, vmem_limit_bytes=mib * 2**20
    )


def cost(flops, moved, exps=0):
    return pl.CostEstimate(flops=int(flops), bytes_accessed=int(moved), transcendentals=int(exps))


def all_of(*shape):
    return pl.BlockSpec(shape, lambda *i: (0,) * len(shape))


ROWS_OF = pl.BlockSpec((ROWS, WIDTH), lambda *i: (0, 0))


def stacked(a_ref, b_ref):
    return jnp.concatenate([a_ref[...], b_ref[...]], axis=0)


def head_sums(v):
    shape = (v.shape[1], v.shape[1])
    lane = lax.shift_right_logical(lax.broadcasted_iota(jnp.int32, shape, 1), 6)
    row = lax.shift_right_logical(lax.broadcasted_iota(jnp.int32, shape, 0), 6)
    ones = jnp.where(lane == row, 1.0, 0.0).astype(BF16)
    high = v.astype(BF16)
    low = (v - high.astype(F32)).astype(BF16)
    return dot(high, ones) + dot(low, ones)


def half_turn(v):
    lane = lax.broadcasted_iota(jnp.int32, v.shape, 1)
    return jnp.where(
        (lane & (HEAD - 1)) < HEAD // 2,
        pltpu.roll(v, v.shape[1] - HEAD // 2, 1),
        pltpu.roll(v, HEAD // 2, 1),
    )


def twice(v):
    return jnp.concatenate([v, v], axis=1)


def project_kernel(*refs):
    xs, (w_ref, gain_ref, cos_ref, sin_ref, head_gain_ref) = refs[:8], refs[8:13]
    normed_ref, q_ref, kv_ref, raw_ref = refs[13:]
    lane = lax.broadcasted_iota(jnp.int32, (PAIR, 2 * HEAD), 1)
    for d in range(4):
        rows = slice(d * PAIR, (d + 1) * PAIR)
        tiles = slice(2 * d, 2 * d + 2)
        x = stacked(*xs[tiles]).astype(F32)
        normed = (x * rms_scale(x) * gain_ref[...]).astype(BF16)
        normed_ref[rows, :] = normed
        raw = dot(normed, w_ref[...])
        heads = raw[:, : 4 * HEAD]
        raw_ref[d] = heads
        scale = lax.rsqrt(head_sums(heads * heads) * (1.0 / HEAD) + EPS)
        v = heads * scale * head_gain_ref[...]
        turned = v * twice(cos_ref[d]) + half_turn(v) * twice(sin_ref[d])
        q_ref[tiles] = turned[:, :QUERY].astype(BF16).reshape(2, ROWS, QUERY)
        kv = jnp.where(lane < HEAD, raw[:, 4 * HEAD :], turned[:, 2 * HEAD :])
        kv_ref[tiles] = kv.astype(BF16).reshape(2, ROWS, 2 * HEAD)


def project(xs, w, gain, cos, sin, head_gain):
    return pl.pallas_call(
        project_kernel,
        out_shape=(
            jax.ShapeDtypeStruct((4 * PAIR, WIDTH), BF16),
            jax.ShapeDtypeStruct((8, ROWS, QUERY), BF16),
            jax.ShapeDtypeStruct((8, ROWS, 2 * HEAD), BF16),
            jax.ShapeDtypeStruct((4, PAIR, 4 * HEAD), F32),
        ),
        grid=(1,),
        in_specs=[ROWS_OF] * 8
        + [all_of(WIDTH, 384), all_of(1, WIDTH)]
        + [all_of(4, PAIR, 2 * HEAD)] * 2
        + [all_of(1, 4 * HEAD)],
        out_specs=(
            all_of(4 * PAIR, WIDTH),
            all_of(8, ROWS, QUERY),
            all_of(8, ROWS, 2 * HEAD),
            all_of(4, PAIR, 4 * HEAD),
        ),
        compiler_params=params(1, 40),
        cost_estimate=cost(8 * PAIR * WIDTH * 384, 1e7),
    )(*xs, w, gain, cos, sin, head_gain)


def turned_back(g, raw, cos, sin, head_gain):
    width = g.shape[1]
    g = g * cos - half_turn(g) * sin
    scale = lax.rsqrt(head_sums(raw * raw) * (1.0 / HEAD) + EPS)
    gain = jnp.sum(g * raw * scale, axis=0, keepdims=True)
    e = g * head_gain[:, -width:]
    inner = head_sums(e * raw) * (1.0 / HEAD)
    return scale * (e - raw * scale * scale * inner), gain


def unproject_q_kernel(gq_ref, raw_ref, cos_ref, sin_ref, head_gain_ref, graw_ref, gain_ref):
    gains = 0.0
    for d in range(4):
        g = gq_ref[2 * d : 2 * d + 2].reshape(PAIR, 4 * HEAD).astype(F32)
        graw, gain = turned_back(
            g, raw_ref[d], twice(cos_ref[d]), twice(sin_ref[d]), head_gain_ref[...]
        )
        graw_ref[d] = graw.astype(BF16)
        gains = gains + gain
    gain_ref[...] = gains


def unproject_q(gq, raw, cos, sin, head_gain):
    return pl.pallas_call(
        unproject_q_kernel,
        out_shape=(
            jax.ShapeDtypeStruct((4, PAIR, 4 * HEAD), BF16),
            jax.ShapeDtypeStruct((1, 4 * HEAD), F32),
        ),
        compiler_params=params(0, 20),
        cost_estimate=cost(1e8, 4e6),
    )(gq, raw, cos, sin, head_gain)


def unproject_kernel(*refs):
    graw_q_ref, g_refs, raw_ref, xs, (w_ref, cos_ref, sin_ref, head_gain_ref) = (
        refs[0], refs[1:7], refs[7], refs[8:12], refs[12:16],
    )
    parts, (gkv_ref, attn_ref, gain_ref) = refs[16:20], refs[20:]
    attn, gains = 0.0, 0.0
    lane = lax.broadcasted_iota(jnp.int32, (PAIR, 2 * HEAD), 1)
    for i in range(2):
        tiles = slice(2 * i, 2 * i + 2)
        gkv = g_refs[0][tiles].astype(F32)
        for ref in g_refs[1:]:
            gkv = gkv + ref[tiles].astype(F32)
        gkv = gkv.reshape(PAIR, 2 * HEAD)
        gk = jnp.where(lane < HEAD, 0.0, (gkv * HEAD**-0.5).astype(BF16).astype(F32))
        graw_k, gain = turned_back(
            gk, raw_ref[i][:, 2 * HEAD :], cos_ref[i], sin_ref[i], head_gain_ref[...]
        )
        gains = gains + gain
        graw_q = graw_q_ref[i].astype(F32)
        graw = [
            graw_q[:, : 2 * HEAD],
            jnp.where(lane < HEAD, graw_q[:, 2 * HEAD :], graw_k),
            jnp.where(lane < HEAD, gkv, 0.0),
        ]
        gkv_ref[i * PAIR : (i + 1) * PAIR, :] = jnp.where(lane < HEAD, gkv, graw_k).astype(BF16)
        grad = dot(jnp.concatenate(graw, axis=1).astype(BF16), w_ref[...], NT)
        x = stacked(*xs[tiles]).astype(F32)
        attn = attn + jnp.sum(grad * x * rms_scale(x), axis=0, keepdims=True)
        grad = grad.astype(BF16)
        parts[2 * i][...] = grad[:ROWS]
        parts[2 * i + 1][...] = grad[ROWS:]
    attn_ref[...] = attn
    gain_ref[...] = gains


def unproject(half, graw_q, gkvs, raw, xs, w, cos, sin, head_gain):
    def at_half(*shape):
        return pl.BlockSpec(shape, lambda i: (half,) + (0,) * (len(shape) - 1))

    table = at_half(2, PAIR, 2 * HEAD)
    outs = (jax.ShapeDtypeStruct((ROWS, WIDTH), BF16),) * 4 + (
        jax.ShapeDtypeStruct((2 * PAIR, 2 * HEAD), BF16),
        jax.ShapeDtypeStruct((1, WIDTH), F32),
        jax.ShapeDtypeStruct((1, 2 * HEAD), F32),
    )
    return pl.pallas_call(
        unproject_kernel,
        out_shape=outs,
        grid=(1,),
        in_specs=[at_half(2, PAIR, 4 * HEAD)]
        + [at_half(4, ROWS, 2 * HEAD)] * 6
        + [at_half(2, PAIR, 4 * HEAD)]
        + [ROWS_OF] * 4
        + [all_of(WIDTH, 6 * HEAD), table, table, all_of(1, 4 * HEAD)],
        out_specs=tuple(all_of(*o.shape) for o in outs),
        compiler_params=params(1, 20),
        cost_estimate=cost(4 * PAIR * WIDTH * 384, 8e6),
    )(graw_q, *gkvs, raw, *xs, w, cos, sin, head_gain)


def ffn_kernel(
    x0_ref, x1_ref, c0_ref, c1_ref, gu_w_ref, d_w_ref,
    part0_ref, part1_ref, out0_ref, out1_ref, act_ref, gu_ref, total, out_total,
):
    y = pl.program_id(0)
    x = stacked(x0_ref, x1_ref)
    gate_up = dot(x, gu_w_ref[0])
    gate, up = gate_up[:, :PADDED], gate_up[:, PADDED:]
    grad_act = dot(stacked(c0_ref, c1_ref), d_w_ref[0])
    own = lax.broadcasted_iota(jnp.int32, (PAIR, PADDED), 1) < PART
    sig = 1.0 / (1.0 + jnp.exp(-gate))
    silu = gate * sig
    act = jnp.where(own, silu * up, 0.0).astype(BF16)
    act_ref[0] = act
    out_part = dot(act, d_w_ref[0], NT)
    grad_act = jnp.where(own, grad_act, 0.0)
    grad_gate = jnp.where(own, grad_act * up * sig * (1.0 + gate * (1.0 - sig)), 0.0)
    grads = jnp.concatenate([grad_gate, jnp.where(own, grad_act * silu, 0.0)], axis=1).astype(BF16)
    gu_ref[0] = grads
    part = dot(grads, gu_w_ref[0], NT)

    @pl.when(y == 0)
    def _():
        total[...] = part
        out_total[...] = out_part

    @pl.when(y == 1)
    def _():
        whole_part = (total[...] + part).astype(BF16)
        part0_ref[...] = whole_part[:ROWS]
        part1_ref[...] = whole_part[ROWS:]
        whole_part = (out_total[...] + out_part).astype(BF16)
        out0_ref[...] = whole_part[:ROWS]
        out1_ref[...] = whole_part[ROWS:]


def ffn(x0, x1, c0, c1, w):
    rows = ROWS_OF
    return pl.pallas_call(
        ffn_kernel,
        out_shape=(jax.ShapeDtypeStruct((ROWS, WIDTH), BF16),) * 4
        + (
            jax.ShapeDtypeStruct((2, PAIR, PADDED), BF16),
            jax.ShapeDtypeStruct((2, PAIR, 2 * PADDED), BF16),
        ),
        grid=(2,),
        in_specs=[rows] * 4
        + [pl.BlockSpec((1, WIDTH, n * PADDED), lambda y, c=c: (y, 0, c)) for n, c in ((2, 0), (1, 2))],
        out_specs=(rows,) * 4
        + (
            pl.BlockSpec((1, PAIR, PADDED), lambda y: (y, 0, 0)),
            pl.BlockSpec((1, PAIR, 2 * PADDED), lambda y: (y, 0, 0)),
        ),
        scratch_shapes=[pltpu.VMEM((PAIR, WIDTH), F32)] * 2,
        compiler_params=params(1, 32),
        cost_estimate=cost(2 * 2 * PAIR * WIDTH * 6 * PADDED, 14e6),
    )(x0, x1, c0, c1, w, w)


def ffn_weights_kernel(*refs):
    xs, cs, gus, acts, out_ref = refs[:8], refs[8:16], refs[16:20], refs[20:24], refs[24]
    def all_tokens(refs):
        return jnp.concatenate([ref[...] for ref in refs], axis=0)

    grad_gu = dot(all_tokens(xs), all_tokens([g.at[0] for g in gus]), TN)
    grad_d = dot(all_tokens(cs), all_tokens([a.at[0] for a in acts]), TN)
    out_ref[0, :, :PART] = grad_gu[:, :PART].astype(BF16)
    out_ref[0, :, PART : 2 * PART] = grad_gu[:, PADDED : PADDED + PART].astype(BF16)
    out_ref[0, :, 2 * PART :] = grad_d[:, :PART].astype(BF16)


def ffn_weights(xs, cs, gus, acts):
    tall = 256
    rows = pl.BlockSpec((ROWS, tall), lambda y, m: (0, m))
    return pl.pallas_call(
        ffn_weights_kernel,
        out_shape=jax.ShapeDtypeStruct((2, WIDTH, 3 * PART), BF16),
        grid=(2, WIDTH // tall),
        in_specs=[rows] * 16
        + [pl.BlockSpec((1, PAIR, 2 * PADDED), lambda y, m: (y, 0, 0))] * 4
        + [pl.BlockSpec((1, PAIR, PADDED), lambda y, m: (y, 0, 0))] * 4,
        out_specs=pl.BlockSpec((1, tall, 3 * PART), lambda y, m: (y, m, 0)),
        compiler_params=params(2, 28),
        cost_estimate=cost(2 * 2 * 1024 * WIDTH * 3 * PADDED, 24e6),
    )(*xs, *cs, *gus, *acts)


def out_project_kernel(mix_ref, w_ref, part0_ref, part1_ref):
    part = dot(mix_ref[...].reshape(PAIR, QUERY), w_ref[...], NT).astype(BF16)
    part0_ref[...] = part[:ROWS]
    part1_ref[...] = part[ROWS:]


def out_project(d, mix, w):
    rows = pl.BlockSpec((ROWS, WIDTH), lambda i: (0, 0))
    return pl.pallas_call(
        out_project_kernel,
        out_shape=(jax.ShapeDtypeStruct((ROWS, WIDTH), BF16),) * 2,
        grid=(1,),
        in_specs=[
            pl.BlockSpec((2, ROWS, QUERY), lambda i: (d, 0, 0)),
            pl.BlockSpec((WIDTH, QUERY), lambda i: (0, 0)),
        ],
        out_specs=(rows, rows),
        compiler_params=params(1, 16),
        cost_estimate=cost(2 * PAIR * WIDTH * QUERY, 2e6),
    )(mix, w)


def out_back_kernel(w_ref, *refs):
    for t in range(8):
        refs[8][t] = dot(refs[t][...], w_ref[...]).astype(BF16)


def out_back(branches, w):
    return pl.pallas_call(
        out_back_kernel,
        out_shape=jax.ShapeDtypeStruct((8, ROWS, QUERY), BF16),
        compiler_params=params(0, 16),
        cost_estimate=cost(8 * PAIR * WIDTH * QUERY, 4e6),
    )(w, *branches)


def out_weights_kernel(mix_ref, *refs):
    branch = jnp.concatenate([b[...] for b in refs[:8]], axis=0)
    refs[8][...] = dot(branch, mix_ref[...].reshape(8 * ROWS, QUERY), TN)


def out_weights(mix, branches):
    return pl.pallas_call(
        out_weights_kernel,
        out_shape=jax.ShapeDtypeStruct((WIDTH, QUERY), F32),
        compiler_params=params(0, 24),
        cost_estimate=cost(2 * 1024 * WIDTH * QUERY, 4e6),
    )(mix, *branches)


def pack_q_kernel(normed_ref, graw_ref, out_grad_ref, sent_ref):
    graw = graw_ref[...].reshape(8 * ROWS, 4 * HEAD)
    sent_ref[:, :QUERY] = dot(normed_ref[...], graw, TN)[:, :QUERY].astype(BF16)
    sent_ref[:, QUERY:] = out_grad_ref[...].astype(BF16)


def pack_q(normed, graw, out_grad):
    tall = 256
    return pl.pallas_call(
        pack_q_kernel,
        out_shape=jax.ShapeDtypeStruct((WIDTH, 2 * QUERY), BF16),
        grid=(WIDTH // tall,),
        in_specs=[
            pl.BlockSpec((8 * ROWS, tall), lambda m: (0, m)),
            all_of(4, PAIR, 4 * HEAD),
            pl.BlockSpec((tall, QUERY), lambda m: (m, 0)),
        ],
        out_specs=pl.BlockSpec((tall, 2 * QUERY), lambda m: (m, 0)),
        compiler_params=params(1, 16),
        cost_estimate=cost(2 * 1024 * WIDTH * 256, 8e6),
    )(normed, graw, out_grad)


def pack_kv_kernel(normed_ref, gkv0_ref, gkv1_ref, gains_ref, sent_ref):
    grad = dot(normed_ref[...], stacked(gkv0_ref, gkv1_ref), TN)
    gains = gains_ref[...]
    high = gains.astype(BF16).astype(F32)
    gains = jnp.concatenate([high, gains - high, jnp.zeros((HEAD - 32, gains.shape[1]), F32)], axis=0)
    sent_ref[:, : 2 * HEAD] = grad.astype(BF16)
    sent_ref[:, 2 * HEAD :] = gains.T.astype(BF16)


def pack_kv(normed, gkvs, gains):
    tall = 256
    return pl.pallas_call(
        pack_kv_kernel,
        out_shape=jax.ShapeDtypeStruct((WIDTH, QUERY), BF16),
        grid=(WIDTH // tall,),
        in_specs=[
            pl.BlockSpec((8 * ROWS, tall), lambda m: (0, m)),
            all_of(4 * ROWS, 2 * HEAD),
            all_of(4 * ROWS, 2 * HEAD),
            pl.BlockSpec((16, tall), lambda m: (0, m)),
        ],
        out_specs=pl.BlockSpec((tall, QUERY), lambda m: (m, 0)),
        compiler_params=params(1, 16),
        cost_estimate=cost(2 * 1024 * WIDTH * 128, 6e6),
    )(normed, *gkvs, gains)


def to_lanes(v):
    parts = []
    for c in (0, 1):
        t = v[c].astype(F32).T
        parts += [t[g * HEAD : (g + 1) * HEAD] for g in range(GROUP)]
    return jnp.concatenate(parts, axis=1)


def from_lanes(t, c):
    at = [(c * GROUP + g) * ROWS for g in range(GROUP)]
    return jnp.concatenate([t[:, i : i + ROWS] for i in at], axis=0).T


def key_loops(plan, at, base, unrolls, start, visit, state):
    p = 2 * pl.program_id(0)
    lo, m1, hi = plan[p, at], plan[p + 1, at + 1], plan[p + 1, at + 3]
    m2 = jnp.maximum(plan[p, at + 2], m1)
    core = plan[0, 15]
    lane = lax.broadcasted_iota(jnp.int32, (1, LANES), 1)
    place = lax.rem(lane, ROWS) + jnp.where(lane < LANES // 2, plan[p + core, 0], plan[p + 1 - core, 0])

    def masked(j, state):
        key = lax.broadcasted_iota(jnp.int32, (KEY_TILE, LANES), 0) + (j * KEY_TILE + base)
        return visit(j, state, (key >= start) & (key <= place))

    state = lax.fori_loop(lo, m1, masked, state)
    done = m1
    for unroll in unrolls:
        steps = lax.div(m2 - done, unroll)

        def several(i, state, done=done, unroll=unroll):
            for k in range(unroll):
                state = visit(done + unroll * i + k, state, None)
            return state

        state = lax.fori_loop(0, steps, several, state)
        done = done + unroll * steps
    return lax.fori_loop(m2, hi, masked, state)


def rows_of(j):
    return pl.ds(pl.multiple_of(j * KEY_TILE, KEY_TILE), KEY_TILE)


def chunks(plan, supers):
    for b in range(supers):
        for half in (0, 1):
            for f in range(8):
                side = plan[0, 10] if half == 0 else 1 - plan[0, 10]
                yield b, half, pl.multiple_of(b * SUPER + f * PAIR + side * ROWS, ROWS), plan[f, 1]


def line_up(plan, kv_refs, kv, kvt):
    @pl.when(pl.program_id(0) == 0)
    def _():
        for b, half, place, sent in chunks(plan, len(kv_refs) // 2):
            block = kv_refs[2 * b + half][sent]
            kv[pl.ds(place, ROWS), :] = block
            kvt[:, pl.ds(place, ROWS)] = block.astype(F32).T.astype(BF16)


def attend_body(at, base, plan, q_ref, start_ref, kv, kvt, state):
    qt = to_lanes(q_ref)
    qt = jnp.concatenate([jnp.zeros_like(qt), qt], axis=0).astype(BF16)

    def visit(j, state, mask):
        total, accum = state
        weights = jnp.exp2(dot(kv[rows_of(j), :], qt) * SCORE)
        if mask is not None:
            weights = jnp.where(mask, weights, 0.0)
        total = total + jnp.sum(weights, axis=0, keepdims=True)
        return total, accum + dot(kvt[:HEAD, rows_of(j)], weights.astype(BF16))

    return key_loops(plan, at, base, (4, 2, 1), start_ref[0], visit, state)


def attend_own_kernel(plan, q_ref, start_ref, *refs):
    kv_refs, (accum_ref, total_ref, kv, kvt) = refs[:2], refs[2:]
    line_up(plan, kv_refs, kv, kvt)
    state = (jnp.zeros((1, LANES), F32), jnp.zeros((HEAD, LANES), F32))
    total, accum = attend_body(6, EARLIER, plan, q_ref, start_ref, kv, kvt, state)
    accum_ref[0] = accum
    total_ref[0] = total


def attend_earlier_kernel(plan, q_ref, start_ref, *refs):
    kv_refs, (accum_ref, total_ref, mix_ref, out_ref, lse_ref, kv, kvt) = refs[:4], refs[4:]
    line_up(plan, kv_refs, kv, kvt)
    state = (total_ref[0], accum_ref[0])
    total, accum = attend_body(2, 0, plan, q_ref, start_ref, kv, kvt, state)
    out = accum / total
    out_ref[0] = out
    for c in (0, 1):
        mix_ref[c] = from_lanes(out, c).astype(BF16)
    lse_ref[0] = jnp.log2(total)


def back_kernel(plan, q_ref, start_ref, *refs):
    kv_refs, (g_ref, out_ref, lse_ref, dq_ref), sent_refs, (kv, kvt, dkv) = (
        refs[:6], refs[6:10], refs[10:16], refs[16:],
    )
    line_up(plan, kv_refs, kv, kvt)

    @pl.when(pl.program_id(0) == 0)
    def _():
        dkv[...] = jnp.zeros_like(dkv)

    qt = to_lanes(q_ref)
    gt = to_lanes(g_ref)
    delta = jnp.sum(gt * out_ref[0], axis=0, keepdims=True)
    zero = jnp.zeros_like(qt)
    gt = jnp.concatenate([gt, zero], axis=0)
    qt = jnp.concatenate([zero, qt], axis=0)
    both_t = jnp.concatenate([gt, qt], axis=1).astype(BF16)
    both = jnp.concatenate([gt.T, qt.T], axis=0).astype(BF16)
    lse = lse_ref[0]

    def visit(j, dqt, mask):
        pair = dot(kv[rows_of(j), :], both_t)
        weights = jnp.exp2(pair[:, LANES:] * SCORE - lse)
        if mask is not None:
            weights = jnp.where(mask, weights, 0.0)
        grads = (weights * (pair[:, :LANES] - delta)).astype(BF16)
        sides = jnp.concatenate([weights.astype(BF16), grads], axis=1)
        dkv[rows_of(j), :] += dot(sides, both)
        return dqt + dot(kvt[HEAD:, rows_of(j)], grads)

    dqt = key_loops(plan, 11, 0, (2, 1), start_ref[0], visit, jnp.zeros((HEAD, LANES), F32))
    for c in (0, 1):
        dq = from_lanes(dqt * HEAD**-0.5, c)
        dq_ref[c] = jnp.concatenate([dq, jnp.zeros((ROWS, HEAD), F32)], axis=1).astype(BF16)

    @pl.when(pl.program_id(0) == 3)
    def _():
        for b, half, place, sent in chunks(plan, 3):
            sent_refs[2 * b + half][sent] = dkv[pl.ds(place, ROWS), :].astype(BF16)


def whole(*shape):
    return pl.BlockSpec(shape, lambda f, plan: (0,) * len(shape))


def tile(*shape):
    return pl.BlockSpec((1,) + shape, lambda f, plan: (f,) + (0,) * len(shape))


def placed(*shape):
    return pl.BlockSpec((2,) + shape, lambda f, plan: (plan[2 * f, 16],) + (0,) * len(shape))


def tiles_call(kernel, supers, outs, more_ins, out_specs, flops, back):
    keys = supers * SUPER
    scratch = [pltpu.VMEM((keys, 2 * HEAD), BF16), pltpu.VMEM((2 * HEAD, keys), BF16)]
    if back:
        scratch.append(pltpu.VMEM((keys, 2 * HEAD), F32))
    ins = [placed(ROWS, QUERY), tile(1, LANES)] + [whole(8, ROWS, 2 * HEAD)] * (2 * supers)
    return pl.pallas_call(
        kernel,
        out_shape=outs,
        grid_spec=pltpu.PrefetchScalarGridSpec(
            num_scalar_prefetch=1,
            grid=(4,),
            in_specs=ins + more_ins,
            out_specs=out_specs,
            scratch_shapes=scratch,
        ),
        compiler_params=params(1, 36 if back else 28),
        cost_estimate=cost(flops, 8e6, 1e7),
    )


TILE_T = jax.ShapeDtypeStruct((4, HEAD, LANES), F32)
TILE_ROW = jax.ShapeDtypeStruct((4, 1, LANES), F32)
STATE = [tile(HEAD, LANES), tile(1, LANES)]


def attend_own(plan, q, start, kvs):
    call = tiles_call(attend_own_kernel, 1, (TILE_T, TILE_ROW), [], tuple(STATE), 4e9, False)
    return call(plan, q, start, *kvs)


def attend_earlier(plan, q, start, kvs, state):
    outs = (jax.ShapeDtypeStruct((8, ROWS, QUERY), BF16), TILE_T, TILE_ROW)
    specs = (placed(ROWS, QUERY),) + tuple(STATE)
    call = tiles_call(attend_earlier_kernel, 2, outs, STATE, specs, 8e9, False)
    return call(plan, q, start, *kvs, *state)


def back(plan, q, start, kvs, grad, out, lse):
    sent = jax.ShapeDtypeStruct((8, ROWS, 2 * HEAD), BF16)
    call = tiles_call(
        back_kernel,
        3,
        [jax.ShapeDtypeStruct((8, ROWS, 4 * HEAD), BF16)] + [sent] * 6,
        [placed(ROWS, QUERY)] + STATE,
        [placed(ROWS, 4 * HEAD)] + [whole(*sent.shape)] * 6,
        30e9,
        True,
    )
    return call(plan, q, start, *kvs, grad, out, lse)


def after(v, *others):
    return lax.optimization_barrier((v,) + others)[0]


def per_device(
    tokens,
    segments,
    attn_gain,
    w_query,
    w_key,
    w_value,
    q_gain,
    k_gain,
    w_out,
    ffn_gain,
    w_gate,
    w_up,
    w_down,
    cotangent,
):
    ylo, z, x, core, yhi = (lax.axis_index(a) for a in ALL)
    sup = ylo * 4 + z

    token_shifts = [shift_x(tokens, d) for d in (1, 2, 3)]
    token_blocks = [[b, swap(b, "core")] for b in [tokens] + token_shifts]
    all_tokens = [b for p in token_blocks for b in p]
    qkv_own = jnp.concatenate(
        [
            w_query.reshape(12, 8, QUERY),
            w_key.reshape(12, 8, HEAD),
            w_value.reshape(12, 8, HEAD),
            jnp.broadcast_to(attn_gain[:, None, None], (12, 8, 1)),
            jnp.broadcast_to(ffn_gain[:, None, None], (12, 8, 1)),
            jnp.zeros((12, 8, HEAD - 2), BF16),
        ],
        axis=-1,
    )
    qkv_own = jnp.pad(jnp.transpose(qkv_own, (1, 0, 2)), ((0, 0), (0, 12), (0, 0)))
    out_own = jnp.transpose(w_out.reshape(4, QUERY, 24), (0, 2, 1))
    out_own = jnp.pad(jnp.concatenate([out_own, out_own], axis=0), ((0, 0), (0, 0), (0, 3 * FREE - QUERY)))
    rows_own = jnp.concatenate(
        [
            part
            for i, w in enumerate((w_gate, w_up, w_down.T))
            for part in (
                w.reshape(24, 8, PART).transpose(1, 0, 2),
                out_own[:, :, i * FREE : (i + 1) * FREE],
            )
        ]
        + [qkv_own],
        axis=-1,
    )
    rows = exchange(rows_own, NEAR)
    ffn_rows = rows[:, :, : 3 * PADDED].reshape(192, 3 * PADDED)
    qkv_rows = rows[:, :12, 3 * PADDED :].reshape(1, 96, 6 * HEAD)
    qkv = exchange(jnp.broadcast_to(qkv_rows, (16, 96, 6 * HEAD)), WIDE)
    qkv = jnp.transpose(qkv.reshape(2, 8, 8, 12, 6 * HEAD), (1, 2, 0, 3, 4)).reshape(WIDTH, 6 * HEAD)
    ffn_full = lax.all_gather(ffn_rows, WIDE, axis=0, tiled=True).reshape(2, WIDTH, 3 * PADDED)
    gain_attn = qkv[:, 5 * HEAD].astype(F32)
    gain_ffn = qkv[:, 5 * HEAD + 1].astype(F32)

    token_index = jnp.arange(segments.shape[0], dtype=jnp.int32)
    begins = jnp.concatenate([jnp.ones((1,), jnp.bool_), segments[1:] != segments[:-1]])
    starts = lax.cummax(jnp.where(begins, token_index, 0), axis=0)
    own_starts = lax.dynamic_slice(
        starts.reshape(8, 8, 2, ROWS), (sup, 0, yhi, 0), (1, 8, 1, ROWS)
    ).reshape(8, ROWS)
    first = sup * SUPER + jnp.arange(8, dtype=jnp.int32) * PAIR + yhi * ROWS
    own_places = first[:, None] + jnp.arange(ROWS, dtype=jnp.int32)[None]
    positions = abs_to_rel((own_places - own_starts).reshape(4, 2, ROWS), x, core)
    frequency = THETA ** (-jnp.arange(HEAD // 2, dtype=F32) * 2.0 / HEAD)
    angles = positions.reshape(4, PAIR, 1).astype(F32) * frequency
    cosine, sine = jnp.cos(angles), jnp.sin(angles)
    cos = jnp.concatenate([cosine] * 4, axis=-1)
    sin = jnp.concatenate([-sine, sine] * 2, axis=-1)
    head_gain = jnp.concatenate([q_gain, q_gain, q_gain, k_gain]).astype(F32)[None]

    window = (sup - 2) * SUPER
    lo = (own_starts[:, 0] - window) // KEY_TILE
    hi = (first + ROWS - 1 - window) // KEY_TILE + 1
    m1 = jnp.clip((own_starts[:, -1] - window + KEY_TILE - 1) // KEY_TILE, lo, hi)
    m2 = jnp.clip((first + 1 - window) // KEY_TILE, m1, hi)
    order = jnp.arange(8, dtype=jnp.int32)
    relative = ((order // 2 - x) % 4) * 2 + (order % 2 + core) % 2
    edge = EARLIER // KEY_TILE
    plan = jnp.stack(
        [first - window, relative]
        + [jnp.minimum(v, edge) for v in (lo, m1, m2, hi)]
        + [jnp.maximum(v - edge, 0) for v in (lo, m1, m2, hi)]
        + [jnp.broadcast_to(yhi, (8,)), lo, m1, m2, hi]
        + [jnp.broadcast_to(core, (8,)), (order // 2 - x) % 4],
        axis=1,
    ).astype(jnp.int32)
    pair_starts = (own_starts - window).reshape(4, 2, 1, ROWS)
    pair_starts = jnp.where(core == 0, pair_starts, pair_starts[:, ::-1])
    start_lanes = jnp.broadcast_to(pair_starts, (4, 2, GROUP, ROWS)).reshape(4, 1, LANES)

    normed, rot_q, kv, raw = project(
        all_tokens, qkv, gain_attn[None], cos, sin, head_gain
    )

    cot_sent = after(cotangent, token_shifts)
    cot_shifts = [shift_x(cot_sent, d) for d in (1, 2, 3)]
    kv, cot_shifts = lax.optimization_barrier((kv, cot_shifts))

    kv_own = [kv, swap(kv, "yhi")]
    kv_sent = kv
    kv_earlier = [shift_super(kv_sent, a, b) for a, b in ((2, 0), (2, 1), (1, 0), (1, 1))]
    state = attend_own(plan, rot_q, start_lanes, kv_own)
    state, kv_earlier = lax.optimization_barrier((state, kv_earlier))
    mix, out_tiles, lse = attend_earlier(plan, rot_q, start_lanes, kv_earlier, state)
    w_out_t = jnp.concatenate(
        [
            lax.dynamic_slice(ffn_full, (x // 2, 0, i * PADDED + PART), (1, WIDTH, FREE))[0]
            for i in range(3)
        ],
        axis=1,
    )[:, :QUERY]
    w_out_t, mix = lax.optimization_barrier((w_out_t, mix))
    cot_blocks = [[b, swap(b, "core")] for b in after([cotangent] + cot_shifts, state)]
    mix, cot_blocks = lax.optimization_barrier((mix, cot_blocks))

    inputs = tokens.astype(F32)
    parts = [None] * 4
    for d in (2, 1, 3, 0):
        parts[d] = out_project(d, mix, w_out_t)
    hidden = inputs + near_sum(near_keep(parts))
    scale_ffn = rms_scale(hidden)
    scaled_ffn = hidden * scale_ffn
    normed_ffn = (scaled_ffn * gain_ffn).astype(BF16)

    ffn_other = swap(normed_ffn, "core")
    near = [shift_x(normed_ffn, d) for d in (1, 3)]
    far = shift_x(after(normed_ffn, ffn_other), 2)
    ffn_blocks = [[b, swap(b, "core")] for b in (near[0], far, near[1])]
    ffn_blocks = [[normed_ffn, ffn_other]] + ffn_blocks
    ffn_calls = [((0, 0), (0, 1)), ((1, 0), (3, 0)), ((2, 0), (1, 1)), ((3, 1), (2, 1))]
    ffn_order = [at for call in ffn_calls for at in call]
    ffn_outs, part_of, out_of = [], {}, {}
    for call in ffn_calls:
        blocks = [ffn_blocks[d][c] for d, c in call]
        if ffn_outs:
            blocks = after(blocks, ffn_outs[-1][0])
        ffn_outs.append(ffn(*blocks, *[cot_blocks[d][c] for d, c in call], ffn_full))
        for i, at in enumerate(call):
            part_of[at], out_of[at] = ffn_outs[-1][i], ffn_outs[-1][2 + i]
    acts, gus = [o[4] for o in ffn_outs], [o[5] for o in ffn_outs]
    kept = near_keep([(part_of[d, 0], part_of[d, 1]) for d in range(4)])
    out_other = [out_of[d, 1] for d in range(4)]
    kept, gus, out_other = lax.optimization_barrier((kept, gus, out_other))
    out_other = swap(jnp.stack(out_other), "core")
    pair_total = near_sum(kept)
    weight_grads = ffn_weights(
        [ffn_blocks[d][c] for d, c in ffn_order],
        [cot_blocks[d][c] for d, c in ffn_order],
        gus,
        acts,
    )
    pair_total, weight_grads, out_other = lax.optimization_barrier((pair_total, weight_grads, out_other))
    ffn_gain_part = jnp.sum(pair_total * scaled_ffn, axis=0)
    grad_hidden = cotangent.astype(F32) + rms_back(pair_total * gain_ffn, hidden, scale_ffn)
    grad_branch = grad_hidden.astype(BF16)
    weight_grads, out_other = lax.optimization_barrier((weight_grads, out_other, grad_branch))[:2]
    ffn_sum = lax.psum_scatter(
        weight_grads.reshape(2 * WIDTH, 3 * PART), WIDE, scatter_dimension=0, tiled=True
    )
    out_kept = jnp.stack([out_of[d, 0] for d in range(4)]).astype(F32) + out_other.astype(F32)
    out_kept = out_kept.astype(BF16)
    branches = [b for p in near_gather(grad_branch) for b in p]
    grad_mix = out_back(branches, w_out_t)
    out_total = near_sum(after([out_kept[d] for d in range(4)], branches))

    back_outs = back(plan, rot_q, start_lanes, kv_earlier + kv_own, grad_mix, out_tiles, lse)
    back_outs, out_total = lax.optimization_barrier((back_outs, out_total))
    grad_q, two_mine, two_theirs, one_mine, one_theirs, mine, theirs = back_outs
    grad_kvs = [
        mine,
        swap(theirs, "yhi"),
        shift_super(one_mine, -1, 0),
        shift_super(one_theirs, -1, 1),
        shift_super(two_mine, -2, 0),
        shift_super(two_theirs, -2, 1),
    ]

    grad_out = out_weights(after(mix, grad_q), branches)
    graw_q, q_gain_part = unproject_q(grad_q, raw, cos, sin, head_gain)
    sent_q = pack_q(normed, graw_q, grad_out)
    grad_kvs, sent_q = lax.optimization_barrier((grad_kvs, sent_q))
    got_q = exchange(sent_q.reshape(8, 192, 2 * QUERY), ("ylo", "z"))

    unprojected = [None] * 2
    for half in (1, 0):
        xs = all_tokens[4 * half : 4 * half + 4]
        unprojected[half] = unproject(half, graw_q, grad_kvs, raw, xs, qkv, cos, sin, head_gain)
    q_gain_part = q_gain_part[0, :HEAD] + q_gain_part[0, HEAD : 2 * HEAD] + q_gain_part[0, 2 * HEAD : QUERY]
    k_gain_part = (unprojected[0][6] + unprojected[1][6])[0, HEAD:]
    head_part = jnp.concatenate([q_gain_part, k_gain_part, jnp.zeros((4,), F32)])
    gain_parts = jnp.concatenate(
        [
            sum(u[5] for u in unprojected),
            ffn_gain_part[None],
            jnp.tile(head_part.reshape(12, 11).T, (1, 128)),
            jnp.zeros((3, WIDTH), F32),
        ],
        axis=0,
    )
    sent = pack_kv(normed, [u[4] for u in unprojected], gain_parts)
    parts = [u[2 * i : 2 * i + 2] for u in unprojected for i in (0, 1)]
    parts, sent = lax.optimization_barrier((parts, sent))
    grad_normed = near_sum(near_keep(parts))
    got = exchange(sent.reshape(8, 192, QUERY), ("ylo", "z"))

    def added(v):
        return jnp.sum(v.astype(F32), axis=0).astype(BF16).reshape(8, 24, -1)

    last = jnp.concatenate([ffn_sum.reshape(8, 24, 3 * PART), added(got_q), added(got)], axis=-1)
    last = exchange(last, NEAR)
    ffn_grad, got = last[:, :, : 3 * PART], last[:, :, 3 * PART :].astype(F32)

    grad_out = got[:, :, QUERY : 2 * QUERY]
    qkv_grad = jnp.concatenate([got[:, :, :QUERY], got[:, :, 2 * QUERY :]], axis=-1)
    here, there = jnp.where(yhi == 0, 0, 1), jnp.where(yhi == 0, 1, 0)

    def half_of(v, axis, which):
        size = v.shape[axis] // 2
        return lax.dynamic_slice_in_dim(v, which * size, size, axis)

    qkv_other = swap(half_of(qkv_grad, 1, there).astype(BF16), "yhi").astype(F32)
    out_other = swap(half_of(grad_out, 0, there).astype(BF16), "yhi").astype(F32)
    qkv_grad = half_of(qkv_grad, 1, here) + qkv_other
    grad_out = half_of(grad_out, 0, here) + out_other
    gains = jnp.sum(qkv_grad[:, :, 5 * HEAD :], axis=0)
    gains = gains[:, :16] + gains[:, 16:32]
    head_gains = gains[:, 2:13].reshape(-1)
    qkv_grad = jnp.transpose(qkv_grad, (1, 0, 2))
    w_out_grad = jnp.transpose(grad_out, (0, 2, 1)).reshape(768, 24)
    w_query_grad = qkv_grad[:, :, :QUERY].reshape(12, -1)
    w_value_grad = qkv_grad[:, :, QUERY : QUERY + HEAD].reshape(12, -1)
    w_key_grad = qkv_grad[:, :, QUERY + HEAD : QUERY + 2 * HEAD].reshape(12, -1)

    output = (hidden + out_total).astype(BF16)
    scale_attn = rms_scale(inputs)
    input_grad = (grad_hidden + rms_back(grad_normed * gain_attn, inputs, scale_attn)).astype(BF16)

    ffn_grad = jnp.transpose(ffn_grad, (1, 0, 2)).astype(F32)
    w_gate_grad, w_up_grad, w_down_grad = (
        ffn_grad[:, :, i * PART : (i + 1) * PART].reshape(24, -1) for i in range(3)
    )
    return (
        output,
        input_grad,
        gains[:, 0],
        w_query_grad,
        w_key_grad,
        w_value_grad,
        head_gains[:HEAD],
        head_gains[HEAD : 2 * HEAD],
        w_out_grad,
        gains[:, 1],
        w_gate_grad,
        w_up_grad,
        w_down_grad.T,
    )


def solution(mesh):
    mesh = Mesh(np.asarray(mesh.devices).reshape(2, 4, 4, 2, 2), ALL)
    rows = P(ALL, None)
    weights = (P("yhi", BLK), P(ALL), P(BLK, "yhi"), P(BLK, "yhi"), P("yhi", BLK))
    placed_in = (rows, P(), P(ALL), rows, rows, rows, P(), P()) + weights + (rows,)
    placed_out = (rows, rows, P(ALL), rows, rows, rows, P(), P()) + weights
    return jax.shard_map(
        per_device, mesh=mesh, in_specs=placed_in, out_specs=placed_out, check_vma=False
    )
```

```python
import functools

import jax
import jax.numpy as jnp
import numpy as np
from jax import lax
from jax.experimental import pallas as pl
from jax.experimental.pallas import tpu as pltpu
from jax.sharding import Mesh
from jax.sharding import PartitionSpec as P

EPS = 1e-05
THETA = 1000000.0
HEAD = 64
ROWS = 128
PAIR = 2 * ROWS
GROUP = 3
QUERY = GROUP * HEAD
LANES = PAIR * GROUP
KEY_TILE = 512
SUPER = 2048
EARLIER = 2 * SUPER
PART = 432
PADDED = 512
FREE = PADDED - PART
WIDTH = 1536
ALL = ("ylo", "z", "x", "core", "yhi")
BLK = ("ylo", "z", "x", "core")
WIDE = ("yhi", "ylo", "z")
NEAR = ("x", "core")
NN = (((1,), (0,)), ((), ()))
NT = (((1,), (1,)), ((), ()))
TN = (((0,), (0,)), ((), ()))
F32 = jnp.float32
BF16 = jnp.bfloat16
SCORE = HEAD**-0.5 * 1.4426950408889634


def dot(a, b, numbers=NN):
    return lax.dot_general(a, b, numbers, preferred_element_type=F32)


def rms_scale(v):
    return lax.rsqrt(jnp.mean(v * v, axis=-1, keepdims=True) + EPS)


def rms_back(grad, v, scale):
    inner = jnp.mean(grad * v, axis=-1, keepdims=True)
    return scale * (grad - v * scale * scale * inner)


def shift_x(v, distance):
    return lax.ppermute(v, "x", [((i + distance) % 4, i) for i in range(4)])


def swap(v, axis):
    return lax.ppermute(v, axis, [(0, 1), (1, 0)])


def shift_super(v, distance, other):
    pairs = [
        (2 * i + h, 2 * (i + distance) + (h + other) % 2)
        for i in range(8)
        for h in (0, 1)
        if 0 <= i + distance < 8
    ]
    return lax.ppermute(v, ("ylo", "z", "yhi"), pairs)


def exchange(v, axes):
    return lax.all_to_all(v, axes, split_axis=0, concat_axis=0, tiled=True)


def near_gather(v):
    blocks = [v] + [shift_x(v, d) for d in (1, 2, 3)]
    return [[b, swap(b, "core")] for b in blocks]


def near_keep(parts):
    return [
        (own.astype(F32) + swap(other, "core").astype(F32)).astype(BF16) for own, other in parts
    ]


def near_sum(kept):
    total = kept[0].astype(F32)
    for d in (1, 2, 3):
        total = total + shift_x(kept[d], -d).astype(F32)
    return total


def rel_to_abs(v, x, core):
    v = jnp.where(core == 0, v, v[:, ::-1])
    return lax.dynamic_slice_in_dim(jnp.concatenate([v, v], axis=0), (4 - x) % 4, 4, 0)


def abs_to_rel(v, x, core):
    v = jnp.where(core == 0, v, v[:, ::-1])
    return lax.dynamic_slice_in_dim(jnp.concatenate([v, v], axis=0), x, 4, 0)


def params(steps, mib):
    return pltpu.CompilerParams(
        dimension_semantics=("arbitrary",) * steps, vmem_limit_bytes=mib * 2**20
    )


def cost(flops, moved, exps=0):
    return pl.CostEstimate(flops=int(flops), bytes_accessed=int(moved), transcendentals=int(exps))


def all_of(*shape):
    return pl.BlockSpec(shape, lambda *i: (0,) * len(shape))


IN_VMEM = pl.BlockSpec(memory_space=pltpu.VMEM)


def stacked(a_ref, b_ref):
    return jnp.concatenate([a_ref[...], b_ref[...]], axis=0)


def head_sums(v):
    shape = (v.shape[1], v.shape[1])
    lane = lax.shift_right_logical(lax.broadcasted_iota(jnp.int32, shape, 1), 6)
    row = lax.shift_right_logical(lax.broadcasted_iota(jnp.int32, shape, 0), 6)
    ones = jnp.where(lane == row, 1.0, 0.0).astype(BF16)
    high = v.astype(BF16)
    low = (v - high.astype(F32)).astype(BF16)
    return dot(high, ones) + dot(low, ones)


def half_turn(v):
    lane = lax.broadcasted_iota(jnp.int32, v.shape, 1)
    return jnp.where(
        (lane & (HEAD - 1)) < HEAD // 2,
        pltpu.roll(v, v.shape[1] - HEAD // 2, 1),
        pltpu.roll(v, HEAD // 2, 1),
    )


def twice(v):
    return jnp.concatenate([v, v], axis=1)


def project_kernel(*refs):
    xs, (w_ref, gain_ref, cos_ref, sin_ref, head_gain_ref) = refs[:8], refs[8:13]
    normed_ref, q_ref, kv_ref, raw_ref = refs[13:]
    lane = lax.broadcasted_iota(jnp.int32, (PAIR, 2 * HEAD), 1)
    for d in range(4):
        rows = slice(d * PAIR, (d + 1) * PAIR)
        tiles = slice(2 * d, 2 * d + 2)
        x = stacked(*xs[tiles]).astype(F32)
        normed = (x * rms_scale(x) * gain_ref[...]).astype(BF16)
        normed_ref[rows, :] = normed
        raw = dot(normed, w_ref[...])
        heads = raw[:, : 4 * HEAD]
        raw_ref[d] = heads
        scale = lax.rsqrt(head_sums(heads * heads) * (1.0 / HEAD) + EPS)
        v = heads * scale * head_gain_ref[...]
        turned = v * twice(cos_ref[d]) + half_turn(v) * twice(sin_ref[d])
        q_ref[tiles] = turned[:, :QUERY].astype(BF16).reshape(2, ROWS, QUERY)
        kv = jnp.where(lane < HEAD, raw[:, 4 * HEAD :], turned[:, 2 * HEAD :])
        kv_ref[tiles] = kv.astype(BF16).reshape(2, ROWS, 2 * HEAD)


def project(xs, w, gain, cos, sin, head_gain):
    return pl.pallas_call(
        project_kernel,
        out_shape=(
            jax.ShapeDtypeStruct((4 * PAIR, WIDTH), BF16),
            jax.ShapeDtypeStruct((8, ROWS, QUERY), BF16),
            jax.ShapeDtypeStruct((8, ROWS, 2 * HEAD), BF16),
            jax.ShapeDtypeStruct((4, PAIR, 4 * HEAD), F32),
        ),
        in_specs=[IN_VMEM] * 13,
        out_specs=(IN_VMEM,) * 4,
        compiler_params=params(0, 20),
        cost_estimate=cost(8 * PAIR * WIDTH * 384, 1e7),
    )(*xs, w, gain, cos, sin, head_gain)


def turned_back(g, raw, cos, sin, head_gain):
    width = g.shape[1]
    g = g * cos - half_turn(g) * sin
    scale = lax.rsqrt(head_sums(raw * raw) * (1.0 / HEAD) + EPS)
    gain = jnp.sum(g * raw * scale, axis=0, keepdims=True)
    e = g * head_gain[:, -width:]
    inner = head_sums(e * raw) * (1.0 / HEAD)
    return scale * (e - raw * scale * scale * inner), gain


def unproject_q_kernel(gq_ref, raw_ref, cos_ref, sin_ref, head_gain_ref, graw_ref, gain_ref):
    gains = 0.0
    for d in range(4):
        g = gq_ref[2 * d : 2 * d + 2].reshape(PAIR, 4 * HEAD).astype(F32)
        graw, gain = turned_back(
            g, raw_ref[d], twice(cos_ref[d]), twice(sin_ref[d]), head_gain_ref[...]
        )
        graw_ref[d] = graw.astype(BF16)
        gains = gains + gain
    gain_ref[...] = gains


def unproject_q(gq, raw, cos, sin, head_gain):
    return pl.pallas_call(
        unproject_q_kernel,
        out_shape=(
            jax.ShapeDtypeStruct((4, PAIR, 4 * HEAD), BF16),
            jax.ShapeDtypeStruct((1, 4 * HEAD), F32),
        ),
        compiler_params=params(0, 20),
        cost_estimate=cost(1e8, 4e6),
    )(gq, raw, cos, sin, head_gain)


def unproject_kernel(half, *refs):
    graw_q_ref, g_refs, raw_ref, xs, (w_ref, cos_ref, sin_ref, head_gain_ref) = (
        refs[0], refs[1:7], refs[7], refs[8:12], refs[12:16],
    )
    parts, (gkv_ref, attn_ref, gain_ref) = refs[16:20], refs[20:]
    attn, gains = 0.0, 0.0
    lane = lax.broadcasted_iota(jnp.int32, (PAIR, 2 * HEAD), 1)
    for i in range(2):
        tiles = slice(2 * i, 2 * i + 2)
        at = 2 * half + i
        there = slice(2 * at, 2 * at + 2)
        gkv = g_refs[0][there].astype(F32)
        for ref in g_refs[1:]:
            gkv = gkv + ref[there].astype(F32)
        gkv = gkv.reshape(PAIR, 2 * HEAD)
        gk = jnp.where(lane < HEAD, 0.0, (gkv * HEAD**-0.5).astype(BF16).astype(F32))
        graw_k, gain = turned_back(
            gk, raw_ref[at][:, 2 * HEAD :], cos_ref[at], sin_ref[at], head_gain_ref[...]
        )
        gains = gains + gain
        graw_q = graw_q_ref[at].astype(F32)
        graw = [
            graw_q[:, : 2 * HEAD],
            jnp.where(lane < HEAD, graw_q[:, 2 * HEAD :], graw_k),
            jnp.where(lane < HEAD, gkv, 0.0),
        ]
        gkv_ref[i * PAIR : (i + 1) * PAIR, :] = jnp.where(lane < HEAD, gkv, graw_k).astype(BF16)
        grad = dot(jnp.concatenate(graw, axis=1).astype(BF16), w_ref[...], NT)
        x = stacked(*xs[tiles]).astype(F32)
        attn = attn + jnp.sum(grad * x * rms_scale(x), axis=0, keepdims=True)
        grad = grad.astype(BF16)
        parts[2 * i][...] = grad[:ROWS]
        parts[2 * i + 1][...] = grad[ROWS:]
    attn_ref[...] = attn
    gain_ref[...] = gains


def unproject(half, graw_q, gkvs, raw, xs, w, cos, sin, head_gain):
    outs = (jax.ShapeDtypeStruct((ROWS, WIDTH), BF16),) * 4 + (
        jax.ShapeDtypeStruct((2 * PAIR, 2 * HEAD), BF16),
        jax.ShapeDtypeStruct((1, WIDTH), F32),
        jax.ShapeDtypeStruct((1, 2 * HEAD), F32),
    )
    return pl.pallas_call(
        functools.partial(unproject_kernel, half),
        out_shape=outs,
        in_specs=[IN_VMEM] * 16,
        out_specs=(IN_VMEM,) * 7,
        compiler_params=params(0, 16),
        cost_estimate=cost(4 * PAIR * WIDTH * 384, 8e6),
    )(graw_q, *gkvs, raw, *xs, w, cos, sin, head_gain)


def ffn_kernel(
    x0_ref, x1_ref, c0_ref, c1_ref, w_ref, part0_ref, part1_ref, out0_ref, out1_ref, act_ref, gu_ref
):
    x, cot = stacked(x0_ref, x1_ref), stacked(c0_ref, c1_ref)
    own = lax.broadcasted_iota(jnp.int32, (PAIR, PADDED), 1) < PART
    part, out_part = 0.0, 0.0
    for y in range(2):
        gate_up = dot(x, w_ref[y, :, : 2 * PADDED])
        gate, up = gate_up[:, :PADDED], gate_up[:, PADDED:]
        grad_act = jnp.where(own, dot(cot, w_ref[y, :, 2 * PADDED :]), 0.0)
        sig = 1.0 / (1.0 + jnp.exp(-gate))
        silu = gate * sig
        act = jnp.where(own, silu * up, 0.0).astype(BF16)
        act_ref[y] = act
        out_part = out_part + dot(act, w_ref[y, :, 2 * PADDED :], NT)
        grad_gate = jnp.where(own, grad_act * up * sig * (1.0 + gate * (1.0 - sig)), 0.0)
        grad_up = jnp.where(own, grad_act * silu, 0.0)
        grads = jnp.concatenate([grad_gate, grad_up], axis=1).astype(BF16)
        gu_ref[y] = grads
        part = part + dot(grads, w_ref[y, :, : 2 * PADDED], NT)
    part, out_part = part.astype(BF16), out_part.astype(BF16)
    part0_ref[...] = part[:ROWS]
    part1_ref[...] = part[ROWS:]
    out0_ref[...] = out_part[:ROWS]
    out1_ref[...] = out_part[ROWS:]


def ffn(x0, x1, c0, c1, w):
    return pl.pallas_call(
        ffn_kernel,
        out_shape=(jax.ShapeDtypeStruct((ROWS, WIDTH), BF16),) * 4
        + (
            jax.ShapeDtypeStruct((2, PAIR, PADDED), BF16),
            jax.ShapeDtypeStruct((2, PAIR, 2 * PADDED), BF16),
        ),
        in_specs=[IN_VMEM] * 5,
        out_specs=(IN_VMEM,) * 6,
        compiler_params=params(0, 36),
        cost_estimate=cost(2 * 2 * PAIR * WIDTH * 6 * PADDED, 14e6),
    )(x0, x1, c0, c1, w)


def ffn_weights_kernel(*refs):
    xs, cs, gus, acts, out_ref = refs[:8], refs[8:16], refs[16:20], refs[20:24], refs[24]
    def all_tokens(refs):
        return jnp.concatenate([ref[...] for ref in refs], axis=0)

    grad_gu = dot(all_tokens(xs), all_tokens([g.at[0] for g in gus]), TN)
    grad_d = dot(all_tokens(cs), all_tokens([a.at[0] for a in acts]), TN)
    out_ref[0, :, :PART] = grad_gu[:, :PART].astype(BF16)
    out_ref[0, :, PART : 2 * PART] = grad_gu[:, PADDED : PADDED + PART].astype(BF16)
    out_ref[0, :, 2 * PART :] = grad_d[:, :PART].astype(BF16)


def ffn_weights(xs, cs, gus, acts):
    tall = 256
    rows = pl.BlockSpec((ROWS, tall), lambda y, m: (0, m))
    return pl.pallas_call(
        ffn_weights_kernel,
        out_shape=jax.ShapeDtypeStruct((2, WIDTH, 3 * PART), BF16),
        grid=(2, WIDTH // tall),
        in_specs=[rows] * 16
        + [pl.BlockSpec((1, PAIR, 2 * PADDED), lambda y, m: (y, 0, 0))] * 4
        + [pl.BlockSpec((1, PAIR, PADDED), lambda y, m: (y, 0, 0))] * 4,
        out_specs=pl.BlockSpec((1, tall, 3 * PART), lambda y, m: (y, m, 0)),
        compiler_params=params(2, 28),
        cost_estimate=cost(2 * 2 * 1024 * WIDTH * 3 * PADDED, 24e6),
    )(*xs, *cs, *gus, *acts)


def out_project_kernel(mix_ref, w_ref, part0_ref, part1_ref):
    part = dot(mix_ref[...].reshape(PAIR, QUERY), w_ref[...], NT).astype(BF16)
    part0_ref[...] = part[:ROWS]
    part1_ref[...] = part[ROWS:]


def out_project(d, mix, w):
    rows = pl.BlockSpec((ROWS, WIDTH), lambda i: (0, 0))
    return pl.pallas_call(
        out_project_kernel,
        out_shape=(jax.ShapeDtypeStruct((ROWS, WIDTH), BF16),) * 2,
        grid=(1,),
        in_specs=[
            pl.BlockSpec((2, ROWS, QUERY), lambda i: (d, 0, 0)),
            pl.BlockSpec((WIDTH, QUERY), lambda i: (0, 0)),
        ],
        out_specs=(rows, rows),
        compiler_params=params(1, 16),
        cost_estimate=cost(2 * PAIR * WIDTH * QUERY, 2e6),
    )(mix, w)


def out_back_kernel(w_ref, *refs):
    for t in range(8):
        refs[8][t] = dot(refs[t][...], w_ref[...]).astype(BF16)


def out_back(branches, w):
    return pl.pallas_call(
        out_back_kernel,
        out_shape=jax.ShapeDtypeStruct((8, ROWS, QUERY), BF16),
        compiler_params=params(0, 16),
        cost_estimate=cost(8 * PAIR * WIDTH * QUERY, 4e6),
    )(w, *branches)


def out_weights_kernel(mix_ref, *refs):
    branch = jnp.concatenate([b[...] for b in refs[:8]], axis=0)
    refs[8][...] = dot(branch, mix_ref[...].reshape(8 * ROWS, QUERY), TN)


def out_weights(mix, branches):
    return pl.pallas_call(
        out_weights_kernel,
        out_shape=jax.ShapeDtypeStruct((WIDTH, QUERY), F32),
        compiler_params=params(0, 24),
        cost_estimate=cost(2 * 1024 * WIDTH * QUERY, 4e6),
    )(mix, *branches)


def pack_q_kernel(normed_ref, graw_ref, out_grad_ref, sent_ref):
    graw = graw_ref[...].reshape(8 * ROWS, 4 * HEAD)
    sent_ref[:, :QUERY] = dot(normed_ref[...], graw, TN)[:, :QUERY].astype(BF16)
    sent_ref[:, QUERY:] = out_grad_ref[...].astype(BF16)


def pack_q(normed, graw, out_grad):
    tall = 256
    return pl.pallas_call(
        pack_q_kernel,
        out_shape=jax.ShapeDtypeStruct((WIDTH, 2 * QUERY), BF16),
        grid=(WIDTH // tall,),
        in_specs=[
            pl.BlockSpec((8 * ROWS, tall), lambda m: (0, m)),
            all_of(4, PAIR, 4 * HEAD),
            pl.BlockSpec((tall, QUERY), lambda m: (m, 0)),
        ],
        out_specs=pl.BlockSpec((tall, 2 * QUERY), lambda m: (m, 0)),
        compiler_params=params(1, 16),
        cost_estimate=cost(2 * 1024 * WIDTH * 256, 8e6),
    )(normed, graw, out_grad)


def pack_kv_kernel(normed_ref, gkv0_ref, gkv1_ref, gains_ref, sent_ref):
    grad = dot(normed_ref[...], stacked(gkv0_ref, gkv1_ref), TN)
    gains = gains_ref[...]
    high = gains.astype(BF16).astype(F32)
    gains = jnp.concatenate([high, gains - high, jnp.zeros((HEAD - 32, gains.shape[1]), F32)], axis=0)
    sent_ref[:, : 2 * HEAD] = grad.astype(BF16)
    sent_ref[:, 2 * HEAD :] = gains.T.astype(BF16)


def pack_kv(normed, gkvs, gains):
    tall = 256
    return pl.pallas_call(
        pack_kv_kernel,
        out_shape=jax.ShapeDtypeStruct((WIDTH, QUERY), BF16),
        grid=(WIDTH // tall,),
        in_specs=[
            pl.BlockSpec((8 * ROWS, tall), lambda m: (0, m)),
            all_of(4 * ROWS, 2 * HEAD),
            all_of(4 * ROWS, 2 * HEAD),
            pl.BlockSpec((16, tall), lambda m: (0, m)),
        ],
        out_specs=pl.BlockSpec((tall, QUERY), lambda m: (m, 0)),
        compiler_params=params(1, 16),
        cost_estimate=cost(2 * 1024 * WIDTH * 128, 6e6),
    )(normed, *gkvs, gains)


def to_lanes(v):
    parts = []
    for c in (0, 1):
        t = v[c].astype(F32).T
        parts += [t[g * HEAD : (g + 1) * HEAD] for g in range(GROUP)]
    return jnp.concatenate(parts, axis=1)


def from_lanes(t, c):
    at = [(c * GROUP + g) * ROWS for g in range(GROUP)]
    return jnp.concatenate([t[:, i : i + ROWS] for i in at], axis=0).T


def key_loops(plan, at, base, unrolls, start, visit, state):
    p = 2 * pl.program_id(0)
    lo, m1, hi = plan[p, at], plan[p + 1, at + 1], plan[p + 1, at + 3]
    m2 = jnp.maximum(plan[p, at + 2], m1)
    core = plan[0, 15]
    lane = lax.broadcasted_iota(jnp.int32, (1, LANES), 1)
    place = lax.rem(lane, ROWS) + jnp.where(lane < LANES // 2, plan[p + core, 0], plan[p + 1 - core, 0])

    def masked(j, state):
        key = lax.broadcasted_iota(jnp.int32, (KEY_TILE, LANES), 0) + (j * KEY_TILE + base)
        return visit(j, state, (key >= start) & (key <= place))

    state = lax.fori_loop(lo, m1, masked, state)
    done = m1
    for unroll in unrolls:
        steps = lax.div(m2 - done, unroll)

        def several(i, state, done=done, unroll=unroll):
            for k in range(unroll):
                state = visit(done + unroll * i + k, state, None)
            return state

        state = lax.fori_loop(0, steps, several, state)
        done = done + unroll * steps
    return lax.fori_loop(m2, hi, masked, state)


def rows_of(j):
    return pl.ds(pl.multiple_of(j * KEY_TILE, KEY_TILE), KEY_TILE)


def chunks(plan, supers):
    for b in range(supers):
        for half in (0, 1):
            for f in range(8):
                side = plan[0, 10] if half == 0 else 1 - plan[0, 10]
                yield b, half, pl.multiple_of(b * SUPER + f * PAIR + side * ROWS, ROWS), plan[f, 1]


def line_up(plan, kv_refs, kv, kvt):
    @pl.when(pl.program_id(0) == 0)
    def _():
        for b, half, place, sent in chunks(plan, len(kv_refs) // 2):
            block = kv_refs[2 * b + half][sent]
            kv[pl.ds(place, ROWS), :] = block
            kvt[:, pl.ds(place, ROWS)] = block.astype(F32).T.astype(BF16)


def attend_body(at, base, plan, q_ref, start_ref, kv, kvt, state):
    qt = to_lanes(q_ref)
    qt = jnp.concatenate([jnp.zeros_like(qt), qt], axis=0).astype(BF16)

    def visit(j, state, mask):
        total, accum = state
        weights = jnp.exp2(dot(kv[rows_of(j), :], qt) * SCORE)
        if mask is not None:
            weights = jnp.where(mask, weights, 0.0)
        total = total + jnp.sum(weights, axis=0, keepdims=True)
        return total, accum + dot(kvt[:HEAD, rows_of(j)], weights.astype(BF16))

    return key_loops(plan, at, base, (4, 2, 1), start_ref[0], visit, state)


def attend_own_kernel(plan, q_ref, start_ref, *refs):
    kv_refs, (accum_ref, total_ref, kv, kvt) = refs[:2], refs[2:]
    line_up(plan, kv_refs, kv, kvt)
    state = (jnp.zeros((1, LANES), F32), jnp.zeros((HEAD, LANES), F32))
    total, accum = attend_body(6, EARLIER, plan, q_ref, start_ref, kv, kvt, state)
    accum_ref[0] = accum
    total_ref[0] = total


def attend_earlier_kernel(plan, q_ref, start_ref, *refs):
    kv_refs, (accum_ref, total_ref, mix_ref, out_ref, lse_ref, kv, kvt) = refs[:4], refs[4:]
    line_up(plan, kv_refs, kv, kvt)
    state = (total_ref[0], accum_ref[0])
    total, accum = attend_body(2, 0, plan, q_ref, start_ref, kv, kvt, state)
    out = accum / total
    out_ref[0] = out
    for c in (0, 1):
        mix_ref[c] = from_lanes(out, c).astype(BF16)
    lse_ref[0] = jnp.log2(total)


def back_kernel(plan, q_ref, start_ref, *refs):
    kv_refs, (g_ref, out_ref, lse_ref, dq_ref), sent_refs, (kv, kvt, dkv) = (
        refs[:6], refs[6:10], refs[10:16], refs[16:],
    )
    line_up(plan, kv_refs, kv, kvt)

    @pl.when(pl.program_id(0) == 0)
    def _():
        dkv[...] = jnp.zeros_like(dkv)

    qt = to_lanes(q_ref)
    gt = to_lanes(g_ref)
    delta = jnp.sum(gt * out_ref[0], axis=0, keepdims=True)
    zero = jnp.zeros_like(qt)
    gt = jnp.concatenate([gt, zero], axis=0)
    qt = jnp.concatenate([zero, qt], axis=0)
    both_t = jnp.concatenate([gt, qt], axis=1).astype(BF16)
    both = jnp.concatenate([gt.T, qt.T], axis=0).astype(BF16)
    lse = lse_ref[0]

    def visit(j, dqt, mask):
        pair = dot(kv[rows_of(j), :], both_t)
        weights = jnp.exp2(pair[:, LANES:] * SCORE - lse)
        if mask is not None:
            weights = jnp.where(mask, weights, 0.0)
        grads = (weights * (pair[:, :LANES] - delta)).astype(BF16)
        sides = jnp.concatenate([weights.astype(BF16), grads], axis=1)
        dkv[rows_of(j), :] += dot(sides, both)
        return dqt + dot(kvt[HEAD:, rows_of(j)], grads)

    dqt = key_loops(plan, 11, 0, (2, 1), start_ref[0], visit, jnp.zeros((HEAD, LANES), F32))
    for c in (0, 1):
        dq = from_lanes(dqt * HEAD**-0.5, c)
        dq_ref[c] = jnp.concatenate([dq, jnp.zeros((ROWS, HEAD), F32)], axis=1).astype(BF16)

    @pl.when(pl.program_id(0) == 3)
    def _():
        for b, half, place, sent in chunks(plan, 3):
            sent_refs[2 * b + half][sent] = dkv[pl.ds(place, ROWS), :].astype(BF16)


def whole(*shape):
    return pl.BlockSpec(shape, lambda f, plan: (0,) * len(shape))


def tile(*shape):
    return pl.BlockSpec((1,) + shape, lambda f, plan: (f,) + (0,) * len(shape))


def placed(*shape):
    return pl.BlockSpec((2,) + shape, lambda f, plan: (plan[2 * f, 16],) + (0,) * len(shape))


def tiles_call(kernel, supers, outs, more_ins, out_specs, flops, back):
    keys = supers * SUPER
    scratch = [pltpu.VMEM((keys, 2 * HEAD), BF16), pltpu.VMEM((2 * HEAD, keys), BF16)]
    if back:
        scratch.append(pltpu.VMEM((keys, 2 * HEAD), F32))
    ins = [placed(ROWS, QUERY), tile(1, LANES)] + [whole(8, ROWS, 2 * HEAD)] * (2 * supers)
    return pl.pallas_call(
        kernel,
        out_shape=outs,
        grid_spec=pltpu.PrefetchScalarGridSpec(
            num_scalar_prefetch=1,
            grid=(4,),
            in_specs=ins + more_ins,
            out_specs=out_specs,
            scratch_shapes=scratch,
        ),
        compiler_params=params(1, 30 if back else 20),
        cost_estimate=cost(flops, 8e6, 1e7),
    )


TILE_T = jax.ShapeDtypeStruct((4, HEAD, LANES), F32)
TILE_ROW = jax.ShapeDtypeStruct((4, 1, LANES), F32)
STATE = [tile(HEAD, LANES), tile(1, LANES)]


def attend_own(plan, q, start, kvs):
    call = tiles_call(attend_own_kernel, 1, (TILE_T, TILE_ROW), [], tuple(STATE), 4e9, False)
    return call(plan, q, start, *kvs)


def attend_earlier(plan, q, start, kvs, state):
    outs = (jax.ShapeDtypeStruct((8, ROWS, QUERY), BF16), TILE_T, TILE_ROW)
    specs = (placed(ROWS, QUERY),) + tuple(STATE)
    call = tiles_call(attend_earlier_kernel, 2, outs, STATE, specs, 8e9, False)
    return call(plan, q, start, *kvs, *state)


def back(plan, q, start, kvs, grad, out, lse):
    sent = jax.ShapeDtypeStruct((8, ROWS, 2 * HEAD), BF16)
    call = tiles_call(
        back_kernel,
        3,
        [jax.ShapeDtypeStruct((8, ROWS, 4 * HEAD), BF16)] + [sent] * 6,
        [placed(ROWS, QUERY)] + STATE,
        [placed(ROWS, 4 * HEAD)] + [whole(*sent.shape)] * 6,
        30e9,
        True,
    )
    return call(plan, q, start, *kvs, grad, out, lse)


def after(v, *others):
    return lax.optimization_barrier((v,) + others)[0]


def per_device(
    tokens,
    segments,
    attn_gain,
    w_query,
    w_key,
    w_value,
    q_gain,
    k_gain,
    w_out,
    ffn_gain,
    w_gate,
    w_up,
    w_down,
    cotangent,
):
    ylo, z, x, core, yhi = (lax.axis_index(a) for a in ALL)
    sup = ylo * 4 + z

    token_shifts = [shift_x(tokens, d) for d in (1, 2, 3)]
    token_blocks = [[b, swap(b, "core")] for b in [tokens] + token_shifts]
    all_tokens = [b for p in token_blocks for b in p]
    qkv_own = jnp.concatenate(
        [
            w_query.reshape(12, 8, QUERY),
            w_key.reshape(12, 8, HEAD),
            w_value.reshape(12, 8, HEAD),
            jnp.broadcast_to(attn_gain[:, None, None], (12, 8, 1)),
            jnp.broadcast_to(ffn_gain[:, None, None], (12, 8, 1)),
            jnp.zeros((12, 8, HEAD - 2), BF16),
        ],
        axis=-1,
    )
    qkv_own = jnp.pad(jnp.transpose(qkv_own, (1, 0, 2)), ((0, 0), (0, 12), (0, 0)))
    out_own = jnp.transpose(w_out.reshape(4, QUERY, 24), (0, 2, 1))
    out_own = jnp.pad(jnp.concatenate([out_own, out_own], axis=0), ((0, 0), (0, 0), (0, 3 * FREE - QUERY)))
    rows_own = jnp.concatenate(
        [
            part
            for i, w in enumerate((w_gate, w_up, w_down.T))
            for part in (
                w.reshape(24, 8, PART).transpose(1, 0, 2),
                out_own[:, :, i * FREE : (i + 1) * FREE],
            )
        ]
        + [qkv_own],
        axis=-1,
    )
    rows = exchange(rows_own, NEAR)
    ffn_rows = rows[:, :, : 3 * PADDED].reshape(192, 3 * PADDED)
    qkv_rows = rows[:, :12, 3 * PADDED :].reshape(1, 96, 6 * HEAD)
    qkv = exchange(jnp.broadcast_to(qkv_rows, (16, 96, 6 * HEAD)), WIDE)
    qkv = jnp.transpose(qkv.reshape(2, 8, 8, 12, 6 * HEAD), (1, 2, 0, 3, 4)).reshape(WIDTH, 6 * HEAD)
    ffn_full = lax.all_gather(ffn_rows, WIDE, axis=0, tiled=True).reshape(2, WIDTH, 3 * PADDED)
    gain_attn = qkv[:, 5 * HEAD].astype(F32)
    gain_ffn = qkv[:, 5 * HEAD + 1].astype(F32)

    token_index = jnp.arange(segments.shape[0], dtype=jnp.int32)
    begins = jnp.concatenate([jnp.ones((1,), jnp.bool_), segments[1:] != segments[:-1]])
    starts = lax.cummax(jnp.where(begins, token_index, 0), axis=0)
    own_starts = lax.dynamic_slice(
        starts.reshape(8, 8, 2, ROWS), (sup, 0, yhi, 0), (1, 8, 1, ROWS)
    ).reshape(8, ROWS)
    first = sup * SUPER + jnp.arange(8, dtype=jnp.int32) * PAIR + yhi * ROWS
    own_places = first[:, None] + jnp.arange(ROWS, dtype=jnp.int32)[None]
    positions = abs_to_rel((own_places - own_starts).reshape(4, 2, ROWS), x, core)
    frequency = THETA ** (-jnp.arange(HEAD // 2, dtype=F32) * 2.0 / HEAD)
    angles = positions.reshape(4, PAIR, 1).astype(F32) * frequency
    cosine, sine = jnp.cos(angles), jnp.sin(angles)
    cos = jnp.concatenate([cosine] * 4, axis=-1)
    sin = jnp.concatenate([-sine, sine] * 2, axis=-1)
    head_gain = jnp.concatenate([q_gain, q_gain, q_gain, k_gain]).astype(F32)[None]

    window = (sup - 2) * SUPER
    lo = (own_starts[:, 0] - window) // KEY_TILE
    hi = (first + ROWS - 1 - window) // KEY_TILE + 1
    m1 = jnp.clip((own_starts[:, -1] - window + KEY_TILE - 1) // KEY_TILE, lo, hi)
    m2 = jnp.clip((first + 1 - window) // KEY_TILE, m1, hi)
    order = jnp.arange(8, dtype=jnp.int32)
    relative = ((order // 2 - x) % 4) * 2 + (order % 2 + core) % 2
    edge = EARLIER // KEY_TILE
    plan = jnp.stack(
        [first - window, relative]
        + [jnp.minimum(v, edge) for v in (lo, m1, m2, hi)]
        + [jnp.maximum(v - edge, 0) for v in (lo, m1, m2, hi)]
        + [jnp.broadcast_to(yhi, (8,)), lo, m1, m2, hi]
        + [jnp.broadcast_to(core, (8,)), (order // 2 - x) % 4],
        axis=1,
    ).astype(jnp.int32)
    pair_starts = (own_starts - window).reshape(4, 2, 1, ROWS)
    pair_starts = jnp.where(core == 0, pair_starts, pair_starts[:, ::-1])
    start_lanes = jnp.broadcast_to(pair_starts, (4, 2, GROUP, ROWS)).reshape(4, 1, LANES)

    normed, rot_q, kv, raw = project(
        all_tokens, qkv, gain_attn[None], cos, sin, head_gain
    )

    cot_sent = after(cotangent, token_shifts)
    cot_shifts = [shift_x(cot_sent, d) for d in (1, 2, 3)]
    kv, cot_shifts = lax.optimization_barrier((kv, cot_shifts))

    kv_own = [kv, swap(kv, "yhi")]
    kv_sent = kv
    kv_earlier = [shift_super(kv_sent, a, b) for a, b in ((2, 0), (2, 1), (1, 0), (1, 1))]
    state = attend_own(plan, rot_q, start_lanes, kv_own)
    state, kv_earlier = lax.optimization_barrier((state, kv_earlier))
    mix, out_tiles, lse = attend_earlier(plan, rot_q, start_lanes, kv_earlier, state)
    w_out_t = jnp.concatenate(
        [
            lax.dynamic_slice(ffn_full, (x // 2, 0, i * PADDED + PART), (1, WIDTH, FREE))[0]
            for i in range(3)
        ],
        axis=1,
    )[:, :QUERY]
    w_out_t, mix = lax.optimization_barrier((w_out_t, mix))
    cot_blocks = [[b, swap(b, "core")] for b in after([cotangent] + cot_shifts, state)]
    mix, cot_blocks = lax.optimization_barrier((mix, cot_blocks))

    inputs = tokens.astype(F32)
    parts = [None] * 4
    for d in (2, 1, 3, 0):
        parts[d] = out_project(d, mix, w_out_t)
    hidden = inputs + near_sum(near_keep(parts))
    scale_ffn = rms_scale(hidden)
    scaled_ffn = hidden * scale_ffn
    normed_ffn = (scaled_ffn * gain_ffn).astype(BF16)

    ffn_other = swap(normed_ffn, "core")
    near = [shift_x(normed_ffn, d) for d in (1, 3)]
    far = shift_x(after(normed_ffn, ffn_other), 2)
    ffn_blocks = [[b, swap(b, "core")] for b in (near[0], far, near[1])]
    ffn_blocks = [[normed_ffn, ffn_other]] + ffn_blocks
    ffn_calls = [((0, 0), (0, 1)), ((1, 0), (3, 0)), ((2, 0), (1, 1)), ((3, 1), (2, 1))]
    ffn_order = [at for call in ffn_calls for at in call]
    ffn_outs, part_of, out_of = [], {}, {}
    for call in ffn_calls:
        blocks = [ffn_blocks[d][c] for d, c in call]
        if ffn_outs:
            blocks = after(blocks, ffn_outs[-1][0])
        ffn_outs.append(ffn(*blocks, *[cot_blocks[d][c] for d, c in call], ffn_full))
        for i, at in enumerate(call):
            part_of[at], out_of[at] = ffn_outs[-1][i], ffn_outs[-1][2 + i]
    acts, gus = [o[4] for o in ffn_outs], [o[5] for o in ffn_outs]
    kept = near_keep([(part_of[d, 0], part_of[d, 1]) for d in range(4)])
    out_other = [out_of[d, 1] for d in range(4)]
    kept, gus, out_other = lax.optimization_barrier((kept, gus, out_other))
    out_other = swap(jnp.stack(out_other), "core")
    pair_total = near_sum(kept)
    weight_grads = ffn_weights(
        [ffn_blocks[d][c] for d, c in ffn_order],
        [cot_blocks[d][c] for d, c in ffn_order],
        gus,
        acts,
    )
    pair_total, weight_grads, out_other = lax.optimization_barrier((pair_total, weight_grads, out_other))
    ffn_gain_part = jnp.sum(pair_total * scaled_ffn, axis=0)
    grad_hidden = cotangent.astype(F32) + rms_back(pair_total * gain_ffn, hidden, scale_ffn)
    grad_branch = grad_hidden.astype(BF16)
    weight_grads, out_other = lax.optimization_barrier((weight_grads, out_other, grad_branch))[:2]
    ffn_sum = lax.psum_scatter(
        weight_grads.reshape(2 * WIDTH, 3 * PART), WIDE, scatter_dimension=0, tiled=True
    )
    out_kept = jnp.stack([out_of[d, 0] for d in range(4)]).astype(F32) + out_other.astype(F32)
    out_kept = out_kept.astype(BF16)
    branches = [b for p in near_gather(grad_branch) for b in p]
    grad_mix = out_back(branches, w_out_t)
    out_total = near_sum(after([out_kept[d] for d in range(4)], branches))

    back_outs = back(plan, rot_q, start_lanes, kv_earlier + kv_own, grad_mix, out_tiles, lse)
    back_outs, out_total = lax.optimization_barrier((back_outs, out_total))
    grad_q, two_mine, two_theirs, one_mine, one_theirs, mine, theirs = back_outs
    grad_kvs = [
        mine,
        swap(theirs, "yhi"),
        shift_super(one_mine, -1, 0),
        shift_super(one_theirs, -1, 1),
        shift_super(two_mine, -2, 0),
        shift_super(two_theirs, -2, 1),
    ]

    grad_out = out_weights(after(mix, grad_q), branches)
    graw_q, q_gain_part = unproject_q(grad_q, raw, cos, sin, head_gain)
    sent_q = pack_q(normed, graw_q, grad_out)
    grad_kvs, sent_q = lax.optimization_barrier((grad_kvs, sent_q))
    got_q = exchange(sent_q.reshape(8, 192, 2 * QUERY), ("ylo", "z"))

    unprojected = [None] * 2
    for half in (1, 0):
        xs = all_tokens[4 * half : 4 * half + 4]
        unprojected[half] = unproject(half, graw_q, grad_kvs, raw, xs, qkv, cos, sin, head_gain)
    q_gain_part = q_gain_part[0, :HEAD] + q_gain_part[0, HEAD : 2 * HEAD] + q_gain_part[0, 2 * HEAD : QUERY]
    k_gain_part = (unprojected[0][6] + unprojected[1][6])[0, HEAD:]
    head_part = jnp.concatenate([q_gain_part, k_gain_part, jnp.zeros((4,), F32)])
    gain_parts = jnp.concatenate(
        [
            sum(u[5] for u in unprojected),
            ffn_gain_part[None],
            jnp.tile(head_part.reshape(12, 11).T, (1, 128)),
            jnp.zeros((3, WIDTH), F32),
        ],
        axis=0,
    )
    sent = pack_kv(normed, [u[4] for u in unprojected], gain_parts)
    parts = [u[2 * i : 2 * i + 2] for u in unprojected for i in (0, 1)]
    parts, sent = lax.optimization_barrier((parts, sent))
    grad_normed = near_sum(near_keep(parts))
    got = exchange(sent.reshape(8, 192, QUERY), ("ylo", "z"))

    def added(v):
        return jnp.sum(v.astype(F32), axis=0).astype(BF16).reshape(8, 24, -1)

    last = jnp.concatenate([ffn_sum.reshape(8, 24, 3 * PART), added(got_q), added(got)], axis=-1)
    last = exchange(last, NEAR)
    ffn_grad, got = last[:, :, : 3 * PART], last[:, :, 3 * PART :].astype(F32)

    grad_out = got[:, :, QUERY : 2 * QUERY]
    qkv_grad = jnp.concatenate([got[:, :, :QUERY], got[:, :, 2 * QUERY :]], axis=-1)
    here, there = jnp.where(yhi == 0, 0, 1), jnp.where(yhi == 0, 1, 0)

    def half_of(v, axis, which):
        size = v.shape[axis] // 2
        return lax.dynamic_slice_in_dim(v, which * size, size, axis)

    qkv_other = swap(half_of(qkv_grad, 1, there).astype(BF16), "yhi").astype(F32)
    out_other = swap(half_of(grad_out, 0, there).astype(BF16), "yhi").astype(F32)
    qkv_grad = half_of(qkv_grad, 1, here) + qkv_other
    grad_out = half_of(grad_out, 0, here) + out_other
    gains = jnp.sum(qkv_grad[:, :, 5 * HEAD :], axis=0)
    gains = gains[:, :16] + gains[:, 16:32]
    head_gains = gains[:, 2:13].reshape(-1)
    qkv_grad = jnp.transpose(qkv_grad, (1, 0, 2))
    w_out_grad = jnp.transpose(grad_out, (0, 2, 1)).reshape(768, 24)
    w_query_grad = qkv_grad[:, :, :QUERY].reshape(12, -1)
    w_value_grad = qkv_grad[:, :, QUERY : QUERY + HEAD].reshape(12, -1)
    w_key_grad = qkv_grad[:, :, QUERY + HEAD : QUERY + 2 * HEAD].reshape(12, -1)

    output = (hidden + out_total).astype(BF16)
    scale_attn = rms_scale(inputs)
    input_grad = (grad_hidden + rms_back(grad_normed * gain_attn, inputs, scale_attn)).astype(BF16)

    ffn_grad = jnp.transpose(ffn_grad, (1, 0, 2)).astype(F32)
    w_gate_grad, w_up_grad, w_down_grad = (
        ffn_grad[:, :, i * PART : (i + 1) * PART].reshape(24, -1) for i in range(3)
    )
    return (
        output,
        input_grad,
        gains[:, 0],
        w_query_grad,
        w_key_grad,
        w_value_grad,
        head_gains[:HEAD],
        head_gains[HEAD : 2 * HEAD],
        w_out_grad,
        gains[:, 1],
        w_gate_grad,
        w_up_grad,
        w_down_grad.T,
    )


def solution(mesh):
    mesh = Mesh(np.asarray(mesh.devices).reshape(2, 4, 4, 2, 2), ALL)
    rows = P(ALL, None)
    weights = (P("yhi", BLK), P(ALL), P(BLK, "yhi"), P(BLK, "yhi"), P("yhi", BLK))
    placed_in = (rows, P(), P(ALL), rows, rows, rows, P(), P()) + weights + (rows,)
    placed_out = (rows, rows, P(ALL), rows, rows, rows, P(), P()) + weights
    return jax.shard_map(
        per_device, mesh=mesh, in_specs=placed_in, out_specs=placed_out, check_vma=False
    )
```

```python
import functools

import jax
import jax.numpy as jnp
import numpy as np
from jax import lax
from jax.experimental import pallas as pl
from jax.experimental.pallas import tpu as pltpu
from jax.sharding import Mesh
from jax.sharding import PartitionSpec as P

EPS = 1e-05
THETA = 1000000.0
HEAD = 64
ROWS = 128
PAIR = 2 * ROWS
GROUP = 3
QUERY = GROUP * HEAD
LANES = PAIR * GROUP
KEY_TILE = 512
SUPER = 2048
EARLIER = 2 * SUPER
PART = 432
PADDED = 512
FREE = PADDED - PART
WIDTH = 1536
ALL = ("ylo", "z", "x", "core", "yhi")
BLK = ("ylo", "z", "x", "core")
WIDE = ("yhi", "ylo", "z")
NEAR = ("x", "core")
NN = (((1,), (0,)), ((), ()))
NT = (((1,), (1,)), ((), ()))
TN = (((0,), (0,)), ((), ()))
F32 = jnp.float32
BF16 = jnp.bfloat16
SCORE = HEAD**-0.5 * 1.4426950408889634


def dot(a, b, numbers=NN):
    return lax.dot_general(a, b, numbers, preferred_element_type=F32)


def rms_scale(v):
    return lax.rsqrt(jnp.mean(v * v, axis=-1, keepdims=True) + EPS)


def rms_back(grad, v, scale):
    inner = jnp.mean(grad * v, axis=-1, keepdims=True)
    return scale * (grad - v * scale * scale * inner)


def shift_x(v, distance):
    return lax.ppermute(v, "x", [((i + distance) % 4, i) for i in range(4)])


def swap(v, axis):
    return lax.ppermute(v, axis, [(0, 1), (1, 0)])


def shift_super(v, distance, other):
    pairs = [
        (2 * i + h, 2 * (i + distance) + (h + other) % 2)
        for i in range(8)
        for h in (0, 1)
        if 0 <= i + distance < 8
    ]
    return lax.ppermute(v, ("ylo", "z", "yhi"), pairs)


def exchange(v, axes):
    return lax.all_to_all(v, axes, split_axis=0, concat_axis=0, tiled=True)


def near_gather(v):
    blocks = [v] + [shift_x(v, d) for d in (1, 2, 3)]
    return [[b, swap(b, "core")] for b in blocks]


def near_keep(parts):
    return [
        (own.astype(F32) + swap(other, "core").astype(F32)).astype(BF16) for own, other in parts
    ]


def near_sum(kept):
    total = kept[0].astype(F32)
    for d in (1, 2, 3):
        total = total + shift_x(kept[d], -d).astype(F32)
    return total


def rel_to_abs(v, x, core):
    v = jnp.where(core == 0, v, v[:, ::-1])
    return lax.dynamic_slice_in_dim(jnp.concatenate([v, v], axis=0), (4 - x) % 4, 4, 0)


def abs_to_rel(v, x, core):
    v = jnp.where(core == 0, v, v[:, ::-1])
    return lax.dynamic_slice_in_dim(jnp.concatenate([v, v], axis=0), x, 4, 0)


def params(steps, mib):
    return pltpu.CompilerParams(
        dimension_semantics=("arbitrary",) * steps, vmem_limit_bytes=mib * 2**20
    )


def cost(flops, moved, exps=0):
    return pl.CostEstimate(flops=int(flops), bytes_accessed=int(moved), transcendentals=int(exps))


def all_of(*shape):
    return pl.BlockSpec(shape, lambda *i: (0,) * len(shape))


IN_VMEM = pl.BlockSpec(memory_space=pltpu.VMEM)


def stacked(a_ref, b_ref):
    return jnp.concatenate([a_ref[...], b_ref[...]], axis=0)


def head_sums(v):
    shape = (v.shape[1], v.shape[1])
    lane = lax.shift_right_logical(lax.broadcasted_iota(jnp.int32, shape, 1), 6)
    row = lax.shift_right_logical(lax.broadcasted_iota(jnp.int32, shape, 0), 6)
    ones = jnp.where(lane == row, 1.0, 0.0).astype(BF16)
    high = v.astype(BF16)
    low = (v - high.astype(F32)).astype(BF16)
    return dot(high, ones) + dot(low, ones)


def half_turn(v):
    lane = lax.broadcasted_iota(jnp.int32, v.shape, 1)
    return jnp.where(
        (lane & (HEAD - 1)) < HEAD // 2,
        pltpu.roll(v, v.shape[1] - HEAD // 2, 1),
        pltpu.roll(v, HEAD // 2, 1),
    )


def twice(v):
    return jnp.concatenate([v, v], axis=1)


def project_kernel(*refs):
    xs, (w_ref, gain_ref, cos_ref, sin_ref, head_gain_ref) = refs[:8], refs[8:13]
    normed_ref, q_ref, kv_ref, raw_ref = refs[13:]
    lane = lax.broadcasted_iota(jnp.int32, (PAIR, 2 * HEAD), 1)
    for d in range(4):
        rows = slice(d * PAIR, (d + 1) * PAIR)
        tiles = slice(2 * d, 2 * d + 2)
        x = stacked(*xs[tiles]).astype(F32)
        normed = (x * rms_scale(x) * gain_ref[...]).astype(BF16)
        normed_ref[rows, :] = normed
        raw = dot(normed, w_ref[...])
        heads = raw[:, : 4 * HEAD]
        raw_ref[d] = heads
        scale = lax.rsqrt(head_sums(heads * heads) * (1.0 / HEAD) + EPS)
        v = heads * scale * head_gain_ref[...]
        turned = v * twice(cos_ref[d]) + half_turn(v) * twice(sin_ref[d])
        q_ref[tiles] = turned[:, :QUERY].astype(BF16).reshape(2, ROWS, QUERY)
        kv = jnp.where(lane < HEAD, raw[:, 4 * HEAD :], turned[:, 2 * HEAD :])
        kv_ref[tiles] = kv.astype(BF16).reshape(2, ROWS, 2 * HEAD)


def project(xs, w, gain, cos, sin, head_gain):
    return pl.pallas_call(
        project_kernel,
        out_shape=(
            jax.ShapeDtypeStruct((4 * PAIR, WIDTH), BF16),
            jax.ShapeDtypeStruct((8, ROWS, QUERY), BF16),
            jax.ShapeDtypeStruct((8, ROWS, 2 * HEAD), BF16),
            jax.ShapeDtypeStruct((4, PAIR, 4 * HEAD), F32),
        ),
        in_specs=[IN_VMEM] * 13,
        out_specs=(IN_VMEM,) * 4,
        compiler_params=params(0, 20),
        cost_estimate=cost(8 * PAIR * WIDTH * 384, 1e7),
    )(*xs, w, gain, cos, sin, head_gain)


def turned_back(g, raw, cos, sin, head_gain):
    width = g.shape[1]
    g = g * cos - half_turn(g) * sin
    scale = lax.rsqrt(head_sums(raw * raw) * (1.0 / HEAD) + EPS)
    gain = jnp.sum(g * raw * scale, axis=0, keepdims=True)
    e = g * head_gain[:, -width:]
    inner = head_sums(e * raw) * (1.0 / HEAD)
    return scale * (e - raw * scale * scale * inner), gain


def unproject_q_kernel(gq_ref, raw_ref, cos_ref, sin_ref, head_gain_ref, graw_ref, gain_ref):
    gains = 0.0
    for d in range(4):
        g = gq_ref[2 * d : 2 * d + 2].reshape(PAIR, 4 * HEAD).astype(F32)
        graw, gain = turned_back(
            g, raw_ref[d], twice(cos_ref[d]), twice(sin_ref[d]), head_gain_ref[...]
        )
        graw_ref[d] = graw.astype(BF16)
        gains = gains + gain
    gain_ref[...] = gains


def unproject_q(gq, raw, cos, sin, head_gain):
    return pl.pallas_call(
        unproject_q_kernel,
        out_shape=(
            jax.ShapeDtypeStruct((4, PAIR, 4 * HEAD), BF16),
            jax.ShapeDtypeStruct((1, 4 * HEAD), F32),
        ),
        compiler_params=params(0, 20),
        cost_estimate=cost(1e8, 4e6),
    )(gq, raw, cos, sin, head_gain)


def unproject_kernel(half, *refs):
    graw_q_ref, g_refs, raw_ref, xs, (w_ref, cos_ref, sin_ref, head_gain_ref) = (
        refs[0], refs[1:7], refs[7], refs[8:12], refs[12:16],
    )
    parts, (gkv_ref, attn_ref, gain_ref) = refs[16:20], refs[20:]
    attn, gains = 0.0, 0.0
    lane = lax.broadcasted_iota(jnp.int32, (PAIR, 2 * HEAD), 1)
    for i in range(2):
        tiles = slice(2 * i, 2 * i + 2)
        at = 2 * half + i
        there = slice(2 * at, 2 * at + 2)
        gkv = g_refs[0][there].astype(F32)
        for ref in g_refs[1:]:
            gkv = gkv + ref[there].astype(F32)
        gkv = gkv.reshape(PAIR, 2 * HEAD)
        gk = jnp.where(lane < HEAD, 0.0, (gkv * HEAD**-0.5).astype(BF16).astype(F32))
        graw_k, gain = turned_back(
            gk, raw_ref[at][:, 2 * HEAD :], cos_ref[at], sin_ref[at], head_gain_ref[...]
        )
        gains = gains + gain
        graw_q = graw_q_ref[at].astype(F32)
        graw = [
            graw_q[:, : 2 * HEAD],
            jnp.where(lane < HEAD, graw_q[:, 2 * HEAD :], graw_k),
            jnp.where(lane < HEAD, gkv, 0.0),
        ]
        gkv_ref[i * PAIR : (i + 1) * PAIR, :] = jnp.where(lane < HEAD, gkv, graw_k).astype(BF16)
        grad = dot(jnp.concatenate(graw, axis=1).astype(BF16), w_ref[...], NT)
        x = stacked(*xs[tiles]).astype(F32)
        attn = attn + jnp.sum(grad * x * rms_scale(x), axis=0, keepdims=True)
        grad = grad.astype(BF16)
        parts[2 * i][...] = grad[:ROWS]
        parts[2 * i + 1][...] = grad[ROWS:]
    attn_ref[...] = attn
    gain_ref[...] = gains


def unproject(half, graw_q, gkvs, raw, xs, w, cos, sin, head_gain):
    outs = (jax.ShapeDtypeStruct((ROWS, WIDTH), BF16),) * 4 + (
        jax.ShapeDtypeStruct((2 * PAIR, 2 * HEAD), BF16),
        jax.ShapeDtypeStruct((1, WIDTH), F32),
        jax.ShapeDtypeStruct((1, 2 * HEAD), F32),
    )
    return pl.pallas_call(
        functools.partial(unproject_kernel, half),
        out_shape=outs,
        in_specs=[IN_VMEM] * 16,
        out_specs=(IN_VMEM,) * 7,
        compiler_params=params(0, 16),
        cost_estimate=cost(4 * PAIR * WIDTH * 384, 8e6),
    )(graw_q, *gkvs, raw, *xs, w, cos, sin, head_gain)


def ffn_kernel(
    x0_ref, x1_ref, c0_ref, c1_ref, w_ref, part0_ref, part1_ref, out0_ref, out1_ref, act_ref, gu_ref
):
    x, cot = stacked(x0_ref, x1_ref), stacked(c0_ref, c1_ref)
    own = lax.broadcasted_iota(jnp.int32, (PAIR, PADDED), 1) < PART
    part, out_part = 0.0, 0.0
    for y in range(2):
        gate_up = dot(x, w_ref[y, :, : 2 * PADDED])
        gate, up = gate_up[:, :PADDED], gate_up[:, PADDED:]
        grad_act = jnp.where(own, dot(cot, w_ref[y, :, 2 * PADDED :]), 0.0)
        sig = 1.0 / (1.0 + jnp.exp(-gate))
        silu = gate * sig
        act = jnp.where(own, silu * up, 0.0).astype(BF16)
        act_ref[y] = act
        out_part = out_part + dot(act, w_ref[y, :, 2 * PADDED :], NT)
        grad_gate = jnp.where(own, grad_act * up * sig * (1.0 + gate * (1.0 - sig)), 0.0)
        grad_up = jnp.where(own, grad_act * silu, 0.0)
        grads = jnp.concatenate([grad_gate, grad_up], axis=1).astype(BF16)
        gu_ref[y] = grads
        part = part + dot(grads, w_ref[y, :, : 2 * PADDED], NT)
    part, out_part = part.astype(BF16), out_part.astype(BF16)
    part0_ref[...] = part[:ROWS]
    part1_ref[...] = part[ROWS:]
    out0_ref[...] = out_part[:ROWS]
    out1_ref[...] = out_part[ROWS:]


def ffn(x0, x1, c0, c1, w):
    return pl.pallas_call(
        ffn_kernel,
        out_shape=(jax.ShapeDtypeStruct((ROWS, WIDTH), BF16),) * 4
        + (
            jax.ShapeDtypeStruct((2, PAIR, PADDED), BF16),
            jax.ShapeDtypeStruct((2, PAIR, 2 * PADDED), BF16),
        ),
        in_specs=[IN_VMEM] * 5,
        out_specs=(IN_VMEM,) * 6,
        compiler_params=params(0, 36),
        cost_estimate=cost(2 * 2 * PAIR * WIDTH * 6 * PADDED, 14e6),
    )(x0, x1, c0, c1, w)


def ffn_weights_kernel(*refs):
    xs, cs, gus, acts, out_ref = refs[:8], refs[8:16], refs[16:20], refs[20:24], refs[24]
    def all_tokens(refs):
        return jnp.concatenate([ref[...] for ref in refs], axis=0)

    grad_gu = dot(all_tokens(xs), all_tokens([g.at[0] for g in gus]), TN)
    grad_d = dot(all_tokens(cs), all_tokens([a.at[0] for a in acts]), TN)
    out_ref[0, :, :PART] = grad_gu[:, :PART].astype(BF16)
    out_ref[0, :, PART : 2 * PART] = grad_gu[:, PADDED : PADDED + PART].astype(BF16)
    out_ref[0, :, 2 * PART :] = grad_d[:, :PART].astype(BF16)


def ffn_weights(xs, cs, gus, acts):
    tall = 256
    rows = pl.BlockSpec((ROWS, tall), lambda y, m: (0, m))
    return pl.pallas_call(
        ffn_weights_kernel,
        out_shape=jax.ShapeDtypeStruct((2, WIDTH, 3 * PART), BF16),
        grid=(2, WIDTH // tall),
        in_specs=[rows] * 16
        + [pl.BlockSpec((1, PAIR, 2 * PADDED), lambda y, m: (y, 0, 0))] * 4
        + [pl.BlockSpec((1, PAIR, PADDED), lambda y, m: (y, 0, 0))] * 4,
        out_specs=pl.BlockSpec((1, tall, 3 * PART), lambda y, m: (y, m, 0)),
        compiler_params=params(2, 28),
        cost_estimate=cost(2 * 2 * 1024 * WIDTH * 3 * PADDED, 24e6),
    )(*xs, *cs, *gus, *acts)


def out_project_kernel(mix_ref, w_ref, part0_ref, part1_ref):
    part = dot(mix_ref[...].reshape(PAIR, QUERY), w_ref[...], NT).astype(BF16)
    part0_ref[...] = part[:ROWS]
    part1_ref[...] = part[ROWS:]


def out_project(d, mix, w):
    rows = pl.BlockSpec((ROWS, WIDTH), lambda i: (0, 0))
    return pl.pallas_call(
        out_project_kernel,
        out_shape=(jax.ShapeDtypeStruct((ROWS, WIDTH), BF16),) * 2,
        grid=(1,),
        in_specs=[
            pl.BlockSpec((2, ROWS, QUERY), lambda i: (d, 0, 0)),
            pl.BlockSpec((WIDTH, QUERY), lambda i: (0, 0)),
        ],
        out_specs=(rows, rows),
        compiler_params=params(1, 16),
        cost_estimate=cost(2 * PAIR * WIDTH * QUERY, 2e6),
    )(mix, w)


def out_back_kernel(w_ref, *refs):
    for t in range(8):
        refs[8][t] = dot(refs[t][...], w_ref[...]).astype(BF16)


def out_back(branches, w):
    return pl.pallas_call(
        out_back_kernel,
        out_shape=jax.ShapeDtypeStruct((8, ROWS, QUERY), BF16),
        compiler_params=params(0, 16),
        cost_estimate=cost(8 * PAIR * WIDTH * QUERY, 4e6),
    )(w, *branches)


def out_weights_kernel(mix_ref, *refs):
    branch = jnp.concatenate([b[...] for b in refs[:8]], axis=0)
    refs[8][...] = dot(branch, mix_ref[...].reshape(8 * ROWS, QUERY), TN)


def out_weights(mix, branches):
    return pl.pallas_call(
        out_weights_kernel,
        out_shape=jax.ShapeDtypeStruct((WIDTH, QUERY), F32),
        compiler_params=params(0, 24),
        cost_estimate=cost(2 * 1024 * WIDTH * QUERY, 4e6),
    )(mix, *branches)


def pack_q_kernel(normed_ref, graw_ref, out_grad_ref, sent_ref):
    graw = graw_ref[...].reshape(8 * ROWS, 4 * HEAD)
    sent_ref[:, :QUERY] = dot(normed_ref[...], graw, TN)[:, :QUERY].astype(BF16)
    sent_ref[:, QUERY:] = out_grad_ref[...].astype(BF16)


def pack_q(normed, graw, out_grad):
    tall = 256
    return pl.pallas_call(
        pack_q_kernel,
        out_shape=jax.ShapeDtypeStruct((WIDTH, 2 * QUERY), BF16),
        grid=(WIDTH // tall,),
        in_specs=[
            pl.BlockSpec((8 * ROWS, tall), lambda m: (0, m)),
            all_of(4, PAIR, 4 * HEAD),
            pl.BlockSpec((tall, QUERY), lambda m: (m, 0)),
        ],
        out_specs=pl.BlockSpec((tall, 2 * QUERY), lambda m: (m, 0)),
        compiler_params=params(1, 16),
        cost_estimate=cost(2 * 1024 * WIDTH * 256, 8e6),
    )(normed, graw, out_grad)


def pack_kv_kernel(normed_ref, gkv0_ref, gkv1_ref, gains_ref, sent_ref):
    grad = dot(normed_ref[...], stacked(gkv0_ref, gkv1_ref), TN)
    gains = gains_ref[...]
    high = gains.astype(BF16).astype(F32)
    gains = jnp.concatenate([high, gains - high, jnp.zeros((HEAD - 32, gains.shape[1]), F32)], axis=0)
    sent_ref[:, : 2 * HEAD] = grad.astype(BF16)
    sent_ref[:, 2 * HEAD :] = gains.T.astype(BF16)


def pack_kv(normed, gkvs, gains):
    tall = 256
    return pl.pallas_call(
        pack_kv_kernel,
        out_shape=jax.ShapeDtypeStruct((WIDTH, QUERY), BF16),
        grid=(WIDTH // tall,),
        in_specs=[
            pl.BlockSpec((8 * ROWS, tall), lambda m: (0, m)),
            all_of(4 * ROWS, 2 * HEAD),
            all_of(4 * ROWS, 2 * HEAD),
            pl.BlockSpec((16, tall), lambda m: (0, m)),
        ],
        out_specs=pl.BlockSpec((tall, QUERY), lambda m: (m, 0)),
        compiler_params=params(1, 16),
        cost_estimate=cost(2 * 1024 * WIDTH * 128, 6e6),
    )(normed, *gkvs, gains)


def to_lanes(v):
    parts = []
    for c in (0, 1):
        t = v[c].astype(F32).T
        parts += [t[g * HEAD : (g + 1) * HEAD] for g in range(GROUP)]
    return jnp.concatenate(parts, axis=1)


def from_lanes(t, c):
    at = [(c * GROUP + g) * ROWS for g in range(GROUP)]
    return jnp.concatenate([t[:, i : i + ROWS] for i in at], axis=0).T


def key_loops(plan, at, base, unrolls, start, visit, state):
    p = 2 * pl.program_id(0)
    lo, m1, hi = plan[p, at], plan[p + 1, at + 1], plan[p + 1, at + 3]
    m2 = jnp.maximum(plan[p, at + 2], m1)
    core = plan[0, 15]
    lane = lax.broadcasted_iota(jnp.int32, (1, LANES), 1)
    place = lax.rem(lane, ROWS) + jnp.where(lane < LANES // 2, plan[p + core, 0], plan[p + 1 - core, 0])

    def masked(j, state):
        key = lax.broadcasted_iota(jnp.int32, (KEY_TILE, LANES), 0) + (j * KEY_TILE + base)
        return visit(j, state, (key >= start) & (key <= place))

    state = lax.fori_loop(lo, m1, masked, state)
    done = m1
    for unroll in unrolls:
        steps = lax.div(m2 - done, unroll)

        def several(i, state, done=done, unroll=unroll):
            for k in range(unroll):
                state = visit(done + unroll * i + k, state, None)
            return state

        state = lax.fori_loop(0, steps, several, state)
        done = done + unroll * steps
    return lax.fori_loop(m2, hi, masked, state)


def rows_of(j):
    return pl.ds(pl.multiple_of(j * KEY_TILE, KEY_TILE), KEY_TILE)


def chunks(plan, supers):
    for b in range(supers):
        for half in (0, 1):
            for f in range(8):
                side = plan[0, 10] if half == 0 else 1 - plan[0, 10]
                yield b, half, pl.multiple_of(b * SUPER + f * PAIR + side * ROWS, ROWS), plan[f, 1]


def line_up(plan, kv_refs, kv, kvt):
    @pl.when(pl.program_id(0) == 0)
    def _():
        for b, half, place, sent in chunks(plan, len(kv_refs) // 2):
            block = kv_refs[2 * b + half][sent]
            kv[pl.ds(place, ROWS), :] = block
            kvt[:, pl.ds(place, ROWS)] = block.astype(F32).T.astype(BF16)


def attend_body(at, base, plan, q_ref, start_ref, kv, kvt, state):
    qt = to_lanes(q_ref)
    qt = jnp.concatenate([jnp.zeros_like(qt), qt], axis=0).astype(BF16)

    def visit(j, state, mask):
        total, accum = state
        weights = jnp.exp2(dot(kv[rows_of(j), :], qt) * SCORE)
        if mask is not None:
            weights = jnp.where(mask, weights, 0.0)
        total = total + jnp.sum(weights, axis=0, keepdims=True)
        return total, accum + dot(kvt[:HEAD, rows_of(j)], weights.astype(BF16))

    return key_loops(plan, at, base, (4, 2, 1), start_ref[0], visit, state)


def attend_own_kernel(plan, q_ref, start_ref, *refs):
    kv_refs, (accum_ref, total_ref, kv, kvt) = refs[:2], refs[2:]
    line_up(plan, kv_refs, kv, kvt)
    state = (jnp.zeros((1, LANES), F32), jnp.zeros((HEAD, LANES), F32))
    total, accum = attend_body(6, EARLIER, plan, q_ref, start_ref, kv, kvt, state)
    accum_ref[0] = accum
    total_ref[0] = total


def attend_earlier_kernel(plan, q_ref, start_ref, *refs):
    kv_refs, (accum_ref, total_ref, mix_ref, out_ref, lse_ref, kv, kvt) = refs[:4], refs[4:]
    line_up(plan, kv_refs, kv, kvt)
    state = (total_ref[0], accum_ref[0])
    total, accum = attend_body(2, 0, plan, q_ref, start_ref, kv, kvt, state)
    out = accum / total
    out_ref[0] = out
    for c in (0, 1):
        mix_ref[c] = from_lanes(out, c).astype(BF16)
    lse_ref[0] = jnp.log2(total)


def back_kernel(plan, q_ref, start_ref, *refs):
    kv_refs, (g_ref, out_ref, lse_ref, dq_ref), sent_refs, (kv, kvt, dkv) = (
        refs[:6], refs[6:10], refs[10:16], refs[16:],
    )
    line_up(plan, kv_refs, kv, kvt)

    @pl.when(pl.program_id(0) == 0)
    def _():
        dkv[...] = jnp.zeros_like(dkv)

    qt = to_lanes(q_ref)
    gt = to_lanes(g_ref)
    delta = jnp.sum(gt * out_ref[0], axis=0, keepdims=True)
    zero = jnp.zeros_like(qt)
    gt = jnp.concatenate([gt, zero], axis=0)
    qt = jnp.concatenate([zero, qt], axis=0)
    both_t = jnp.concatenate([gt, qt], axis=1).astype(BF16)
    both = jnp.concatenate([gt.T, qt.T], axis=0).astype(BF16)
    lse = lse_ref[0]

    def visit(j, dqt, mask):
        pair = dot(kv[rows_of(j), :], both_t)
        weights = jnp.exp2(pair[:, LANES:] * SCORE - lse)
        if mask is not None:
            weights = jnp.where(mask, weights, 0.0)
        grads = (weights * (pair[:, :LANES] - delta)).astype(BF16)
        sides = jnp.concatenate([weights.astype(BF16), grads], axis=1)
        dkv[rows_of(j), :] += dot(sides, both)
        return dqt + dot(kvt[HEAD:, rows_of(j)], grads)

    dqt = key_loops(plan, 11, 0, (4, 2, 1), start_ref[0], visit, jnp.zeros((HEAD, LANES), F32))
    for c in (0, 1):
        dq = from_lanes(dqt * HEAD**-0.5, c)
        dq_ref[c] = jnp.concatenate([dq, jnp.zeros((ROWS, HEAD), F32)], axis=1).astype(BF16)

    @pl.when(pl.program_id(0) == 3)
    def _():
        for b, half, place, sent in chunks(plan, 3):
            sent_refs[2 * b + half][sent] = dkv[pl.ds(place, ROWS), :].astype(BF16)


def whole(*shape):
    return pl.BlockSpec(shape, lambda f, plan: (0,) * len(shape))


def tile(*shape):
    return pl.BlockSpec((1,) + shape, lambda f, plan: (f,) + (0,) * len(shape))


def placed(*shape):
    return pl.BlockSpec((2,) + shape, lambda f, plan: (plan[2 * f, 16],) + (0,) * len(shape))


def tiles_call(kernel, supers, outs, more_ins, out_specs, flops, back):
    keys = supers * SUPER
    scratch = [pltpu.VMEM((keys, 2 * HEAD), BF16), pltpu.VMEM((2 * HEAD, keys), BF16)]
    if back:
        scratch.append(pltpu.VMEM((keys, 2 * HEAD), F32))
    ins = [placed(ROWS, QUERY), tile(1, LANES)] + [whole(8, ROWS, 2 * HEAD)] * (2 * supers)
    return pl.pallas_call(
        kernel,
        out_shape=outs,
        grid_spec=pltpu.PrefetchScalarGridSpec(
            num_scalar_prefetch=1,
            grid=(4,),
            in_specs=ins + more_ins,
            out_specs=out_specs,
            scratch_shapes=scratch,
        ),
        compiler_params=params(1, 30 if back else 20),
        cost_estimate=cost(flops, 8e6, 1e7),
    )


TILE_T = jax.ShapeDtypeStruct((4, HEAD, LANES), F32)
TILE_ROW = jax.ShapeDtypeStruct((4, 1, LANES), F32)
STATE = [tile(HEAD, LANES), tile(1, LANES)]


def attend_own(plan, q, start, kvs):
    call = tiles_call(attend_own_kernel, 1, (TILE_T, TILE_ROW), [], tuple(STATE), 4e9, False)
    return call(plan, q, start, *kvs)


def attend_earlier(plan, q, start, kvs, state):
    outs = (jax.ShapeDtypeStruct((8, ROWS, QUERY), BF16), TILE_T, TILE_ROW)
    specs = (placed(ROWS, QUERY),) + tuple(STATE)
    call = tiles_call(attend_earlier_kernel, 2, outs, STATE, specs, 8e9, False)
    return call(plan, q, start, *kvs, *state)


def back(plan, q, start, kvs, grad, out, lse):
    sent = jax.ShapeDtypeStruct((8, ROWS, 2 * HEAD), BF16)
    call = tiles_call(
        back_kernel,
        3,
        [jax.ShapeDtypeStruct((8, ROWS, 4 * HEAD), BF16)] + [sent] * 6,
        [placed(ROWS, QUERY)] + STATE,
        [placed(ROWS, 4 * HEAD)] + [whole(*sent.shape)] * 6,
        30e9,
        True,
    )
    return call(plan, q, start, *kvs, grad, out, lse)


def after(v, *others):
    return lax.optimization_barrier((v,) + others)[0]


def per_device(
    tokens,
    segments,
    attn_gain,
    w_query,
    w_key,
    w_value,
    q_gain,
    k_gain,
    w_out,
    ffn_gain,
    w_gate,
    w_up,
    w_down,
    cotangent,
):
    ylo, z, x, core, yhi = (lax.axis_index(a) for a in ALL)
    sup = ylo * 4 + z

    token_shifts = [shift_x(tokens, d) for d in (1, 2, 3)]
    token_blocks = [[b, swap(b, "core")] for b in [tokens] + token_shifts]
    all_tokens = [b for p in token_blocks for b in p]
    qkv_own = jnp.concatenate(
        [
            w_query.reshape(12, 8, QUERY),
            w_key.reshape(12, 8, HEAD),
            w_value.reshape(12, 8, HEAD),
            jnp.broadcast_to(attn_gain[:, None, None], (12, 8, 1)),
            jnp.broadcast_to(ffn_gain[:, None, None], (12, 8, 1)),
            jnp.zeros((12, 8, HEAD - 2), BF16),
        ],
        axis=-1,
    )
    qkv_own = jnp.pad(jnp.transpose(qkv_own, (1, 0, 2)), ((0, 0), (0, 12), (0, 0)))
    out_own = jnp.transpose(w_out.reshape(4, QUERY, 24), (0, 2, 1))
    out_own = jnp.pad(jnp.concatenate([out_own, out_own], axis=0), ((0, 0), (0, 0), (0, 3 * FREE - QUERY)))
    rows_own = jnp.concatenate(
        [
            part
            for i, w in enumerate((w_gate, w_up, w_down.T))
            for part in (
                w.reshape(24, 8, PART).transpose(1, 0, 2),
                out_own[:, :, i * FREE : (i + 1) * FREE],
            )
        ]
        + [qkv_own],
        axis=-1,
    )
    rows = exchange(rows_own, NEAR)
    ffn_rows = rows[:, :, : 3 * PADDED].reshape(192, 3 * PADDED)
    qkv_rows = rows[:, :12, 3 * PADDED :].reshape(1, 96, 6 * HEAD)
    qkv = exchange(jnp.broadcast_to(qkv_rows, (16, 96, 6 * HEAD)), WIDE)
    qkv = jnp.transpose(qkv.reshape(2, 8, 8, 12, 6 * HEAD), (1, 2, 0, 3, 4)).reshape(WIDTH, 6 * HEAD)
    ffn_full = lax.all_gather(ffn_rows, WIDE, axis=0, tiled=True).reshape(2, WIDTH, 3 * PADDED)
    gain_attn = qkv[:, 5 * HEAD].astype(F32)
    gain_ffn = qkv[:, 5 * HEAD + 1].astype(F32)

    token_index = jnp.arange(segments.shape[0], dtype=jnp.int32)
    begins = jnp.concatenate([jnp.ones((1,), jnp.bool_), segments[1:] != segments[:-1]])
    starts = lax.cummax(jnp.where(begins, token_index, 0), axis=0)
    own_starts = lax.dynamic_slice(
        starts.reshape(8, 8, 2, ROWS), (sup, 0, yhi, 0), (1, 8, 1, ROWS)
    ).reshape(8, ROWS)
    first = sup * SUPER + jnp.arange(8, dtype=jnp.int32) * PAIR + yhi * ROWS
    own_places = first[:, None] + jnp.arange(ROWS, dtype=jnp.int32)[None]
    positions = abs_to_rel((own_places - own_starts).reshape(4, 2, ROWS), x, core)
    frequency = THETA ** (-jnp.arange(HEAD // 2, dtype=F32) * 2.0 / HEAD)
    angles = positions.reshape(4, PAIR, 1).astype(F32) * frequency
    cosine, sine = jnp.cos(angles), jnp.sin(angles)
    cos = jnp.concatenate([cosine] * 4, axis=-1)
    sin = jnp.concatenate([-sine, sine] * 2, axis=-1)
    head_gain = jnp.concatenate([q_gain, q_gain, q_gain, k_gain]).astype(F32)[None]

    window = (sup - 2) * SUPER
    lo = (own_starts[:, 0] - window) // KEY_TILE
    hi = (first + ROWS - 1 - window) // KEY_TILE + 1
    m1 = jnp.clip((own_starts[:, -1] - window + KEY_TILE - 1) // KEY_TILE, lo, hi)
    m2 = jnp.clip((first + 1 - window) // KEY_TILE, m1, hi)
    order = jnp.arange(8, dtype=jnp.int32)
    relative = ((order // 2 - x) % 4) * 2 + (order % 2 + core) % 2
    edge = EARLIER // KEY_TILE
    plan = jnp.stack(
        [first - window, relative]
        + [jnp.minimum(v, edge) for v in (lo, m1, m2, hi)]
        + [jnp.maximum(v - edge, 0) for v in (lo, m1, m2, hi)]
        + [jnp.broadcast_to(yhi, (8,)), lo, m1, m2, hi]
        + [jnp.broadcast_to(core, (8,)), (order // 2 - x) % 4],
        axis=1,
    ).astype(jnp.int32)
    pair_starts = (own_starts - window).reshape(4, 2, 1, ROWS)
    pair_starts = jnp.where(core == 0, pair_starts, pair_starts[:, ::-1])
    start_lanes = jnp.broadcast_to(pair_starts, (4, 2, GROUP, ROWS)).reshape(4, 1, LANES)

    normed, rot_q, kv, raw = project(
        all_tokens, qkv, gain_attn[None], cos, sin, head_gain
    )

    cot_sent = after(cotangent, token_shifts)
    cot_shifts = [shift_x(cot_sent, d) for d in (1, 2, 3)]
    kv, cot_shifts = lax.optimization_barrier((kv, cot_shifts))

    kv_own = [kv, swap(kv, "yhi")]
    kv_sent = kv
    kv_earlier = [shift_super(kv_sent, a, b) for a, b in ((2, 0), (2, 1), (1, 0), (1, 1))]
    state = attend_own(plan, rot_q, start_lanes, kv_own)
    state, kv_earlier = lax.optimization_barrier((state, kv_earlier))
    mix, out_tiles, lse = attend_earlier(plan, rot_q, start_lanes, kv_earlier, state)
    w_out_t = jnp.concatenate(
        [
            lax.dynamic_slice(ffn_full, (x // 2, 0, i * PADDED + PART), (1, WIDTH, FREE))[0]
            for i in range(3)
        ],
        axis=1,
    )[:, :QUERY]
    w_out_t, mix = lax.optimization_barrier((w_out_t, mix))
    cot_blocks = [[b, swap(b, "core")] for b in after([cotangent] + cot_shifts, state)]
    mix, cot_blocks = lax.optimization_barrier((mix, cot_blocks))

    inputs = tokens.astype(F32)
    parts = [None] * 4
    for d in (2, 1, 3, 0):
        parts[d] = out_project(d, mix, w_out_t)
    hidden = inputs + near_sum(near_keep(parts))
    scale_ffn = rms_scale(hidden)
    scaled_ffn = hidden * scale_ffn
    normed_ffn = (scaled_ffn * gain_ffn).astype(BF16)

    ffn_other = swap(normed_ffn, "core")
    near = [shift_x(normed_ffn, d) for d in (1, 3)]
    far = shift_x(after(normed_ffn, ffn_other), 2)
    ffn_blocks = [[b, swap(b, "core")] for b in (near[0], far, near[1])]
    ffn_blocks = [[normed_ffn, ffn_other]] + ffn_blocks
    ffn_calls = [((0, 0), (0, 1)), ((1, 0), (3, 0)), ((2, 0), (1, 1)), ((3, 1), (2, 1))]
    ffn_order = [at for call in ffn_calls for at in call]
    ffn_outs, part_of, out_of = [], {}, {}
    for call in ffn_calls:
        blocks = [ffn_blocks[d][c] for d, c in call]
        if ffn_outs:
            blocks = after(blocks, ffn_outs[-1][0])
        ffn_outs.append(ffn(*blocks, *[cot_blocks[d][c] for d, c in call], ffn_full))
        for i, at in enumerate(call):
            part_of[at], out_of[at] = ffn_outs[-1][i], ffn_outs[-1][2 + i]
    acts, gus = [o[4] for o in ffn_outs], [o[5] for o in ffn_outs]
    kept = near_keep([(part_of[d, 0], part_of[d, 1]) for d in range(4)])
    out_other = [out_of[d, 1] for d in range(4)]
    kept, gus, out_other = lax.optimization_barrier((kept, gus, out_other))
    out_other = swap(jnp.stack(out_other), "core")
    pair_total = near_sum(kept)
    weight_grads = ffn_weights(
        [ffn_blocks[d][c] for d, c in ffn_order],
        [cot_blocks[d][c] for d, c in ffn_order],
        gus,
        acts,
    )
    pair_total, weight_grads, out_other = lax.optimization_barrier((pair_total, weight_grads, out_other))
    ffn_gain_part = jnp.sum(pair_total * scaled_ffn, axis=0)
    grad_hidden = cotangent.astype(F32) + rms_back(pair_total * gain_ffn, hidden, scale_ffn)
    grad_branch = grad_hidden.astype(BF16)
    weight_grads, out_other = lax.optimization_barrier((weight_grads, out_other, grad_branch))[:2]
    ffn_sum = lax.psum_scatter(
        weight_grads.reshape(2 * WIDTH, 3 * PART), WIDE, scatter_dimension=0, tiled=True
    )
    out_kept = jnp.stack([out_of[d, 0] for d in range(4)]).astype(F32) + out_other.astype(F32)
    out_kept = out_kept.astype(BF16)
    branches = [b for p in near_gather(grad_branch) for b in p]
    grad_mix = out_back(branches, w_out_t)
    out_total = near_sum(after([out_kept[d] for d in range(4)], branches))

    back_outs = back(plan, rot_q, start_lanes, kv_earlier + kv_own, grad_mix, out_tiles, lse)
    back_outs, out_total = lax.optimization_barrier((back_outs, out_total))
    grad_q, two_mine, two_theirs, one_mine, one_theirs, mine, theirs = back_outs
    grad_kvs = [
        mine,
        swap(theirs, "yhi"),
        shift_super(one_mine, -1, 0),
        shift_super(one_theirs, -1, 1),
        shift_super(two_mine, -2, 0),
        shift_super(two_theirs, -2, 1),
    ]

    grad_out = out_weights(after(mix, grad_q), branches)
    graw_q, q_gain_part = unproject_q(grad_q, raw, cos, sin, head_gain)
    sent_q = pack_q(normed, graw_q, grad_out)
    grad_kvs, sent_q = lax.optimization_barrier((grad_kvs, sent_q))
    got_q = exchange(sent_q.reshape(8, 192, 2 * QUERY), ("ylo", "z"))

    unprojected = [None] * 2
    for half in (1, 0):
        xs = all_tokens[4 * half : 4 * half + 4]
        unprojected[half] = unproject(half, graw_q, grad_kvs, raw, xs, qkv, cos, sin, head_gain)
    q_gain_part = q_gain_part[0, :HEAD] + q_gain_part[0, HEAD : 2 * HEAD] + q_gain_part[0, 2 * HEAD : QUERY]
    k_gain_part = (unprojected[0][6] + unprojected[1][6])[0, HEAD:]
    head_part = jnp.concatenate([q_gain_part, k_gain_part, jnp.zeros((4,), F32)])
    gain_parts = jnp.concatenate(
        [
            sum(u[5] for u in unprojected),
            ffn_gain_part[None],
            jnp.tile(head_part.reshape(12, 11).T, (1, 128)),
            jnp.zeros((3, WIDTH), F32),
        ],
        axis=0,
    )
    sent = pack_kv(normed, [u[4] for u in unprojected], gain_parts)
    parts = [u[2 * i : 2 * i + 2] for u in unprojected for i in (0, 1)]
    parts, sent = lax.optimization_barrier((parts, sent))
    grad_normed = near_sum(near_keep(parts))
    got = exchange(sent.reshape(8, 192, QUERY), ("ylo", "z"))

    def added(v):
        return jnp.sum(v.astype(F32), axis=0).astype(BF16).reshape(8, 24, -1)

    last = jnp.concatenate([ffn_sum.reshape(8, 24, 3 * PART), added(got_q), added(got)], axis=-1)
    last = exchange(last, NEAR)
    ffn_grad, got = last[:, :, : 3 * PART], last[:, :, 3 * PART :].astype(F32)

    grad_out = got[:, :, QUERY : 2 * QUERY]
    qkv_grad = jnp.concatenate([got[:, :, :QUERY], got[:, :, 2 * QUERY :]], axis=-1)
    here, there = jnp.where(yhi == 0, 0, 1), jnp.where(yhi == 0, 1, 0)

    def half_of(v, axis, which):
        size = v.shape[axis] // 2
        return lax.dynamic_slice_in_dim(v, which * size, size, axis)

    qkv_other = swap(half_of(qkv_grad, 1, there).astype(BF16), "yhi").astype(F32)
    out_other = swap(half_of(grad_out, 0, there).astype(BF16), "yhi").astype(F32)
    qkv_grad = half_of(qkv_grad, 1, here) + qkv_other
    grad_out = half_of(grad_out, 0, here) + out_other
    gains = jnp.sum(qkv_grad[:, :, 5 * HEAD :], axis=0)
    gains = gains[:, :16] + gains[:, 16:32]
    head_gains = gains[:, 2:13].reshape(-1)
    qkv_grad = jnp.transpose(qkv_grad, (1, 0, 2))
    w_out_grad = jnp.transpose(grad_out, (0, 2, 1)).reshape(768, 24)
    w_query_grad = qkv_grad[:, :, :QUERY].reshape(12, -1)
    w_value_grad = qkv_grad[:, :, QUERY : QUERY + HEAD].reshape(12, -1)
    w_key_grad = qkv_grad[:, :, QUERY + HEAD : QUERY + 2 * HEAD].reshape(12, -1)

    output = (hidden + out_total).astype(BF16)
    scale_attn = rms_scale(inputs)
    input_grad = (grad_hidden + rms_back(grad_normed * gain_attn, inputs, scale_attn)).astype(BF16)

    ffn_grad = jnp.transpose(ffn_grad, (1, 0, 2)).astype(F32)
    w_gate_grad, w_up_grad, w_down_grad = (
        ffn_grad[:, :, i * PART : (i + 1) * PART].reshape(24, -1) for i in range(3)
    )
    return (
        output,
        input_grad,
        gains[:, 0],
        w_query_grad,
        w_key_grad,
        w_value_grad,
        head_gains[:HEAD],
        head_gains[HEAD : 2 * HEAD],
        w_out_grad,
        gains[:, 1],
        w_gate_grad,
        w_up_grad,
        w_down_grad.T,
    )


def solution(mesh):
    mesh = Mesh(np.asarray(mesh.devices).reshape(2, 4, 4, 2, 2), ALL)
    rows = P(ALL, None)
    weights = (P("yhi", BLK), P(ALL), P(BLK, "yhi"), P(BLK, "yhi"), P("yhi", BLK))
    placed_in = (rows, P(), P(ALL), rows, rows, rows, P(), P()) + weights + (rows,)
    placed_out = (rows, rows, P(ALL), rows, rows, rows, P(), P()) + weights
    return jax.shard_map(
        per_device, mesh=mesh, in_specs=placed_in, out_specs=placed_out, check_vma=False
    )
```

```python
import functools

import jax
import jax.numpy as jnp
import numpy as np
from jax import lax
from jax.experimental import pallas as pl
from jax.experimental.pallas import tpu as pltpu
from jax.sharding import Mesh
from jax.sharding import PartitionSpec as P

EPS = 1e-05
THETA = 1000000.0
HEAD = 64
ROWS = 128
PAIR = 2 * ROWS
GROUP = 3
QUERY = GROUP * HEAD
LANES = PAIR * GROUP
KEY_TILE = 512
SUPER = 2048
EARLIER = 2 * SUPER
PART = 432
PADDED = 512
FREE = PADDED - PART
WIDTH = 1536
ALL = ("ylo", "z", "x", "core", "yhi")
BLK = ("ylo", "z", "x", "core")
WIDE = ("yhi", "ylo", "z")
NEAR = ("x", "core")
NN = (((1,), (0,)), ((), ()))
NT = (((1,), (1,)), ((), ()))
TN = (((0,), (0,)), ((), ()))
F32 = jnp.float32
BF16 = jnp.bfloat16
SCORE = HEAD**-0.5 * 1.4426950408889634


def dot(a, b, numbers=NN):
    return lax.dot_general(a, b, numbers, preferred_element_type=F32)


def rms_scale(v):
    return lax.rsqrt(jnp.mean(v * v, axis=-1, keepdims=True) + EPS)


def rms_back(grad, v, scale):
    inner = jnp.mean(grad * v, axis=-1, keepdims=True)
    return scale * (grad - v * scale * scale * inner)


def shift_x(v, distance):
    return lax.ppermute(v, "x", [((i + distance) % 4, i) for i in range(4)])


def swap(v, axis):
    return lax.ppermute(v, axis, [(0, 1), (1, 0)])


def shift_super(v, distance, other):
    pairs = [
        (2 * i + h, 2 * (i + distance) + (h + other) % 2)
        for i in range(8)
        for h in (0, 1)
        if 0 <= i + distance < 8
    ]
    return lax.ppermute(v, ("ylo", "z", "yhi"), pairs)


def exchange(v, axes):
    return lax.all_to_all(v, axes, split_axis=0, concat_axis=0, tiled=True)


def near_gather(v):
    blocks = [v] + [shift_x(v, d) for d in (1, 2, 3)]
    return [[b, swap(b, "core")] for b in blocks]


def near_keep(parts):
    return [
        (own.astype(F32) + swap(other, "core").astype(F32)).astype(BF16) for own, other in parts
    ]


def near_sum(kept):
    total = kept[0].astype(F32)
    for d in (1, 2, 3):
        total = total + shift_x(kept[d], -d).astype(F32)
    return total


def rel_to_abs(v, x, core):
    v = jnp.where(core == 0, v, v[:, ::-1])
    return lax.dynamic_slice_in_dim(jnp.concatenate([v, v], axis=0), (4 - x) % 4, 4, 0)


def abs_to_rel(v, x, core):
    v = jnp.where(core == 0, v, v[:, ::-1])
    return lax.dynamic_slice_in_dim(jnp.concatenate([v, v], axis=0), x, 4, 0)


def params(steps, mib):
    return pltpu.CompilerParams(
        dimension_semantics=("arbitrary",) * steps, vmem_limit_bytes=mib * 2**20
    )


def cost(flops, moved, exps=0):
    return pl.CostEstimate(flops=int(flops), bytes_accessed=int(moved), transcendentals=int(exps))


def all_of(*shape):
    return pl.BlockSpec(shape, lambda *i: (0,) * len(shape))


IN_VMEM = pl.BlockSpec(memory_space=pltpu.VMEM)


def stacked(a_ref, b_ref):
    return jnp.concatenate([a_ref[...], b_ref[...]], axis=0)


def head_sums(v):
    shape = (v.shape[1], v.shape[1])
    lane = lax.shift_right_logical(lax.broadcasted_iota(jnp.int32, shape, 1), 6)
    row = lax.shift_right_logical(lax.broadcasted_iota(jnp.int32, shape, 0), 6)
    ones = jnp.where(lane == row, 1.0, 0.0).astype(BF16)
    high = v.astype(BF16)
    low = (v - high.astype(F32)).astype(BF16)
    return dot(high, ones) + dot(low, ones)


def half_turn(v):
    lane = lax.broadcasted_iota(jnp.int32, v.shape, 1)
    return jnp.where(
        (lane & (HEAD - 1)) < HEAD // 2,
        pltpu.roll(v, v.shape[1] - HEAD // 2, 1),
        pltpu.roll(v, HEAD // 2, 1),
    )


def twice(v):
    return jnp.concatenate([v, v], axis=1)


def project_kernel(*refs):
    xs, (w_ref, gain_ref, cos_ref, sin_ref, head_gain_ref) = refs[:8], refs[8:13]
    normed_ref, q_ref, kv_ref, raw_ref = refs[13:]
    lane = lax.broadcasted_iota(jnp.int32, (PAIR, 2 * HEAD), 1)
    for d in range(4):
        rows = slice(d * PAIR, (d + 1) * PAIR)
        tiles = slice(2 * d, 2 * d + 2)
        x = stacked(*xs[tiles]).astype(F32)
        normed = (x * rms_scale(x) * gain_ref[...]).astype(BF16)
        normed_ref[rows, :] = normed
        raw = dot(normed, w_ref[...])
        heads = raw[:, : 4 * HEAD]
        raw_ref[d] = heads
        scale = lax.rsqrt(head_sums(heads * heads) * (1.0 / HEAD) + EPS)
        v = heads * scale * head_gain_ref[...]
        turned = v * twice(cos_ref[d]) + half_turn(v) * twice(sin_ref[d])
        q_ref[tiles] = turned[:, :QUERY].astype(BF16).reshape(2, ROWS, QUERY)
        kv = jnp.where(lane < HEAD, raw[:, 4 * HEAD :], turned[:, 2 * HEAD :])
        kv_ref[tiles] = kv.astype(BF16).reshape(2, ROWS, 2 * HEAD)


def project(xs, w, gain, cos, sin, head_gain):
    return pl.pallas_call(
        project_kernel,
        out_shape=(
            jax.ShapeDtypeStruct((4 * PAIR, WIDTH), BF16),
            jax.ShapeDtypeStruct((8, ROWS, QUERY), BF16),
            jax.ShapeDtypeStruct((8, ROWS, 2 * HEAD), BF16),
            jax.ShapeDtypeStruct((4, PAIR, 4 * HEAD), F32),
        ),
        in_specs=[IN_VMEM] * 13,
        out_specs=(IN_VMEM,) * 4,
        compiler_params=params(0, 20),
        cost_estimate=cost(8 * PAIR * WIDTH * 384, 1e7),
    )(*xs, w, gain, cos, sin, head_gain)


def turned_back(g, raw, cos, sin, head_gain):
    width = g.shape[1]
    g = g * cos - half_turn(g) * sin
    scale = lax.rsqrt(head_sums(raw * raw) * (1.0 / HEAD) + EPS)
    gain = jnp.sum(g * raw * scale, axis=0, keepdims=True)
    e = g * head_gain[:, -width:]
    inner = head_sums(e * raw) * (1.0 / HEAD)
    return scale * (e - raw * scale * scale * inner), gain


def unproject_q_kernel(gq_ref, raw_ref, cos_ref, sin_ref, head_gain_ref, graw_ref, gain_ref):
    gains = 0.0
    for d in range(4):
        g = gq_ref[2 * d : 2 * d + 2].reshape(PAIR, 4 * HEAD).astype(F32)
        graw, gain = turned_back(
            g, raw_ref[d], twice(cos_ref[d]), twice(sin_ref[d]), head_gain_ref[...]
        )
        graw_ref[d] = graw.astype(BF16)
        gains = gains + gain
    gain_ref[...] = gains


def unproject_q(gq, raw, cos, sin, head_gain):
    return pl.pallas_call(
        unproject_q_kernel,
        out_shape=(
            jax.ShapeDtypeStruct((4, PAIR, 4 * HEAD), BF16),
            jax.ShapeDtypeStruct((1, 4 * HEAD), F32),
        ),
        compiler_params=params(0, 20),
        cost_estimate=cost(1e8, 4e6),
    )(gq, raw, cos, sin, head_gain)


def unproject_kernel(half, *refs):
    graw_q_ref, g_refs, raw_ref, xs, (w_ref, cos_ref, sin_ref, head_gain_ref) = (
        refs[0], refs[1:7], refs[7], refs[8:12], refs[12:16],
    )
    parts, (gkv_ref, attn_ref, gain_ref) = refs[16:20], refs[20:]
    attn, gains = 0.0, 0.0
    lane = lax.broadcasted_iota(jnp.int32, (PAIR, 2 * HEAD), 1)
    for i in range(2):
        tiles = slice(2 * i, 2 * i + 2)
        at = 2 * half + i
        there = slice(2 * at, 2 * at + 2)
        gkv = g_refs[0][there].astype(F32)
        for ref in g_refs[1:]:
            gkv = gkv + ref[there].astype(F32)
        gkv = gkv.reshape(PAIR, 2 * HEAD)
        gk = jnp.where(lane < HEAD, 0.0, (gkv * HEAD**-0.5).astype(BF16).astype(F32))
        graw_k, gain = turned_back(
            gk, raw_ref[at][:, 2 * HEAD :], cos_ref[at], sin_ref[at], head_gain_ref[...]
        )
        gains = gains + gain
        graw_q = graw_q_ref[at].astype(F32)
        graw = [
            graw_q[:, : 2 * HEAD],
            jnp.where(lane < HEAD, graw_q[:, 2 * HEAD :], graw_k),
            jnp.where(lane < HEAD, gkv, 0.0),
        ]
        gkv_ref[i * PAIR : (i + 1) * PAIR, :] = jnp.where(lane < HEAD, gkv, graw_k).astype(BF16)
        grad = dot(jnp.concatenate(graw, axis=1).astype(BF16), w_ref[...], NT)
        x = stacked(*xs[tiles]).astype(F32)
        attn = attn + jnp.sum(grad * x * rms_scale(x), axis=0, keepdims=True)
        grad = grad.astype(BF16)
        parts[2 * i][...] = grad[:ROWS]
        parts[2 * i + 1][...] = grad[ROWS:]
    attn_ref[...] = attn
    gain_ref[...] = gains


def unproject(half, graw_q, gkvs, raw, xs, w, cos, sin, head_gain):
    outs = (jax.ShapeDtypeStruct((ROWS, WIDTH), BF16),) * 4 + (
        jax.ShapeDtypeStruct((2 * PAIR, 2 * HEAD), BF16),
        jax.ShapeDtypeStruct((1, WIDTH), F32),
        jax.ShapeDtypeStruct((1, 2 * HEAD), F32),
    )
    return pl.pallas_call(
        functools.partial(unproject_kernel, half),
        out_shape=outs,
        in_specs=[IN_VMEM] * 16,
        out_specs=(IN_VMEM,) * 7,
        compiler_params=params(0, 16),
        cost_estimate=cost(4 * PAIR * WIDTH * 384, 8e6),
    )(graw_q, *gkvs, raw, *xs, w, cos, sin, head_gain)


def ffn_kernel(
    x0_ref, x1_ref, c0_ref, c1_ref, w_ref, part0_ref, part1_ref, out0_ref, out1_ref, act_ref, gu_ref
):
    x, cot = stacked(x0_ref, x1_ref), stacked(c0_ref, c1_ref)
    own = lax.broadcasted_iota(jnp.int32, (PAIR, PADDED), 1) < PART
    part, out_part = 0.0, 0.0
    for y in range(2):
        gate_up = dot(x, w_ref[y, :, : 2 * PADDED])
        gate, up = gate_up[:, :PADDED], gate_up[:, PADDED:]
        grad_act = jnp.where(own, dot(cot, w_ref[y, :, 2 * PADDED :]), 0.0)
        sig = 1.0 / (1.0 + jnp.exp(-gate))
        silu = gate * sig
        act = jnp.where(own, silu * up, 0.0).astype(BF16)
        act_ref[y] = act
        out_part = out_part + dot(act, w_ref[y, :, 2 * PADDED :], NT)
        grad_gate = jnp.where(own, grad_act * up * sig * (1.0 + gate * (1.0 - sig)), 0.0)
        grad_up = jnp.where(own, grad_act * silu, 0.0)
        grads = jnp.concatenate([grad_gate, grad_up], axis=1).astype(BF16)
        gu_ref[y] = grads
        part = part + dot(grads, w_ref[y, :, : 2 * PADDED], NT)
    part, out_part = part.astype(BF16), out_part.astype(BF16)
    part0_ref[...] = part[:ROWS]
    part1_ref[...] = part[ROWS:]
    out0_ref[...] = out_part[:ROWS]
    out1_ref[...] = out_part[ROWS:]


def ffn(x0, x1, c0, c1, w):
    return pl.pallas_call(
        ffn_kernel,
        out_shape=(jax.ShapeDtypeStruct((ROWS, WIDTH), BF16),) * 4
        + (
            jax.ShapeDtypeStruct((2, PAIR, PADDED), BF16),
            jax.ShapeDtypeStruct((2, PAIR, 2 * PADDED), BF16),
        ),
        in_specs=[IN_VMEM] * 5,
        out_specs=(IN_VMEM,) * 6,
        compiler_params=params(0, 36),
        cost_estimate=cost(2 * 2 * PAIR * WIDTH * 6 * PADDED, 14e6),
    )(x0, x1, c0, c1, w)


def ffn_weights_kernel(*refs):
    xs, cs, gus, acts, out_ref = refs[:8], refs[8:16], refs[16:20], refs[20:24], refs[24]
    def all_tokens(refs):
        return jnp.concatenate([ref[...] for ref in refs], axis=0)

    grad_gu = dot(all_tokens(xs), all_tokens([g.at[0] for g in gus]), TN)
    grad_d = dot(all_tokens(cs), all_tokens([a.at[0] for a in acts]), TN)
    out_ref[0, :, :PART] = grad_gu[:, :PART].astype(BF16)
    out_ref[0, :, PART : 2 * PART] = grad_gu[:, PADDED : PADDED + PART].astype(BF16)
    out_ref[0, :, 2 * PART :] = grad_d[:, :PART].astype(BF16)


def ffn_weights(xs, cs, gus, acts):
    tall = 256
    rows = pl.BlockSpec((ROWS, tall), lambda y, m: (0, m))
    return pl.pallas_call(
        ffn_weights_kernel,
        out_shape=jax.ShapeDtypeStruct((2, WIDTH, 3 * PART), BF16),
        grid=(2, WIDTH // tall),
        in_specs=[rows] * 16
        + [pl.BlockSpec((1, PAIR, 2 * PADDED), lambda y, m: (y, 0, 0))] * 4
        + [pl.BlockSpec((1, PAIR, PADDED), lambda y, m: (y, 0, 0))] * 4,
        out_specs=pl.BlockSpec((1, tall, 3 * PART), lambda y, m: (y, m, 0)),
        compiler_params=params(2, 28),
        cost_estimate=cost(2 * 2 * 1024 * WIDTH * 3 * PADDED, 24e6),
    )(*xs, *cs, *gus, *acts)


def out_project_kernel(mix_ref, w_ref, part0_ref, part1_ref):
    part = dot(mix_ref[...].reshape(PAIR, QUERY), w_ref[...], NT).astype(BF16)
    part0_ref[...] = part[:ROWS]
    part1_ref[...] = part[ROWS:]


def out_project(d, mix, w):
    rows = pl.BlockSpec((ROWS, WIDTH), lambda i: (0, 0))
    return pl.pallas_call(
        out_project_kernel,
        out_shape=(jax.ShapeDtypeStruct((ROWS, WIDTH), BF16),) * 2,
        grid=(1,),
        in_specs=[
            pl.BlockSpec((2, ROWS, QUERY), lambda i: (d, 0, 0)),
            pl.BlockSpec((WIDTH, QUERY), lambda i: (0, 0)),
        ],
        out_specs=(rows, rows),
        compiler_params=params(1, 16),
        cost_estimate=cost(2 * PAIR * WIDTH * QUERY, 2e6),
    )(mix, w)


def out_back_kernel(w_ref, *refs):
    for t in range(8):
        refs[8][t] = dot(refs[t][...], w_ref[...]).astype(BF16)


def out_back(branches, w):
    return pl.pallas_call(
        out_back_kernel,
        out_shape=jax.ShapeDtypeStruct((8, ROWS, QUERY), BF16),
        compiler_params=params(0, 16),
        cost_estimate=cost(8 * PAIR * WIDTH * QUERY, 4e6),
    )(w, *branches)


def out_weights_kernel(mix_ref, *refs):
    branch = jnp.concatenate([b[...] for b in refs[:8]], axis=0)
    refs[8][...] = dot(branch, mix_ref[...].reshape(8 * ROWS, QUERY), TN)


def out_weights(mix, branches):
    return pl.pallas_call(
        out_weights_kernel,
        out_shape=jax.ShapeDtypeStruct((WIDTH, QUERY), F32),
        compiler_params=params(0, 24),
        cost_estimate=cost(2 * 1024 * WIDTH * QUERY, 4e6),
    )(mix, *branches)


def pack_q_kernel(normed_ref, graw_ref, out_grad_ref, sent_ref):
    graw = graw_ref[...].reshape(8 * ROWS, 4 * HEAD)
    sent_ref[:, :QUERY] = dot(normed_ref[...], graw, TN)[:, :QUERY].astype(BF16)
    sent_ref[:, QUERY:] = out_grad_ref[...].astype(BF16)


def pack_q(normed, graw, out_grad):
    tall = 512
    return pl.pallas_call(
        pack_q_kernel,
        out_shape=jax.ShapeDtypeStruct((WIDTH, 2 * QUERY), BF16),
        grid=(WIDTH // tall,),
        in_specs=[
            pl.BlockSpec((8 * ROWS, tall), lambda m: (0, m)),
            all_of(4, PAIR, 4 * HEAD),
            pl.BlockSpec((tall, QUERY), lambda m: (m, 0)),
        ],
        out_specs=pl.BlockSpec((tall, 2 * QUERY), lambda m: (m, 0)),
        compiler_params=params(1, 16),
        cost_estimate=cost(2 * 1024 * WIDTH * 256, 8e6),
    )(normed, graw, out_grad)


def pack_kv_kernel(normed_ref, gkv0_ref, gkv1_ref, gains_ref, sent_ref):
    grad = dot(normed_ref[...], stacked(gkv0_ref, gkv1_ref), TN)
    gains = gains_ref[...]
    high = gains.astype(BF16).astype(F32)
    gains = jnp.concatenate([high, gains - high, jnp.zeros((HEAD - 32, gains.shape[1]), F32)], axis=0)
    sent_ref[:, : 2 * HEAD] = grad.astype(BF16)
    sent_ref[:, 2 * HEAD :] = gains.T.astype(BF16)


def pack_kv(normed, gkvs, gains):
    tall = 512
    return pl.pallas_call(
        pack_kv_kernel,
        out_shape=jax.ShapeDtypeStruct((WIDTH, QUERY), BF16),
        grid=(WIDTH // tall,),
        in_specs=[
            pl.BlockSpec((8 * ROWS, tall), lambda m: (0, m)),
            all_of(4 * ROWS, 2 * HEAD),
            all_of(4 * ROWS, 2 * HEAD),
            pl.BlockSpec((16, tall), lambda m: (0, m)),
        ],
        out_specs=pl.BlockSpec((tall, QUERY), lambda m: (m, 0)),
        compiler_params=params(1, 16),
        cost_estimate=cost(2 * 1024 * WIDTH * 128, 6e6),
    )(normed, *gkvs, gains)


def to_lanes(v):
    parts = []
    for c in (0, 1):
        t = v[c].astype(F32).T
        parts += [t[g * HEAD : (g + 1) * HEAD] for g in range(GROUP)]
    return jnp.concatenate(parts, axis=1)


def from_lanes(t, c):
    at = [(c * GROUP + g) * ROWS for g in range(GROUP)]
    return jnp.concatenate([t[:, i : i + ROWS] for i in at], axis=0).T


def key_loops(plan, at, base, unrolls, start, visit, state):
    p = 2 * pl.program_id(0)
    lo, m1, hi = plan[p, at], plan[p + 1, at + 1], plan[p + 1, at + 3]
    m2 = jnp.maximum(plan[p, at + 2], m1)
    core = plan[0, 15]
    lane = lax.broadcasted_iota(jnp.int32, (1, LANES), 1)
    place = lax.rem(lane, ROWS) + jnp.where(lane < LANES // 2, plan[p + core, 0], plan[p + 1 - core, 0])

    def masked(j, state):
        key = lax.broadcasted_iota(jnp.int32, (KEY_TILE, LANES), 0) + (j * KEY_TILE + base)
        return visit(j, state, (key >= start) & (key <= place))

    state = lax.fori_loop(lo, m1, masked, state)
    done = m1
    for unroll in unrolls:
        steps = lax.div(m2 - done, unroll)

        def several(i, state, done=done, unroll=unroll):
            for k in range(unroll):
                state = visit(done + unroll * i + k, state, None)
            return state

        state = lax.fori_loop(0, steps, several, state)
        done = done + unroll * steps
    return lax.fori_loop(m2, hi, masked, state)


def rows_of(j):
    return pl.ds(pl.multiple_of(j * KEY_TILE, KEY_TILE), KEY_TILE)


def chunks(plan, supers):
    for b in range(supers):
        for half in (0, 1):
            for f in range(8):
                side = plan[0, 10] if half == 0 else 1 - plan[0, 10]
                yield b, half, pl.multiple_of(b * SUPER + f * PAIR + side * ROWS, ROWS), plan[f, 1]


def line_up(plan, kv_refs, kv, kvt):
    @pl.when(pl.program_id(0) == 0)
    def _():
        for b, half, place, sent in chunks(plan, len(kv_refs) // 2):
            block = kv_refs[2 * b + half][sent]
            kv[pl.ds(place, ROWS), :] = block
            kvt[:, pl.ds(place, ROWS)] = block.astype(F32).T.astype(BF16)


def attend_body(at, base, plan, q_ref, start_ref, kv, kvt, state):
    qt = to_lanes(q_ref)
    qt = jnp.concatenate([jnp.zeros_like(qt), qt], axis=0).astype(BF16)

    def visit(j, state, mask):
        total, accum = state
        weights = jnp.exp2(dot(kv[rows_of(j), :], qt) * SCORE)
        if mask is not None:
            weights = jnp.where(mask, weights, 0.0)
        total = total + jnp.sum(weights, axis=0, keepdims=True)
        return total, accum + dot(kvt[:HEAD, rows_of(j)], weights.astype(BF16))

    return key_loops(plan, at, base, (8, 4, 2, 1), start_ref[0], visit, state)


def attend_own_kernel(plan, q_ref, start_ref, *refs):
    kv_refs, (accum_ref, total_ref, kv, kvt) = refs[:2], refs[2:]
    line_up(plan, kv_refs, kv, kvt)
    state = (jnp.zeros((1, LANES), F32), jnp.zeros((HEAD, LANES), F32))
    total, accum = attend_body(6, EARLIER, plan, q_ref, start_ref, kv, kvt, state)
    accum_ref[0] = accum
    total_ref[0] = total


def attend_earlier_kernel(plan, q_ref, start_ref, *refs):
    kv_refs, (accum_ref, total_ref, mix_ref, out_ref, lse_ref, kv, kvt) = refs[:4], refs[4:]
    line_up(plan, kv_refs, kv, kvt)
    state = (total_ref[0], accum_ref[0])
    total, accum = attend_body(2, 0, plan, q_ref, start_ref, kv, kvt, state)
    out = accum / total
    out_ref[0] = out
    for c in (0, 1):
        mix_ref[c] = from_lanes(out, c).astype(BF16)
    lse_ref[0] = jnp.log2(total)


def back_kernel(plan, q_ref, start_ref, *refs):
    kv_refs, (g_ref, out_ref, lse_ref, dq_ref), sent_refs, (kv, kvt, dkv) = (
        refs[:6], refs[6:10], refs[10:16], refs[16:],
    )
    line_up(plan, kv_refs, kv, kvt)

    @pl.when(pl.program_id(0) == 0)
    def _():
        dkv[...] = jnp.zeros_like(dkv)

    qt = to_lanes(q_ref)
    gt = to_lanes(g_ref)
    delta = jnp.sum(gt * out_ref[0], axis=0, keepdims=True)
    zero = jnp.zeros_like(qt)
    gt = jnp.concatenate([gt, zero], axis=0)
    qt = jnp.concatenate([zero, qt], axis=0)
    both_t = jnp.concatenate([gt, qt], axis=1).astype(BF16)
    both = jnp.concatenate([gt.T, qt.T], axis=0).astype(BF16)
    lse = lse_ref[0]

    def visit(j, dqt, mask):
        pair = dot(kv[rows_of(j), :], both_t)
        weights = jnp.exp2(pair[:, LANES:] * SCORE - lse)
        if mask is not None:
            weights = jnp.where(mask, weights, 0.0)
        grads = (weights * (pair[:, :LANES] - delta)).astype(BF16)
        sides = jnp.concatenate([weights.astype(BF16), grads], axis=1)
        dkv[rows_of(j), :] += dot(sides, both)
        return dqt + dot(kvt[HEAD:, rows_of(j)], grads)

    dqt = key_loops(plan, 11, 0, (4, 2, 1), start_ref[0], visit, jnp.zeros((HEAD, LANES), F32))
    for c in (0, 1):
        dq = from_lanes(dqt * HEAD**-0.5, c)
        dq_ref[c] = jnp.concatenate([dq, jnp.zeros((ROWS, HEAD), F32)], axis=1).astype(BF16)

    @pl.when(pl.program_id(0) == 3)
    def _():
        for b, half, place, sent in chunks(plan, 3):
            sent_refs[2 * b + half][sent] = dkv[pl.ds(place, ROWS), :].astype(BF16)


def whole(*shape):
    return pl.BlockSpec(shape, lambda f, plan: (0,) * len(shape))


def tile(*shape):
    return pl.BlockSpec((1,) + shape, lambda f, plan: (f,) + (0,) * len(shape))


def placed(*shape):
    return pl.BlockSpec((2,) + shape, lambda f, plan: (plan[2 * f, 16],) + (0,) * len(shape))


def tiles_call(kernel, supers, outs, more_ins, out_specs, flops, back):
    keys = supers * SUPER
    scratch = [pltpu.VMEM((keys, 2 * HEAD), BF16), pltpu.VMEM((2 * HEAD, keys), BF16)]
    if back:
        scratch.append(pltpu.VMEM((keys, 2 * HEAD), F32))
    ins = [placed(ROWS, QUERY), tile(1, LANES)] + [whole(8, ROWS, 2 * HEAD)] * (2 * supers)
    return pl.pallas_call(
        kernel,
        out_shape=outs,
        grid_spec=pltpu.PrefetchScalarGridSpec(
            num_scalar_prefetch=1,
            grid=(4,),
            in_specs=ins + more_ins,
            out_specs=out_specs,
            scratch_shapes=scratch,
        ),
        compiler_params=params(1, 30 if back else 20),
        cost_estimate=cost(flops, 8e6, 1e7),
    )


TILE_T = jax.ShapeDtypeStruct((4, HEAD, LANES), F32)
TILE_ROW = jax.ShapeDtypeStruct((4, 1, LANES), F32)
STATE = [tile(HEAD, LANES), tile(1, LANES)]


def attend_own(plan, q, start, kvs):
    call = tiles_call(attend_own_kernel, 1, (TILE_T, TILE_ROW), [], tuple(STATE), 4e9, False)
    return call(plan, q, start, *kvs)


def attend_earlier(plan, q, start, kvs, state):
    outs = (jax.ShapeDtypeStruct((8, ROWS, QUERY), BF16), TILE_T, TILE_ROW)
    specs = (placed(ROWS, QUERY),) + tuple(STATE)
    call = tiles_call(attend_earlier_kernel, 2, outs, STATE, specs, 8e9, False)
    return call(plan, q, start, *kvs, *state)


def back(plan, q, start, kvs, grad, out, lse):
    sent = jax.ShapeDtypeStruct((8, ROWS, 2 * HEAD), BF16)
    call = tiles_call(
        back_kernel,
        3,
        [jax.ShapeDtypeStruct((8, ROWS, 4 * HEAD), BF16)] + [sent] * 6,
        [placed(ROWS, QUERY)] + STATE,
        [placed(ROWS, 4 * HEAD)] + [whole(*sent.shape)] * 6,
        30e9,
        True,
    )
    return call(plan, q, start, *kvs, grad, out, lse)


def after(v, *others):
    return lax.optimization_barrier((v,) + others)[0]


def per_device(
    tokens,
    segments,
    attn_gain,
    w_query,
    w_key,
    w_value,
    q_gain,
    k_gain,
    w_out,
    ffn_gain,
    w_gate,
    w_up,
    w_down,
    cotangent,
):
    ylo, z, x, core, yhi = (lax.axis_index(a) for a in ALL)
    sup = ylo * 4 + z

    token_shifts = [shift_x(tokens, d) for d in (1, 2, 3)]
    token_blocks = [[b, swap(b, "core")] for b in [tokens] + token_shifts]
    all_tokens = [b for p in token_blocks for b in p]
    qkv_own = jnp.concatenate(
        [
            w_query.reshape(12, 8, QUERY),
            w_key.reshape(12, 8, HEAD),
            w_value.reshape(12, 8, HEAD),
            jnp.broadcast_to(attn_gain[:, None, None], (12, 8, 1)),
            jnp.broadcast_to(ffn_gain[:, None, None], (12, 8, 1)),
            jnp.zeros((12, 8, HEAD - 2), BF16),
        ],
        axis=-1,
    )
    qkv_own = jnp.pad(jnp.transpose(qkv_own, (1, 0, 2)), ((0, 0), (0, 12), (0, 0)))
    out_own = jnp.transpose(w_out.reshape(4, QUERY, 24), (0, 2, 1))
    out_own = jnp.pad(jnp.concatenate([out_own, out_own], axis=0), ((0, 0), (0, 0), (0, 3 * FREE - QUERY)))
    rows_own = jnp.concatenate(
        [
            part
            for i, w in enumerate((w_gate, w_up, w_down.T))
            for part in (
                w.reshape(24, 8, PART).transpose(1, 0, 2),
                out_own[:, :, i * FREE : (i + 1) * FREE],
            )
        ]
        + [qkv_own],
        axis=-1,
    )
    rows = exchange(rows_own, NEAR)
    ffn_rows = rows[:, :, : 3 * PADDED].reshape(192, 3 * PADDED)
    qkv_rows = rows[:, :12, 3 * PADDED :].reshape(1, 96, 6 * HEAD)
    qkv = exchange(jnp.broadcast_to(qkv_rows, (16, 96, 6 * HEAD)), WIDE)
    qkv = jnp.transpose(qkv.reshape(2, 8, 8, 12, 6 * HEAD), (1, 2, 0, 3, 4)).reshape(WIDTH, 6 * HEAD)
    ffn_full = lax.all_gather(ffn_rows, WIDE, axis=0, tiled=True).reshape(2, WIDTH, 3 * PADDED)
    gain_attn = qkv[:, 5 * HEAD].astype(F32)
    gain_ffn = qkv[:, 5 * HEAD + 1].astype(F32)

    token_index = jnp.arange(segments.shape[0], dtype=jnp.int32)
    begins = jnp.concatenate([jnp.ones((1,), jnp.bool_), segments[1:] != segments[:-1]])
    starts = lax.cummax(jnp.where(begins, token_index, 0), axis=0)
    own_starts = lax.dynamic_slice(
        starts.reshape(8, 8, 2, ROWS), (sup, 0, yhi, 0), (1, 8, 1, ROWS)
    ).reshape(8, ROWS)
    first = sup * SUPER + jnp.arange(8, dtype=jnp.int32) * PAIR + yhi * ROWS
    own_places = first[:, None] + jnp.arange(ROWS, dtype=jnp.int32)[None]
    positions = abs_to_rel((own_places - own_starts).reshape(4, 2, ROWS), x, core)
    frequency = THETA ** (-jnp.arange(HEAD // 2, dtype=F32) * 2.0 / HEAD)
    angles = positions.reshape(4, PAIR, 1).astype(F32) * frequency
    cosine, sine = jnp.cos(angles), jnp.sin(angles)
    cos = jnp.concatenate([cosine] * 4, axis=-1)
    sin = jnp.concatenate([-sine, sine] * 2, axis=-1)
    head_gain = jnp.concatenate([q_gain, q_gain, q_gain, k_gain]).astype(F32)[None]

    window = (sup - 2) * SUPER
    lo = (own_starts[:, 0] - window) // KEY_TILE
    hi = (first + ROWS - 1 - window) // KEY_TILE + 1
    m1 = jnp.clip((own_starts[:, -1] - window + KEY_TILE - 1) // KEY_TILE, lo, hi)
    m2 = jnp.clip((first + 1 - window) // KEY_TILE, m1, hi)
    order = jnp.arange(8, dtype=jnp.int32)
    relative = ((order // 2 - x) % 4) * 2 + (order % 2 + core) % 2
    edge = EARLIER // KEY_TILE
    plan = jnp.stack(
        [first - window, relative]
        + [jnp.minimum(v, edge) for v in (lo, m1, m2, hi)]
        + [jnp.maximum(v - edge, 0) for v in (lo, m1, m2, hi)]
        + [jnp.broadcast_to(yhi, (8,)), lo, m1, m2, hi]
        + [jnp.broadcast_to(core, (8,)), (order // 2 - x) % 4],
        axis=1,
    ).astype(jnp.int32)
    pair_starts = (own_starts - window).reshape(4, 2, 1, ROWS)
    pair_starts = jnp.where(core == 0, pair_starts, pair_starts[:, ::-1])
    start_lanes = jnp.broadcast_to(pair_starts, (4, 2, GROUP, ROWS)).reshape(4, 1, LANES)

    normed, rot_q, kv, raw = project(
        all_tokens, qkv, gain_attn[None], cos, sin, head_gain
    )

    cot_sent = after(cotangent, token_shifts)
    cot_shifts = [shift_x(cot_sent, d) for d in (1, 2, 3)]
    kv, cot_shifts = lax.optimization_barrier((kv, cot_shifts))

    kv_own = [kv, swap(kv, "yhi")]
    kv_sent = kv
    kv_earlier = [shift_super(kv_sent, a, b) for a, b in ((2, 0), (2, 1), (1, 0), (1, 1))]
    state = attend_own(plan, rot_q, start_lanes, kv_own)
    state, kv_earlier = lax.optimization_barrier((state, kv_earlier))
    mix, out_tiles, lse = attend_earlier(plan, rot_q, start_lanes, kv_earlier, state)
    w_out_t = jnp.concatenate(
        [
            lax.dynamic_slice(ffn_full, (x // 2, 0, i * PADDED + PART), (1, WIDTH, FREE))[0]
            for i in range(3)
        ],
        axis=1,
    )[:, :QUERY]
    w_out_t, mix = lax.optimization_barrier((w_out_t, mix))
    cot_blocks = [[b, swap(b, "core")] for b in after([cotangent] + cot_shifts, state)]
    mix, cot_blocks = lax.optimization_barrier((mix, cot_blocks))

    inputs = tokens.astype(F32)
    parts = [None] * 4
    for d in (2, 1, 3, 0):
        parts[d] = out_project(d, mix, w_out_t)
    hidden = inputs + near_sum(near_keep(parts))
    scale_ffn = rms_scale(hidden)
    scaled_ffn = hidden * scale_ffn
    normed_ffn = (scaled_ffn * gain_ffn).astype(BF16)

    ffn_other = swap(normed_ffn, "core")
    near = [shift_x(normed_ffn, d) for d in (1, 3)]
    far = shift_x(after(normed_ffn, ffn_other), 2)
    ffn_blocks = [[b, swap(b, "core")] for b in (near[0], far, near[1])]
    ffn_blocks = [[normed_ffn, ffn_other]] + ffn_blocks
    ffn_calls = [((0, 0), (0, 1)), ((1, 0), (3, 0)), ((2, 0), (1, 1)), ((3, 1), (2, 1))]
    ffn_order = [at for call in ffn_calls for at in call]
    ffn_outs, part_of, out_of = [], {}, {}
    for call in ffn_calls:
        blocks = [ffn_blocks[d][c] for d, c in call]
        if ffn_outs:
            blocks = after(blocks, ffn_outs[-1][0])
        ffn_outs.append(ffn(*blocks, *[cot_blocks[d][c] for d, c in call], ffn_full))
        for i, at in enumerate(call):
            part_of[at], out_of[at] = ffn_outs[-1][i], ffn_outs[-1][2 + i]
    acts, gus = [o[4] for o in ffn_outs], [o[5] for o in ffn_outs]
    kept = near_keep([(part_of[d, 0], part_of[d, 1]) for d in range(4)])
    out_other = [out_of[d, 1] for d in range(4)]
    kept, gus, out_other = lax.optimization_barrier((kept, gus, out_other))
    out_other = swap(jnp.stack(out_other), "core")
    pair_total = near_sum(kept)
    weight_grads = ffn_weights(
        [ffn_blocks[d][c] for d, c in ffn_order],
        [cot_blocks[d][c] for d, c in ffn_order],
        gus,
        acts,
    )
    pair_total, weight_grads, out_other = lax.optimization_barrier((pair_total, weight_grads, out_other))
    ffn_gain_part = jnp.sum(pair_total * scaled_ffn, axis=0)
    grad_hidden = cotangent.astype(F32) + rms_back(pair_total * gain_ffn, hidden, scale_ffn)
    grad_branch = grad_hidden.astype(BF16)
    weight_grads, out_other = lax.optimization_barrier((weight_grads, out_other, grad_branch))[:2]
    ffn_sum = lax.psum_scatter(
        weight_grads.reshape(2 * WIDTH, 3 * PART), WIDE, scatter_dimension=0, tiled=True
    )
    out_kept = jnp.stack([out_of[d, 0] for d in range(4)]).astype(F32) + out_other.astype(F32)
    out_kept = out_kept.astype(BF16)
    branches = [b for p in near_gather(grad_branch) for b in p]
    grad_mix = out_back(branches, w_out_t)
    out_total = near_sum(after([out_kept[d] for d in range(4)], branches))

    back_outs = back(plan, rot_q, start_lanes, kv_earlier + kv_own, grad_mix, out_tiles, lse)
    back_outs, out_total = lax.optimization_barrier((back_outs, out_total))
    grad_q, two_mine, two_theirs, one_mine, one_theirs, mine, theirs = back_outs
    grad_kvs = [
        mine,
        swap(theirs, "yhi"),
        shift_super(one_mine, -1, 0),
        shift_super(one_theirs, -1, 1),
        shift_super(two_mine, -2, 0),
        shift_super(two_theirs, -2, 1),
    ]

    grad_out = out_weights(after(mix, grad_q), branches)
    graw_q, q_gain_part = unproject_q(grad_q, raw, cos, sin, head_gain)
    sent_q = pack_q(normed, graw_q, grad_out)
    grad_kvs, sent_q = lax.optimization_barrier((grad_kvs, sent_q))
    got_q = exchange(sent_q.reshape(8, 192, 2 * QUERY), ("ylo", "z"))

    unprojected = [None] * 2
    for half in (1, 0):
        xs = all_tokens[4 * half : 4 * half + 4]
        unprojected[half] = unproject(half, graw_q, grad_kvs, raw, xs, qkv, cos, sin, head_gain)
    q_gain_part = q_gain_part[0, :HEAD] + q_gain_part[0, HEAD : 2 * HEAD] + q_gain_part[0, 2 * HEAD : QUERY]
    k_gain_part = (unprojected[0][6] + unprojected[1][6])[0, HEAD:]
    head_part = jnp.concatenate([q_gain_part, k_gain_part, jnp.zeros((4,), F32)])
    gain_parts = jnp.concatenate(
        [
            sum(u[5] for u in unprojected),
            ffn_gain_part[None],
            jnp.tile(head_part.reshape(12, 11).T, (1, 128)),
            jnp.zeros((3, WIDTH), F32),
        ],
        axis=0,
    )
    sent = pack_kv(normed, [u[4] for u in unprojected], gain_parts)
    parts = [u[2 * i : 2 * i + 2] for u in unprojected for i in (0, 1)]
    parts, sent = lax.optimization_barrier((parts, sent))
    grad_normed = near_sum(near_keep(parts))
    got = exchange(sent.reshape(8, 192, QUERY), ("ylo", "z"))

    def added(v):
        return jnp.sum(v.astype(F32), axis=0).astype(BF16).reshape(8, 24, -1)

    last = jnp.concatenate([ffn_sum.reshape(8, 24, 3 * PART), added(got_q), added(got)], axis=-1)
    last = exchange(last, NEAR)
    ffn_grad, got = last[:, :, : 3 * PART], last[:, :, 3 * PART :].astype(F32)

    grad_out = got[:, :, QUERY : 2 * QUERY]
    qkv_grad = jnp.concatenate([got[:, :, :QUERY], got[:, :, 2 * QUERY :]], axis=-1)
    here, there = jnp.where(yhi == 0, 0, 1), jnp.where(yhi == 0, 1, 0)

    def half_of(v, axis, which):
        size = v.shape[axis] // 2
        return lax.dynamic_slice_in_dim(v, which * size, size, axis)

    qkv_other = swap(half_of(qkv_grad, 1, there).astype(BF16), "yhi").astype(F32)
    out_other = swap(half_of(grad_out, 0, there).astype(BF16), "yhi").astype(F32)
    qkv_grad = half_of(qkv_grad, 1, here) + qkv_other
    grad_out = half_of(grad_out, 0, here) + out_other
    gains = jnp.sum(qkv_grad[:, :, 5 * HEAD :], axis=0)
    gains = gains[:, :16] + gains[:, 16:32]
    head_gains = gains[:, 2:13].reshape(-1)
    qkv_grad = jnp.transpose(qkv_grad, (1, 0, 2))
    w_out_grad = jnp.transpose(grad_out, (0, 2, 1)).reshape(768, 24)
    w_query_grad = qkv_grad[:, :, :QUERY].reshape(12, -1)
    w_value_grad = qkv_grad[:, :, QUERY : QUERY + HEAD].reshape(12, -1)
    w_key_grad = qkv_grad[:, :, QUERY + HEAD : QUERY + 2 * HEAD].reshape(12, -1)

    output = (hidden + out_total).astype(BF16)
    scale_attn = rms_scale(inputs)
    input_grad = (grad_hidden + rms_back(grad_normed * gain_attn, inputs, scale_attn)).astype(BF16)

    ffn_grad = jnp.transpose(ffn_grad, (1, 0, 2)).astype(F32)
    w_gate_grad, w_up_grad, w_down_grad = (
        ffn_grad[:, :, i * PART : (i + 1) * PART].reshape(24, -1) for i in range(3)
    )
    return (
        output,
        input_grad,
        gains[:, 0],
        w_query_grad,
        w_key_grad,
        w_value_grad,
        head_gains[:HEAD],
        head_gains[HEAD : 2 * HEAD],
        w_out_grad,
        gains[:, 1],
        w_gate_grad,
        w_up_grad,
        w_down_grad.T,
    )


def solution(mesh):
    mesh = Mesh(np.asarray(mesh.devices).reshape(2, 4, 4, 2, 2), ALL)
    rows = P(ALL, None)
    weights = (P("yhi", BLK), P(ALL), P(BLK, "yhi"), P(BLK, "yhi"), P("yhi", BLK))
    placed_in = (rows, P(), P(ALL), rows, rows, rows, P(), P()) + weights + (rows,)
    placed_out = (rows, rows, P(ALL), rows, rows, rows, P(), P()) + weights
    return jax.shard_map(
        per_device, mesh=mesh, in_specs=placed_in, out_specs=placed_out, check_vma=False
    )
```
